128 devices in a mesh: ctx: 32 (over z, x, y_hi), tp: 4 (over y_lo, core).
Axes of the slice: x: 4, y: 4 (y_hi: 2, y_lo: 2; y = y_hi * 2 + y_lo), z: 4, core: 2. Of those that a mesh axis runs over, the one named last changes fastest.
Arguments:
- block_input: bfloat16 [2, 4096, 1024], P(None, 'ctx'), may hold values from -40 to 40
- cotangent: bfloat16 [2, 4096, 1024], P(None, 'ctx'), may hold values from -6 to 6
- w_query: bfloat16 [1024, 1024], P('ctx', 'tp'), may hold values from -0.1875 to 0.1875
- key_weight: bfloat16 [1024, 512], P('ctx', 'tp'), may hold values from -0.1875 to 0.1875
- w_value: bfloat16 [1024, 512], P('ctx', 'tp'), may hold values from -0.1875 to 0.1875
- w_out: bfloat16 [1024, 1024], P('ctx', 'tp'), may hold values from -2 to 2
- w_gate: bfloat16 [1024, 4608], P('ctx', 'tp'), may hold values from -0.1875 to 0.1875
- w_up: bfloat16 [1024, 4608], P('ctx', 'tp'), may hold values from -0.1875 to 0.1875
- w_down: bfloat16 [1024, 4608], P('ctx', 'tp'), may hold values from -0.09375 to 0.09375
- norm_gains: bfloat16 [2, 1024], P(None, 'ctx'), may hold values from 0.5 to 1.5
- head_gains: bfloat16 [2, 64], P(None, 'ctx'), may hold values from 0.5 to 1.5
Outputs:
- block_output: bfloat16 [2, 4096, 1024], P(None, 'ctx')
- input_grad: float32 [2, 4096, 1024], P(None, 'ctx')
- grad_query: float32 [1024, 1024], P('ctx', 'tp')
- grad_key: float32 [1024, 512], P('ctx', 'tp')
- grad_value: float32 [1024, 512], P('ctx', 'tp')
- grad_out: float32 [1024, 1024], P('ctx', 'tp')
- grad_gate: float32 [1024, 4608], P('ctx', 'tp')
- grad_up: float32 [1024, 4608], P('ctx', 'tp')
- grad_down: float32 [1024, 4608], P('ctx', 'tp')
- grad_norm_gains: float32 [2, 1024], P(None, 'ctx')
- grad_head_gains: float32 [2, 64], P(None, 'ctx')
The draws below stay inside these ranges and needn't reach their ends.
All inputs are finite; a program needn't handle non-finite values.
Results may differ from the reference program's by a relative error of at most 0.035.
Values may be sent and summed in bfloat16 or wider, within the bound.
A program may use at most 128 MiB of HBM per device.

```python
import math
import jax
import jax.numpy as jnp
from jax import lax

D = 1024
QUERY_HEADS = 16
KEY_VALUE_HEADS = 8
HEAD_SIZE = 64
FF = 4608
SEQS = 2
QD = 1024
KD = 512
LENGTH = 4096


def draw_block_input(key, part):
    noise_key, row_key, column_key = jax.random.split(key, 3)
    noise = jnp.clip(jax.random.normal(noise_key, (SEQS, LENGTH, D), jnp.float32), -4.0, 4.0)
    row_scale = jnp.exp(jax.random.uniform(row_key, (SEQS, LENGTH, 1), jnp.float32, 0.0, 2.4))
    column_scale = jnp.exp(jax.random.uniform(column_key, (1, 1, D), jnp.float32, 0.0, 2.4))
    return (noise * row_scale * column_scale * 0.08).astype(jnp.bfloat16)


def strengthened(drawn, key, source, target, blocks, factor):
    owner, partner = [(jnp.arange(drawn.shape[position]) // (drawn.shape[position] // blocks)).reshape([-1 if axis == position else 1 for axis in range(drawn.ndim)]) for position in (source, target)]
    chosen = jax.random.permutation(key, blocks)[partner]
    strong = (owner == chosen) | (owner == (partner + blocks // 2) % blocks)
    return jnp.where(strong, factor * drawn, drawn)


def levels(stream_key, dims, cuts, smallest, high):
    def one(axis_at, parts):
        steps = jax.random.uniform(jax.random.fold_in(jax.random.fold_in(stream_key, 6), axis_at), (parts,), jnp.float32, smallest / len(cuts), high / len(cuts))
        return jnp.repeat(jnp.exp(steps), dims[axis_at] // parts).reshape((-1,) + (1,) * (len(dims) - axis_at - 1))

    gain = one(*cuts[0])
    for cut in cuts[1:]:
        gain = gain * one(*cut)
    return gain


def centred(stream_key, extent, scale, limit, shards=(), kind=jnp.bfloat16):
    entries = jax.random.normal(stream_key, extent, jnp.float32) * scale
    if len(shards) > 0:
        entries = levels(stream_key, extent, shards, -0.22, 0.18) * entries
    return jnp.clip(entries, min=-limit, max=limit).astype(kind)


def heavy_noise(rng, extent, deviation, limit, cuts, heavy, held_as=jnp.bfloat16):
    array = deviation * jax.random.normal(rng, extent, jnp.float32)
    if cuts:
        array = array * levels(rng, extent, cuts, -0.22, 0.18)
    return jnp.clip(strengthened(array, jax.random.fold_in(rng, 3), *heavy), -limit, limit).astype(held_as)


def setup_inputs(seed: int = 0) -> dict:
    keys = jax.random.split(jax.random.key(seed), 12)
    return {
        "block_input": draw_block_input(jax.random.fold_in(keys[11], 71), 0),
        "cotangent": heavy_noise(keys[1], (SEQS, LENGTH, D), 1.0, 6.0, ((1, 32),), (1, 2, 32, 2.75)),
        "w_query": centred(keys[2], (D, QD), D ** -0.5, 0.1875, ((0, 32), (1, 4))),
        "key_weight": centred(keys[3], (D, KD), D ** -0.5, 0.1875, ((0, 32), (1, 4))),
        "w_value": centred(keys[4], (D, KD), D ** -0.5, 0.1875, ((0, 32), (1, 4))),
        "w_out": centred(keys[5], (D, QD), (max(QD * 32 // LENGTH, 1)) ** -0.5, 2.0, ((0, 32), (1, 4))),
        "w_gate": centred(keys[6], (D, FF), D ** -0.5, 0.1875, ((0, 32), (1, 4))),
        "w_up": centred(keys[7], (D, FF), D ** -0.5, 0.1875, ((0, 32), (1, 4))),
        "w_down": centred(keys[8], (D, FF), FF ** -0.5, 0.09375, ((0, 32), (1, 4))),
        "norm_gains": jnp.clip(1.0 + 0.1 * jax.random.normal(keys[9], (2, D), jnp.float32), 0.5, 1.5).astype(jnp.bfloat16),
        "head_gains": jnp.clip(1.0 + 0.1 * jax.random.normal(keys[10], (2, HEAD_SIZE), jnp.float32), 0.5, 1.5).astype(jnp.bfloat16),
    }


EPSILON = 1e-06
ROPE_BASE = 1000000.0

def rounded_value(value_rows):
    return lax.optimization_barrier(value_rows.astype(jnp.bfloat16))

def widened_heads(value_rows):
    return value_rows.astype(jnp.float32)

def rms_scale(value_rows):
    return lax.rsqrt(lax.optimization_barrier(jnp.mean(value_rows * value_rows, axis=-1, keepdims=True)) + EPSILON)

def rope_tables(sequence_length, offset, width):
    half_width = width // 2
    inverse = ROPE_BASE ** (-(jnp.arange(half_width, dtype=jnp.float32) * 2.0 / width))
    places = (offset + jnp.arange(sequence_length, dtype=jnp.int32)).astype(jnp.float32)
    angles = places[:, None] * inverse[None, :]
    return (jnp.cos(angles), jnp.sin(angles))

def rotary_apply(value_rows, cosine_table, sine_table, direction):
    half_width = value_rows.shape[-1] // 2
    former = value_rows[..., :half_width]
    latter = value_rows[..., half_width:]
    cosine = cosine_table[:, None, :]
    sine = sine_table[:, None, :] * direction
    return jnp.concatenate([former * cosine - latter * sine, latter * cosine + former * sine], axis=-1)

def head_norm(value_rows, gain_row):
    hatted = value_rows * rms_scale(value_rows)
    return (hatted * gain_row, hatted)

def head_norm_reverse(grads, value_rows, hatted, gain_row):
    scaled = grads * gain_row
    return rms_scale(value_rows) * (scaled - hatted * lax.optimization_barrier(jnp.mean(scaled * hatted, axis=-1, keepdims=True)))

def row_norm_back(grads, normed, scale_rows, gain_row):
    scaled = grads * gain_row
    return scale_rows * (scaled - normed * lax.optimization_barrier(jnp.mean(scaled * normed, axis=-1, keepdims=True)))

def one_sequence(block_input, cotangent, w_query, key_weight, w_value, w_out, w_gate, w_up, w_down, norm_gains, head_gains):
    sequence_length = block_input.shape[0]
    query_group_count = QUERY_HEADS // KEY_VALUE_HEADS
    score_scale = HEAD_SIZE ** (-0.5)
    inputs = block_input.astype(jnp.float32)
    gain_attn = norm_gains[0].astype(jnp.float32)
    gain_ffn = norm_gains[1].astype(jnp.float32)
    gain_query = head_gains[0].astype(jnp.float32)
    key_gain_vector = head_gains[1].astype(jnp.float32)
    scale_attn = rms_scale(inputs)
    normed_attn = inputs * scale_attn
    attention_hidden = rounded_value(normed_attn * gain_attn)
    query_raw = jnp.dot(attention_hidden, w_query, preferred_element_type=jnp.float32).reshape(sequence_length, QUERY_HEADS, HEAD_SIZE)
    key_projected = jnp.dot(attention_hidden, key_weight, preferred_element_type=jnp.float32).reshape(sequence_length, KEY_VALUE_HEADS, HEAD_SIZE)
    value_rows = rounded_value(jnp.dot(attention_hidden, w_value, preferred_element_type=jnp.float32))
    query_normed, query_hat = head_norm(query_raw, gain_query)
    key_after_norm, key_unit_scaled = head_norm(key_projected, key_gain_vector)
    cosine_table, sine_table = rope_tables(sequence_length, 0, HEAD_SIZE)
    query_rotated = rounded_value(rotary_apply(query_normed, cosine_table, sine_table, 1.0)).reshape(sequence_length, QUERY_HEADS * HEAD_SIZE)
    key_rotated = rounded_value(rotary_apply(key_after_norm, cosine_table, sine_table, 1.0)).reshape(sequence_length, KEY_VALUE_HEADS * HEAD_SIZE)
    query_widened = widened_heads(query_rotated).reshape(sequence_length, KEY_VALUE_HEADS, query_group_count, HEAD_SIZE)
    key_widened = widened_heads(key_rotated).reshape(sequence_length, KEY_VALUE_HEADS, HEAD_SIZE)
    value_widened = widened_heads(value_rows).reshape(sequence_length, KEY_VALUE_HEADS, HEAD_SIZE)
    block_rows = math.gcd(sequence_length, 512)
    positions = jnp.arange(sequence_length, dtype=jnp.int32)
    attended_parts = []
    log_parts = []
    for number in range(sequence_length // block_rows):
        begin = number * block_rows
        finish = begin + block_rows
        scores = jnp.einsum('tkgd,skd->kgts', query_widened[begin:finish], key_widened[:finish]) * score_scale
        causal = positions[begin:finish, None] >= positions[None, :finish]
        powered = jnp.where(causal, jnp.exp(scores), 0.0)
        denominator = lax.optimization_barrier(jnp.sum(powered, axis=-1))
        weighted = jnp.einsum('kgts,skd->tkgd', widened_heads(rounded_value(powered)), value_widened[:finish])
        attended_parts.append(weighted / denominator.transpose(2, 0, 1)[..., None])
        log_parts.append(jnp.log(denominator))
    attended = rounded_value(jnp.concatenate(attended_parts, axis=0)).reshape(sequence_length, QUERY_HEADS * HEAD_SIZE)
    log_total = jnp.concatenate(log_parts, axis=2)
    residual = inputs + jnp.dot(attended, w_out.T, preferred_element_type=jnp.float32)
    scale_ffn = rms_scale(residual)
    normed_ffn = residual * scale_ffn
    hidden_ffn = rounded_value(normed_ffn * gain_ffn)
    gate_raw = jnp.dot(hidden_ffn, w_gate, preferred_element_type=jnp.float32)
    up_raw = jnp.dot(hidden_ffn, w_up, preferred_element_type=jnp.float32)
    sigmoid_gate = jax.nn.sigmoid(gate_raw)
    activated = gate_raw * sigmoid_gate
    hidden_units = rounded_value(activated * up_raw)
    block_output = (residual + jnp.dot(hidden_units, w_down.T, preferred_element_type=jnp.float32)).astype(jnp.bfloat16)
    upstream = cotangent.astype(jnp.float32)
    grad_units = jnp.dot(cotangent, w_down, preferred_element_type=jnp.float32)
    grad_down = jnp.dot(cotangent.T, hidden_units, preferred_element_type=jnp.float32)
    grad_gate_in = rounded_value(grad_units * up_raw * sigmoid_gate * (1.0 + gate_raw * (1.0 - sigmoid_gate)))
    grad_up_in = rounded_value(grad_units * activated)
    grad_gate = jnp.dot(hidden_ffn.T, grad_gate_in, preferred_element_type=jnp.float32)
    grad_up = jnp.dot(hidden_ffn.T, grad_up_in, preferred_element_type=jnp.float32)
    grad_hidden_ffn = jnp.dot(grad_gate_in, w_gate.T, preferred_element_type=jnp.float32) + jnp.dot(grad_up_in, w_up.T, preferred_element_type=jnp.float32)
    ffn_gain_grad = lax.optimization_barrier(jnp.sum(grad_hidden_ffn * normed_ffn, axis=0))
    grad_residual = upstream + row_norm_back(grad_hidden_ffn, normed_ffn, scale_ffn, gain_ffn)
    residual_bf = rounded_value(grad_residual)
    attended_gradient = rounded_value(jnp.dot(residual_bf, w_out, preferred_element_type=jnp.float32))
    grad_out = jnp.dot(residual_bf.T, attended, preferred_element_type=jnp.float32)
    products_total = lax.optimization_barrier(jnp.sum((widened_heads(attended_gradient) * widened_heads(attended)).reshape(sequence_length, QUERY_HEADS, HEAD_SIZE), axis=-1))
    delta_overall = products_total.reshape(sequence_length, KEY_VALUE_HEADS, query_group_count).transpose(1, 2, 0)
    widened_gradient = widened_heads(attended_gradient).reshape(sequence_length, KEY_VALUE_HEADS, query_group_count, HEAD_SIZE)
    key_gradient = jnp.zeros((sequence_length, KEY_VALUE_HEADS, HEAD_SIZE), jnp.float32)
    value_gradient = jnp.zeros((sequence_length, KEY_VALUE_HEADS, HEAD_SIZE), jnp.float32)
    query_parts = []
    for number in range(sequence_length // block_rows):
        begin = number * block_rows
        finish = begin + block_rows
        query_block = query_widened[begin:finish]
        grad_block = widened_gradient[begin:finish]
        scores = jnp.einsum('tkgd,skd->kgts', query_block, key_widened[:finish]) * score_scale
        causal = positions[begin:finish, None] >= positions[None, :finish]
        probs = jnp.where(causal, jnp.exp(scores - log_total[:, :, begin:finish][..., None]), 0.0)
        probs_bf = widened_heads(rounded_value(probs))
        grad_probs = jnp.einsum('tkgd,skd->kgts', grad_block, value_widened[:finish])
        grad_scores = widened_heads(rounded_value(probs * (grad_probs - delta_overall[:, :, begin:finish][..., None]) * score_scale))
        query_parts.append(jnp.einsum('kgts,skd->tkgd', grad_scores, key_widened[:finish]).reshape(block_rows, QUERY_HEADS, HEAD_SIZE))
        key_gradient = key_gradient.at[:finish].add(jnp.einsum('kgts,tkgd->skd', grad_scores, query_block))
        value_gradient = value_gradient.at[:finish].add(jnp.einsum('kgts,tkgd->skd', probs_bf, grad_block))
    grad_query_rot = jnp.concatenate(query_parts, axis=0)
    grad_query_heads = rotary_apply(grad_query_rot, cosine_table, sine_table, -1.0)
    query_gain_grad = lax.optimization_barrier(jnp.sum(grad_query_heads * query_hat, axis=(0, 1)))
    grad_query_in = rounded_value(head_norm_reverse(grad_query_heads, query_raw, query_hat, gain_query)).reshape(sequence_length, QUERY_HEADS * HEAD_SIZE)
    key_heads_gradient = rotary_apply(key_gradient, cosine_table, sine_table, -1.0)
    key_gain_grad = lax.optimization_barrier(jnp.sum(key_heads_gradient * key_unit_scaled, axis=(0, 1)))
    key_input_gradient = rounded_value(head_norm_reverse(key_heads_gradient, key_projected, key_unit_scaled, key_gain_vector)).reshape(sequence_length, KEY_VALUE_HEADS * HEAD_SIZE)
    value_input = rounded_value(value_gradient.reshape(sequence_length, KEY_VALUE_HEADS * HEAD_SIZE))
    grad_query = jnp.dot(attention_hidden.T, grad_query_in, preferred_element_type=jnp.float32)
    grad_key = jnp.dot(attention_hidden.T, key_input_gradient, preferred_element_type=jnp.float32)
    grad_value = jnp.dot(attention_hidden.T, value_input, preferred_element_type=jnp.float32)
    grad_hidden_attn = jnp.dot(grad_query_in, w_query.T, preferred_element_type=jnp.float32) + jnp.dot(key_input_gradient, key_weight.T, preferred_element_type=jnp.float32) + jnp.dot(value_input, w_value.T, preferred_element_type=jnp.float32)
    attn_gain_grad = lax.optimization_barrier(jnp.sum(grad_hidden_attn * normed_attn, axis=0))
    input_grad = grad_residual + row_norm_back(grad_hidden_attn, normed_attn, scale_attn, gain_attn)
    grad_norm_gains = jnp.stack([attn_gain_grad, ffn_gain_grad])
    grad_head_gains = jnp.stack([query_gain_grad, key_gain_grad])
    grads = (grad_query, grad_key, grad_value, grad_out, grad_gate, grad_up, grad_down, grad_norm_gains, grad_head_gains)
    return (block_output, input_grad, grads)

def reference(block_input, cotangent, w_query, key_weight, w_value, w_out, w_gate, w_up, w_down, norm_gains, head_gains):

    def step(totals, pair):
        block_output, input_grad, grads = one_sequence(pair[0], pair[1], w_query, key_weight, w_value, w_out, w_gate, w_up, w_down, norm_gains, head_gains)
        updated = tuple((total + grad for total, grad in zip(totals, grads)))
        return (updated, (block_output, input_grad))
    shapes = (w_query.shape, key_weight.shape, w_value.shape, w_out.shape, w_gate.shape, w_up.shape, w_down.shape, norm_gains.shape, head_gains.shape)
    start = tuple((jnp.zeros(shape, jnp.float32) for shape in shapes))
    totals, (block_output, input_grad) = lax.scan(step, start, (block_input, cotangent))
    return (block_output, input_grad, totals[0], totals[1], totals[2], totals[3], totals[4], totals[5], totals[6], totals[7], totals[8])
```

```python
import functools

import jax
import jax.numpy as jnp
from jax import lax
from jax.experimental import pallas as pl
from jax.experimental.pallas import tpu as pltpu
from jax.sharding import PartitionSpec as P

HEAD_SIZE = 64
EPSILON = 1e-06
ROPE_BASE = 1000000.0
MESH = pl.DeviceIdType.MESH
F32 = jnp.float32
BF16 = jnp.bfloat16
ANY = pl.BlockSpec(memory_space=pl.ANY)
VMEM = pl.BlockSpec(memory_space=pltpu.VMEM)
NCTX = 32
PAIRS = 4
WORKERS = 8
SLOTS = 4
BLOCK = 128


def group(kind):
    c, t = lax.axis_index("ctx"), lax.axis_index("tp")
    h = lax.rem(c, 2)
    if kind == "ctx":
        return NCTX, c, lambda p: (p, t)
    if kind == "tp":
        return 4, t, lambda p: (c, p)
    if kind == "pair":
        return 2, h, lambda p: (c - h + p, t)
    return 8, h * 4 + t, lambda p: (c - h + p // 4, lax.rem(p, 4))


PICKS = {
    "same": lambda ref, p: ref,
    "own": lambda ref, p: ref.at[p],
    "half": lambda ref, p: ref.at[lax.rem(p, 2)],
    "plane": lambda ref, p: ref.at[p // WORKERS],
}


def greet(kinds):
    barrier = pltpu.get_barrier_semaphore()
    total = 0
    for kind in kinds:
        n, me, dev = group(kind)

        @pl.loop(1, n)
        def _(i):
            pl.semaphore_signal(
                barrier, inc=1, device_id=dev(lax.rem(me + i, n)), device_id_type=MESH
            )

        total += n - 1
    pl.semaphore_wait(barrier, total)


def begin(kind, pick, src, dst, send, recv):
    n, me, dev = group(kind)
    choose = PICKS[pick]

    @pl.loop(1, n)
    def _(i):
        p = lax.rem(me + i, n)
        pltpu.make_async_remote_copy(
            src_ref=choose(src, p),
            dst_ref=dst.at[me],
            send_sem=send.at[p],
            recv_sem=recv.at[me],
            device_id=dev(p),
            device_id_type=MESH,
        ).start()

    pltpu.make_async_copy(choose(src, me), dst.at[me], recv.at[me]).start()


def finish(kind, pick, src, dst, send, recv):
    n, me, dev = group(kind)
    choose = PICKS[pick]

    @pl.loop(1, n)
    def _(i):
        p = lax.rem(me + i, n)
        copy = pltpu.make_async_remote_copy(
            src_ref=choose(src, p),
            dst_ref=dst.at[p],
            send_sem=send.at[p],
            recv_sem=recv.at[p],
            device_id=dev(p),
            device_id_type=MESH,
        )
        copy.wait_send()
        copy.wait_recv()

    pltpu.make_async_copy(choose(src, me), dst.at[me], recv.at[me]).wait()


SIZES = {"ctx": NCTX, "tp": 4, "pair": 2, "rows": 8}


def piece_shape(pick, array):
    return array.shape if pick == "same" else array.shape[1:]


def landing(kind, pick, array):
    return jax.ShapeDtypeStruct((SIZES[kind], *piece_shape(pick, array)), array.dtype)


def sems(kinds):
    return [pltpu.SemaphoreType.DMA((SIZES[k],)) for k in kinds for _ in range(2)]


def exchange_body(plan, kinds, *refs):
    n = len(plan)
    srcs, dsts, rest = refs[:n], refs[n : 2 * n], refs[2 * n :]
    greet(kinds)
    for k, (kind, pick) in enumerate(plan):
        begin(kind, pick, srcs[k], dsts[k], rest[2 * k], rest[2 * k + 1])
    for k, (kind, pick) in enumerate(plan):
        finish(kind, pick, srcs[k], dsts[k], rest[2 * k], rest[2 * k + 1])


def exchange(number, kinds, items):
    plan = tuple((kind, pick) for kind, pick, _ in items)
    return pl.pallas_call(
        functools.partial(exchange_body, plan, kinds),
        out_shape=[landing(*item) for item in items],
        in_specs=[ANY] * len(items),
        out_specs=[ANY] * len(items),
        scratch_shapes=sems([kind for kind, _ in plan]),
        compiler_params=pltpu.CompilerParams(collective_id=number, has_side_effects=True),
        name=f"exchange{number}",
    )(*[array for _, _, array in items])


def places():
    c, t = lax.axis_index("ctx"), lax.axis_index("tp")
    slot, low = c // WORKERS, lax.rem(c, WORKERS)
    to = low + lax.rem(slot, 2) * (WORKERS - 1 - 2 * low)
    return c, t, slot, low, to


def block_of(low, j):
    return j * WORKERS + (low if j % 2 == 0 else WORKERS - 1 - low)


def to_workers(src, dst, send, recv, act):
    c, t, slot, low, to = places()
    for p in range(PAIRS):
        target = p * WORKERS + to
        far = pltpu.make_async_remote_copy(
            src_ref=src.at[p],
            dst_ref=dst.at[slot],
            send_sem=send.at[p],
            recv_sem=recv.at[slot],
            device_id=(target, t),
            device_id_type=MESH,
        )
        near = pltpu.make_async_copy(src.at[p], dst.at[slot], send.at[p])

        @pl.when(target != c)
        def _():
            far.start() if act == "start" else far.wait_send()

        @pl.when(target == c)
        def _():
            near.start() if act == "start" else near.wait()


def from_owners(src, dst, send, recv):
    c, t, slot, low, to = places()
    for j in range(SLOTS):
        owner = block_of(low, j)

        @pl.when(owner != c)
        def _():
            pltpu.make_async_remote_copy(
                src_ref=src.at[j],
                dst_ref=dst.at[j],
                send_sem=send.at[j],
                recv_sem=recv.at[j],
                device_id=(owner, t),
                device_id_type=MESH,
            ).wait_recv()


def to_owner(src, dst, send, recv, j, act):
    c, t, slot, low, to = places()
    owner = block_of(low, j)
    far = pltpu.make_async_remote_copy(
        src_ref=src.at[j],
        dst_ref=dst.at[slot],
        send_sem=send.at[j],
        recv_sem=recv.at[slot],
        device_id=(owner, t),
        device_id_type=MESH,
    )
    near = pltpu.make_async_copy(src.at[j], dst.at[slot], send.at[j])

    @pl.when(owner != c)
    def _():
        far.start() if act == "start" else far.wait_send()

    @pl.when(owner == c)
    def _():
        near.start() if act == "start" else near.wait()


def from_workers(src, dst, send, recv):
    c, t, slot, low, to = places()
    for p in range(PAIRS):
        target = p * WORKERS + to

        @pl.when(target != c)
        def _():
            pltpu.make_async_remote_copy(
                src_ref=src.at[p],
                dst_ref=dst.at[p],
                send_sem=send.at[p],
                recv_sem=recv.at[p],
                device_id=(target, t),
                device_id_type=MESH,
            ).wait_recv()


def last_dims(a, b):
    return lax.dot_general(a, b, (((1,), (1,)), ((), ())), preferred_element_type=F32)


def first_dims(a, b):
    return lax.dot_general(a, b, (((0,), (0,)), ((), ())), preferred_element_type=F32)


def causal_mask(b, i):
    shape = (2 * BLOCK, 2 * BLOCK)
    rows = lax.broadcasted_iota(jnp.int32, shape, 0)
    token = b * BLOCK + jnp.where(rows >= BLOCK, rows - BLOCK, rows)
    key = i * 2 * BLOCK + lax.broadcasted_iota(jnp.int32, shape, 1)
    return token >= key


FORWARD_PLAN = (("ctx", "same"), ("ctx", "half"), ("ctx", "half"), ("pair", "same"))


def forward_body(
    q_src, kv_src, wo, gu, dn, cot,
    att, q_buf, kv_buf, o_buf, log_buf, wo_all, gu_all, dn_all, cot_all,
    acc, den, q_send, q_recv, o_send, o_recv, kv_send, kv_recv, *rest,
):
    c, t, slot, low, to = places()
    background = list(zip(FORWARD_PLAN, (wo, gu, dn, cot), (wo_all, gu_all, dn_all, cot_all)))
    greet(["ctx"])
    to_workers(q_src, q_buf, q_send, q_recv, "start")
    begin("ctx", "plane", kv_src, kv_buf, kv_send, kv_recv)
    for k, ((kind, pick), src, dst) in enumerate(background):
        begin(kind, pick, src, dst, rest[2 * k], rest[2 * k + 1])
    to_workers(q_src, q_buf, q_send, q_recv, "wait")
    from_owners(q_src, q_buf, q_send, q_recv)
    finish("ctx", "plane", kv_src, kv_buf, kv_send, kv_recv)
    lanes = lax.broadcasted_iota(jnp.int32, (2 * BLOCK, BLOCK), 1)
    for j in range(SLOTS):
        b = block_of(low, j)
        acc[...] = jnp.zeros_like(acc)
        den[...] = jnp.zeros_like(den)

        def chunk(i, masked):
            q = q_buf[j]
            kv = kv_buf[pl.ds(2 * i, 2)].reshape(2 * BLOCK, BLOCK)
            powered = jnp.exp(last_dims(q, kv))
            if masked:
                powered = jnp.where(causal_mask(b, i), powered, 0.0)
            den[...] += powered[:, :BLOCK] + powered[:, BLOCK:]
            acc[...] += jnp.dot(powered.astype(BF16), kv, preferred_element_type=F32)

        pl.loop(0, b // 2)(lambda i: chunk(i, False))
        chunk(b // 2, True)
        total = jnp.sum(den[...], axis=1, keepdims=True)
        o_buf[j] = jnp.where(lanes >= HEAD_SIZE, acc[...] / total, 0.0).astype(BF16)
        log_buf[j] = jnp.broadcast_to(jnp.log(total), (2 * BLOCK, BLOCK))
        to_owner(o_buf, att, o_send, o_recv, j, "start")
    for j in range(SLOTS):
        to_owner(o_buf, att, o_send, o_recv, j, "wait")
    from_workers(o_buf, att, o_send, o_recv)
    for k, ((kind, pick), src, dst) in enumerate(background):
        finish(kind, pick, src, dst, rest[2 * k], rest[2 * k + 1])


def forward(q_src, kv_src, wo, gu, dn, cot):
    stack = jax.ShapeDtypeStruct((SLOTS, 2 * BLOCK, BLOCK), BF16)
    kinds = [kind for kind, _ in FORWARD_PLAN]
    return pl.pallas_call(
        forward_body,
        out_shape=[
            stack,
            stack,
            jax.ShapeDtypeStruct((NCTX, BLOCK, BLOCK), BF16),
            stack,
            jax.ShapeDtypeStruct((SLOTS, 2 * BLOCK, BLOCK), F32),
        ]
        + [landing(k, p, a) for (k, p), a in zip(FORWARD_PLAN, (wo, gu, dn, cot))],
        in_specs=[ANY] * 6,
        out_specs=[ANY] + [VMEM] * 4 + [ANY] * 4,
        scratch_shapes=[
            pltpu.VMEM((2 * BLOCK, BLOCK), F32),
            pltpu.VMEM((2 * BLOCK, BLOCK), F32),
        ]
        + [pltpu.SemaphoreType.DMA((SLOTS,))] * 4
        + sems(["ctx"] + kinds),
        compiler_params=pltpu.CompilerParams(
            collective_id=2, has_side_effects=True, vmem_limit_bytes=24 * 2**20
        ),
        name="attention_forward",
    )(q_src, kv_src, wo, gu, dn, cot)


BACKWARD_PLAN = (("ctx", "own"), ("ctx", "own"), ("ctx", "own"), ("rows", "own"))


def backward_body(
    do_src, q_buf, kv_buf, o_buf, log_buf, wo, gu, dn, ffn,
    dq_all, dkv_all, wo_all, gu_all, dn_all, ffn_all,
    do_buf, dq_buf, dkv_buf, acc, dkv, do_send, do_recv, dq_send, dq_recv, kv_send, kv_recv, *rest,
):
    c, t, slot, low, to = places()
    background = list(zip(BACKWARD_PLAN, (wo, gu, dn, ffn), (wo_all, gu_all, dn_all, ffn_all)))
    greet(["ctx", "rows"])
    to_workers(do_src, do_buf, do_send, do_recv, "start")
    for k, ((kind, pick), src, dst) in enumerate(background):
        begin(kind, pick, src, dst, rest[2 * k], rest[2 * k + 1])
    dkv[...] = jnp.zeros_like(dkv)
    to_workers(do_src, do_buf, do_send, do_recv, "wait")
    from_owners(do_src, do_buf, do_send, do_recv)
    for j in range(SLOTS):
        b = block_of(low, j)
        acc[...] = jnp.zeros_like(acc)
        delta = jnp.sum(do_buf[j].astype(F32) * o_buf[j].astype(F32), axis=1, keepdims=True)

        def chunk(i, masked):
            q, do = q_buf[j], do_buf[j]
            kv = kv_buf[pl.ds(2 * i, 2)].reshape(2 * BLOCK, BLOCK)
            logs = log_buf[j]
            scores = last_dims(q, kv)
            probs = jnp.exp(scores - jnp.concatenate([logs, logs], axis=1))
            if masked:
                probs = jnp.where(causal_mask(b, i), probs, 0.0)
            grads = (probs * (last_dims(do, kv) - delta)).astype(BF16)
            acc[...] += jnp.dot(grads, kv, preferred_element_type=F32)
            update = first_dims(grads, q) + first_dims(probs.astype(BF16), do)
            dkv[pl.ds(2 * i, 2)] += update.reshape(2, BLOCK, BLOCK)

        pl.loop(0, b // 2)(lambda i: chunk(i, False))
        chunk(b // 2, True)
        dq_buf[j] = (acc[...] * (HEAD_SIZE**-0.5)).astype(BF16)
        to_owner(dq_buf, dq_all, dq_send, dq_recv, j, "start")
    dkv_buf[...] = dkv[...].astype(BF16)
    begin("ctx", "own", dkv_buf, dkv_all, kv_send, kv_recv)
    for j in range(SLOTS):
        to_owner(dq_buf, dq_all, dq_send, dq_recv, j, "wait")
    from_workers(dq_buf, dq_all, dq_send, dq_recv)
    finish("ctx", "own", dkv_buf, dkv_all, kv_send, kv_recv)
    for k, ((kind, pick), src, dst) in enumerate(background):
        finish(kind, pick, src, dst, rest[2 * k], rest[2 * k + 1])


def backward(do_src, q_buf, kv_buf, o_buf, log_buf, wo, gu, dn, ffn):
    kinds = [kind for kind, _ in BACKWARD_PLAN]
    return pl.pallas_call(
        backward_body,
        out_shape=[
            jax.ShapeDtypeStruct((SLOTS, 2 * BLOCK, BLOCK), BF16),
            jax.ShapeDtypeStruct((NCTX, BLOCK, BLOCK), BF16),
        ]
        + [landing(k, p, a) for (k, p), a in zip(BACKWARD_PLAN, (wo, gu, dn, ffn))],
        in_specs=[ANY] + [VMEM] * 4 + [ANY] * 4,
        out_specs=[ANY] * 6,
        scratch_shapes=[
            pltpu.VMEM((SLOTS, 2 * BLOCK, BLOCK), BF16),
            pltpu.VMEM((SLOTS, 2 * BLOCK, BLOCK), BF16),
            pltpu.VMEM((NCTX, BLOCK, BLOCK), BF16),
            pltpu.VMEM((2 * BLOCK, BLOCK), F32),
            pltpu.VMEM((NCTX, BLOCK, BLOCK), F32),
        ]
        + [pltpu.SemaphoreType.DMA((SLOTS,))] * 4
        + sems(["ctx"] + kinds),
        compiler_params=pltpu.CompilerParams(
            collective_id=6, has_side_effects=True, vmem_limit_bytes=24 * 2**20
        ),
        name="attention_backward",
    )(do_src, q_buf, kv_buf, o_buf, log_buf, wo, gu, dn, ffn)


def rms_scale(rows):
    return lax.rsqrt(jnp.mean(rows * rows, axis=-1, keepdims=True) + EPSILON)


def rope_tables(tokens, offset):
    half = HEAD_SIZE // 2
    inverse = ROPE_BASE ** (-(jnp.arange(half, dtype=F32) * 2.0 / HEAD_SIZE))
    places_ = (offset + jnp.arange(tokens, dtype=jnp.int32)).astype(F32)
    angles = places_[:, None] * inverse[None, :]
    return jnp.cos(angles), jnp.sin(angles)


def rotary(rows, cosine, sine, direction):
    half = HEAD_SIZE // 2
    first, second = rows[..., :half], rows[..., half:]
    cosine = cosine[:, None, :]
    sine = sine[:, None, :] * direction
    return jnp.concatenate([first * cosine - second * sine, second * cosine + first * sine], -1)


def head_back(grads, hatted, scale, gain):
    scaled = grads * gain
    return scale * (scaled - hatted * jnp.mean(scaled * hatted, axis=-1, keepdims=True))


def row_back(grads, normed, scale, gain):
    scaled = grads * gain
    return scale * (scaled - normed * jnp.mean(scaled * normed, axis=-1, keepdims=True))


def to_pairs(rows, heads, left):
    s, tokens = rows.shape[:2]
    kv = rows.shape[2] // heads
    x = rows.reshape(s, tokens, kv, heads, HEAD_SIZE).transpose(2, 0, 3, 1, 4)
    x = x.reshape(kv * s, heads * tokens, HEAD_SIZE)
    side = (0, HEAD_SIZE) if left else (HEAD_SIZE, 0)
    return jnp.pad(x, ((0, 0), (0, 0), side))


def from_pairs(x, s, heads):
    kv = x.shape[0] // s
    tokens = x.shape[1] // heads
    x = x.reshape(kv, s, heads, tokens, HEAD_SIZE).transpose(1, 3, 0, 2, 4)
    return x.reshape(s, tokens, kv * heads, HEAD_SIZE)


def halves(w):
    half = w.shape[1] // 2
    return jnp.stack([w[:, :half], w[:, half:]])


def local(
    block_input, cotangent, w_query, key_weight, w_value, w_out, w_gate, w_up, w_down,
    norm_gains, head_gains,
):
    c, t = lax.axis_index("ctx"), lax.axis_index("tp")
    seqs, tokens, width = block_input.shape
    rows = seqs * tokens
    own = rows // 4
    unit_half = w_gate.shape[1] // 2

    def mine(x):
        return lax.dynamic_slice_in_dim(x, t * own, own, 0)

    weight_rows = jnp.concatenate([w_query, key_weight, w_value], axis=1)
    gains = jnp.zeros((16, 128), BF16)
    gains = gains.at[0:2, 0:32].set(norm_gains).at[2:4, 0:2].set(head_gains)
    weights_all, gains_all = exchange(
        1, ["ctx"], [("ctx", "same", weight_rows), ("ctx", "same", gains)]
    )
    qkv_full = weights_all.reshape(width, weight_rows.shape[1])
    gain_attn = gains_all[:, 0, :32].reshape(width).astype(F32)
    gain_ffn = gains_all[:, 1, :32].reshape(width).astype(F32)
    gain_query = gains_all[:, 2, :2].reshape(HEAD_SIZE).astype(F32)
    gain_key = gains_all[:, 3, :2].reshape(HEAD_SIZE).astype(F32)

    inputs = block_input.astype(F32).reshape(rows, width)
    scale_attn = rms_scale(inputs)
    normed_attn = inputs * scale_attn
    hidden_attn = (normed_attn * gain_attn).astype(BF16)
    raw = jnp.dot(hidden_attn, qkv_full, preferred_element_type=F32)
    query_raw = raw[:, :256].reshape(seqs, tokens, 4, HEAD_SIZE)
    key_raw = raw[:, 256:384].reshape(seqs, tokens, 2, HEAD_SIZE)
    values = raw[:, 384:].astype(BF16).reshape(seqs, tokens, 2, HEAD_SIZE)
    query_scale, key_scale = rms_scale(query_raw), rms_scale(key_raw)
    query_hat, key_hat = query_raw * query_scale, key_raw * key_scale
    cosine, sine = rope_tables(tokens, c * tokens)
    query_rot = rotary(query_hat * gain_query, cosine, sine, 1.0).astype(BF16)
    key_rot = rotary(key_hat * gain_key, cosine, sine, 1.0).astype(BF16)
    q_src = to_pairs(query_rot * jnp.asarray(HEAD_SIZE**-0.5, BF16), 2, True)
    kv_src = jnp.concatenate([key_rot, values], axis=-1).transpose(2, 0, 1, 3)
    kv_src = kv_src.reshape(PAIRS, tokens, 2 * HEAD_SIZE)

    gu_src = jnp.concatenate([halves(w_gate), halves(w_up)], axis=2)
    dn_src = halves(w_down)
    att, q_buf, kv_buf, o_buf, log_buf, wo_all, gu_all, dn_all, cot_all = forward(
        q_src, kv_src, w_out, gu_src, dn_src, cotangent.reshape(rows, width)
    )
    attended = from_pairs(att[..., HEAD_SIZE:], seqs, 2).reshape(rows, 256)
    out_full = wo_all.reshape(width, 256)
    gu_full = gu_all.reshape(width, 2 * unit_half)
    dn_full = dn_all.reshape(width, unit_half)
    cot_rows = cot_all.reshape(2 * rows, width)

    attn_part = last_dims(attended, out_full).astype(BF16)
    (attn_parts,) = exchange(3, ["tp"], [("tp", "own", attn_part.reshape(4, own, width))])
    residual = mine(inputs) + jnp.sum(attn_parts.astype(F32), axis=0)
    scale_ffn = rms_scale(residual)
    normed_ffn = residual * scale_ffn
    hidden_own = (normed_ffn * gain_ffn).astype(BF16)
    (hidden_all,) = exchange(4, ["rows"], [("rows", "same", hidden_own)])
    hidden_ffn = hidden_all.reshape(2 * rows, width)

    gu_raw = jnp.dot(hidden_ffn, gu_full, preferred_element_type=F32)
    gate_raw, up_raw = gu_raw[:, :unit_half], gu_raw[:, unit_half:]
    sigmoid = jax.nn.sigmoid(gate_raw)
    activated = gate_raw * sigmoid
    hidden_units = (activated * up_raw).astype(BF16)
    grad_units = jnp.dot(cot_rows, dn_full, preferred_element_type=F32)
    grad_gate_in = grad_units * up_raw * sigmoid * (1.0 + gate_raw * (1.0 - sigmoid))
    grad_up_in = grad_units * activated
    grad_gu_in = jnp.concatenate([grad_gate_in, grad_up_in], axis=1).astype(BF16)
    ffn_back = last_dims(grad_gu_in, gu_full).astype(BF16)
    (back_parts,) = exchange(5, ["rows"], [("rows", "own", ffn_back.reshape(8, own, width))])
    grad_hidden_ffn = jnp.sum(back_parts.astype(F32), axis=0)
    ffn_gain_part = jnp.sum(grad_hidden_ffn * normed_ffn, axis=0)
    cot_own = mine(cotangent.reshape(rows, width)).astype(F32)
    grad_residual = cot_own + row_back(grad_hidden_ffn, normed_ffn, scale_ffn, gain_ffn)
    (residual_all,) = exchange(7, ["tp"], [("tp", "same", grad_residual.astype(BF16))])
    residual_bf = residual_all.reshape(rows, width)

    grad_attended = jnp.dot(residual_bf, out_full, preferred_element_type=F32).astype(BF16)
    do_src = to_pairs(grad_attended.reshape(seqs, tokens, 4, HEAD_SIZE), 2, False)
    grad_out = first_dims(residual_bf, attended).astype(BF16)
    grad_gu = first_dims(hidden_ffn, grad_gu_in).astype(BF16)
    grad_dn = first_dims(cot_rows, hidden_units).astype(BF16)
    ffn_part = last_dims(hidden_units, dn_full).astype(BF16)
    dq_all, dkv_all, wo_parts, gu_parts, dn_parts, ffn_parts = backward(
        do_src, q_buf, kv_buf, o_buf, log_buf,
        grad_out.reshape(NCTX, 32, 256),
        grad_gu.reshape(NCTX, 32, 2 * unit_half),
        grad_dn.reshape(NCTX, 32, unit_half),
        ffn_part.reshape(8, own, width),
    )

    output_own = (residual + jnp.sum(ffn_parts.astype(F32), axis=0)).astype(BF16)
    grad_query_rot = from_pairs(dq_all[..., :HEAD_SIZE].astype(F32), seqs, 2)
    dkv = jnp.sum(dkv_all.reshape(PAIRS, WORKERS, tokens, 2 * HEAD_SIZE).astype(F32), axis=1)
    key_grad = from_pairs(dkv[..., :HEAD_SIZE], seqs, 1)
    value_in = from_pairs(dkv[..., HEAD_SIZE:], seqs, 1).astype(BF16).reshape(rows, 128)
    gq = rotary(grad_query_rot, cosine, sine, -1.0)
    gk = rotary(key_grad, cosine, sine, -1.0)
    query_gain_part = jnp.sum(gq * query_hat, axis=(0, 1, 2))
    key_gain_part = jnp.sum(gk * key_hat, axis=(0, 1, 2))
    query_in = head_back(gq, query_hat, query_scale, gain_query).astype(BF16).reshape(rows, 256)
    key_in = head_back(gk, key_hat, key_scale, gain_key).astype(BF16).reshape(rows, 128)
    grad_in = jnp.concatenate([query_in, key_in, value_in], axis=1)
    grad_qkv = first_dims(hidden_attn, grad_in).astype(BF16)
    attn_back = last_dims(grad_in, qkv_full)
    attn_gain_part = jnp.sum(attn_back * normed_attn, axis=0)
    gain_parts = jnp.zeros((NCTX, 8, 128), F32)
    gain_parts = gain_parts.at[:, 0, :32].set(attn_gain_part.reshape(NCTX, 32))
    gain_parts = gain_parts.at[:, 1, :32].set(ffn_gain_part.reshape(NCTX, 32))
    gain_parts = gain_parts.at[:, 2, :2].set(query_gain_part.reshape(NCTX, 2))
    gain_parts = gain_parts.at[:, 3, :2].set(key_gain_part.reshape(NCTX, 2))
    attn_parts, qkv_parts, gain_all, output_all = exchange(
        8,
        ["ctx", "tp"],
        [
            ("tp", "own", attn_back.astype(BF16).reshape(4, own, width)),
            ("ctx", "own", grad_qkv.reshape(NCTX, 32, 512)),
            ("ctx", "own", gain_parts),
            ("tp", "same", output_own),
        ],
    )
    grad_hidden_attn = jnp.sum(attn_parts.astype(F32), axis=0)
    input_own = grad_residual + row_back(
        grad_hidden_attn, mine(normed_attn), mine(scale_attn), gain_attn
    )
    input_all, gain_tp = exchange(
        9,
        ["tp"],
        [("tp", "same", input_own.astype(BF16)), ("tp", "same", jnp.sum(gain_all, axis=0))],
    )
    gain_sum = jnp.sum(gain_tp, axis=0)
    qkv_grad = jnp.sum(qkv_parts.astype(F32), axis=0)
    out_grad = jnp.sum(wo_parts.astype(F32), axis=0)
    gu_grad = jnp.sum(gu_parts.reshape(16, 2, 32, 2 * unit_half).astype(F32), axis=0)
    dn_grad = jnp.sum(dn_parts.reshape(16, 2, 32, unit_half).astype(F32), axis=0)
    gate_grad = jnp.concatenate([gu_grad[0, :, :unit_half], gu_grad[1, :, :unit_half]], axis=1)
    up_grad = jnp.concatenate([gu_grad[0, :, unit_half:], gu_grad[1, :, unit_half:]], axis=1)
    down_grad = jnp.concatenate([dn_grad[0], dn_grad[1]], axis=1)
    return (
        output_all.reshape(seqs, tokens, width),
        input_all.astype(F32).reshape(seqs, tokens, width),
        qkv_grad[:, :256],
        qkv_grad[:, 256:384],
        qkv_grad[:, 384:],
        out_grad,
        gate_grad,
        up_grad,
        down_grad,
        gain_sum[0:2, :32],
        gain_sum[2:4, :2],
    )


def solution(mesh):
    tokens, weights = P(None, "ctx", None), P("ctx", "tp")
    return jax.shard_map(
        local,
        mesh=mesh,
        in_specs=(tokens,) * 2 + (weights,) * 7 + (P(None, "ctx"),) * 2,
        out_specs=(tokens,) * 2 + (weights,) * 7 + (P(None, "ctx"),) * 2,
        check_vma=False,
    )
```

```python
import functools

import jax
import jax.numpy as jnp
from jax import lax
from jax.experimental import pallas as pl
from jax.experimental.pallas import tpu as pltpu
from jax.sharding import PartitionSpec as P

HEAD_SIZE = 64
EPSILON = 1e-06
ROPE_BASE = 1000000.0
MESH = pl.DeviceIdType.MESH
F32 = jnp.float32
BF16 = jnp.bfloat16
ANY = pl.BlockSpec(memory_space=pl.ANY)
VMEM = pl.BlockSpec(memory_space=pltpu.VMEM)
NCTX = 32
PAIRS = 4
WORKERS = 8
SLOTS = 4
BLOCK = 128


def group(kind):
    c, t = lax.axis_index("ctx"), lax.axis_index("tp")
    h = lax.rem(c, 2)
    if kind == "ctx":
        return NCTX, c, lambda p: (p, t)
    if kind == "tp":
        return 4, t, lambda p: (c, p)
    if kind == "pair":
        return 2, h, lambda p: (c - h + p, t)
    return 8, h * 4 + t, lambda p: (c - h + p // 4, lax.rem(p, 4))


PICKS = {
    "same": lambda ref, p: ref,
    "own": lambda ref, p: ref.at[p],
    "half": lambda ref, p: ref.at[lax.rem(p, 2)],
    "plane": lambda ref, p: ref.at[p // WORKERS],
}


def greet(kinds):
    barrier = pltpu.get_barrier_semaphore()
    total = 0
    for kind in kinds:
        n, me, dev = group(kind)

        @pl.loop(1, n)
        def _(i):
            pl.semaphore_signal(
                barrier, inc=1, device_id=dev(lax.rem(me + i, n)), device_id_type=MESH
            )

        total += n - 1
    pl.semaphore_wait(barrier, total)


def begin(kind, pick, src, dst, send, recv):
    n, me, dev = group(kind)
    choose = PICKS[pick]

    @pl.loop(1, n)
    def _(i):
        p = lax.rem(me + 5 * i, n)
        pltpu.make_async_remote_copy(
            src_ref=choose(src, p),
            dst_ref=dst.at[me],
            send_sem=send.at[p],
            recv_sem=recv.at[me],
            device_id=dev(p),
            device_id_type=MESH,
        ).start()

    pltpu.make_async_copy(choose(src, me), dst.at[me], recv.at[me]).start()


def finish(kind, pick, src, dst, send, recv):
    n, me, dev = group(kind)
    choose = PICKS[pick]

    @pl.loop(1, n)
    def _(i):
        p = lax.rem(me + i, n)
        copy = pltpu.make_async_remote_copy(
            src_ref=choose(src, p),
            dst_ref=dst.at[p],
            send_sem=send.at[p],
            recv_sem=recv.at[p],
            device_id=dev(p),
            device_id_type=MESH,
        )
        copy.wait_send()
        copy.wait_recv()

    pltpu.make_async_copy(choose(src, me), dst.at[me], recv.at[me]).wait()


SIZES = {"ctx": NCTX, "tp": 4, "pair": 2, "rows": 8}


def piece_shape(pick, array):
    return array.shape if pick == "same" else array.shape[1:]


def landing(kind, pick, array):
    return jax.ShapeDtypeStruct((SIZES[kind], *piece_shape(pick, array)), array.dtype)


def sems(kinds):
    return [pltpu.SemaphoreType.DMA((SIZES[k],)) for k in kinds for _ in range(2)]


def exchange_body(plan, kinds, *refs):
    n = len(plan)
    srcs, dsts, rest = refs[:n], refs[n : 2 * n], refs[2 * n :]
    greet(kinds)
    for k, (kind, pick) in enumerate(plan):
        begin(kind, pick, srcs[k], dsts[k], rest[2 * k], rest[2 * k + 1])
    for k, (kind, pick) in enumerate(plan):
        finish(kind, pick, srcs[k], dsts[k], rest[2 * k], rest[2 * k + 1])


def exchange(number, kinds, items):
    plan = tuple((kind, pick) for kind, pick, _ in items)
    return pl.pallas_call(
        functools.partial(exchange_body, plan, kinds),
        out_shape=[landing(*item) for item in items],
        in_specs=[ANY] * len(items),
        out_specs=[ANY] * len(items),
        scratch_shapes=sems([kind for kind, _ in plan]),
        compiler_params=pltpu.CompilerParams(collective_id=number, has_side_effects=True),
        name=f"exchange{number}",
    )(*[array for _, _, array in items])


def places():
    c, t = lax.axis_index("ctx"), lax.axis_index("tp")
    slot, low = c // WORKERS, lax.rem(c, WORKERS)
    to = low + lax.rem(slot, 2) * (WORKERS - 1 - 2 * low)
    return c, t, slot, low, to


def block_of(low, j):
    return j * WORKERS + (low if j % 2 == 0 else WORKERS - 1 - low)


def to_workers(src, dst, send, recv, act):
    c, t, slot, low, to = places()
    for p in range(PAIRS):
        target = p * WORKERS + to
        far = pltpu.make_async_remote_copy(
            src_ref=src.at[p],
            dst_ref=dst.at[slot],
            send_sem=send.at[p],
            recv_sem=recv.at[slot],
            device_id=(target, t),
            device_id_type=MESH,
        )
        near = pltpu.make_async_copy(src.at[p], dst.at[slot], send.at[p])

        @pl.when(target != c)
        def _():
            far.start() if act == "start" else far.wait_send()

        @pl.when(target == c)
        def _():
            near.start() if act == "start" else near.wait()


def from_owners(src, dst, send, recv):
    c, t, slot, low, to = places()
    for j in range(SLOTS):
        owner = block_of(low, j)

        @pl.when(owner != c)
        def _():
            pltpu.make_async_remote_copy(
                src_ref=src.at[j],
                dst_ref=dst.at[j],
                send_sem=send.at[j],
                recv_sem=recv.at[j],
                device_id=(owner, t),
                device_id_type=MESH,
            ).wait_recv()


def to_owner(src, dst, send, recv, j, act):
    c, t, slot, low, to = places()
    owner = block_of(low, j)
    far = pltpu.make_async_remote_copy(
        src_ref=src.at[j],
        dst_ref=dst.at[slot],
        send_sem=send.at[j],
        recv_sem=recv.at[slot],
        device_id=(owner, t),
        device_id_type=MESH,
    )
    near = pltpu.make_async_copy(src.at[j], dst.at[slot], send.at[j])

    @pl.when(owner != c)
    def _():
        far.start() if act == "start" else far.wait_send()

    @pl.when(owner == c)
    def _():
        near.start() if act == "start" else near.wait()


def from_workers(src, dst, send, recv):
    c, t, slot, low, to = places()
    for p in range(PAIRS):
        target = p * WORKERS + to

        @pl.when(target != c)
        def _():
            pltpu.make_async_remote_copy(
                src_ref=src.at[p],
                dst_ref=dst.at[p],
                send_sem=send.at[p],
                recv_sem=recv.at[p],
                device_id=(target, t),
                device_id_type=MESH,
            ).wait_recv()


def last_dims(a, b):
    return lax.dot_general(a, b, (((1,), (1,)), ((), ())), preferred_element_type=F32)


def first_dims(a, b):
    return lax.dot_general(a, b, (((0,), (0,)), ((), ())), preferred_element_type=F32)


def causal_mask(b, i):
    shape = (2 * BLOCK, 2 * BLOCK)
    rows = lax.broadcasted_iota(jnp.int32, shape, 0)
    token = b * BLOCK + jnp.where(rows >= BLOCK, rows - BLOCK, rows)
    key = i * 2 * BLOCK + lax.broadcasted_iota(jnp.int32, shape, 1)
    return token >= key


FORWARD_PLAN = (("ctx", "same"), ("pair", "same"))


def forward_body(
    q_src, kv_src, wo, cot,
    att, q_buf, kv_buf, o_buf, log_buf, wo_all, cot_all,
    acc, den, q_send, q_recv, o_send, o_recv, kv_send, kv_recv, *rest,
):
    c, t, slot, low, to = places()
    background = list(zip(FORWARD_PLAN, (wo, cot), (wo_all, cot_all)))
    greet(["ctx"])
    to_workers(q_src, q_buf, q_send, q_recv, "start")
    begin("ctx", "plane", kv_src, kv_buf, kv_send, kv_recv)
    for k, ((kind, pick), src, dst) in enumerate(background):
        begin(kind, pick, src, dst, rest[2 * k], rest[2 * k + 1])
    to_workers(q_src, q_buf, q_send, q_recv, "wait")
    from_owners(q_src, q_buf, q_send, q_recv)
    finish("ctx", "plane", kv_src, kv_buf, kv_send, kv_recv)
    lanes = lax.broadcasted_iota(jnp.int32, (2 * BLOCK, BLOCK), 1)
    for j in range(SLOTS):
        b = block_of(low, j)
        acc[...] = jnp.zeros_like(acc)
        den[...] = jnp.zeros_like(den)

        def chunk(i, masked):
            q = q_buf[j]
            kv = kv_buf[pl.ds(2 * i, 2)].reshape(2 * BLOCK, BLOCK)
            powered = jnp.exp(last_dims(q, kv))
            if masked:
                powered = jnp.where(causal_mask(b, i), powered, 0.0)
            den[...] += powered[:, :BLOCK] + powered[:, BLOCK:]
            acc[...] += jnp.dot(powered.astype(BF16), kv, preferred_element_type=F32)

        pl.loop(0, b // 2)(lambda i: chunk(i, False))
        chunk(b // 2, True)
        total = jnp.sum(den[...], axis=1, keepdims=True)
        o_buf[j] = jnp.where(lanes >= HEAD_SIZE, acc[...] / total, 0.0).astype(BF16)
        log_buf[j] = jnp.broadcast_to(jnp.log(total), (2 * BLOCK, BLOCK))
        to_owner(o_buf, att, o_send, o_recv, j, "start")
    for j in range(SLOTS):
        to_owner(o_buf, att, o_send, o_recv, j, "wait")
    from_workers(o_buf, att, o_send, o_recv)
    for k, ((kind, pick), src, dst) in enumerate(background):
        finish(kind, pick, src, dst, rest[2 * k], rest[2 * k + 1])


def forward(q_src, kv_src, wo, cot):
    stack = jax.ShapeDtypeStruct((SLOTS, 2 * BLOCK, BLOCK), BF16)
    kinds = [kind for kind, _ in FORWARD_PLAN]
    return pl.pallas_call(
        forward_body,
        out_shape=[
            stack,
            stack,
            jax.ShapeDtypeStruct((NCTX, BLOCK, BLOCK), BF16),
            stack,
            jax.ShapeDtypeStruct((SLOTS, 2 * BLOCK, BLOCK), F32),
        ]
        + [landing(k, p, a) for (k, p), a in zip(FORWARD_PLAN, (wo, cot))],
        in_specs=[ANY] * 4,
        out_specs=[ANY] + [VMEM] * 4 + [ANY] * 2,
        scratch_shapes=[
            pltpu.VMEM((2 * BLOCK, BLOCK), F32),
            pltpu.VMEM((2 * BLOCK, BLOCK), F32),
        ]
        + [pltpu.SemaphoreType.DMA((SLOTS,))] * 4
        + sems(["ctx"] + kinds),
        compiler_params=pltpu.CompilerParams(
            collective_id=2, has_side_effects=True, vmem_limit_bytes=24 * 2**20
        ),
        name="attention_forward",
    )(q_src, kv_src, wo, cot)


BACKWARD_PLAN = (("ctx", "own"), ("ctx", "own"), ("ctx", "own"), ("rows", "own"))


def backward_body(
    do_src, q_buf, kv_buf, o_buf, log_buf, wo, gu, dn, ffn,
    dq_all, dkv_all, wo_all, gu_all, dn_all, ffn_all,
    do_buf, dq_buf, dkv_buf, acc, dkv, do_send, do_recv, dq_send, dq_recv, kv_send, kv_recv, *rest,
):
    c, t, slot, low, to = places()
    background = list(zip(BACKWARD_PLAN, (wo, gu, dn, ffn), (wo_all, gu_all, dn_all, ffn_all)))
    greet(["ctx", "rows"])
    to_workers(do_src, do_buf, do_send, do_recv, "start")
    for k, ((kind, pick), src, dst) in enumerate(background):
        begin(kind, pick, src, dst, rest[2 * k], rest[2 * k + 1])
    dkv[...] = jnp.zeros_like(dkv)
    to_workers(do_src, do_buf, do_send, do_recv, "wait")
    from_owners(do_src, do_buf, do_send, do_recv)
    for j in range(SLOTS):
        b = block_of(low, j)
        acc[...] = jnp.zeros_like(acc)
        delta = jnp.sum(do_buf[j].astype(F32) * o_buf[j].astype(F32), axis=1, keepdims=True)

        def chunk(i, masked):
            q, do = q_buf[j], do_buf[j]
            kv = kv_buf[pl.ds(2 * i, 2)].reshape(2 * BLOCK, BLOCK)
            logs = log_buf[j]
            scores = last_dims(q, kv)
            probs = jnp.exp(scores - jnp.concatenate([logs, logs], axis=1))
            if masked:
                probs = jnp.where(causal_mask(b, i), probs, 0.0)
            grads = (probs * (last_dims(do, kv) - delta)).astype(BF16)
            acc[...] += jnp.dot(grads, kv, preferred_element_type=F32)
            update = first_dims(grads, q) + first_dims(probs.astype(BF16), do)
            dkv[pl.ds(2 * i, 2)] += update.reshape(2, BLOCK, BLOCK)

        pl.loop(0, b // 2)(lambda i: chunk(i, False))
        chunk(b // 2, True)
        dq_buf[j] = (acc[...] * (HEAD_SIZE**-0.5)).astype(BF16)
        to_owner(dq_buf, dq_all, dq_send, dq_recv, j, "start")
    dkv_buf[...] = dkv[...].astype(BF16)
    begin("ctx", "own", dkv_buf, dkv_all, kv_send, kv_recv)
    for j in range(SLOTS):
        to_owner(dq_buf, dq_all, dq_send, dq_recv, j, "wait")
    from_workers(dq_buf, dq_all, dq_send, dq_recv)
    finish("ctx", "own", dkv_buf, dkv_all, kv_send, kv_recv)
    for k, ((kind, pick), src, dst) in enumerate(background):
        finish(kind, pick, src, dst, rest[2 * k], rest[2 * k + 1])


def backward(do_src, q_buf, kv_buf, o_buf, log_buf, wo, gu, dn, ffn):
    kinds = [kind for kind, _ in BACKWARD_PLAN]
    return pl.pallas_call(
        backward_body,
        out_shape=[
            jax.ShapeDtypeStruct((SLOTS, 2 * BLOCK, BLOCK), BF16),
            jax.ShapeDtypeStruct((NCTX, BLOCK, BLOCK), BF16),
        ]
        + [landing(k, p, a) for (k, p), a in zip(BACKWARD_PLAN, (wo, gu, dn, ffn))],
        in_specs=[ANY] + [VMEM] * 4 + [ANY] * 4,
        out_specs=[ANY] * 6,
        scratch_shapes=[
            pltpu.VMEM((SLOTS, 2 * BLOCK, BLOCK), BF16),
            pltpu.VMEM((SLOTS, 2 * BLOCK, BLOCK), BF16),
            pltpu.VMEM((NCTX, BLOCK, BLOCK), BF16),
            pltpu.VMEM((2 * BLOCK, BLOCK), F32),
            pltpu.VMEM((NCTX, BLOCK, BLOCK), F32),
        ]
        + [pltpu.SemaphoreType.DMA((SLOTS,))] * 4
        + sems(["ctx"] + kinds),
        compiler_params=pltpu.CompilerParams(
            collective_id=6, has_side_effects=True, vmem_limit_bytes=24 * 2**20
        ),
        name="attention_backward",
    )(do_src, q_buf, kv_buf, o_buf, log_buf, wo, gu, dn, ffn)


def rms_scale(rows):
    return lax.rsqrt(jnp.mean(rows * rows, axis=-1, keepdims=True) + EPSILON)


def rope_tables(tokens, offset):
    half = HEAD_SIZE // 2
    inverse = ROPE_BASE ** (-(jnp.arange(half, dtype=F32) * 2.0 / HEAD_SIZE))
    places_ = (offset + jnp.arange(tokens, dtype=jnp.int32)).astype(F32)
    angles = places_[:, None] * inverse[None, :]
    return jnp.cos(angles), jnp.sin(angles)


def rotary(rows, cosine, sine, direction):
    half = HEAD_SIZE // 2
    first, second = rows[..., :half], rows[..., half:]
    cosine = cosine[:, None, :]
    sine = sine[:, None, :] * direction
    return jnp.concatenate([first * cosine - second * sine, second * cosine + first * sine], -1)


def head_back(grads, hatted, scale, gain):
    scaled = grads * gain
    return scale * (scaled - hatted * jnp.mean(scaled * hatted, axis=-1, keepdims=True))


def row_back(grads, normed, scale, gain):
    scaled = grads * gain
    return scale * (scaled - normed * jnp.mean(scaled * normed, axis=-1, keepdims=True))


def to_pairs(rows, heads, left):
    s, tokens = rows.shape[:2]
    kv = rows.shape[2] // heads
    x = rows.reshape(s, tokens, kv, heads, HEAD_SIZE).transpose(2, 0, 3, 1, 4)
    x = x.reshape(kv * s, heads * tokens, HEAD_SIZE)
    side = (0, HEAD_SIZE) if left else (HEAD_SIZE, 0)
    return jnp.pad(x, ((0, 0), (0, 0), side))


def from_pairs(x, s, heads):
    kv = x.shape[0] // s
    tokens = x.shape[1] // heads
    x = x.reshape(kv, s, heads, tokens, HEAD_SIZE).transpose(1, 3, 0, 2, 4)
    return x.reshape(s, tokens, kv * heads, HEAD_SIZE)


def halves(w):
    half = w.shape[1] // 2
    return jnp.stack([w[:, :half], w[:, half:]])


def local(
    block_input, cotangent, w_query, key_weight, w_value, w_out, w_gate, w_up, w_down,
    norm_gains, head_gains,
):
    c, t = lax.axis_index("ctx"), lax.axis_index("tp")
    seqs, tokens, width = block_input.shape
    rows = seqs * tokens
    own = rows // 4
    unit_half = w_gate.shape[1] // 2

    def mine(x):
        return lax.dynamic_slice_in_dim(x, t * own, own, 0)

    weight_rows = jnp.concatenate([w_query, key_weight, w_value], axis=1)
    gains = jnp.zeros((16, 128), BF16)
    gains = gains.at[0:2, 0:32].set(norm_gains).at[2:4, 0:2].set(head_gains)
    ffn_rows = jnp.concatenate([halves(w_gate), halves(w_up), halves(w_down)], axis=2)
    weights_all, gains_all, ffn_pair = exchange(
        1,
        ["ctx"],
        [("ctx", "same", weight_rows), ("ctx", "same", gains), ("pair", "own", ffn_rows)],
    )
    planes = [[2 * g + h for g in range(NCTX // 2)] for h in range(2)]
    ffn_full = lax.all_gather(
        ffn_pair.reshape(2 * 32, 3 * unit_half), "ctx", axis_index_groups=planes, tiled=True
    )
    qkv_full = weights_all.reshape(width, weight_rows.shape[1])
    gain_attn = gains_all[:, 0, :32].reshape(width).astype(F32)
    gain_ffn = gains_all[:, 1, :32].reshape(width).astype(F32)
    gain_query = gains_all[:, 2, :2].reshape(HEAD_SIZE).astype(F32)
    gain_key = gains_all[:, 3, :2].reshape(HEAD_SIZE).astype(F32)

    inputs = block_input.astype(F32).reshape(rows, width)
    scale_attn = rms_scale(inputs)
    normed_attn = inputs * scale_attn
    hidden_attn = (normed_attn * gain_attn).astype(BF16)
    raw = jnp.dot(hidden_attn, qkv_full, preferred_element_type=F32)
    query_raw = raw[:, :256].reshape(seqs, tokens, 4, HEAD_SIZE)
    key_raw = raw[:, 256:384].reshape(seqs, tokens, 2, HEAD_SIZE)
    values = raw[:, 384:].astype(BF16).reshape(seqs, tokens, 2, HEAD_SIZE)
    query_scale, key_scale = rms_scale(query_raw), rms_scale(key_raw)
    query_hat, key_hat = query_raw * query_scale, key_raw * key_scale
    cosine, sine = rope_tables(tokens, c * tokens)
    query_rot = rotary(query_hat * gain_query, cosine, sine, 1.0).astype(BF16)
    key_rot = rotary(key_hat * gain_key, cosine, sine, 1.0).astype(BF16)
    q_src = to_pairs(query_rot * jnp.asarray(HEAD_SIZE**-0.5, BF16), 2, True)
    kv_src = jnp.concatenate([key_rot, values], axis=-1).transpose(2, 0, 1, 3)
    kv_src = kv_src.reshape(PAIRS, tokens, 2 * HEAD_SIZE)

    att, q_buf, kv_buf, o_buf, log_buf, wo_all, cot_all = forward(
        q_src, kv_src, w_out, cotangent.reshape(rows, width)
    )
    attended = from_pairs(att[..., HEAD_SIZE:], seqs, 2).reshape(rows, 256)
    out_full = wo_all.reshape(width, 256)
    gu_full = ffn_full[:, : 2 * unit_half]
    dn_full = ffn_full[:, 2 * unit_half :]
    cot_rows = cot_all.reshape(2 * rows, width)

    attn_part = last_dims(attended, out_full).astype(BF16)
    (attn_parts,) = exchange(3, ["tp"], [("tp", "own", attn_part.reshape(4, own, width))])
    residual = mine(inputs) + jnp.sum(attn_parts.astype(F32), axis=0)
    scale_ffn = rms_scale(residual)
    normed_ffn = residual * scale_ffn
    hidden_own = (normed_ffn * gain_ffn).astype(BF16)
    (hidden_all,) = exchange(4, ["rows"], [("rows", "same", hidden_own)])
    hidden_ffn = hidden_all.reshape(2 * rows, width)

    gu_raw = jnp.dot(hidden_ffn, gu_full, preferred_element_type=F32)
    gate_raw, up_raw = gu_raw[:, :unit_half], gu_raw[:, unit_half:]
    sigmoid = jax.nn.sigmoid(gate_raw)
    activated = gate_raw * sigmoid
    hidden_units = (activated * up_raw).astype(BF16)
    grad_units = jnp.dot(cot_rows, dn_full, preferred_element_type=F32)
    grad_gate_in = grad_units * up_raw * sigmoid * (1.0 + gate_raw * (1.0 - sigmoid))
    grad_up_in = grad_units * activated
    grad_gu_in = jnp.concatenate([grad_gate_in, grad_up_in], axis=1).astype(BF16)
    ffn_back = last_dims(grad_gu_in, gu_full).astype(BF16)
    (back_parts,) = exchange(5, ["rows"], [("rows", "own", ffn_back.reshape(8, own, width))])
    grad_hidden_ffn = jnp.sum(back_parts.astype(F32), axis=0)
    ffn_gain_part = jnp.sum(grad_hidden_ffn * normed_ffn, axis=0)
    cot_own = mine(cotangent.reshape(rows, width)).astype(F32)
    grad_residual = cot_own + row_back(grad_hidden_ffn, normed_ffn, scale_ffn, gain_ffn)
    (residual_all,) = exchange(7, ["tp"], [("tp", "same", grad_residual.astype(BF16))])
    residual_bf = residual_all.reshape(rows, width)

    grad_attended = jnp.dot(residual_bf, out_full, preferred_element_type=F32).astype(BF16)
    do_src = to_pairs(grad_attended.reshape(seqs, tokens, 4, HEAD_SIZE), 2, False)
    grad_out = first_dims(residual_bf, attended).astype(BF16)
    grad_gu = first_dims(hidden_ffn, grad_gu_in).astype(BF16)
    grad_dn = first_dims(cot_rows, hidden_units).astype(BF16)
    ffn_part = last_dims(hidden_units, dn_full).astype(BF16)
    dq_all, dkv_all, wo_parts, gu_parts, dn_parts, ffn_parts = backward(
        do_src, q_buf, kv_buf, o_buf, log_buf,
        grad_out.reshape(NCTX, 32, 256),
        grad_gu.reshape(NCTX, 32, 2 * unit_half),
        grad_dn.reshape(NCTX, 32, unit_half),
        ffn_part.reshape(8, own, width),
    )

    output_own = (residual + jnp.sum(ffn_parts.astype(F32), axis=0)).astype(BF16)
    grad_query_rot = from_pairs(dq_all[..., :HEAD_SIZE].astype(F32), seqs, 2)
    dkv = jnp.sum(dkv_all.reshape(PAIRS, WORKERS, tokens, 2 * HEAD_SIZE).astype(F32), axis=1)
    key_grad = from_pairs(dkv[..., :HEAD_SIZE], seqs, 1)
    value_in = from_pairs(dkv[..., HEAD_SIZE:], seqs, 1).astype(BF16).reshape(rows, 128)
    gq = rotary(grad_query_rot, cosine, sine, -1.0)
    gk = rotary(key_grad, cosine, sine, -1.0)
    query_gain_part = jnp.sum(gq * query_hat, axis=(0, 1, 2))
    key_gain_part = jnp.sum(gk * key_hat, axis=(0, 1, 2))
    query_in = head_back(gq, query_hat, query_scale, gain_query).astype(BF16).reshape(rows, 256)
    key_in = head_back(gk, key_hat, key_scale, gain_key).astype(BF16).reshape(rows, 128)
    grad_in = jnp.concatenate([query_in, key_in, value_in], axis=1)
    grad_qkv = first_dims(hidden_attn, grad_in).astype(BF16)
    attn_back = last_dims(grad_in, qkv_full)
    attn_gain_part = jnp.sum(attn_back * normed_attn, axis=0)
    gain_parts = jnp.zeros((NCTX, 8, 128), F32)
    gain_parts = gain_parts.at[:, 0, :32].set(attn_gain_part.reshape(NCTX, 32))
    gain_parts = gain_parts.at[:, 1, :32].set(ffn_gain_part.reshape(NCTX, 32))
    gain_parts = gain_parts.at[:, 2, :2].set(query_gain_part.reshape(NCTX, 2))
    gain_parts = gain_parts.at[:, 3, :2].set(key_gain_part.reshape(NCTX, 2))
    attn_parts, qkv_parts, gain_all, output_all = exchange(
        8,
        ["ctx", "tp"],
        [
            ("tp", "own", attn_back.astype(BF16).reshape(4, own, width)),
            ("ctx", "own", grad_qkv.reshape(NCTX, 32, 512)),
            ("ctx", "own", gain_parts),
            ("tp", "same", output_own),
        ],
    )
    grad_hidden_attn = jnp.sum(attn_parts.astype(F32), axis=0)
    input_own = grad_residual + row_back(
        grad_hidden_attn, mine(normed_attn), mine(scale_attn), gain_attn
    )
    input_all, gain_tp = exchange(
        9,
        ["tp"],
        [("tp", "same", input_own.astype(BF16)), ("tp", "same", jnp.sum(gain_all, axis=0))],
    )
    gain_sum = jnp.sum(gain_tp, axis=0)
    qkv_grad = jnp.sum(qkv_parts.astype(F32), axis=0)
    out_grad = jnp.sum(wo_parts.astype(F32), axis=0)
    gu_grad = jnp.sum(gu_parts.reshape(16, 2, 32, 2 * unit_half).astype(F32), axis=0)
    dn_grad = jnp.sum(dn_parts.reshape(16, 2, 32, unit_half).astype(F32), axis=0)
    gate_grad = jnp.concatenate([gu_grad[0, :, :unit_half], gu_grad[1, :, :unit_half]], axis=1)
    up_grad = jnp.concatenate([gu_grad[0, :, unit_half:], gu_grad[1, :, unit_half:]], axis=1)
    down_grad = jnp.concatenate([dn_grad[0], dn_grad[1]], axis=1)
    return (
        output_all.reshape(seqs, tokens, width),
        input_all.astype(F32).reshape(seqs, tokens, width),
        qkv_grad[:, :256],
        qkv_grad[:, 256:384],
        qkv_grad[:, 384:],
        out_grad,
        gate_grad,
        up_grad,
        down_grad,
        gain_sum[0:2, :32],
        gain_sum[2:4, :2],
    )


def solution(mesh):
    tokens, weights = P(None, "ctx", None), P("ctx", "tp")
    return jax.shard_map(
        local,
        mesh=mesh,
        in_specs=(tokens,) * 2 + (weights,) * 7 + (P(None, "ctx"),) * 2,
        out_specs=(tokens,) * 2 + (weights,) * 7 + (P(None, "ctx"),) * 2,
        check_vma=False,
    )
```

```python
import functools

import jax
import jax.numpy as jnp
from jax import lax
from jax.experimental import pallas as pl
from jax.experimental.pallas import tpu as pltpu
from jax.sharding import PartitionSpec as P

HEAD_SIZE = 64
EPSILON = 1e-06
ROPE_BASE = 1000000.0
MESH = pl.DeviceIdType.MESH
F32 = jnp.float32
BF16 = jnp.bfloat16
ANY = pl.BlockSpec(memory_space=pl.ANY)
VMEM = pl.BlockSpec(memory_space=pltpu.VMEM)
NCTX = 32
PAIRS = 4
WORKERS = 8
SLOTS = 4
BLOCK = 128


def group(kind):
    c, t = lax.axis_index("ctx"), lax.axis_index("tp")
    h = lax.rem(c, 2)
    if kind == "ctx":
        return NCTX, c, lambda p: (p, t)
    if kind == "tp":
        return 4, t, lambda p: (c, p)
    if kind == "pair":
        return 2, h, lambda p: (c - h + p, t)
    return 8, h * 4 + t, lambda p: (c - h + p // 4, lax.rem(p, 4))


PICKS = {
    "same": lambda ref, p: ref,
    "own": lambda ref, p: ref.at[p],
    "half": lambda ref, p: ref.at[lax.rem(p, 2)],
    "plane": lambda ref, p: ref.at[p // WORKERS],
}


def greet(kinds):
    barrier = pltpu.get_barrier_semaphore()
    total = 0
    for kind in kinds:
        n, me, dev = group(kind)

        @pl.loop(1, n)
        def _(i):
            pl.semaphore_signal(
                barrier, inc=1, device_id=dev(lax.rem(me + i, n)), device_id_type=MESH
            )

        total += n - 1
    pl.semaphore_wait(barrier, total)


def begin(kind, pick, src, dst, send, recv):
    n, me, dev = group(kind)
    choose = PICKS[pick]

    @pl.loop(1, n)
    def _(i):
        p = lax.rem(me + 5 * i, n)
        pltpu.make_async_remote_copy(
            src_ref=choose(src, p),
            dst_ref=dst.at[me],
            send_sem=send.at[p],
            recv_sem=recv.at[me],
            device_id=dev(p),
            device_id_type=MESH,
        ).start()

    pltpu.make_async_copy(choose(src, me), dst.at[me], recv.at[me]).start()


def finish(kind, pick, src, dst, send, recv):
    n, me, dev = group(kind)
    choose = PICKS[pick]

    @pl.loop(1, n)
    def _(i):
        p = lax.rem(me + i, n)
        copy = pltpu.make_async_remote_copy(
            src_ref=choose(src, p),
            dst_ref=dst.at[p],
            send_sem=send.at[p],
            recv_sem=recv.at[p],
            device_id=dev(p),
            device_id_type=MESH,
        )
        copy.wait_send()
        copy.wait_recv()

    pltpu.make_async_copy(choose(src, me), dst.at[me], recv.at[me]).wait()


SIZES = {"ctx": NCTX, "tp": 4, "pair": 2, "rows": 8}


def piece_shape(pick, array):
    return array.shape if pick == "same" else array.shape[1:]


def landing(kind, pick, array):
    return jax.ShapeDtypeStruct((SIZES[kind], *piece_shape(pick, array)), array.dtype)


def sems(kinds):
    return [pltpu.SemaphoreType.DMA((SIZES[k],)) for k in kinds for _ in range(2)]


def exchange_body(plan, kinds, *refs):
    n = len(plan)
    srcs, dsts, rest = refs[:n], refs[n : 2 * n], refs[2 * n :]
    greet(kinds)
    for k, (kind, pick) in enumerate(plan):
        begin(kind, pick, srcs[k], dsts[k], rest[2 * k], rest[2 * k + 1])
    for k, (kind, pick) in enumerate(plan):
        finish(kind, pick, srcs[k], dsts[k], rest[2 * k], rest[2 * k + 1])


def exchange(number, kinds, items):
    plan = tuple((kind, pick) for kind, pick, _ in items)
    return pl.pallas_call(
        functools.partial(exchange_body, plan, kinds),
        out_shape=[landing(*item) for item in items],
        in_specs=[ANY] * len(items),
        out_specs=[ANY] * len(items),
        scratch_shapes=sems([kind for kind, _ in plan]),
        compiler_params=pltpu.CompilerParams(collective_id=number, has_side_effects=True),
        name=f"exchange{number}",
    )(*[array for _, _, array in items])


def places():
    c, t = lax.axis_index("ctx"), lax.axis_index("tp")
    slot, low = c // WORKERS, lax.rem(c, WORKERS)
    to = low + lax.rem(slot, 2) * (WORKERS - 1 - 2 * low)
    return c, t, slot, low, to


def block_of(low, j):
    return j * WORKERS + (low if j % 2 == 0 else WORKERS - 1 - low)


def to_workers(src, dst, send, recv, act):
    c, t, slot, low, to = places()
    for p in range(PAIRS):
        target = p * WORKERS + to
        far = pltpu.make_async_remote_copy(
            src_ref=src.at[p],
            dst_ref=dst.at[slot],
            send_sem=send.at[p],
            recv_sem=recv.at[slot],
            device_id=(target, t),
            device_id_type=MESH,
        )
        near = pltpu.make_async_copy(src.at[p], dst.at[slot], send.at[p])

        @pl.when(target != c)
        def _():
            far.start() if act == "start" else far.wait_send()

        @pl.when(target == c)
        def _():
            near.start() if act == "start" else near.wait()


def from_owners(src, dst, send, recv):
    c, t, slot, low, to = places()
    for j in range(SLOTS):
        owner = block_of(low, j)

        @pl.when(owner != c)
        def _():
            pltpu.make_async_remote_copy(
                src_ref=src.at[j],
                dst_ref=dst.at[j],
                send_sem=send.at[j],
                recv_sem=recv.at[j],
                device_id=(owner, t),
                device_id_type=MESH,
            ).wait_recv()


def to_owner(src, dst, send, recv, j, act):
    c, t, slot, low, to = places()
    owner = block_of(low, j)
    far = pltpu.make_async_remote_copy(
        src_ref=src.at[j],
        dst_ref=dst.at[slot],
        send_sem=send.at[j],
        recv_sem=recv.at[slot],
        device_id=(owner, t),
        device_id_type=MESH,
    )
    near = pltpu.make_async_copy(src.at[j], dst.at[slot], send.at[j])

    @pl.when(owner != c)
    def _():
        far.start() if act == "start" else far.wait_send()

    @pl.when(owner == c)
    def _():
        near.start() if act == "start" else near.wait()


def from_workers(src, dst, send, recv):
    c, t, slot, low, to = places()
    for p in range(PAIRS):
        target = p * WORKERS + to

        @pl.when(target != c)
        def _():
            pltpu.make_async_remote_copy(
                src_ref=src.at[p],
                dst_ref=dst.at[p],
                send_sem=send.at[p],
                recv_sem=recv.at[p],
                device_id=(target, t),
                device_id_type=MESH,
            ).wait_recv()


def last_dims(a, b):
    return lax.dot_general(a, b, (((1,), (1,)), ((), ())), preferred_element_type=F32)


def first_dims(a, b):
    return lax.dot_general(a, b, (((0,), (0,)), ((), ())), preferred_element_type=F32)


def causal_mask(b, i):
    shape = (2 * BLOCK, 2 * BLOCK)
    rows = lax.broadcasted_iota(jnp.int32, shape, 0)
    token = b * BLOCK + jnp.where(rows >= BLOCK, rows - BLOCK, rows)
    key = i * 2 * BLOCK + lax.broadcasted_iota(jnp.int32, shape, 1)
    return token >= key


FORWARD_PLAN = (("ctx", "same"), ("pair", "same"))


def forward_body(
    q_src, kv_src, wo, cot,
    att, q_buf, kv_buf, o_buf, log_buf, wo_all, cot_all,
    acc, den, q_send, q_recv, o_send, o_recv, kv_send, kv_recv, *rest,
):
    c, t, slot, low, to = places()
    background = list(zip(FORWARD_PLAN, (wo, cot), (wo_all, cot_all)))
    greet(["ctx"])
    to_workers(q_src, q_buf, q_send, q_recv, "start")
    begin("ctx", "plane", kv_src, kv_buf, kv_send, kv_recv)
    for k, ((kind, pick), src, dst) in enumerate(background):
        begin(kind, pick, src, dst, rest[2 * k], rest[2 * k + 1])
    to_workers(q_src, q_buf, q_send, q_recv, "wait")
    from_owners(q_src, q_buf, q_send, q_recv)
    finish("ctx", "plane", kv_src, kv_buf, kv_send, kv_recv)
    lanes = lax.broadcasted_iota(jnp.int32, (2 * BLOCK, BLOCK), 1)
    for j in range(SLOTS):
        b = block_of(low, j)
        acc[...] = jnp.zeros_like(acc)
        den[...] = jnp.zeros_like(den)

        def chunk(i, masked):
            q = q_buf[j]
            kv = kv_buf[pl.ds(2 * i, 2)].reshape(2 * BLOCK, BLOCK)
            powered = jnp.exp(last_dims(q, kv))
            if masked:
                powered = jnp.where(causal_mask(b, i), powered, 0.0)
            den[...] += powered[:, :BLOCK] + powered[:, BLOCK:]
            acc[...] += jnp.dot(powered.astype(BF16), kv, preferred_element_type=F32)

        pl.loop(0, b // 2)(lambda i: chunk(i, False))
        chunk(b // 2, True)
        total = jnp.sum(den[...], axis=1, keepdims=True)
        o_buf[j] = jnp.where(lanes >= HEAD_SIZE, acc[...] / total, 0.0).astype(BF16)
        log_buf[j] = jnp.broadcast_to(jnp.log(total), (2 * BLOCK, BLOCK))
        to_owner(o_buf, att, o_send, o_recv, j, "start")
    for j in range(SLOTS):
        to_owner(o_buf, att, o_send, o_recv, j, "wait")
    from_workers(o_buf, att, o_send, o_recv)
    for k, ((kind, pick), src, dst) in enumerate(background):
        finish(kind, pick, src, dst, rest[2 * k], rest[2 * k + 1])


def forward(q_src, kv_src, wo, cot):
    stack = jax.ShapeDtypeStruct((SLOTS, 2 * BLOCK, BLOCK), BF16)
    kinds = [kind for kind, _ in FORWARD_PLAN]
    return pl.pallas_call(
        forward_body,
        out_shape=[
            stack,
            stack,
            jax.ShapeDtypeStruct((NCTX, BLOCK, BLOCK), BF16),
            stack,
            jax.ShapeDtypeStruct((SLOTS, 2 * BLOCK, BLOCK), F32),
        ]
        + [landing(k, p, a) for (k, p), a in zip(FORWARD_PLAN, (wo, cot))],
        in_specs=[ANY] * 4,
        out_specs=[ANY] + [VMEM] * 4 + [ANY] * 2,
        scratch_shapes=[
            pltpu.VMEM((2 * BLOCK, BLOCK), F32),
            pltpu.VMEM((2 * BLOCK, BLOCK), F32),
        ]
        + [pltpu.SemaphoreType.DMA((SLOTS,))] * 4
        + sems(["ctx"] + kinds),
        compiler_params=pltpu.CompilerParams(
            collective_id=2, has_side_effects=True, vmem_limit_bytes=24 * 2**20
        ),
        name="attention_forward",
    )(q_src, kv_src, wo, cot)


BACKWARD_PLAN = (("rows", "own"),)


def backward_body(
    do_src, q_buf, kv_buf, o_buf, log_buf, ffn, dq_all, dkv_all, ffn_all,
    do_buf, dq_buf, dkv_buf, acc, dkv, do_send, do_recv, dq_send, dq_recv, kv_send, kv_recv, *rest,
):
    c, t, slot, low, to = places()
    background = list(zip(BACKWARD_PLAN, (ffn,), (ffn_all,)))
    greet(["ctx", "rows"])
    to_workers(do_src, do_buf, do_send, do_recv, "start")
    for k, ((kind, pick), src, dst) in enumerate(background):
        begin(kind, pick, src, dst, rest[2 * k], rest[2 * k + 1])
    dkv[...] = jnp.zeros_like(dkv)
    to_workers(do_src, do_buf, do_send, do_recv, "wait")
    from_owners(do_src, do_buf, do_send, do_recv)
    for j in range(SLOTS):
        b = block_of(low, j)
        acc[...] = jnp.zeros_like(acc)
        delta = jnp.sum(do_buf[j].astype(F32) * o_buf[j].astype(F32), axis=1, keepdims=True)

        def chunk(i, masked):
            q, do = q_buf[j], do_buf[j]
            kv = kv_buf[pl.ds(2 * i, 2)].reshape(2 * BLOCK, BLOCK)
            logs = log_buf[j]
            scores = last_dims(q, kv)
            probs = jnp.exp(scores - jnp.concatenate([logs, logs], axis=1))
            if masked:
                probs = jnp.where(causal_mask(b, i), probs, 0.0)
            grads = (probs * (last_dims(do, kv) - delta)).astype(BF16)
            acc[...] += jnp.dot(grads, kv, preferred_element_type=F32)
            update = first_dims(grads, q) + first_dims(probs.astype(BF16), do)
            dkv[pl.ds(2 * i, 2)] += update.reshape(2, BLOCK, BLOCK)

        pl.loop(0, b // 2)(lambda i: chunk(i, False))
        chunk(b // 2, True)
        dq_buf[j] = (acc[...] * (HEAD_SIZE**-0.5)).astype(BF16)
        to_owner(dq_buf, dq_all, dq_send, dq_recv, j, "start")
    dkv_buf[...] = dkv[...].astype(BF16)
    begin("ctx", "own", dkv_buf, dkv_all, kv_send, kv_recv)
    for j in range(SLOTS):
        to_owner(dq_buf, dq_all, dq_send, dq_recv, j, "wait")
    from_workers(dq_buf, dq_all, dq_send, dq_recv)
    finish("ctx", "own", dkv_buf, dkv_all, kv_send, kv_recv)
    for k, ((kind, pick), src, dst) in enumerate(background):
        finish(kind, pick, src, dst, rest[2 * k], rest[2 * k + 1])


def backward(do_src, q_buf, kv_buf, o_buf, log_buf, ffn):
    kinds = [kind for kind, _ in BACKWARD_PLAN]
    return pl.pallas_call(
        backward_body,
        out_shape=[
            jax.ShapeDtypeStruct((SLOTS, 2 * BLOCK, BLOCK), BF16),
            jax.ShapeDtypeStruct((NCTX, BLOCK, BLOCK), BF16),
        ]
        + [landing(k, p, a) for (k, p), a in zip(BACKWARD_PLAN, (ffn,))],
        in_specs=[ANY] + [VMEM] * 4 + [ANY],
        out_specs=[ANY] * 3,
        scratch_shapes=[
            pltpu.VMEM((SLOTS, 2 * BLOCK, BLOCK), BF16),
            pltpu.VMEM((SLOTS, 2 * BLOCK, BLOCK), BF16),
            pltpu.VMEM((NCTX, BLOCK, BLOCK), BF16),
            pltpu.VMEM((2 * BLOCK, BLOCK), F32),
            pltpu.VMEM((NCTX, BLOCK, BLOCK), F32),
        ]
        + [pltpu.SemaphoreType.DMA((SLOTS,))] * 4
        + sems(["ctx"] + kinds),
        compiler_params=pltpu.CompilerParams(
            collective_id=6, has_side_effects=True, vmem_limit_bytes=24 * 2**20
        ),
        name="attention_backward",
    )(do_src, q_buf, kv_buf, o_buf, log_buf, ffn)


def row_scale(rows):
    return lax.rsqrt(jnp.mean(rows * rows, axis=1, keepdims=True) + EPSILON)


def row_back(grads, normed, scale, gain):
    scaled = grads * gain
    return scale * (scaled - normed * jnp.mean(scaled * normed, axis=1, keepdims=True))


def summed(ref):
    total = ref[0].astype(F32)
    for k in range(1, ref.shape[0]):
        total += ref[k].astype(F32)
    return total


def norm_body(
    parts, inputs, gain, residual, hidden_all, landed, hidden, send0, recv0, send1, recv1
):
    greet(["rows"])
    begin("tp", "own", parts, landed, send0, recv0)
    finish("tp", "own", parts, landed, send0, recv0)
    total = inputs[...] + summed(landed)
    residual[...] = total
    hidden[...] = (total * row_scale(total) * gain[...]).astype(BF16)
    begin("rows", "same", hidden, hidden_all, send1, recv1)
    finish("rows", "same", hidden, hidden_all, send1, recv1)


def norm_step(parts, inputs, gain):
    own, width = inputs.shape
    return pl.pallas_call(
        norm_body,
        out_shape=[
            jax.ShapeDtypeStruct((own, width), F32),
            jax.ShapeDtypeStruct((8, own, width), BF16),
        ],
        in_specs=[VMEM] * 3,
        out_specs=[VMEM, ANY],
        scratch_shapes=[pltpu.VMEM((4, own, width), BF16), pltpu.VMEM((own, width), BF16)]
        + sems(["tp", "rows"]),
        compiler_params=pltpu.CompilerParams(collective_id=3, has_side_effects=True),
        name="norm_step",
    )(parts, inputs, gain)


def norm_back_body(
    parts, residual, cot, gain, grad_residual, gain_part, grad_all,
    landed, grad_bf, send0, recv0, send1, recv1,
):
    greet(["rows"])
    begin("rows", "own", parts, landed, send0, recv0)
    rows = residual[...]
    scale = row_scale(rows)
    normed = rows * scale
    finish("rows", "own", parts, landed, send0, recv0)
    grads = summed(landed)
    result = cot[...].astype(F32) + row_back(grads, normed, scale, gain[...])
    grad_bf[...] = result.astype(BF16)
    begin("tp", "same", grad_bf, grad_all, send1, recv1)
    grad_residual[...] = result
    gain_part[...] = jnp.sum(grads * normed, axis=0, keepdims=True)
    finish("tp", "same", grad_bf, grad_all, send1, recv1)


def norm_back_step(parts, residual, cot, gain):
    own, width = residual.shape
    return pl.pallas_call(
        norm_back_body,
        out_shape=[
            jax.ShapeDtypeStruct((own, width), F32),
            jax.ShapeDtypeStruct((1, width), F32),
            jax.ShapeDtypeStruct((4, own, width), BF16),
        ],
        in_specs=[VMEM] * 4,
        out_specs=[VMEM, VMEM, ANY],
        scratch_shapes=[pltpu.VMEM((8, own, width), BF16), pltpu.VMEM((own, width), BF16)]
        + sems(["rows", "tp"]),
        compiler_params=pltpu.CompilerParams(collective_id=5, has_side_effects=True),
        name="norm_back_step",
    )(parts, residual, cot, gain)


def last_body(
    parts, qkv, gains, output, grad_residual, inputs, gain,
    qkv_all, output_all, input_all, gain_tp,
    landed, gain_all, input_bf, gain_sum, *sem,
):
    greet(["ctx", "tp"])
    begin("tp", "own", parts, landed, sem[0], sem[1])
    begin("ctx", "own", gains, gain_all, sem[2], sem[3])
    begin("ctx", "own", qkv, qkv_all, sem[4], sem[5])
    begin("tp", "same", output, output_all, sem[6], sem[7])
    rows = inputs[...]
    scale = row_scale(rows)
    normed = rows * scale
    finish("tp", "own", parts, landed, sem[0], sem[1])
    result = grad_residual[...] + row_back(summed(landed), normed, scale, gain[...])
    input_bf[...] = result.astype(BF16)
    begin("tp", "same", input_bf, input_all, sem[8], sem[9])
    finish("ctx", "own", gains, gain_all, sem[2], sem[3])
    gain_sum[...] = summed(gain_all)
    begin("tp", "same", gain_sum, gain_tp, sem[10], sem[11])
    finish("tp", "same", output, output_all, sem[6], sem[7])
    finish("tp", "same", input_bf, input_all, sem[8], sem[9])
    finish("tp", "same", gain_sum, gain_tp, sem[10], sem[11])
    finish("ctx", "own", qkv, qkv_all, sem[4], sem[5])


def last_step(parts, qkv, gains, output, grad_residual, inputs, gain):
    own, width = inputs.shape
    return pl.pallas_call(
        last_body,
        out_shape=[
            jax.ShapeDtypeStruct(qkv.shape, BF16),
            jax.ShapeDtypeStruct((4, own, width), BF16),
            jax.ShapeDtypeStruct((4, own, width), BF16),
            jax.ShapeDtypeStruct((4, *gains.shape[1:]), F32),
        ],
        in_specs=[VMEM, ANY, VMEM, VMEM, VMEM, VMEM, VMEM],
        out_specs=[ANY] * 4,
        scratch_shapes=[
            pltpu.VMEM((4, own, width), BF16),
            pltpu.VMEM(gains.shape, F32),
            pltpu.VMEM((own, width), BF16),
            pltpu.VMEM(gains.shape[1:], F32),
        ]
        + sems(["tp", "ctx", "ctx", "tp", "tp", "tp"]),
        compiler_params=pltpu.CompilerParams(collective_id=8, has_side_effects=True),
        name="last_step",
    )(parts, qkv, gains, output, grad_residual, inputs, gain)


def rms_scale(rows):
    return lax.rsqrt(jnp.mean(rows * rows, axis=-1, keepdims=True) + EPSILON)


def rope_tables(tokens, offset):
    half = HEAD_SIZE // 2
    inverse = ROPE_BASE ** (-(jnp.arange(half, dtype=F32) * 2.0 / HEAD_SIZE))
    places_ = (offset + jnp.arange(tokens, dtype=jnp.int32)).astype(F32)
    angles = places_[:, None] * inverse[None, :]
    return jnp.cos(angles), jnp.sin(angles)


def rotary(rows, cosine, sine, direction):
    half = HEAD_SIZE // 2
    first, second = rows[..., :half], rows[..., half:]
    cosine = cosine[:, None, :]
    sine = sine[:, None, :] * direction
    return jnp.concatenate([first * cosine - second * sine, second * cosine + first * sine], -1)


def head_back(grads, hatted, scale, gain):
    scaled = grads * gain
    return scale * (scaled - hatted * jnp.mean(scaled * hatted, axis=-1, keepdims=True))


def to_pairs(rows, heads, left):
    s, tokens = rows.shape[:2]
    kv = rows.shape[2] // heads
    x = rows.reshape(s, tokens, kv, heads, HEAD_SIZE).transpose(2, 0, 3, 1, 4)
    x = x.reshape(kv * s, heads * tokens, HEAD_SIZE)
    side = (0, HEAD_SIZE) if left else (HEAD_SIZE, 0)
    return jnp.pad(x, ((0, 0), (0, 0), side))


def from_pairs(x, s, heads):
    kv = x.shape[0] // s
    tokens = x.shape[1] // heads
    x = x.reshape(kv, s, heads, tokens, HEAD_SIZE).transpose(1, 3, 0, 2, 4)
    return x.reshape(s, tokens, kv * heads, HEAD_SIZE)


def halves(w):
    half = w.shape[1] // 2
    return jnp.stack([w[:, :half], w[:, half:]])


def local(
    block_input, cotangent, w_query, key_weight, w_value, w_out, w_gate, w_up, w_down,
    norm_gains, head_gains,
):
    c, t = lax.axis_index("ctx"), lax.axis_index("tp")
    seqs, tokens, width = block_input.shape
    rows = seqs * tokens
    own = rows // 4
    unit_half = w_gate.shape[1] // 2

    def mine(x):
        return lax.dynamic_slice_in_dim(x, t * own, own, 0)

    weight_rows = jnp.concatenate([w_query, key_weight, w_value], axis=1)
    gains = jnp.zeros((16, 128), BF16)
    gains = gains.at[0:2, 0:32].set(norm_gains).at[2:4, 0:2].set(head_gains)
    ffn_rows = jnp.concatenate([halves(w_gate), halves(w_up), halves(w_down)], axis=2)
    weights_all, gains_all, ffn_pair = exchange(
        1,
        ["ctx"],
        [("ctx", "same", weight_rows), ("ctx", "same", gains), ("pair", "own", ffn_rows)],
    )
    planes = [[2 * g + h for g in range(NCTX // 2)] for h in range(2)]
    ffn_full = lax.all_gather(
        ffn_pair.reshape(2 * 32, 3 * unit_half), "ctx", axis_index_groups=planes, tiled=True
    )
    qkv_full = weights_all.reshape(width, weight_rows.shape[1])
    gain_attn = gains_all[:, 0, :32].reshape(width).astype(F32)
    gain_ffn = gains_all[:, 1, :32].reshape(width).astype(F32)
    gain_query = gains_all[:, 2, :2].reshape(HEAD_SIZE).astype(F32)
    gain_key = gains_all[:, 3, :2].reshape(HEAD_SIZE).astype(F32)

    inputs = block_input.astype(F32).reshape(rows, width)
    scale_attn = rms_scale(inputs)
    normed_attn = inputs * scale_attn
    hidden_attn = (normed_attn * gain_attn).astype(BF16)
    raw = jnp.dot(hidden_attn, qkv_full, preferred_element_type=F32)
    query_raw = raw[:, :256].reshape(seqs, tokens, 4, HEAD_SIZE)
    key_raw = raw[:, 256:384].reshape(seqs, tokens, 2, HEAD_SIZE)
    values = raw[:, 384:].astype(BF16).reshape(seqs, tokens, 2, HEAD_SIZE)
    query_scale, key_scale = rms_scale(query_raw), rms_scale(key_raw)
    query_hat, key_hat = query_raw * query_scale, key_raw * key_scale
    cosine, sine = rope_tables(tokens, c * tokens)
    query_rot = rotary(query_hat * gain_query, cosine, sine, 1.0).astype(BF16)
    key_rot = rotary(key_hat * gain_key, cosine, sine, 1.0).astype(BF16)
    q_src = to_pairs(query_rot * jnp.asarray(HEAD_SIZE**-0.5, BF16), 2, True)
    kv_src = jnp.concatenate([key_rot, values], axis=-1).transpose(2, 0, 1, 3)
    kv_src = kv_src.reshape(PAIRS, tokens, 2 * HEAD_SIZE)

    att, q_buf, kv_buf, o_buf, log_buf, wo_all, cot_all = forward(
        q_src, kv_src, w_out, cotangent.reshape(rows, width)
    )
    attended = from_pairs(att[..., HEAD_SIZE:], seqs, 2).reshape(rows, 256)
    out_full = wo_all.reshape(width, 256)
    gu_full = ffn_full[:, : 2 * unit_half]
    dn_full = ffn_full[:, 2 * unit_half :]
    cot_rows = cot_all.reshape(2 * rows, width)

    attn_part = last_dims(attended, out_full).astype(BF16)
    inputs_own = mine(inputs)
    residual, hidden_all = norm_step(
        attn_part.reshape(4, own, width), inputs_own, gain_ffn.reshape(1, width)
    )
    hidden_ffn = hidden_all.reshape(2 * rows, width)

    gu_raw = jnp.dot(hidden_ffn, gu_full, preferred_element_type=F32)
    gate_raw, up_raw = gu_raw[:, :unit_half], gu_raw[:, unit_half:]
    sigmoid = jax.nn.sigmoid(gate_raw)
    activated = gate_raw * sigmoid
    hidden_units = (activated * up_raw).astype(BF16)
    grad_units = jnp.dot(cot_rows, dn_full, preferred_element_type=F32)
    grad_gate_in = grad_units * up_raw * sigmoid * (1.0 + gate_raw * (1.0 - sigmoid))
    grad_up_in = grad_units * activated
    grad_gu_in = jnp.concatenate([grad_gate_in, grad_up_in], axis=1).astype(BF16)
    ffn_back = last_dims(grad_gu_in, gu_full).astype(BF16)
    cot_own = mine(cotangent.reshape(rows, width))
    grad_residual, ffn_gain_part, residual_all = norm_back_step(
        ffn_back.reshape(8, own, width), residual, cot_own, gain_ffn.reshape(1, width)
    )
    residual_bf = residual_all.reshape(rows, width)

    grad_attended = jnp.dot(residual_bf, out_full, preferred_element_type=F32).astype(BF16)
    do_src = to_pairs(grad_attended.reshape(seqs, tokens, 4, HEAD_SIZE), 2, False)
    grad_out = first_dims(residual_bf, attended).astype(BF16)
    grad_gu = first_dims(hidden_ffn, grad_gu_in).astype(BF16)
    grad_dn = first_dims(cot_rows, hidden_units).astype(BF16)
    ffn_part = last_dims(hidden_units, dn_full).astype(BF16)
    grads_own = lax.psum_scatter(
        jnp.concatenate([grad_gu, grad_out, grad_dn], axis=1),
        "ctx",
        axis_index_groups=planes,
        tiled=True,
    )
    dq_all, dkv_all, ffn_parts = backward(
        do_src, q_buf, kv_buf, o_buf, log_buf, ffn_part.reshape(8, own, width)
    )

    output_own = (residual + jnp.sum(ffn_parts.astype(F32), axis=0)).astype(BF16)
    grad_query_rot = from_pairs(dq_all[..., :HEAD_SIZE].astype(F32), seqs, 2)
    dkv = jnp.sum(dkv_all.reshape(PAIRS, WORKERS, tokens, 2 * HEAD_SIZE).astype(F32), axis=1)
    key_grad = from_pairs(dkv[..., :HEAD_SIZE], seqs, 1)
    value_in = from_pairs(dkv[..., HEAD_SIZE:], seqs, 1).astype(BF16).reshape(rows, 128)
    gq = rotary(grad_query_rot, cosine, sine, -1.0)
    gk = rotary(key_grad, cosine, sine, -1.0)
    query_gain_part = jnp.sum(gq * query_hat, axis=(0, 1, 2))
    key_gain_part = jnp.sum(gk * key_hat, axis=(0, 1, 2))
    query_in = head_back(gq, query_hat, query_scale, gain_query).astype(BF16).reshape(rows, 256)
    key_in = head_back(gk, key_hat, key_scale, gain_key).astype(BF16).reshape(rows, 128)
    grad_in = jnp.concatenate([query_in, key_in, value_in], axis=1)
    grad_qkv = first_dims(hidden_attn, grad_in).astype(BF16)
    attn_back = last_dims(grad_in, qkv_full)
    attn_gain_part = jnp.sum(attn_back * normed_attn, axis=0)
    gain_parts = jnp.zeros((NCTX, 8, 128), F32)
    gain_parts = gain_parts.at[:, 0, :32].set(attn_gain_part.reshape(NCTX, 32))
    gain_parts = gain_parts.at[:, 1, :32].set(ffn_gain_part.reshape(NCTX, 32))
    gain_parts = gain_parts.at[:, 2, :2].set(query_gain_part.reshape(NCTX, 2))
    gain_parts = gain_parts.at[:, 3, :2].set(key_gain_part.reshape(NCTX, 2))
    qkv_parts, output_all, input_all, gain_tp = last_step(
        attn_back.astype(BF16).reshape(4, own, width),
        grad_qkv.reshape(NCTX, 32, 512),
        gain_parts,
        output_own,
        grad_residual,
        inputs_own,
        gain_attn.reshape(1, width),
    )
    (pair_grads,) = exchange(9, ["pair"], [("pair", "own", grads_own.reshape(2, 32, -1))])
    pair_grads = pair_grads.astype(F32)
    gain_sum = jnp.sum(gain_tp, axis=0)
    qkv_grad = jnp.sum(qkv_parts.astype(F32), axis=0)
    gu, end = 2 * unit_half, 2 * unit_half + 256
    out_grad = jnp.sum(pair_grads[:, :, gu:end], axis=0)

    def joined(first, last):
        return jnp.concatenate([pair_grads[0, :, first:last], pair_grads[1, :, first:last]], axis=1)

    gate_grad = joined(0, unit_half)
    up_grad = joined(unit_half, gu)
    down_grad = joined(end, end + unit_half)
    return (
        output_all.reshape(seqs, tokens, width),
        input_all.astype(F32).reshape(seqs, tokens, width),
        qkv_grad[:, :256],
        qkv_grad[:, 256:384],
        qkv_grad[:, 384:],
        out_grad,
        gate_grad,
        up_grad,
        down_grad,
        gain_sum[0:2, :32],
        gain_sum[2:4, :2],
    )


def solution(mesh):
    tokens, weights = P(None, "ctx", None), P("ctx", "tp")
    return jax.shard_map(
        local,
        mesh=mesh,
        in_specs=(tokens,) * 2 + (weights,) * 7 + (P(None, "ctx"),) * 2,
        out_specs=(tokens,) * 2 + (weights,) * 7 + (P(None, "ctx"),) * 2,
        check_vma=False,
    )
```

```python
import functools

import jax
import jax.numpy as jnp
from jax import lax
from jax.experimental import pallas as pl
from jax.experimental.pallas import tpu as pltpu
from jax.sharding import PartitionSpec as P

HEAD_SIZE = 64
EPSILON = 1e-06
ROPE_BASE = 1000000.0
MESH = pl.DeviceIdType.MESH
F32 = jnp.float32
BF16 = jnp.bfloat16
ANY = pl.BlockSpec(memory_space=pl.ANY)
VMEM = pl.BlockSpec(memory_space=pltpu.VMEM)
NCTX = 32
PAIRS = 4
WORKERS = 8
SLOTS = 4
BLOCK = 128


def group(kind):
    c, t = lax.axis_index("ctx"), lax.axis_index("tp")
    h = lax.rem(c, 2)
    if kind == "ctx":
        return NCTX, c, lambda p: (p, t)
    if kind == "tp":
        return 4, t, lambda p: (c, p)
    if kind == "pair":
        return 2, h, lambda p: (c - h + p, t)
    z, x, core = c // 8, lax.rem(c // 2, 4), lax.rem(t, 2)
    if kind == "z":
        return 4, z, lambda p: (c + (p - z) * 8, t)
    if kind == "x":
        return 4, x, lambda p: (c + (p - x) * 2, t)
    if kind == "core":
        return 2, core, lambda p: (c, t - core + p)
    if kind == "ring":
        return 4, h * 2 + t // 2, lambda p: (c - h + p // 2, lax.rem(p, 2) * 2 + core)
    return 8, h * 4 + t, lambda p: (c - h + p // 4, lax.rem(p, 4))


PICKS = {
    "same": lambda ref, p: ref,
    "own": lambda ref, p: ref.at[p],
    "half": lambda ref, p: ref.at[lax.rem(p, 2)],
    "plane": lambda ref, p: ref.at[p // WORKERS],
}


def greet(kinds):
    barrier = pltpu.get_barrier_semaphore()
    total = 0
    for kind in kinds:
        n, me, dev = group(kind)

        @pl.loop(1, n)
        def _(i):
            pl.semaphore_signal(
                barrier, inc=1, device_id=dev(lax.rem(me + i, n)), device_id_type=MESH
            )

        total += n - 1
    pl.semaphore_wait(barrier, total)


def begin(kind, pick, src, dst, send, recv):
    n, me, dev = group(kind)
    choose = PICKS[pick]

    @pl.loop(1, n)
    def _(i):
        p = lax.rem(me + 5 * i, n)
        pltpu.make_async_remote_copy(
            src_ref=choose(src, p),
            dst_ref=dst.at[me],
            send_sem=send.at[p],
            recv_sem=recv.at[me],
            device_id=dev(p),
            device_id_type=MESH,
        ).start()

    pltpu.make_async_copy(choose(src, me), dst.at[me], recv.at[me]).start()


def finish(kind, pick, src, dst, send, recv):
    n, me, dev = group(kind)
    choose = PICKS[pick]

    @pl.loop(1, n)
    def _(i):
        p = lax.rem(me + i, n)
        copy = pltpu.make_async_remote_copy(
            src_ref=choose(src, p),
            dst_ref=dst.at[p],
            send_sem=send.at[p],
            recv_sem=recv.at[p],
            device_id=dev(p),
            device_id_type=MESH,
        )
        copy.wait_send()
        copy.wait_recv()

    pltpu.make_async_copy(choose(src, me), dst.at[me], recv.at[me]).wait()


def push(kind, src_of, dst_of, send, recv, local=False):
    n, me, dev = group(kind)

    @pl.loop(1, n)
    def _(i):
        p = lax.rem(me + i, n)
        pltpu.make_async_remote_copy(
            src_ref=src_of(p),
            dst_ref=dst_of(me),
            send_sem=send.at[p],
            recv_sem=recv.at[me],
            device_id=dev(p),
            device_id_type=MESH,
        ).start()

    if local:
        pltpu.make_async_copy(src_of(me), dst_of(me), recv.at[me]).start()


def settle(kind, src_of, dst_of, send, recv, local=False):
    n, me, dev = group(kind)

    @pl.loop(1, n)
    def _(i):
        p = lax.rem(me + i, n)
        copy = pltpu.make_async_remote_copy(
            src_ref=src_of(p),
            dst_ref=dst_of(p),
            send_sem=send.at[p],
            recv_sem=recv.at[p],
            device_id=dev(p),
            device_id_type=MESH,
        )
        copy.wait_send()
        copy.wait_recv()

    if local:
        pltpu.make_async_copy(src_of(me), dst_of(me), recv.at[me]).wait()


def stage(*moves):
    for move in moves:
        push(*move)
    for move in moves:
        settle(*move)


class Sems:
    def __init__(self, refs):
        self.refs = list(refs)

    def two(self):
        return self.refs.pop(0), self.refs.pop(0)


def position():
    c = lax.axis_index("ctx")
    return c // 8, lax.rem(c // 2, 4), lax.rem(c, 2)


SIZES = {"ctx": NCTX, "tp": 4, "pair": 2, "rows": 8, "z": 4, "x": 4, "core": 2, "ring": 4}


def gather_body(w, gains, ffn, w_all, gains_all, ffn_pair, *sem):
    z, x, h = position()
    take = Sems(sem)
    greet(["z", "x", "pair"])
    swap = ("pair", lambda p: ffn.at[p], lambda q: ffn_pair.at[q], *take.two(), True)
    first = [
        ("pair", lambda p: w, lambda q: w_all.at[z, x, q], *take.two(), True),
        ("pair", lambda p: gains, lambda q: gains_all.at[z, x, q], *take.two(), True),
    ]
    for move in first:
        push(*move)
    push(*swap)
    for move in first:
        settle(*move)
    stage(
        ("x", lambda p: w_all.at[z, x, :, 0], lambda q: w_all.at[z, q, :, 0], *take.two()),
        ("z", lambda p: w_all.at[z, x, :, 1], lambda q: w_all.at[q, x, :, 1], *take.two()),
        ("x", lambda p: gains_all.at[z, x], lambda q: gains_all.at[z, q], *take.two()),
    )
    stage(
        ("z", lambda p: w_all.at[z, :, :, 0], lambda q: w_all.at[q, :, :, 0], *take.two()),
        ("x", lambda p: w_all.at[:, x, :, 1], lambda q: w_all.at[:, q, :, 1], *take.two()),
        ("z", lambda p: gains_all.at[z], lambda q: gains_all.at[q], *take.two()),
    )
    settle(*swap)


def gather(w, gains, ffn):
    return pl.pallas_call(
        gather_body,
        out_shape=[
            jax.ShapeDtypeStruct((4, 4, 2, *w.shape), BF16),
            jax.ShapeDtypeStruct((4, 4, 2, *gains.shape), BF16),
            jax.ShapeDtypeStruct(ffn.shape, BF16),
        ],
        in_specs=[ANY] * 3,
        out_specs=[VMEM, VMEM, ANY],
        scratch_shapes=sems(["pair"] * 3 + ["x", "z", "x", "z", "x", "z"]),
        compiler_params=pltpu.CompilerParams(collective_id=1, has_side_effects=True),
        name="gather",
    )(w, gains, ffn)


def piece_shape(pick, array):
    return array.shape if pick == "same" else array.shape[1:]


def landing(kind, pick, array):
    return jax.ShapeDtypeStruct((SIZES[kind], *piece_shape(pick, array)), array.dtype)


def sems(kinds):
    return [pltpu.SemaphoreType.DMA((SIZES[k],)) for k in kinds for _ in range(2)]


def exchange_body(plan, kinds, *refs):
    n = len(plan)
    srcs, dsts, rest = refs[:n], refs[n : 2 * n], refs[2 * n :]
    greet(kinds)
    for k, (kind, pick) in enumerate(plan):
        begin(kind, pick, srcs[k], dsts[k], rest[2 * k], rest[2 * k + 1])
    for k, (kind, pick) in enumerate(plan):
        finish(kind, pick, srcs[k], dsts[k], rest[2 * k], rest[2 * k + 1])


def exchange(number, kinds, items):
    plan = tuple((kind, pick) for kind, pick, _ in items)
    return pl.pallas_call(
        functools.partial(exchange_body, plan, kinds),
        out_shape=[landing(*item) for item in items],
        in_specs=[ANY] * len(items),
        out_specs=[ANY] * len(items),
        scratch_shapes=sems([kind for kind, _ in plan]),
        compiler_params=pltpu.CompilerParams(collective_id=number, has_side_effects=True),
        name=f"exchange{number}",
    )(*[array for _, _, array in items])


def places():
    c, t = lax.axis_index("ctx"), lax.axis_index("tp")
    slot, low = c // WORKERS, lax.rem(c, WORKERS)
    to = low + lax.rem(slot, 2) * (WORKERS - 1 - 2 * low)
    return c, t, slot, low, to


def block_of(low, j):
    return j * WORKERS + (low if j % 2 == 0 else WORKERS - 1 - low)


def greet_attention(kinds):
    c, t, slot, low, to = places()
    barrier = pltpu.get_barrier_semaphore()
    total = 0
    others = [p * WORKERS + to for p in range(PAIRS)] + [block_of(low, j) for j in range(SLOTS)]
    for other in others:

        @pl.when(other != c)
        def _():
            pl.semaphore_signal(barrier, inc=1, device_id=(other, t), device_id_type=MESH)

        total = total + jnp.where(other != c, 1, 0)
    for kind in kinds:
        n, me, dev = group(kind)

        @pl.loop(1, n)
        def _(i):
            pl.semaphore_signal(
                barrier, inc=1, device_id=dev(lax.rem(me + i, n)), device_id_type=MESH
            )

        total = total + (n - 1)
    pl.semaphore_wait(barrier, total)


def to_workers(src, dst, send, recv, act):
    c, t, slot, low, to = places()
    for p in range(PAIRS):
        target = p * WORKERS + to
        far = pltpu.make_async_remote_copy(
            src_ref=src.at[p],
            dst_ref=dst.at[slot],
            send_sem=send.at[p],
            recv_sem=recv.at[slot],
            device_id=(target, t),
            device_id_type=MESH,
        )
        near = pltpu.make_async_copy(src.at[p], dst.at[slot], send.at[p])

        @pl.when(target != c)
        def _():
            far.start() if act == "start" else far.wait_send()

        @pl.when(target == c)
        def _():
            near.start() if act == "start" else near.wait()


def from_owners(src, dst, send, recv):
    c, t, slot, low, to = places()
    for j in range(SLOTS):
        owner = block_of(low, j)

        @pl.when(owner != c)
        def _():
            pltpu.make_async_remote_copy(
                src_ref=src.at[j],
                dst_ref=dst.at[j],
                send_sem=send.at[j],
                recv_sem=recv.at[j],
                device_id=(owner, t),
                device_id_type=MESH,
            ).wait_recv()


def to_owner(src, dst, send, recv, j, act):
    c, t, slot, low, to = places()
    owner = block_of(low, j)
    far = pltpu.make_async_remote_copy(
        src_ref=src.at[j],
        dst_ref=dst.at[slot],
        send_sem=send.at[j],
        recv_sem=recv.at[slot],
        device_id=(owner, t),
        device_id_type=MESH,
    )
    near = pltpu.make_async_copy(src.at[j], dst.at[slot], send.at[j])

    @pl.when(owner != c)
    def _():
        far.start() if act == "start" else far.wait_send()

    @pl.when(owner == c)
    def _():
        near.start() if act == "start" else near.wait()


def from_workers(src, dst, send, recv):
    c, t, slot, low, to = places()
    for p in range(PAIRS):
        target = p * WORKERS + to

        @pl.when(target != c)
        def _():
            pltpu.make_async_remote_copy(
                src_ref=src.at[p],
                dst_ref=dst.at[p],
                send_sem=send.at[p],
                recv_sem=recv.at[p],
                device_id=(target, t),
                device_id_type=MESH,
            ).wait_recv()


def last_dims(a, b):
    return lax.dot_general(a, b, (((1,), (1,)), ((), ())), preferred_element_type=F32)


def first_dims(a, b):
    return lax.dot_general(a, b, (((0,), (0,)), ((), ())), preferred_element_type=F32)


def causal_mask(b, i):
    shape = (2 * BLOCK, 2 * BLOCK)
    rows = lax.broadcasted_iota(jnp.int32, shape, 0)
    token = b * BLOCK + jnp.where(rows >= BLOCK, rows - BLOCK, rows)
    key = i * 2 * BLOCK + lax.broadcasted_iota(jnp.int32, shape, 1)
    return token >= key


def forward_body(
    q_src, kv_src, wo, cot, att, q_buf, kv_buf, o_buf, log_buf, wo_all, cot_all,
    acc, den, q_send, q_recv, o_send, o_recv, *sem,
):
    c, t, slot, low, to = places()
    z, x, h = position()
    take = Sems(sem)
    greet_attention(["z", "x", "pair"])
    near = ("z", lambda p: kv_src.at[p], lambda q: kv_buf.at[q, x, h], *take.two(), True)
    out_first = ("pair", lambda p: wo, lambda q: wo_all.at[z, x, q], *take.two(), True)
    push(*near)
    to_workers(q_src, q_buf, q_send, q_recv, "start")
    push(*out_first)
    settle(*near)
    stage(
        ("x", lambda p: kv_buf.at[:, x, h, 0], lambda q: kv_buf.at[:, q, h, 0], *take.two()),
        ("pair", lambda p: kv_buf.at[:, x, h, 1], lambda q: kv_buf.at[:, x, q, 1], *take.two()),
    )
    stage(
        ("pair", lambda p: kv_buf.at[:, :, h, 0], lambda q: kv_buf.at[:, :, q, 0], *take.two()),
        ("x", lambda p: kv_buf.at[:, x, :, 1], lambda q: kv_buf.at[:, q, :, 1], *take.two()),
    )
    settle(*out_first)
    out_second = [
        ("x", lambda p: wo_all.at[z, x, :, 0], lambda q: wo_all.at[z, q, :, 0], *take.two()),
        ("z", lambda p: wo_all.at[z, x, :, 1], lambda q: wo_all.at[q, x, :, 1], *take.two()),
    ]
    out_third = [
        ("z", lambda p: wo_all.at[z, :, :, 0], lambda q: wo_all.at[q, :, :, 0], *take.two()),
        ("x", lambda p: wo_all.at[:, x, :, 1], lambda q: wo_all.at[:, q, :, 1], *take.two()),
    ]
    swap = ("pair", lambda p: cot, lambda q: cot_all.at[q], *take.two(), True)
    for move in out_second:
        push(*move)
    push(*swap)
    to_workers(q_src, q_buf, q_send, q_recv, "wait")
    from_owners(q_src, q_buf, q_send, q_recv)
    lanes = lax.broadcasted_iota(jnp.int32, (2 * BLOCK, BLOCK), 1)
    for j in range(SLOTS):
        b = block_of(low, j)
        acc[...] = jnp.zeros_like(acc)
        den[...] = jnp.zeros_like(den)

        def chunk(i, masked):
            q = q_buf[j]
            kv = kv_buf[i // 4, lax.rem(i, 4)].reshape(2 * BLOCK, BLOCK)
            powered = jnp.exp(last_dims(q, kv))
            if masked:
                powered = jnp.where(causal_mask(b, i), powered, 0.0)
            den[...] += powered[:, :BLOCK] + powered[:, BLOCK:]
            acc[...] += jnp.dot(powered.astype(BF16), kv, preferred_element_type=F32)

        pl.loop(0, b // 2)(lambda i: chunk(i, False))
        chunk(b // 2, True)
        total = jnp.sum(den[...], axis=1, keepdims=True)
        o_buf[j] = jnp.where(lanes >= HEAD_SIZE, acc[...] / total, 0.0).astype(BF16)
        log_buf[j] = jnp.broadcast_to(jnp.log(total), (2 * BLOCK, BLOCK))
        to_owner(o_buf, att, o_send, o_recv, j, "start")
        if j == 1:
            for move in out_second:
                settle(*move)
            for move in out_third:
                push(*move)
    for j in range(SLOTS):
        to_owner(o_buf, att, o_send, o_recv, j, "wait")
    from_workers(o_buf, att, o_send, o_recv)
    for move in out_third:
        settle(*move)
    settle(*swap)


def forward(q_src, kv_src, wo, cot):
    stack = jax.ShapeDtypeStruct((SLOTS, 2 * BLOCK, BLOCK), BF16)
    return pl.pallas_call(
        forward_body,
        out_shape=[
            stack,
            stack,
            jax.ShapeDtypeStruct((4, 4, 2, 2, BLOCK // 2, BLOCK), BF16),
            stack,
            jax.ShapeDtypeStruct((SLOTS, 2 * BLOCK, BLOCK), F32),
            jax.ShapeDtypeStruct((4, 4, 2, *wo.shape), BF16),
            jax.ShapeDtypeStruct((2, *cot.shape), BF16),
        ],
        in_specs=[ANY] * 4,
        out_specs=[ANY] + [VMEM] * 5 + [ANY],
        scratch_shapes=[
            pltpu.VMEM((2 * BLOCK, BLOCK), F32),
            pltpu.VMEM((2 * BLOCK, BLOCK), F32),
        ]
        + [pltpu.SemaphoreType.DMA((SLOTS,))] * 4
        + sems(["z", "pair", "x", "pair", "pair", "x", "x", "z", "z", "x", "pair"]),
        compiler_params=pltpu.CompilerParams(
            collective_id=2, has_side_effects=True, vmem_limit_bytes=24 * 2**20
        ),
        name="attention_forward",
    )(q_src, kv_src, wo, cot)


def backward_body(
    do_src, q_buf, kv_buf, o_buf, log_buf, ffn, dq_all, dkv_all, ffn_all,
    do_buf, dq_buf, dkv_buf, acc, dkv, one_a, one_b, sum_a, sum_b, two_a, two_b, sum_all,
    do_send, do_recv, dq_send, dq_recv, *sem,
):
    c, t, slot, low, to = places()
    z, x, h = position()
    take = Sems(sem)
    greet_attention(["z", "x", "rows"])
    to_workers(do_src, do_buf, do_send, do_recv, "start")
    ffn_sems = take.two()
    begin("rows", "own", ffn, ffn_all, *ffn_sems)
    dkv[...] = jnp.zeros_like(dkv)
    to_workers(do_src, do_buf, do_send, do_recv, "wait")
    from_owners(do_src, do_buf, do_send, do_recv)
    for j in range(SLOTS):
        b = block_of(low, j)
        acc[...] = jnp.zeros_like(acc)
        delta = jnp.sum(do_buf[j].astype(F32) * o_buf[j].astype(F32), axis=1, keepdims=True)

        def chunk(i, masked):
            q, do = q_buf[j], do_buf[j]
            kv = kv_buf[i // 4, lax.rem(i, 4)].reshape(2 * BLOCK, BLOCK)
            logs = log_buf[j]
            scores = last_dims(q, kv)
            probs = jnp.exp(scores - jnp.concatenate([logs, logs], axis=1))
            if masked:
                probs = jnp.where(causal_mask(b, i), probs, 0.0)
            grads = (probs * (last_dims(do, kv) - delta)).astype(BF16)
            acc[...] += jnp.dot(grads, kv, preferred_element_type=F32)
            update = first_dims(grads, q) + first_dims(probs.astype(BF16), do)
            dkv[i // 4, lax.rem(i, 4)] += update.reshape(2, 2, BLOCK // 2, BLOCK)

        pl.loop(0, b // 2)(lambda i: chunk(i, False))
        chunk(b // 2, True)
        dq_buf[j] = (acc[...] * (HEAD_SIZE**-0.5)).astype(BF16)
        to_owner(dq_buf, dq_all, dq_send, dq_recv, j, "start")
    dkv_buf[...] = dkv[...].astype(BF16)
    stage(
        ("x", lambda p: dkv_buf.at[:, p, :, 0], lambda q: one_a.at[q], *take.two(), True),
        ("pair", lambda p: dkv_buf.at[:, :, p, 1], lambda q: one_b.at[q], *take.two(), True),
    )
    sum_a[...] = summed(one_a).astype(BF16)
    sum_b[...] = summed(one_b).astype(BF16)
    stage(
        ("pair", lambda p: sum_a.at[:, p], lambda q: two_a.at[q], *take.two(), True),
        ("x", lambda p: sum_b.at[:, p], lambda q: two_b.at[q], *take.two(), True),
    )
    sum_all[:, 0] = summed(two_a).astype(BF16)
    sum_all[:, 1] = summed(two_b).astype(BF16)
    stage(("z", lambda p: sum_all.at[p], lambda q: dkv_all.at[q], *take.two(), True))
    for j in range(SLOTS):
        to_owner(dq_buf, dq_all, dq_send, dq_recv, j, "wait")
    from_workers(dq_buf, dq_all, dq_send, dq_recv)
    finish("rows", "own", ffn, ffn_all, *ffn_sems)


def backward(do_src, q_buf, kv_buf, o_buf, log_buf, ffn):
    half = BLOCK // 2
    return pl.pallas_call(
        backward_body,
        out_shape=[
            jax.ShapeDtypeStruct((SLOTS, 2 * BLOCK, BLOCK), BF16),
            jax.ShapeDtypeStruct((PAIRS, 2, half, BLOCK), BF16),
            landing("rows", "own", ffn),
        ],
        in_specs=[ANY] + [VMEM] * 4 + [ANY],
        out_specs=[ANY] * 3,
        scratch_shapes=[
            pltpu.VMEM((SLOTS, 2 * BLOCK, BLOCK), BF16),
            pltpu.VMEM((SLOTS, 2 * BLOCK, BLOCK), BF16),
            pltpu.VMEM((4, 4, 2, 2, half, BLOCK), BF16),
            pltpu.VMEM((2 * BLOCK, BLOCK), F32),
            pltpu.VMEM((4, 4, 2, 2, half, BLOCK), F32),
            pltpu.VMEM((4, 4, 2, half, BLOCK), BF16),
            pltpu.VMEM((2, 4, 4, half, BLOCK), BF16),
            pltpu.VMEM((4, 2, half, BLOCK), BF16),
            pltpu.VMEM((4, 4, half, BLOCK), BF16),
            pltpu.VMEM((2, 4, half, BLOCK), BF16),
            pltpu.VMEM((4, 4, half, BLOCK), BF16),
            pltpu.VMEM((4, 2, half, BLOCK), BF16),
        ]
        + [pltpu.SemaphoreType.DMA((SLOTS,))] * 4
        + sems(["rows", "x", "pair", "pair", "x", "z"]),
        compiler_params=pltpu.CompilerParams(
            collective_id=6, has_side_effects=True, vmem_limit_bytes=24 * 2**20
        ),
        name="attention_backward",
    )(do_src, q_buf, kv_buf, o_buf, log_buf, ffn)


def row_scale(rows):
    return lax.rsqrt(jnp.mean(rows * rows, axis=1, keepdims=True) + EPSILON)


def row_back(grads, normed, scale, gain):
    scaled = grads * gain
    return scale * (scaled - normed * jnp.mean(scaled * normed, axis=1, keepdims=True))


def summed(ref):
    total = ref[0].astype(F32)
    for k in range(1, ref.shape[0]):
        total += ref[k].astype(F32)
    return total


def norm_body(
    parts, inputs, gain, residual, hidden_all, landed, hidden,
    send0, recv0, send1, recv1, send2, recv2,
):
    greet(["tp", "ring"])
    begin("tp", "own", parts, landed, send0, recv0)
    finish("tp", "own", parts, landed, send0, recv0)
    total = inputs[...] + summed(landed)
    residual[...] = total
    hidden[...] = (total * row_scale(total) * gain[...]).astype(BF16)
    core = lax.rem(lax.axis_index("tp"), 2)
    stage(("ring", lambda p: hidden, lambda q: hidden_all.at[q, core], send1, recv1, True))
    stage(("core", lambda p: hidden_all.at[:, core], lambda q: hidden_all.at[:, q], send2, recv2))


def norm_step(parts, inputs, gain):
    own, width = inputs.shape
    return pl.pallas_call(
        norm_body,
        out_shape=[
            jax.ShapeDtypeStruct((own, width), F32),
            jax.ShapeDtypeStruct((4, 2, own, width), BF16),
        ],
        in_specs=[VMEM] * 3,
        out_specs=[VMEM, VMEM],
        scratch_shapes=[pltpu.VMEM((4, own, width), BF16), pltpu.VMEM((own, width), BF16)]
        + sems(["tp", "ring", "core"]),
        compiler_params=pltpu.CompilerParams(collective_id=3, has_side_effects=True),
        name="norm_step",
    )(parts, inputs, gain)


def norm_back_body(
    parts, residual, cot, gain, grad_residual, gain_part, grad_all,
    halved, chip, landed, grad_bf, send0, recv0, send1, recv1, send2, recv2,
):
    greet(["tp", "ring"])
    both = ("core", lambda p: parts.at[:, p], lambda q: halved.at[q], send2, recv2, True)
    push(*both)
    rows = residual[...]
    scale = row_scale(rows)
    normed = rows * scale
    settle(*both)
    chip[...] = summed(halved).astype(BF16)
    stage(("ring", lambda p: chip.at[p], lambda q: landed.at[q], send0, recv0, True))
    grads = summed(landed)
    result = cot[...].astype(F32) + row_back(grads, normed, scale, gain[...])
    grad_bf[...] = result.astype(BF16)
    begin("tp", "same", grad_bf, grad_all, send1, recv1)
    grad_residual[...] = result
    gain_part[...] = jnp.sum(grads * normed, axis=0, keepdims=True)
    finish("tp", "same", grad_bf, grad_all, send1, recv1)


def norm_back_step(parts, residual, cot, gain):
    own, width = residual.shape
    return pl.pallas_call(
        norm_back_body,
        out_shape=[
            jax.ShapeDtypeStruct((own, width), F32),
            jax.ShapeDtypeStruct((1, width), F32),
            jax.ShapeDtypeStruct((4, own, width), BF16),
        ],
        in_specs=[VMEM] * 4,
        out_specs=[VMEM, VMEM, ANY],
        scratch_shapes=[
            pltpu.VMEM((2, 4, own, width), BF16),
            pltpu.VMEM((4, own, width), BF16),
            pltpu.VMEM((4, own, width), BF16),
            pltpu.VMEM((own, width), BF16),
        ]
        + sems(["ring", "tp", "core"]),
        compiler_params=pltpu.CompilerParams(collective_id=5, has_side_effects=True),
        name="norm_back_step",
    )(parts, residual, cot, gain)


def last_body(
    parts, qkv, gains, output, grad_residual, inputs, gain,
    qkv_grad, output_all, input_all, gain_tp,
    landed, input_bf, one_a, one_b, one_g, sum_a, sum_b, sum_g, two_a, two_b, two_g,
    part_a, part_b, part_g, three_a, three_b, three_g, gain_sum, *sem,
):
    take = Sems(sem)
    greet(["z", "x", "pair", "tp"])
    rows_sums, rows_output, rows_input, gains_out = [take.two() for _ in range(4)]
    begin("tp", "own", parts, landed, *rows_sums)
    first = [
        ("x", lambda p: qkv.at[:, p, :, 0], lambda q: one_a.at[q], *take.two(), True),
        ("z", lambda p: qkv.at[p, :, :, 1], lambda q: one_b.at[q], *take.two(), True),
        ("x", lambda p: gains.at[:, p], lambda q: one_g.at[q], *take.two(), True),
    ]
    for move in first:
        push(*move)
    rows = inputs[...]
    scale = row_scale(rows)
    normed = rows * scale
    finish("tp", "own", parts, landed, *rows_sums)
    result = grad_residual[...] + row_back(summed(landed), normed, scale, gain[...])
    input_bf[...] = result.astype(BF16)
    begin("tp", "same", input_bf, input_all, *rows_input)
    begin("tp", "same", output, output_all, *rows_output)
    for move in first:
        settle(*move)
    sum_a[...] = summed(one_a).astype(BF16)
    sum_b[...] = summed(one_b).astype(BF16)
    sum_g[...] = summed(one_g)
    stage(
        ("z", lambda p: sum_a.at[p], lambda q: two_a.at[q], *take.two(), True),
        ("x", lambda p: sum_b.at[p], lambda q: two_b.at[q], *take.two(), True),
        ("z", lambda p: sum_g.at[p], lambda q: two_g.at[q], *take.two(), True),
    )
    part_a[...] = summed(two_a).astype(BF16)
    part_b[...] = summed(two_b).astype(BF16)
    part_g[...] = summed(two_g)
    stage(
        ("pair", lambda p: part_a.at[p], lambda q: three_a.at[q], *take.two(), True),
        ("pair", lambda p: part_b.at[p], lambda q: three_b.at[q], *take.two(), True),
        ("pair", lambda p: part_g.at[p], lambda q: three_g.at[q], *take.two(), True),
    )
    gain_sum[...] = summed(three_g)
    begin("tp", "same", gain_sum, gain_tp, *gains_out)
    qkv_grad[0] = summed(three_a)
    qkv_grad[1] = summed(three_b)
    finish("tp", "same", output, output_all, *rows_output)
    finish("tp", "same", input_bf, input_all, *rows_input)
    finish("tp", "same", gain_sum, gain_tp, *gains_out)


def last_step(parts, qkv, gains, output, grad_residual, inputs, gain):
    own, width = inputs.shape
    piece, small = qkv.shape[4:], gains.shape[3:]

    def scratch(*shape):
        return [pltpu.VMEM((*shape, *piece), BF16)] * 2 + [pltpu.VMEM((*shape, *small), F32)]

    return pl.pallas_call(
        last_body,
        out_shape=[
            jax.ShapeDtypeStruct((2, *piece), F32),
            jax.ShapeDtypeStruct((4, own, width), BF16),
            jax.ShapeDtypeStruct((4, own, width), BF16),
            jax.ShapeDtypeStruct((4, *small), F32),
        ],
        in_specs=[VMEM] * 7,
        out_specs=[VMEM] + [ANY] * 3,
        scratch_shapes=[pltpu.VMEM((4, own, width), BF16), pltpu.VMEM((own, width), BF16)]
        + scratch(4, 4, 2)
        + scratch(4, 2)
        + scratch(4, 2)
        + scratch(2)
        + scratch(2)
        + [pltpu.VMEM(small, F32)]
        + sems(["tp"] * 4 + ["x", "z", "x", "z", "x", "z"] + ["pair"] * 3),
        compiler_params=pltpu.CompilerParams(
            collective_id=8, has_side_effects=True, vmem_limit_bytes=24 * 2**20
        ),
        name="last_step",
    )(parts, qkv, gains, output, grad_residual, inputs, gain)


def rms_scale(rows):
    return lax.rsqrt(jnp.mean(rows * rows, axis=-1, keepdims=True) + EPSILON)


def rope_tables(tokens, offset):
    half = HEAD_SIZE // 2
    inverse = ROPE_BASE ** (-(jnp.arange(half, dtype=F32) * 2.0 / HEAD_SIZE))
    places_ = (offset + jnp.arange(tokens, dtype=jnp.int32)).astype(F32)
    angles = places_[:, None] * inverse[None, :]
    return jnp.cos(angles), jnp.sin(angles)


def rotary(rows, cosine, sine, direction):
    half = HEAD_SIZE // 2
    first, second = rows[..., :half], rows[..., half:]
    cosine = cosine[:, None, :]
    sine = sine[:, None, :] * direction
    return jnp.concatenate([first * cosine - second * sine, second * cosine + first * sine], -1)


def head_back(grads, hatted, scale, gain):
    scaled = grads * gain
    return scale * (scaled - hatted * jnp.mean(scaled * hatted, axis=-1, keepdims=True))


def to_pairs(rows, heads, left):
    s, tokens = rows.shape[:2]
    kv = rows.shape[2] // heads
    x = rows.reshape(s, tokens, kv, heads, HEAD_SIZE).transpose(2, 0, 3, 1, 4)
    x = x.reshape(kv * s, heads * tokens, HEAD_SIZE)
    side = (0, HEAD_SIZE) if left else (HEAD_SIZE, 0)
    return jnp.pad(x, ((0, 0), (0, 0), side))


def from_pairs(x, s, heads):
    kv = x.shape[0] // s
    tokens = x.shape[1] // heads
    x = x.reshape(kv, s, heads, tokens, HEAD_SIZE).transpose(1, 3, 0, 2, 4)
    return x.reshape(s, tokens, kv * heads, HEAD_SIZE)


def halves(w):
    half = w.shape[1] // 2
    return jnp.stack([w[:, :half], w[:, half:]])


def local(
    block_input, cotangent, w_query, key_weight, w_value, w_out, w_gate, w_up, w_down,
    norm_gains, head_gains,
):
    c, t = lax.axis_index("ctx"), lax.axis_index("tp")
    seqs, tokens, width = block_input.shape
    rows = seqs * tokens
    own = rows // 4
    unit_half = w_gate.shape[1] // 2

    def mine(x):
        return lax.dynamic_slice_in_dim(x, t * own, own, 0)

    weight_rows = jnp.concatenate([w_query, key_weight, w_value], axis=1)
    gains = jnp.zeros((16, 128), BF16)
    gains = gains.at[0:2, 0:32].set(norm_gains).at[2:4, 0:2].set(head_gains)
    ffn_rows = jnp.concatenate([halves(w_gate), halves(w_up), halves(w_down)], axis=2)
    weights_all, gains_all, ffn_pair = gather(
        weight_rows.reshape(2, 16, weight_rows.shape[1]), gains, ffn_rows
    )
    gains_all = gains_all.reshape(NCTX, 16, 128)
    planes = [[2 * g + h for g in range(NCTX // 2)] for h in range(2)]
    ffn_full = lax.all_gather(
        ffn_pair.reshape(2 * 32, 3 * unit_half), "ctx", axis_index_groups=planes, tiled=True
    )
    qkv_full = weights_all.reshape(width, weight_rows.shape[1])
    gain_attn = gains_all[:, 0, :32].reshape(width).astype(F32)
    gain_ffn = gains_all[:, 1, :32].reshape(width).astype(F32)
    gain_query = gains_all[:, 2, :2].reshape(HEAD_SIZE).astype(F32)
    gain_key = gains_all[:, 3, :2].reshape(HEAD_SIZE).astype(F32)

    inputs = block_input.astype(F32).reshape(rows, width)
    scale_attn = rms_scale(inputs)
    normed_attn = inputs * scale_attn
    hidden_attn = (normed_attn * gain_attn).astype(BF16)
    raw = jnp.dot(hidden_attn, qkv_full, preferred_element_type=F32)
    query_raw = raw[:, :256].reshape(seqs, tokens, 4, HEAD_SIZE)
    key_raw = raw[:, 256:384].reshape(seqs, tokens, 2, HEAD_SIZE)
    values = raw[:, 384:].astype(BF16).reshape(seqs, tokens, 2, HEAD_SIZE)
    query_scale, key_scale = rms_scale(query_raw), rms_scale(key_raw)
    query_hat, key_hat = query_raw * query_scale, key_raw * key_scale
    cosine, sine = rope_tables(tokens, c * tokens)
    query_rot = rotary(query_hat * gain_query, cosine, sine, 1.0).astype(BF16)
    key_rot = rotary(key_hat * gain_key, cosine, sine, 1.0).astype(BF16)
    q_src = to_pairs(query_rot * jnp.asarray(HEAD_SIZE**-0.5, BF16), 2, True)
    kv_src = jnp.concatenate([key_rot, values], axis=-1).transpose(2, 0, 1, 3)
    kv_src = kv_src.reshape(PAIRS, 2, tokens // 2, 2 * HEAD_SIZE)

    att, q_buf, kv_buf, o_buf, log_buf, wo_all, cot_all = forward(
        q_src, kv_src, w_out.reshape(2, 16, 256), cotangent.reshape(rows, width)
    )
    attended = from_pairs(att[..., HEAD_SIZE:], seqs, 2).reshape(rows, 256)
    out_full = wo_all.reshape(width, 256)
    gu_full = ffn_full[:, : 2 * unit_half]
    dn_full = ffn_full[:, 2 * unit_half :]
    cot_rows = cot_all.reshape(2 * rows, width)

    attn_part = last_dims(attended, out_full).astype(BF16)
    inputs_own = mine(inputs)
    residual, hidden_all = norm_step(
        attn_part.reshape(4, own, width), inputs_own, gain_ffn.reshape(1, width)
    )
    hidden_ffn = hidden_all.reshape(2 * rows, width)

    gu_raw = jnp.dot(hidden_ffn, gu_full, preferred_element_type=F32)
    gate_raw, up_raw = gu_raw[:, :unit_half], gu_raw[:, unit_half:]
    sigmoid = jax.nn.sigmoid(gate_raw)
    activated = gate_raw * sigmoid
    hidden_units = (activated * up_raw).astype(BF16)
    grad_units = jnp.dot(cot_rows, dn_full, preferred_element_type=F32)
    grad_gate_in = grad_units * up_raw * sigmoid * (1.0 + gate_raw * (1.0 - sigmoid))
    grad_up_in = grad_units * activated
    grad_gu_in = jnp.concatenate([grad_gate_in, grad_up_in], axis=1).astype(BF16)
    ffn_back = last_dims(grad_gu_in, gu_full).astype(BF16)
    cot_own = mine(cotangent.reshape(rows, width))
    grad_residual, ffn_gain_part, residual_all = norm_back_step(
        ffn_back.reshape(4, 2, own, width), residual, cot_own, gain_ffn.reshape(1, width)
    )
    residual_bf = residual_all.reshape(rows, width)

    grad_attended = jnp.dot(residual_bf, out_full, preferred_element_type=F32).astype(BF16)
    do_src = to_pairs(grad_attended.reshape(seqs, tokens, 4, HEAD_SIZE), 2, False)
    grad_out = first_dims(residual_bf, attended).astype(BF16)
    grad_gu = first_dims(hidden_ffn, grad_gu_in).astype(BF16)
    grad_dn = first_dims(cot_rows, hidden_units).astype(BF16)
    ffn_part = last_dims(hidden_units, dn_full).astype(BF16)
    grads_own = lax.psum_scatter(
        jnp.concatenate([grad_gu, grad_out, grad_dn], axis=1),
        "ctx",
        axis_index_groups=planes,
        tiled=True,
    )
    dq_all, dkv_all, ffn_parts = backward(
        do_src, q_buf, kv_buf, o_buf, log_buf, ffn_part.reshape(8, own, width)
    )

    output_own = (residual + jnp.sum(ffn_parts.astype(F32), axis=0)).astype(BF16)
    grad_query_rot = from_pairs(dq_all[..., :HEAD_SIZE].astype(F32), seqs, 2)
    dkv = dkv_all.reshape(PAIRS, tokens, 2 * HEAD_SIZE).astype(F32)
    key_grad = from_pairs(dkv[..., :HEAD_SIZE], seqs, 1)
    value_in = from_pairs(dkv[..., HEAD_SIZE:], seqs, 1).astype(BF16).reshape(rows, 128)
    gq = rotary(grad_query_rot, cosine, sine, -1.0)
    gk = rotary(key_grad, cosine, sine, -1.0)
    query_gain_part = jnp.sum(gq * query_hat, axis=(0, 1, 2))
    key_gain_part = jnp.sum(gk * key_hat, axis=(0, 1, 2))
    query_in = head_back(gq, query_hat, query_scale, gain_query).astype(BF16).reshape(rows, 256)
    key_in = head_back(gk, key_hat, key_scale, gain_key).astype(BF16).reshape(rows, 128)
    grad_in = jnp.concatenate([query_in, key_in, value_in], axis=1)
    grad_qkv = first_dims(hidden_attn, grad_in).astype(BF16)
    attn_back = last_dims(grad_in, qkv_full)
    attn_gain_part = jnp.sum(attn_back * normed_attn, axis=0)
    gain_parts = jnp.zeros((NCTX, 8, 128), F32)
    gain_parts = gain_parts.at[:, 0, :32].set(attn_gain_part.reshape(NCTX, 32))
    gain_parts = gain_parts.at[:, 1, :32].set(ffn_gain_part.reshape(NCTX, 32))
    gain_parts = gain_parts.at[:, 2, :2].set(query_gain_part.reshape(NCTX, 2))
    gain_parts = gain_parts.at[:, 3, :2].set(key_gain_part.reshape(NCTX, 2))
    qkv_grad, output_all, input_all, gain_tp = last_step(
        attn_back.astype(BF16).reshape(4, own, width),
        grad_qkv.reshape(4, 4, 2, 2, 16, 512),
        gain_parts.reshape(4, 4, 2, 8, 128),
        output_own,
        grad_residual,
        inputs_own,
        gain_attn.reshape(1, width),
    )
    (pair_grads,) = exchange(9, ["pair"], [("pair", "own", grads_own.reshape(2, 32, -1))])
    pair_grads = pair_grads.astype(F32)
    gain_sum = jnp.sum(gain_tp, axis=0)
    qkv_grad = qkv_grad.reshape(32, 512)
    gu, end = 2 * unit_half, 2 * unit_half + 256
    out_grad = jnp.sum(pair_grads[:, :, gu:end], axis=0)

    def joined(first, last):
        return jnp.concatenate([pair_grads[0, :, first:last], pair_grads[1, :, first:last]], axis=1)

    gate_grad = joined(0, unit_half)
    up_grad = joined(unit_half, gu)
    down_grad = joined(end, end + unit_half)
    return (
        output_all.reshape(seqs, tokens, width),
        input_all.astype(F32).reshape(seqs, tokens, width),
        qkv_grad[:, :256],
        qkv_grad[:, 256:384],
        qkv_grad[:, 384:],
        out_grad,
        gate_grad,
        up_grad,
        down_grad,
        gain_sum[0:2, :32],
        gain_sum[2:4, :2],
    )


def solution(mesh):
    tokens, weights = P(None, "ctx", None), P("ctx", "tp")
    return jax.shard_map(
        local,
        mesh=mesh,
        in_specs=(tokens,) * 2 + (weights,) * 7 + (P(None, "ctx"),) * 2,
        out_specs=(tokens,) * 2 + (weights,) * 7 + (P(None, "ctx"),) * 2,
        check_vma=False,
    )
```

```python
import functools

import jax
import jax.numpy as jnp
from jax import lax
from jax.experimental import pallas as pl
from jax.experimental.pallas import tpu as pltpu
from jax.sharding import PartitionSpec as P

HEAD_SIZE = 64
EPSILON = 1e-06
ROPE_BASE = 1000000.0
MESH = pl.DeviceIdType.MESH
F32 = jnp.float32
BF16 = jnp.bfloat16
ANY = pl.BlockSpec(memory_space=pl.ANY)
VMEM = pl.BlockSpec(memory_space=pltpu.VMEM)
NCTX = 32
PAIRS = 4
WORKERS = 8
SLOTS = 4
BLOCK = 128


def group(kind):
    c, t = lax.axis_index("ctx"), lax.axis_index("tp")
    h = lax.rem(c, 2)
    if kind == "ctx":
        return NCTX, c, lambda p: (p, t)
    if kind == "tp":
        return 4, t, lambda p: (c, p)
    if kind == "pair":
        return 2, h, lambda p: (c - h + p, t)
    z, x, core = c // 8, lax.rem(c // 2, 4), lax.rem(t, 2)
    if kind == "z":
        return 4, z, lambda p: (c + (p - z) * 8, t)
    if kind == "x":
        return 4, x, lambda p: (c + (p - x) * 2, t)
    if kind == "core":
        return 2, core, lambda p: (c, t - core + p)
    if kind == "ring":
        return 4, h * 2 + t // 2, lambda p: (c - h + p // 2, lax.rem(p, 2) * 2 + core)
    return 8, h * 4 + t, lambda p: (c - h + p // 4, lax.rem(p, 4))


PICKS = {
    "same": lambda ref, p: ref,
    "own": lambda ref, p: ref.at[p],
    "half": lambda ref, p: ref.at[lax.rem(p, 2)],
    "plane": lambda ref, p: ref.at[p // WORKERS],
}


def greet(kinds):
    barrier = pltpu.get_barrier_semaphore()
    total = 0
    for kind in kinds:
        n, me, dev = group(kind)

        @pl.loop(1, n)
        def _(i):
            pl.semaphore_signal(
                barrier, inc=1, device_id=dev(lax.rem(me + i, n)), device_id_type=MESH
            )

        total += n - 1
    pl.semaphore_wait(barrier, total)


def begin(kind, pick, src, dst, send, recv):
    n, me, dev = group(kind)
    choose = PICKS[pick]

    @pl.loop(1, n)
    def _(i):
        p = lax.rem(me + 5 * i, n)
        pltpu.make_async_remote_copy(
            src_ref=choose(src, p),
            dst_ref=dst.at[me],
            send_sem=send.at[p],
            recv_sem=recv.at[me],
            device_id=dev(p),
            device_id_type=MESH,
        ).start()

    pltpu.make_async_copy(choose(src, me), dst.at[me], recv.at[me]).start()


def finish(kind, pick, src, dst, send, recv):
    n, me, dev = group(kind)
    choose = PICKS[pick]

    @pl.loop(1, n)
    def _(i):
        p = lax.rem(me + i, n)
        copy = pltpu.make_async_remote_copy(
            src_ref=choose(src, p),
            dst_ref=dst.at[p],
            send_sem=send.at[p],
            recv_sem=recv.at[p],
            device_id=dev(p),
            device_id_type=MESH,
        )
        copy.wait_send()
        copy.wait_recv()

    pltpu.make_async_copy(choose(src, me), dst.at[me], recv.at[me]).wait()


def push(kind, src_of, dst_of, send, recv, local=False):
    n, me, dev = group(kind)

    @pl.loop(1, n)
    def _(i):
        p = lax.rem(me + i, n)
        pltpu.make_async_remote_copy(
            src_ref=src_of(p),
            dst_ref=dst_of(me),
            send_sem=send.at[p],
            recv_sem=recv.at[me],
            device_id=dev(p),
            device_id_type=MESH,
        ).start()

    if local:
        pltpu.make_async_copy(src_of(me), dst_of(me), recv.at[me]).start()


def settle(kind, src_of, dst_of, send, recv, local=False):
    n, me, dev = group(kind)

    @pl.loop(1, n)
    def _(i):
        p = lax.rem(me + i, n)
        copy = pltpu.make_async_remote_copy(
            src_ref=src_of(p),
            dst_ref=dst_of(p),
            send_sem=send.at[p],
            recv_sem=recv.at[p],
            device_id=dev(p),
            device_id_type=MESH,
        )
        copy.wait_send()
        copy.wait_recv()

    if local:
        pltpu.make_async_copy(src_of(me), dst_of(me), recv.at[me]).wait()


def stage(*moves):
    for move in moves:
        push(*move)
    for move in moves:
        settle(*move)


class Sems:
    def __init__(self, refs):
        self.refs = list(refs)

    def two(self):
        return self.refs.pop(0), self.refs.pop(0)


def position():
    c = lax.axis_index("ctx")
    return c // 8, lax.rem(c // 2, 4), lax.rem(c, 2)


SIZES = {"ctx": NCTX, "tp": 4, "pair": 2, "rows": 8, "z": 4, "x": 4, "core": 2, "ring": 4}


def gather_body(w, gains, ffn, w_all, gains_all, ffn_pair, *sem):
    z, x, h = position()
    take = Sems(sem)
    greet(["z", "x", "pair"])
    swap = ("pair", lambda p: ffn.at[p], lambda q: ffn_pair.at[q], *take.two(), True)
    first = [
        ("pair", lambda p: w, lambda q: w_all.at[z, x, q], *take.two(), True),
        ("pair", lambda p: gains, lambda q: gains_all.at[z, x, q], *take.two(), True),
    ]
    for move in first:
        push(*move)
    push(*swap)
    for move in first:
        settle(*move)
    stage(
        ("x", lambda p: w_all.at[z, x, :, 0], lambda q: w_all.at[z, q, :, 0], *take.two()),
        ("z", lambda p: w_all.at[z, x, :, 1], lambda q: w_all.at[q, x, :, 1], *take.two()),
        ("x", lambda p: gains_all.at[z, x], lambda q: gains_all.at[z, q], *take.two()),
    )
    stage(
        ("z", lambda p: w_all.at[z, :, :, 0], lambda q: w_all.at[q, :, :, 0], *take.two()),
        ("x", lambda p: w_all.at[:, x, :, 1], lambda q: w_all.at[:, q, :, 1], *take.two()),
        ("z", lambda p: gains_all.at[z], lambda q: gains_all.at[q], *take.two()),
    )
    settle(*swap)


def gather(w, gains, ffn):
    return pl.pallas_call(
        gather_body,
        out_shape=[
            jax.ShapeDtypeStruct((4, 4, 2, *w.shape), BF16),
            jax.ShapeDtypeStruct((4, 4, 2, *gains.shape), BF16),
            jax.ShapeDtypeStruct(ffn.shape, BF16),
        ],
        in_specs=[ANY] * 3,
        out_specs=[VMEM, VMEM, ANY],
        scratch_shapes=sems(["pair"] * 3 + ["x", "z", "x", "z", "x", "z"]),
        compiler_params=pltpu.CompilerParams(collective_id=1, has_side_effects=True),
        name="gather",
    )(w, gains, ffn)


def piece_shape(pick, array):
    return array.shape if pick == "same" else array.shape[1:]


def landing(kind, pick, array):
    return jax.ShapeDtypeStruct((SIZES[kind], *piece_shape(pick, array)), array.dtype)


def sems(kinds):
    return [pltpu.SemaphoreType.DMA((SIZES[k],)) for k in kinds for _ in range(2)]


def exchange_body(plan, kinds, *refs):
    n = len(plan)
    srcs, dsts, rest = refs[:n], refs[n : 2 * n], refs[2 * n :]
    greet(kinds)
    for k, (kind, pick) in enumerate(plan):
        begin(kind, pick, srcs[k], dsts[k], rest[2 * k], rest[2 * k + 1])
    for k, (kind, pick) in enumerate(plan):
        finish(kind, pick, srcs[k], dsts[k], rest[2 * k], rest[2 * k + 1])


def exchange(number, kinds, items):
    plan = tuple((kind, pick) for kind, pick, _ in items)
    return pl.pallas_call(
        functools.partial(exchange_body, plan, kinds),
        out_shape=[landing(*item) for item in items],
        in_specs=[ANY] * len(items),
        out_specs=[ANY] * len(items),
        scratch_shapes=sems([kind for kind, _ in plan]),
        compiler_params=pltpu.CompilerParams(collective_id=number, has_side_effects=True),
        name=f"exchange{number}",
    )(*[array for _, _, array in items])


def places():
    c, t = lax.axis_index("ctx"), lax.axis_index("tp")
    slot, low = c // WORKERS, lax.rem(c, WORKERS)
    to = low + lax.rem(slot, 2) * (WORKERS - 1 - 2 * low)
    return c, t, slot, low, to


def block_of(low, j):
    return j * WORKERS + (low if j % 2 == 0 else WORKERS - 1 - low)


def greet_attention(kinds):
    c, t, slot, low, to = places()
    barrier = pltpu.get_barrier_semaphore()
    total = 0
    others = [p * WORKERS + to for p in range(PAIRS)] + [block_of(low, j) for j in range(SLOTS)]
    for other in others:

        @pl.when(other != c)
        def _():
            pl.semaphore_signal(barrier, inc=1, device_id=(other, t), device_id_type=MESH)

        total = total + jnp.where(other != c, 1, 0)
    for kind in kinds:
        n, me, dev = group(kind)

        @pl.loop(1, n)
        def _(i):
            pl.semaphore_signal(
                barrier, inc=1, device_id=dev(lax.rem(me + i, n)), device_id_type=MESH
            )

        total = total + (n - 1)
    pl.semaphore_wait(barrier, total)


def to_workers(src, dst, send, recv, act):
    c, t, slot, low, to = places()
    for p in range(PAIRS):
        target = p * WORKERS + to
        far = pltpu.make_async_remote_copy(
            src_ref=src.at[p],
            dst_ref=dst.at[slot],
            send_sem=send.at[p],
            recv_sem=recv.at[slot],
            device_id=(target, t),
            device_id_type=MESH,
        )
        near = pltpu.make_async_copy(src.at[p], dst.at[slot], send.at[p])

        @pl.when(target != c)
        def _():
            far.start() if act == "start" else far.wait_send()

        @pl.when(target == c)
        def _():
            near.start() if act == "start" else near.wait()


def from_owners(src, dst, send, recv):
    c, t, slot, low, to = places()
    for j in range(SLOTS):
        owner = block_of(low, j)

        @pl.when(owner != c)
        def _():
            pltpu.make_async_remote_copy(
                src_ref=src.at[j],
                dst_ref=dst.at[j],
                send_sem=send.at[j],
                recv_sem=recv.at[j],
                device_id=(owner, t),
                device_id_type=MESH,
            ).wait_recv()


def to_owner(src, dst, send, recv, j, act):
    c, t, slot, low, to = places()
    owner = block_of(low, j)
    far = pltpu.make_async_remote_copy(
        src_ref=src.at[j],
        dst_ref=dst.at[slot],
        send_sem=send.at[j],
        recv_sem=recv.at[slot],
        device_id=(owner, t),
        device_id_type=MESH,
    )
    near = pltpu.make_async_copy(src.at[j], dst.at[slot], send.at[j])

    @pl.when(owner != c)
    def _():
        far.start() if act == "start" else far.wait_send()

    @pl.when(owner == c)
    def _():
        near.start() if act == "start" else near.wait()


def from_workers(src, dst, send, recv):
    c, t, slot, low, to = places()
    for p in range(PAIRS):
        target = p * WORKERS + to

        @pl.when(target != c)
        def _():
            pltpu.make_async_remote_copy(
                src_ref=src.at[p],
                dst_ref=dst.at[p],
                send_sem=send.at[p],
                recv_sem=recv.at[p],
                device_id=(target, t),
                device_id_type=MESH,
            ).wait_recv()


def last_dims(a, b):
    return lax.dot_general(a, b, (((1,), (1,)), ((), ())), preferred_element_type=F32)


def first_dims(a, b):
    return lax.dot_general(a, b, (((0,), (0,)), ((), ())), preferred_element_type=F32)


def causal_mask(b, i):
    shape = (2 * BLOCK, 2 * BLOCK)
    rows = lax.broadcasted_iota(jnp.int32, shape, 0)
    token = b * BLOCK + jnp.where(rows >= BLOCK, rows - BLOCK, rows)
    key = i * 2 * BLOCK + lax.broadcasted_iota(jnp.int32, shape, 1)
    return token >= key


def forward_body(
    q_src, kv_src, wo, cot, att, q_buf, kv_buf, o_buf, log_buf, wo_all, cot_all,
    acc, den, q_send, q_recv, o_send, o_recv, *sem,
):
    c, t, slot, low, to = places()
    z, x, h = position()
    take = Sems(sem)
    greet_attention(["z", "x", "pair"])
    near = ("z", lambda p: kv_src.at[p], lambda q: kv_buf.at[q, x, h], *take.two(), True)
    out_first = ("pair", lambda p: wo, lambda q: wo_all.at[z, x, q], *take.two(), True)
    push(*near)
    to_workers(q_src, q_buf, q_send, q_recv, "start")
    push(*out_first)
    settle(*near)
    stage(
        ("x", lambda p: kv_buf.at[:, x, h, 0], lambda q: kv_buf.at[:, q, h, 0], *take.two()),
        ("pair", lambda p: kv_buf.at[:, x, h, 1], lambda q: kv_buf.at[:, x, q, 1], *take.two()),
    )
    stage(
        ("pair", lambda p: kv_buf.at[:, :, h, 0], lambda q: kv_buf.at[:, :, q, 0], *take.two()),
        ("x", lambda p: kv_buf.at[:, x, :, 1], lambda q: kv_buf.at[:, q, :, 1], *take.two()),
    )
    settle(*out_first)
    out_second = [
        ("x", lambda p: wo_all.at[z, x, :, 0], lambda q: wo_all.at[z, q, :, 0], *take.two()),
        ("z", lambda p: wo_all.at[z, x, :, 1], lambda q: wo_all.at[q, x, :, 1], *take.two()),
    ]
    out_third = [
        ("z", lambda p: wo_all.at[z, :, :, 0], lambda q: wo_all.at[q, :, :, 0], *take.two()),
        ("x", lambda p: wo_all.at[:, x, :, 1], lambda q: wo_all.at[:, q, :, 1], *take.two()),
    ]
    swap = ("pair", lambda p: cot, lambda q: cot_all.at[q], *take.two(), True)
    for move in out_second:
        push(*move)
    push(*swap)
    to_workers(q_src, q_buf, q_send, q_recv, "wait")
    from_owners(q_src, q_buf, q_send, q_recv)
    lanes = lax.broadcasted_iota(jnp.int32, (2 * BLOCK, BLOCK), 1)
    for j in range(SLOTS):
        b = block_of(low, j)
        acc[...] = jnp.zeros_like(acc)
        den[...] = jnp.zeros_like(den)

        def chunk(i, masked):
            q = q_buf[j]
            kv = kv_buf[i // 4, lax.rem(i, 4)].reshape(2 * BLOCK, BLOCK)
            powered = jnp.exp(last_dims(q, kv))
            if masked:
                powered = jnp.where(causal_mask(b, i), powered, 0.0)
            den[...] += powered[:, :BLOCK] + powered[:, BLOCK:]
            acc[...] += jnp.dot(powered.astype(BF16), kv, preferred_element_type=F32)

        pl.loop(0, b // 2)(lambda i: chunk(i, False))
        chunk(b // 2, True)
        total = jnp.sum(den[...], axis=1, keepdims=True)
        o_buf[j] = jnp.where(lanes >= HEAD_SIZE, acc[...] / total, 0.0).astype(BF16)
        log_buf[j] = jnp.broadcast_to(jnp.log(total), (2 * BLOCK, BLOCK))
        to_owner(o_buf, att, o_send, o_recv, j, "start")
        if j == 1:
            for move in out_second:
                settle(*move)
            for move in out_third:
                push(*move)
    for j in range(SLOTS):
        to_owner(o_buf, att, o_send, o_recv, j, "wait")
    from_workers(o_buf, att, o_send, o_recv)
    for move in out_third:
        settle(*move)
    settle(*swap)


def forward(q_src, kv_src, wo, cot):
    stack = jax.ShapeDtypeStruct((SLOTS, 2 * BLOCK, BLOCK), BF16)
    return pl.pallas_call(
        forward_body,
        out_shape=[
            stack,
            stack,
            jax.ShapeDtypeStruct((4, 4, 2, 2, BLOCK // 2, BLOCK), BF16),
            stack,
            jax.ShapeDtypeStruct((SLOTS, 2 * BLOCK, BLOCK), F32),
            jax.ShapeDtypeStruct((4, 4, 2, *wo.shape), BF16),
            jax.ShapeDtypeStruct((2, *cot.shape), BF16),
        ],
        in_specs=[ANY] * 4,
        out_specs=[ANY] + [VMEM] * 5 + [ANY],
        scratch_shapes=[
            pltpu.VMEM((2 * BLOCK, BLOCK), F32),
            pltpu.VMEM((2 * BLOCK, BLOCK), F32),
        ]
        + [pltpu.SemaphoreType.DMA((SLOTS,))] * 4
        + sems(["z", "pair", "x", "pair", "pair", "x", "x", "z", "z", "x", "pair"]),
        compiler_params=pltpu.CompilerParams(
            collective_id=2, has_side_effects=True, vmem_limit_bytes=24 * 2**20
        ),
        name="attention_forward",
    )(q_src, kv_src, wo, cot)


def backward_body(
    do_src, q_buf, kv_buf, o_buf, log_buf, ffn, dq_all, dkv_all, ffn_all,
    do_buf, dq_buf, dkv_buf, acc, dkv, one_a, one_b, sum_a, sum_b, two_a, two_b, sum_all,
    do_send, do_recv, dq_send, dq_recv, *sem,
):
    c, t, slot, low, to = places()
    z, x, h = position()
    take = Sems(sem)
    greet_attention(["z", "x", "rows"])
    to_workers(do_src, do_buf, do_send, do_recv, "start")
    ffn_sems = take.two()
    begin("rows", "own", ffn, ffn_all, *ffn_sems)
    dkv[...] = jnp.zeros_like(dkv)
    to_workers(do_src, do_buf, do_send, do_recv, "wait")
    from_owners(do_src, do_buf, do_send, do_recv)
    for j in range(SLOTS):
        b = block_of(low, j)
        acc[...] = jnp.zeros_like(acc)
        delta = jnp.sum(do_buf[j].astype(F32) * o_buf[j].astype(F32), axis=1, keepdims=True)

        def chunk(i, masked):
            q, do = q_buf[j], do_buf[j]
            kv = kv_buf[i // 4, lax.rem(i, 4)].reshape(2 * BLOCK, BLOCK)
            logs = log_buf[j]
            scores = last_dims(q, kv)
            probs = jnp.exp(scores - jnp.concatenate([logs, logs], axis=1))
            if masked:
                probs = jnp.where(causal_mask(b, i), probs, 0.0)
            grads = (probs * (last_dims(do, kv) - delta)).astype(BF16)
            acc[...] += jnp.dot(grads, kv, preferred_element_type=F32)
            update = first_dims(grads, q) + first_dims(probs.astype(BF16), do)
            dkv[i // 4, lax.rem(i, 4)] += update.reshape(2, 2, BLOCK // 2, BLOCK)

        pl.loop(0, b // 2)(lambda i: chunk(i, False))
        chunk(b // 2, True)
        dq_buf[j] = (acc[...] * (HEAD_SIZE**-0.5)).astype(BF16)
        to_owner(dq_buf, dq_all, dq_send, dq_recv, j, "start")
    dkv_buf[...] = dkv[...].astype(BF16)
    stage(
        ("x", lambda p: dkv_buf.at[:, p, :, 0], lambda q: one_a.at[q], *take.two(), True),
        ("pair", lambda p: dkv_buf.at[:, :, p, 1], lambda q: one_b.at[q], *take.two(), True),
    )
    sum_a[...] = summed(one_a).astype(BF16)
    sum_b[...] = summed(one_b).astype(BF16)
    stage(
        ("pair", lambda p: sum_a.at[:, p], lambda q: two_a.at[q], *take.two(), True),
        ("x", lambda p: sum_b.at[:, p], lambda q: two_b.at[q], *take.two(), True),
    )
    sum_all[:, 0] = summed(two_a).astype(BF16)
    sum_all[:, 1] = summed(two_b).astype(BF16)
    stage(("z", lambda p: sum_all.at[p], lambda q: dkv_all.at[q], *take.two(), True))
    for j in range(SLOTS):
        to_owner(dq_buf, dq_all, dq_send, dq_recv, j, "wait")
    from_workers(dq_buf, dq_all, dq_send, dq_recv)
    finish("rows", "own", ffn, ffn_all, *ffn_sems)


def backward(do_src, q_buf, kv_buf, o_buf, log_buf, ffn):
    half = BLOCK // 2
    return pl.pallas_call(
        backward_body,
        out_shape=[
            jax.ShapeDtypeStruct((SLOTS, 2 * BLOCK, BLOCK), BF16),
            jax.ShapeDtypeStruct((PAIRS, 2, half, BLOCK), BF16),
            landing("rows", "own", ffn),
        ],
        in_specs=[ANY] + [VMEM] * 4 + [ANY],
        out_specs=[ANY] * 3,
        scratch_shapes=[
            pltpu.VMEM((SLOTS, 2 * BLOCK, BLOCK), BF16),
            pltpu.VMEM((SLOTS, 2 * BLOCK, BLOCK), BF16),
            pltpu.VMEM((4, 4, 2, 2, half, BLOCK), BF16),
            pltpu.VMEM((2 * BLOCK, BLOCK), F32),
            pltpu.VMEM((4, 4, 2, 2, half, BLOCK), F32),
            pltpu.VMEM((4, 4, 2, half, BLOCK), BF16),
            pltpu.VMEM((2, 4, 4, half, BLOCK), BF16),
            pltpu.VMEM((4, 2, half, BLOCK), BF16),
            pltpu.VMEM((4, 4, half, BLOCK), BF16),
            pltpu.VMEM((2, 4, half, BLOCK), BF16),
            pltpu.VMEM((4, 4, half, BLOCK), BF16),
            pltpu.VMEM((4, 2, half, BLOCK), BF16),
        ]
        + [pltpu.SemaphoreType.DMA((SLOTS,))] * 4
        + sems(["rows", "x", "pair", "pair", "x", "z"]),
        compiler_params=pltpu.CompilerParams(
            collective_id=6, has_side_effects=True, vmem_limit_bytes=24 * 2**20
        ),
        name="attention_backward",
    )(do_src, q_buf, kv_buf, o_buf, log_buf, ffn)


def row_scale(rows):
    return lax.rsqrt(jnp.mean(rows * rows, axis=1, keepdims=True) + EPSILON)


def row_back(grads, normed, scale, gain):
    scaled = grads * gain
    return scale * (scaled - normed * jnp.mean(scaled * normed, axis=1, keepdims=True))


def summed(ref):
    total = ref[0].astype(F32)
    for k in range(1, ref.shape[0]):
        total += ref[k].astype(F32)
    return total


UNITS = 640


def feed_body(
    parts, inputs, gain, w, cot, cot_own,
    residual, grad_residual, gain_part, grad_all, grads, ffn_part,
    landed, hidden, hidden_all, grad_units, units, grad_in, back, halved, chip, ringed, grad_bf, *sem,
):
    take = Sems(sem)
    core = lax.rem(lax.axis_index("tp"), 2)
    greet(["tp", "ring"])
    share = ("tp", lambda p: parts.at[p], lambda q: landed.at[q], *take.two(), True)
    push(*share)

    @pl.loop(0, 4)
    def _(m):
        at = pl.ds(pl.multiple_of(m * 128, 128), 128)
        grad_units[at] = jnp.dot(cot[at], w[:, 2 * UNITS :], preferred_element_type=F32)

    settle(*share)
    rows = inputs[...] + summed(landed)
    residual[...] = rows
    scale = row_scale(rows)
    hidden[...] = (rows * scale * gain[...]).astype(BF16)
    stage(("ring", lambda p: hidden, lambda q: hidden_all.at[q, core], *take.two(), True))
    stage(("core", lambda p: hidden_all.at[:, core], lambda q: hidden_all.at[:, q], *take.two()))

    @pl.loop(0, 2)
    def _(m):
        at = pl.ds(pl.multiple_of(m * 256, 256), 256)
        some = hidden_all[pl.ds(2 * m, 2)].reshape(256, hidden.shape[1])
        gate = jnp.dot(some, w[:, :UNITS], preferred_element_type=F32)
        up = jnp.dot(some, w[:, UNITS : 2 * UNITS], preferred_element_type=F32)
        sigmoid = jax.nn.sigmoid(gate)
        activated = gate * sigmoid
        units[at] = (activated * up).astype(BF16)
        grad = grad_units[at]
        grad_in[at, :UNITS] = (grad * up * sigmoid * (1.0 + gate * (1.0 - sigmoid))).astype(BF16)
        grad_in[at, UNITS:] = (grad * activated).astype(BF16)
        step = last_dims(grad_in[at], w[:, : 2 * UNITS]).astype(BF16)
        back[pl.ds(2 * m, 2)] = step.reshape(2, *back.shape[1:])

    both = ("core", lambda p: back.at[:, p], lambda q: halved.at[q], *take.two(), True)
    push(*both)

    @pl.loop(0, 2)
    def _(m):
        at = pl.ds(pl.multiple_of(m * 256, 256), 256)
        step = last_dims(units[at], w[:, 2 * UNITS :]).astype(BF16)
        ffn_part[pl.ds(4 * m, 4)] = step.reshape(4, *ffn_part.shape[1:])

    settle(*both)
    chip[...] = summed(halved).astype(BF16)
    ring = ("ring", lambda p: chip.at[p], lambda q: ringed.at[q], *take.two(), True)
    push(*ring)

    @pl.loop(0, 4)
    def _(m):
        at = pl.ds(pl.multiple_of(m * 256, 256), 256)
        some = hidden_all[:, :, :, at].reshape(512, 256)
        grads[at, : 2 * UNITS] = first_dims(some, grad_in[...]).astype(BF16)

    settle(*ring)
    total = summed(ringed)
    rows = residual[...]
    scale = row_scale(rows)
    normed = rows * scale
    result = cot_own[...].astype(F32) + row_back(total, normed, scale, gain[...])
    grad_bf[...] = result.astype(BF16)
    last = ("tp", lambda p: grad_bf, lambda q: grad_all.at[q], *take.two(), True)
    push(*last)
    grad_residual[...] = result
    gain_part[...] = jnp.sum(total * normed, axis=0, keepdims=True)

    @pl.loop(0, 4)
    def _(m):
        at = pl.ds(pl.multiple_of(m * 256, 256), 256)
        grads[at, 2 * UNITS :] = first_dims(cot[:, at], units[...]).astype(BF16)

    settle(*last)


def feed_step(parts, inputs, gain, w, cot, cot_own):
    own, width = inputs.shape
    rows = cot.shape[0]
    return pl.pallas_call(
        feed_body,
        out_shape=[
            jax.ShapeDtypeStruct((own, width), F32),
            jax.ShapeDtypeStruct((own, width), F32),
            jax.ShapeDtypeStruct((1, width), F32),
            jax.ShapeDtypeStruct((4, own, width), BF16),
            jax.ShapeDtypeStruct(w.shape, BF16),
            jax.ShapeDtypeStruct((8, own, width), BF16),
        ],
        in_specs=[VMEM] * 6,
        out_specs=[VMEM] * 6,
        scratch_shapes=[
            pltpu.VMEM((4, own, width), BF16),
            pltpu.VMEM((own, width), BF16),
            pltpu.VMEM((4, 2, own, width), BF16),
            pltpu.VMEM((rows, UNITS), F32),
            pltpu.VMEM((rows, UNITS), BF16),
            pltpu.VMEM((rows, 2 * UNITS), BF16),
            pltpu.VMEM((4, 2, own, width), BF16),
            pltpu.VMEM((2, 4, own, width), BF16),
            pltpu.VMEM((4, own, width), BF16),
            pltpu.VMEM((4, own, width), BF16),
            pltpu.VMEM((own, width), BF16),
        ]
        + sems(["tp", "ring", "core", "core", "ring", "tp"]),
        compiler_params=pltpu.CompilerParams(
            collective_id=3, has_side_effects=True, vmem_limit_bytes=40 * 2**20
        ),
        name="feed_forward",
    )(parts, inputs, gain, w, cot, cot_own)


def last_body(
    parts, hidden, grad_in, res_rows, attended, ffn, gains, output, grad_residual, inputs, gain,
    qkv_grad, ffn_all, output_all, input_all, gain_tp,
    qkv, landed, input_bf, one_a, one_b, one_g, sum_a, sum_b, sum_g, two_a, two_b, two_g,
    part_a, part_b, part_g, three_a, three_b, three_g, gain_sum, *sem,
):
    take = Sems(sem)
    greet(["z", "x", "pair", "tp"])
    rows_sums, rows_output, rows_input, gains_out = [take.two() for _ in range(4)]
    begin("tp", "own", parts, landed, *rows_sums)

    @pl.loop(0, 4)
    def _(m):
        at = pl.ds(pl.multiple_of(m * 256, 256), 256)
        wide = grad_in.shape[1]
        step = first_dims(hidden[:, at], grad_in[...]).astype(BF16)
        qkv[m, :, :, :, :, :wide] = step.reshape(4, 2, 2, 16, wide)
        step = first_dims(res_rows[:, at], attended[...]).astype(BF16)
        qkv[m, :, :, :, :, wide:] = step.reshape(4, 2, 2, 16, attended.shape[1])

    first = [
        ("x", lambda p: qkv.at[:, p, :, 0], lambda q: one_a.at[q], *take.two(), True),
        ("z", lambda p: qkv.at[p, :, :, 1], lambda q: one_b.at[q], *take.two(), True),
        ("x", lambda p: gains.at[:, p], lambda q: one_g.at[q], *take.two(), True),
    ]
    for move in first:
        push(*move)
    rows = inputs[...]
    scale = row_scale(rows)
    normed = rows * scale
    finish("tp", "own", parts, landed, *rows_sums)
    result = grad_residual[...] + row_back(summed(landed), normed, scale, gain[...])
    input_bf[...] = result.astype(BF16)
    begin("tp", "same", input_bf, input_all, *rows_input)
    begin("tp", "same", output, output_all, *rows_output)
    swap = ("pair", lambda p: ffn.at[p], lambda q: ffn_all.at[q], *take.two(), True)
    push(*swap)
    for move in first:
        settle(*move)
    sum_a[...] = summed(one_a).astype(BF16)
    sum_b[...] = summed(one_b).astype(BF16)
    sum_g[...] = summed(one_g)
    stage(
        ("z", lambda p: sum_a.at[p], lambda q: two_a.at[q], *take.two(), True),
        ("x", lambda p: sum_b.at[p], lambda q: two_b.at[q], *take.two(), True),
        ("z", lambda p: sum_g.at[p], lambda q: two_g.at[q], *take.two(), True),
    )
    part_a[...] = summed(two_a).astype(BF16)
    part_b[...] = summed(two_b).astype(BF16)
    part_g[...] = summed(two_g)
    stage(
        ("pair", lambda p: part_a.at[p], lambda q: three_a.at[q], *take.two(), True),
        ("pair", lambda p: part_b.at[p], lambda q: three_b.at[q], *take.two(), True),
        ("pair", lambda p: part_g.at[p], lambda q: three_g.at[q], *take.two(), True),
    )
    gain_sum[...] = summed(three_g)
    begin("tp", "same", gain_sum, gain_tp, *gains_out)
    qkv_grad[0] = summed(three_a)
    qkv_grad[1] = summed(three_b)
    finish("tp", "same", output, output_all, *rows_output)
    finish("tp", "same", input_bf, input_all, *rows_input)
    finish("tp", "same", gain_sum, gain_tp, *gains_out)
    settle(*swap)


def last_step(
    parts, hidden, grad_in, res_rows, attended, ffn, gains, output, grad_residual, inputs, gain
):
    own, width = inputs.shape
    piece, small = (16, grad_in.shape[1] + attended.shape[1]), gains.shape[3:]

    def scratch(*shape):
        return [pltpu.VMEM((*shape, *piece), BF16)] * 2 + [pltpu.VMEM((*shape, *small), F32)]

    return pl.pallas_call(
        last_body,
        out_shape=[
            jax.ShapeDtypeStruct((2, *piece), F32),
            jax.ShapeDtypeStruct(ffn.shape, BF16),
            jax.ShapeDtypeStruct((4, own, width), BF16),
            jax.ShapeDtypeStruct((4, own, width), BF16),
            jax.ShapeDtypeStruct((4, *small), F32),
        ],
        in_specs=[VMEM] * 5 + [ANY] + [VMEM] * 5,
        out_specs=[VMEM] + [ANY] * 4,
        scratch_shapes=[pltpu.VMEM((4, 4, 2, 2, *piece), BF16)]
        + [pltpu.VMEM((4, own, width), BF16), pltpu.VMEM((own, width), BF16)]
        + scratch(4, 4, 2)
        + scratch(4, 2)
        + scratch(4, 2)
        + scratch(2)
        + scratch(2)
        + [pltpu.VMEM(small, F32)]
        + sems(["tp"] * 4 + ["x", "z", "x", "pair", "z", "x", "z"] + ["pair"] * 3),
        compiler_params=pltpu.CompilerParams(
            collective_id=8, has_side_effects=True, vmem_limit_bytes=24 * 2**20
        ),
        name="last_step",
    )(parts, hidden, grad_in, res_rows, attended, ffn, gains, output, grad_residual, inputs, gain)


def rms_scale(rows):
    return lax.rsqrt(jnp.mean(rows * rows, axis=-1, keepdims=True) + EPSILON)


def rope_tables(tokens, offset):
    half = HEAD_SIZE // 2
    inverse = ROPE_BASE ** (-(jnp.arange(half, dtype=F32) * 2.0 / HEAD_SIZE))
    places_ = (offset + jnp.arange(tokens, dtype=jnp.int32)).astype(F32)
    angles = places_[:, None] * inverse[None, :]
    return jnp.cos(angles), jnp.sin(angles)


def rotary(rows, cosine, sine, direction):
    half = HEAD_SIZE // 2
    first, second = rows[..., :half], rows[..., half:]
    cosine = cosine[:, None, :]
    sine = sine[:, None, :] * direction
    return jnp.concatenate([first * cosine - second * sine, second * cosine + first * sine], -1)


def head_back(grads, hatted, scale, gain):
    scaled = grads * gain
    return scale * (scaled - hatted * jnp.mean(scaled * hatted, axis=-1, keepdims=True))


def to_pairs(rows, heads, left):
    s, tokens = rows.shape[:2]
    kv = rows.shape[2] // heads
    x = rows.reshape(s, tokens, kv, heads, HEAD_SIZE).transpose(2, 0, 3, 1, 4)
    x = x.reshape(kv * s, heads * tokens, HEAD_SIZE)
    side = (0, HEAD_SIZE) if left else (HEAD_SIZE, 0)
    return jnp.pad(x, ((0, 0), (0, 0), side))


def from_pairs(x, s, heads):
    kv = x.shape[0] // s
    tokens = x.shape[1] // heads
    x = x.reshape(kv, s, heads, tokens, HEAD_SIZE).transpose(1, 3, 0, 2, 4)
    return x.reshape(s, tokens, kv * heads, HEAD_SIZE)


def halves(*weights):
    rows, cols = weights[0].shape
    w = jnp.stack(weights).reshape(len(weights), rows, 2, cols // 2)
    w = jnp.pad(w, ((0, 0), (0, 0), (0, 0), (0, UNITS - cols // 2)))
    return w.transpose(2, 1, 0, 3).reshape(2, rows, len(weights) * UNITS)


def local(
    block_input, cotangent, w_query, key_weight, w_value, w_out, w_gate, w_up, w_down,
    norm_gains, head_gains,
):
    c, t = lax.axis_index("ctx"), lax.axis_index("tp")
    seqs, tokens, width = block_input.shape
    rows = seqs * tokens
    own = rows // 4
    unit_half = w_gate.shape[1] // 2

    def mine(x):
        return lax.dynamic_slice_in_dim(x, t * own, own, 0)

    weight_rows = jnp.concatenate([w_query, key_weight, w_value], axis=1)
    gains = jnp.pad(norm_gains, ((0, 14), (0, 96))) + jnp.pad(head_gains, ((2, 12), (0, 126)))
    ffn_rows = halves(w_gate, w_up, w_down)
    weights_all, gains_all, ffn_pair = gather(
        weight_rows.reshape(2, 16, weight_rows.shape[1]), gains, ffn_rows
    )
    gains_all = gains_all.reshape(NCTX, 16, 128)
    planes = [[2 * g + h for g in range(NCTX // 2)] for h in range(2)]
    ffn_full = lax.all_gather(
        ffn_pair.reshape(2 * 32, 3 * UNITS), "ctx", axis_index_groups=planes, tiled=True
    )
    qkv_full = weights_all.reshape(width, weight_rows.shape[1])
    gain_attn = gains_all[:, 0, :32].reshape(width).astype(F32)
    gain_ffn = gains_all[:, 1, :32].reshape(width).astype(F32)
    gain_query = gains_all[:, 2, :2].reshape(HEAD_SIZE).astype(F32)
    gain_key = gains_all[:, 3, :2].reshape(HEAD_SIZE).astype(F32)

    inputs = block_input.astype(F32).reshape(rows, width)
    scale_attn = rms_scale(inputs)
    normed_attn = inputs * scale_attn
    hidden_attn = (normed_attn * gain_attn).astype(BF16)
    raw = jnp.dot(hidden_attn, qkv_full, preferred_element_type=F32)
    query_raw = raw[:, :256].reshape(seqs, tokens, 4, HEAD_SIZE)
    key_raw = raw[:, 256:384].reshape(seqs, tokens, 2, HEAD_SIZE)
    values = raw[:, 384:].astype(BF16).reshape(seqs, tokens, 2, HEAD_SIZE)
    query_scale, key_scale = rms_scale(query_raw), rms_scale(key_raw)
    query_hat, key_hat = query_raw * query_scale, key_raw * key_scale
    cosine, sine = rope_tables(tokens, c * tokens)
    query_rot = rotary(query_hat * gain_query, cosine, sine, 1.0).astype(BF16)
    key_rot = rotary(key_hat * gain_key, cosine, sine, 1.0).astype(BF16)
    q_src = to_pairs(query_rot * jnp.asarray(HEAD_SIZE**-0.5, BF16), 2, True)
    kv_src = jnp.concatenate([key_rot, values], axis=-1).transpose(2, 0, 1, 3)
    kv_src = kv_src.reshape(PAIRS, 2, tokens // 2, 2 * HEAD_SIZE)

    att, q_buf, kv_buf, o_buf, log_buf, wo_all, cot_all = forward(
        q_src, kv_src, w_out.reshape(2, 16, 256), cotangent.reshape(rows, width)
    )
    attended = from_pairs(att[..., HEAD_SIZE:], seqs, 2).reshape(rows, 256)
    out_full = wo_all.reshape(width, 256)
    cot_rows = cot_all.reshape(2 * rows, width)
    attn_part = last_dims(attended, out_full).astype(BF16)
    inputs_own = mine(inputs)
    cot_own = mine(cotangent.reshape(rows, width))
    residual, grad_residual, ffn_gain_part, residual_all, ffn_grads, ffn_part = feed_step(
        attn_part.reshape(4, own, width),
        inputs_own,
        gain_ffn.reshape(1, width),
        ffn_full,
        cot_rows,
        cot_own,
    )
    grads_own = lax.psum_scatter(ffn_grads, "ctx", axis_index_groups=planes, tiled=True)
    residual_bf = residual_all.reshape(rows, width)

    grad_attended = jnp.dot(residual_bf, out_full, preferred_element_type=F32).astype(BF16)
    do_src = to_pairs(grad_attended.reshape(seqs, tokens, 4, HEAD_SIZE), 2, False)
    dq_all, dkv_all, ffn_parts = backward(
        do_src, q_buf, kv_buf, o_buf, log_buf, ffn_part
    )

    output_own = (residual + jnp.sum(ffn_parts.astype(F32), axis=0)).astype(BF16)
    grad_query_rot = from_pairs(dq_all[..., :HEAD_SIZE].astype(F32), seqs, 2)
    dkv = dkv_all.reshape(PAIRS, tokens, 2 * HEAD_SIZE).astype(F32)
    key_grad = from_pairs(dkv[..., :HEAD_SIZE], seqs, 1)
    value_in = from_pairs(dkv[..., HEAD_SIZE:], seqs, 1).astype(BF16).reshape(rows, 128)
    gq = rotary(grad_query_rot, cosine, sine, -1.0)
    gk = rotary(key_grad, cosine, sine, -1.0)
    query_gain_part = jnp.sum(gq * query_hat, axis=(0, 1, 2))
    key_gain_part = jnp.sum(gk * key_hat, axis=(0, 1, 2))
    query_in = head_back(gq, query_hat, query_scale, gain_query).astype(BF16).reshape(rows, 256)
    key_in = head_back(gk, key_hat, key_scale, gain_key).astype(BF16).reshape(rows, 128)
    grad_in = jnp.concatenate([query_in, key_in, value_in], axis=1)
    attn_back = last_dims(grad_in, qkv_full)
    attn_gain_part = jnp.sum(attn_back * normed_attn, axis=0)

    def placed(row, part):
        part = part.reshape(NCTX, 1, -1)
        return jnp.pad(part, ((0, 0), (row, 7 - row), (0, 128 - part.shape[2])))

    gain_parts = placed(0, attn_gain_part) + placed(1, ffn_gain_part)
    gain_parts = gain_parts + placed(2, query_gain_part) + placed(3, key_gain_part)
    qkv_grad, pair_grads, output_all, input_all, gain_tp = last_step(
        attn_back.astype(BF16).reshape(4, own, width),
        hidden_attn,
        grad_in,
        residual_bf,
        attended,
        grads_own.reshape(2, 32, -1),
        gain_parts.reshape(4, 4, 2, 8, 128),
        output_own,
        grad_residual,
        inputs_own,
        gain_attn.reshape(1, width),
    )
    pair_grads = pair_grads.astype(F32)
    gain_sum = jnp.sum(gain_tp, axis=0)
    qkv_grad = qkv_grad.reshape(32, 768)

    def joined(first):
        last = first + unit_half
        return jnp.concatenate([pair_grads[0, :, first:last], pair_grads[1, :, first:last]], axis=1)

    gate_grad, up_grad, down_grad = joined(0), joined(UNITS), joined(2 * UNITS)
    return (
        output_all.reshape(seqs, tokens, width),
        input_all.astype(F32).reshape(seqs, tokens, width),
        qkv_grad[:, :256],
        qkv_grad[:, 256:384],
        qkv_grad[:, 384:512],
        qkv_grad[:, 512:],
        gate_grad,
        up_grad,
        down_grad,
        gain_sum[0:2, :32],
        gain_sum[2:4, :2],
    )


def solution(mesh):
    tokens, weights = P(None, "ctx", None), P("ctx", "tp")
    return jax.shard_map(
        local,
        mesh=mesh,
        in_specs=(tokens,) * 2 + (weights,) * 7 + (P(None, "ctx"),) * 2,
        out_specs=(tokens,) * 2 + (weights,) * 7 + (P(None, "ctx"),) * 2,
        check_vma=False,
    )
```

```python
import functools

import jax
import jax.numpy as jnp
from jax import lax
from jax.experimental import pallas as pl
from jax.experimental.pallas import tpu as pltpu
from jax.sharding import PartitionSpec as P

HEAD_SIZE = 64
EPSILON = 1e-06
ROPE_BASE = 1000000.0
MESH = pl.DeviceIdType.MESH
F32 = jnp.float32
BF16 = jnp.bfloat16
ANY = pl.BlockSpec(memory_space=pl.ANY)
VMEM = pl.BlockSpec(memory_space=pltpu.VMEM)
NCTX = 32
PAIRS = 4
WORKERS = 8
SLOTS = 4
BLOCK = 128


def group(kind):
    c, t = lax.axis_index("ctx"), lax.axis_index("tp")
    h = lax.rem(c, 2)
    if kind == "ctx":
        return NCTX, c, lambda p: (p, t)
    if kind == "tp":
        return 4, t, lambda p: (c, p)
    if kind == "pair":
        return 2, h, lambda p: (c - h + p, t)
    z, x, core = c // 8, lax.rem(c // 2, 4), lax.rem(t, 2)
    if kind == "z":
        return 4, z, lambda p: (c + (p - z) * 8, t)
    if kind == "x":
        return 4, x, lambda p: (c + (p - x) * 2, t)
    if kind == "core":
        return 2, core, lambda p: (c, t - core + p)
    if kind == "ring":
        return 4, h * 2 + t // 2, lambda p: (c - h + p // 2, lax.rem(p, 2) * 2 + core)
    return 8, h * 4 + t, lambda p: (c - h + p // 4, lax.rem(p, 4))


PICKS = {
    "same": lambda ref, p: ref,
    "own": lambda ref, p: ref.at[p],
    "half": lambda ref, p: ref.at[lax.rem(p, 2)],
    "plane": lambda ref, p: ref.at[p // WORKERS],
}


def greet(kinds):
    barrier = pltpu.get_barrier_semaphore()
    total = 0
    for kind in kinds:
        n, me, dev = group(kind)

        @pl.loop(1, n)
        def _(i):
            pl.semaphore_signal(
                barrier, inc=1, device_id=dev(lax.rem(me + i, n)), device_id_type=MESH
            )

        total += n - 1
    pl.semaphore_wait(barrier, total)


def begin(kind, pick, src, dst, send, recv):
    n, me, dev = group(kind)
    choose = PICKS[pick]

    @pl.loop(1, n)
    def _(i):
        p = lax.rem(me + 5 * i, n)
        pltpu.make_async_remote_copy(
            src_ref=choose(src, p),
            dst_ref=dst.at[me],
            send_sem=send.at[p],
            recv_sem=recv.at[me],
            device_id=dev(p),
            device_id_type=MESH,
        ).start()

    pltpu.make_async_copy(choose(src, me), dst.at[me], recv.at[me]).start()


def finish(kind, pick, src, dst, send, recv):
    n, me, dev = group(kind)
    choose = PICKS[pick]

    @pl.loop(1, n)
    def _(i):
        p = lax.rem(me + i, n)
        copy = pltpu.make_async_remote_copy(
            src_ref=choose(src, p),
            dst_ref=dst.at[p],
            send_sem=send.at[p],
            recv_sem=recv.at[p],
            device_id=dev(p),
            device_id_type=MESH,
        )
        copy.wait_send()
        copy.wait_recv()

    pltpu.make_async_copy(choose(src, me), dst.at[me], recv.at[me]).wait()


def push(kind, src_of, dst_of, send, recv, local=False):
    n, me, dev = group(kind)

    @pl.loop(1, n)
    def _(i):
        p = lax.rem(me + i, n)
        pltpu.make_async_remote_copy(
            src_ref=src_of(p),
            dst_ref=dst_of(me),
            send_sem=send.at[p],
            recv_sem=recv.at[me],
            device_id=dev(p),
            device_id_type=MESH,
        ).start()

    if local:
        pltpu.make_async_copy(src_of(me), dst_of(me), recv.at[me]).start()


def settle(kind, src_of, dst_of, send, recv, local=False):
    n, me, dev = group(kind)

    @pl.loop(1, n)
    def _(i):
        p = lax.rem(me + i, n)
        copy = pltpu.make_async_remote_copy(
            src_ref=src_of(p),
            dst_ref=dst_of(p),
            send_sem=send.at[p],
            recv_sem=recv.at[p],
            device_id=dev(p),
            device_id_type=MESH,
        )
        copy.wait_send()
        copy.wait_recv()

    if local:
        pltpu.make_async_copy(src_of(me), dst_of(me), recv.at[me]).wait()


def stage(*moves):
    for move in moves:
        push(*move)
    for move in moves:
        settle(*move)


class Sems:
    def __init__(self, refs):
        self.refs = list(refs)

    def two(self):
        return self.refs.pop(0), self.refs.pop(0)


def position():
    c = lax.axis_index("ctx")
    return c // 8, lax.rem(c // 2, 4), lax.rem(c, 2)


SIZES = {"ctx": NCTX, "tp": 4, "pair": 2, "rows": 8, "z": 4, "x": 4, "core": 2, "ring": 4}


def iota(shape, axis):
    return lax.broadcasted_iota(jnp.int32, shape, axis)


def two_parts(v):
    high = v.astype(BF16)
    return high, (v - high.astype(F32)).astype(BF16)


def exact_dot(v, pattern):
    high, low = two_parts(v)
    return jnp.dot(high, pattern, preferred_element_type=F32) + jnp.dot(
        low, pattern, preferred_element_type=F32
    )


def head_mean(v):
    n = v.shape[1]
    same = lax.div(iota((n, n), 0), HEAD_SIZE) == lax.div(iota((n, n), 1), HEAD_SIZE)
    return exact_dot(v, jnp.where(same, 1.0 / HEAD_SIZE, 0.0).astype(BF16))


def head_scale(v):
    return lax.rsqrt(head_mean(v * v) + EPSILON)


def turned(u, cosine, sine):
    half, n = HEAD_SIZE // 2, 2 * HEAD_SIZE
    first = lax.rem(iota(u.shape, 1), HEAD_SIZE) < half
    other = jnp.where(first, pltpu.roll(u, n - half, 1), pltpu.roll(u, half, 1))
    return u * cosine + other * sine


def crossed(tile):
    return pltpu.roll(tile, HEAD_SIZE, 1)


def left_lanes(tile):
    return iota(tile.shape, 1) < HEAD_SIZE


def spread_gain(pieces, row, per, lanes):
    pattern = (lax.rem(iota((128, lanes), 1), per) == iota((128, lanes), 0)).astype(F32)
    wide = jnp.dot(pieces, pattern.astype(BF16), preferred_element_type=F32)
    r, lane = iota(wide.shape, 0), iota(wide.shape, 1)
    owner = lax.div(lax.rem(lane, NCTX * per), per)
    keep = jnp.logical_and(lax.rem(r, 16) == row, lax.div(r, 16) == owner)
    return jnp.sum(jnp.where(keep, wide, 0.0), axis=0, keepdims=True)


def owner_pieces(vector, per):
    lanes = vector.shape[1]
    shape = (NCTX, lanes)
    owner = lax.div(lax.rem(iota(shape, 1), NCTX * per), per)
    parts = jnp.where(owner == iota(shape, 0), jnp.broadcast_to(vector, shape), 0.0)
    pattern = (lax.rem(iota((lanes, 128), 0), per) == iota((lanes, 128), 1)).astype(F32)
    return exact_dot(parts, pattern.astype(BF16))


def row_scale(rows):
    return lax.rsqrt(jnp.mean(rows * rows, axis=1, keepdims=True) + EPSILON)


def twice(table):
    return jnp.concatenate([table[...], table[...]], axis=0)


def gather_body(
    w, gains, ffn, rows_in, cosine, sine,
    w_all, ffn_pair, hidden, raw, q_src, kv_src, gain_attn, gain_ffn, gain_query, gain_key,
    gains_all, *sem,
):
    z, x, h = position()
    take = Sems(sem)
    greet(["z", "x", "pair"])
    swap = ("pair", lambda p: ffn.at[p], lambda q: ffn_pair.at[q], *take.two(), True)
    first = [
        ("pair", lambda p: w, lambda q: w_all.at[z, x, q], *take.two(), True),
        ("pair", lambda p: gains, lambda q: gains_all.at[z, x, q], *take.two(), True),
    ]
    for move in first:
        push(*move)
    push(*swap)
    for move in first:
        settle(*move)
    stage(
        ("x", lambda p: w_all.at[z, x, :, 0], lambda q: w_all.at[z, q, :, 0], *take.two()),
        ("z", lambda p: w_all.at[z, x, :, 1], lambda q: w_all.at[q, x, :, 1], *take.two()),
        ("x", lambda p: gains_all.at[z, x], lambda q: gains_all.at[z, q], *take.two()),
    )
    stage(
        ("z", lambda p: w_all.at[z, :, :, 0], lambda q: w_all.at[q, :, :, 0], *take.two()),
        ("x", lambda p: w_all.at[:, x, :, 1], lambda q: w_all.at[:, q, :, 1], *take.two()),
        ("z", lambda p: gains_all.at[z], lambda q: gains_all.at[q], *take.two()),
    )
    pieces = gains_all[...].reshape(NCTX * 16, 128)
    gain_attn[...] = spread_gain(pieces, 0, 32, gain_attn.shape[1])
    gain_ffn[...] = spread_gain(pieces, 1, 32, gain_ffn.shape[1])
    gain_query[...] = spread_gain(pieces, 2, 2, 128)
    gain_key[...] = spread_gain(pieces, 3, 2, 128)
    rows = rows_in[...].astype(F32)
    hidden[...] = (rows * row_scale(rows) * gain_attn[...]).astype(BF16)
    weights = w_all[...].reshape(hidden.shape[1], w_all.shape[5])
    raw[...] = jnp.dot(hidden[...], weights, preferred_element_type=F32)
    cos, sin = twice(cosine), twice(sine)
    for k in range(2):
        tile = raw[:, k * 128 : k * 128 + 128]
        tile = turned(tile * head_scale(tile) * gain_query[...], cos, sin) * (HEAD_SIZE**-0.5)
        for a, one in enumerate((tile, crossed(tile))):
            one = jnp.where(left_lanes(one), one, 0.0).astype(BF16)
            for s in range(2):
                q_src[2 * k + s, a * BLOCK : (a + 1) * BLOCK] = one[s * BLOCK : (s + 1) * BLOCK]
    tile = raw[:, 256:384]
    keys = turned(tile * head_scale(tile) * gain_key[...], cos, sin)
    values = raw[:, 384:512]
    for k in range(2):
        key, value = (keys, crossed(values)) if k == 0 else (crossed(keys), values)
        one = jnp.where(left_lanes(key), key, value).astype(BF16)
        for s in range(2):
            part = one[s * BLOCK : (s + 1) * BLOCK]
            kv_src[2 * k + s] = part.reshape(2, BLOCK // 2, 128)
    settle(*swap)


def gather(w, gains, ffn, rows_in, cosine, sine):
    rows, width = rows_in.shape
    vector = jax.ShapeDtypeStruct((1, width), F32)
    short = jax.ShapeDtypeStruct((1, 128), F32)
    return pl.pallas_call(
        gather_body,
        out_shape=[
            jax.ShapeDtypeStruct((4, 4, 2, *w.shape), BF16),
            jax.ShapeDtypeStruct(ffn.shape, BF16),
            jax.ShapeDtypeStruct((rows, width), BF16),
            jax.ShapeDtypeStruct((rows, w.shape[2]), F32),
            jax.ShapeDtypeStruct((PAIRS, 2 * BLOCK, BLOCK), BF16),
            jax.ShapeDtypeStruct((PAIRS, 2, BLOCK // 2, BLOCK), BF16),
            vector,
            vector,
            short,
            short,
        ],
        in_specs=[ANY] * 3 + [VMEM] * 3,
        out_specs=[VMEM, ANY] + [VMEM] * 8,
        scratch_shapes=[pltpu.VMEM((4, 4, 2, *gains.shape), BF16)]
        + sems(["pair"] * 3 + ["x", "z", "x", "z", "x", "z"]),
        compiler_params=pltpu.CompilerParams(
            collective_id=1, has_side_effects=True, vmem_limit_bytes=24 * 2**20
        ),
        name="gather",
    )(w, gains, ffn, rows_in, cosine, sine)


def piece_shape(pick, array):
    return array.shape if pick == "same" else array.shape[1:]


def landing(kind, pick, array):
    return jax.ShapeDtypeStruct((SIZES[kind], *piece_shape(pick, array)), array.dtype)


def sems(kinds):
    return [pltpu.SemaphoreType.DMA((SIZES[k],)) for k in kinds for _ in range(2)]


def places():
    c, t = lax.axis_index("ctx"), lax.axis_index("tp")
    slot, low = c // WORKERS, lax.rem(c, WORKERS)
    to = low + lax.rem(slot, 2) * (WORKERS - 1 - 2 * low)
    return c, t, slot, low, to


def block_of(low, j):
    return j * WORKERS + (low if j % 2 == 0 else WORKERS - 1 - low)


def greet_attention(kinds):
    c, t, slot, low, to = places()
    barrier = pltpu.get_barrier_semaphore()
    total = 0
    others = [p * WORKERS + to for p in range(PAIRS)] + [block_of(low, j) for j in range(SLOTS)]
    for other in others:

        @pl.when(other != c)
        def _():
            pl.semaphore_signal(barrier, inc=1, device_id=(other, t), device_id_type=MESH)

        total = total + jnp.where(other != c, 1, 0)
    for kind in kinds:
        n, me, dev = group(kind)

        @pl.loop(1, n)
        def _(i):
            pl.semaphore_signal(
                barrier, inc=1, device_id=dev(lax.rem(me + i, n)), device_id_type=MESH
            )

        total = total + (n - 1)
    pl.semaphore_wait(barrier, total)


def to_workers(src, dst, send, recv, act):
    c, t, slot, low, to = places()
    for p in range(PAIRS):
        target = p * WORKERS + to
        far = pltpu.make_async_remote_copy(
            src_ref=src.at[p],
            dst_ref=dst.at[slot],
            send_sem=send.at[p],
            recv_sem=recv.at[slot],
            device_id=(target, t),
            device_id_type=MESH,
        )
        near = pltpu.make_async_copy(src.at[p], dst.at[slot], send.at[p])

        @pl.when(target != c)
        def _():
            far.start() if act == "start" else far.wait_send()

        @pl.when(target == c)
        def _():
            near.start() if act == "start" else near.wait()


def from_owners(src, dst, send, recv):
    c, t, slot, low, to = places()
    for j in range(SLOTS):
        owner = block_of(low, j)

        @pl.when(owner != c)
        def _():
            pltpu.make_async_remote_copy(
                src_ref=src.at[j],
                dst_ref=dst.at[j],
                send_sem=send.at[j],
                recv_sem=recv.at[j],
                device_id=(owner, t),
                device_id_type=MESH,
            ).wait_recv()


def to_owner(src, dst, send, recv, j, act):
    c, t, slot, low, to = places()
    owner = block_of(low, j)
    far = pltpu.make_async_remote_copy(
        src_ref=src.at[j],
        dst_ref=dst.at[slot],
        send_sem=send.at[j],
        recv_sem=recv.at[slot],
        device_id=(owner, t),
        device_id_type=MESH,
    )
    near = pltpu.make_async_copy(src.at[j], dst.at[slot], send.at[j])

    @pl.when(owner != c)
    def _():
        far.start() if act == "start" else far.wait_send()

    @pl.when(owner == c)
    def _():
        near.start() if act == "start" else near.wait()


def from_workers(src, dst, send, recv):
    c, t, slot, low, to = places()
    for p in range(PAIRS):
        target = p * WORKERS + to

        @pl.when(target != c)
        def _():
            pltpu.make_async_remote_copy(
                src_ref=src.at[p],
                dst_ref=dst.at[p],
                send_sem=send.at[p],
                recv_sem=recv.at[p],
                device_id=(target, t),
                device_id_type=MESH,
            ).wait_recv()


def last_dims(a, b):
    return lax.dot_general(a, b, (((1,), (1,)), ((), ())), preferred_element_type=F32)


def first_dims(a, b):
    return lax.dot_general(a, b, (((0,), (0,)), ((), ())), preferred_element_type=F32)


def causal_mask(b, i):
    shape = (2 * BLOCK, 2 * BLOCK)
    rows = lax.broadcasted_iota(jnp.int32, shape, 0)
    token = b * BLOCK + jnp.where(rows >= BLOCK, rows - BLOCK, rows)
    key = i * 2 * BLOCK + lax.broadcasted_iota(jnp.int32, shape, 1)
    return token >= key


def forward_body(
    q_src, kv_src, wo, cot, att, q_buf, kv_buf, o_buf, log_buf, wo_all, cot_all,
    acc, den, q_send, q_recv, o_send, o_recv, *sem,
):
    c, t, slot, low, to = places()
    z, x, h = position()
    take = Sems(sem)
    greet_attention(["z", "x", "pair"])
    near = ("z", lambda p: kv_src.at[p], lambda q: kv_buf.at[q, x, h], *take.two(), True)
    out_first = ("pair", lambda p: wo, lambda q: wo_all.at[z, x, q], *take.two(), True)
    push(*near)
    to_workers(q_src, q_buf, q_send, q_recv, "start")
    push(*out_first)
    settle(*near)
    stage(
        ("x", lambda p: kv_buf.at[:, x, h, 0], lambda q: kv_buf.at[:, q, h, 0], *take.two()),
        ("pair", lambda p: kv_buf.at[:, x, h, 1], lambda q: kv_buf.at[:, x, q, 1], *take.two()),
    )
    stage(
        ("pair", lambda p: kv_buf.at[:, :, h, 0], lambda q: kv_buf.at[:, :, q, 0], *take.two()),
        ("x", lambda p: kv_buf.at[:, x, :, 1], lambda q: kv_buf.at[:, q, :, 1], *take.two()),
    )
    settle(*out_first)
    out_second = [
        ("x", lambda p: wo_all.at[z, x, :, 0], lambda q: wo_all.at[z, q, :, 0], *take.two()),
        ("z", lambda p: wo_all.at[z, x, :, 1], lambda q: wo_all.at[q, x, :, 1], *take.two()),
    ]
    out_third = [
        ("z", lambda p: wo_all.at[z, :, :, 0], lambda q: wo_all.at[q, :, :, 0], *take.two()),
        ("x", lambda p: wo_all.at[:, x, :, 1], lambda q: wo_all.at[:, q, :, 1], *take.two()),
    ]
    swap = ("pair", lambda p: cot, lambda q: cot_all.at[q], *take.two(), True)
    for move in out_second:
        push(*move)
    push(*swap)
    to_workers(q_src, q_buf, q_send, q_recv, "wait")
    from_owners(q_src, q_buf, q_send, q_recv)
    lanes = lax.broadcasted_iota(jnp.int32, (2 * BLOCK, BLOCK), 1)
    for j in range(SLOTS):
        b = block_of(low, j)
        acc[...] = jnp.zeros_like(acc)
        den[...] = jnp.zeros_like(den)

        def chunk(i, masked):
            q = q_buf[j]
            kv = kv_buf[i // 4, lax.rem(i, 4)].reshape(2 * BLOCK, BLOCK)
            powered = jnp.exp(last_dims(q, kv))
            if masked:
                powered = jnp.where(causal_mask(b, i), powered, 0.0)
            den[...] += powered[:, :BLOCK] + powered[:, BLOCK:]
            acc[...] += jnp.dot(powered.astype(BF16), kv, preferred_element_type=F32)

        pl.loop(0, b // 2)(lambda i: chunk(i, False))
        chunk(b // 2, True)
        total = jnp.sum(den[...], axis=1, keepdims=True)
        o_buf[j] = jnp.where(lanes >= HEAD_SIZE, acc[...] / total, 0.0).astype(BF16)
        log_buf[j] = jnp.broadcast_to(jnp.log(total), (2 * BLOCK, BLOCK))
        to_owner(o_buf, att, o_send, o_recv, j, "start")
        if j == 1:
            for move in out_second:
                settle(*move)
            for move in out_third:
                push(*move)
    for j in range(SLOTS):
        to_owner(o_buf, att, o_send, o_recv, j, "wait")
    from_workers(o_buf, att, o_send, o_recv)
    for move in out_third:
        settle(*move)
    settle(*swap)


def forward(q_src, kv_src, wo, cot):
    stack = jax.ShapeDtypeStruct((SLOTS, 2 * BLOCK, BLOCK), BF16)
    return pl.pallas_call(
        forward_body,
        out_shape=[
            stack,
            stack,
            jax.ShapeDtypeStruct((4, 4, 2, 2, BLOCK // 2, BLOCK), BF16),
            stack,
            jax.ShapeDtypeStruct((SLOTS, 2 * BLOCK, BLOCK), F32),
            jax.ShapeDtypeStruct((4, 4, 2, *wo.shape), BF16),
            jax.ShapeDtypeStruct((2, *cot.shape), BF16),
        ],
        in_specs=[ANY] * 4,
        out_specs=[ANY] + [VMEM] * 5 + [ANY],
        scratch_shapes=[
            pltpu.VMEM((2 * BLOCK, BLOCK), F32),
            pltpu.VMEM((2 * BLOCK, BLOCK), F32),
        ]
        + [pltpu.SemaphoreType.DMA((SLOTS,))] * 4
        + sems(["z", "pair", "x", "pair", "pair", "x", "x", "z", "z", "x", "pair"]),
        compiler_params=pltpu.CompilerParams(
            collective_id=2, has_side_effects=True, vmem_limit_bytes=24 * 2**20
        ),
        name="attention_forward",
    )(q_src, kv_src, wo, cot)


def backward_body(
    do_src, q_buf, kv_buf, o_buf, log_buf, ffn, dq_all, dkv_all, ffn_all,
    do_buf, dq_buf, dkv_buf, acc, dkv, one_a, one_b, sum_a, sum_b, two_a, two_b, sum_all,
    do_send, do_recv, dq_send, dq_recv, *sem,
):
    c, t, slot, low, to = places()
    z, x, h = position()
    take = Sems(sem)
    greet_attention(["z", "x", "rows"])
    to_workers(do_src, do_buf, do_send, do_recv, "start")
    ffn_sems = take.two()
    begin("rows", "own", ffn, ffn_all, *ffn_sems)
    dkv[...] = jnp.zeros_like(dkv)
    to_workers(do_src, do_buf, do_send, do_recv, "wait")
    from_owners(do_src, do_buf, do_send, do_recv)
    for j in range(SLOTS):
        b = block_of(low, j)
        acc[...] = jnp.zeros_like(acc)
        delta = jnp.sum(do_buf[j].astype(F32) * o_buf[j].astype(F32), axis=1, keepdims=True)

        def chunk(i, masked):
            q, do = q_buf[j], do_buf[j]
            kv = kv_buf[i // 4, lax.rem(i, 4)].reshape(2 * BLOCK, BLOCK)
            logs = log_buf[j]
            scores = last_dims(q, kv)
            probs = jnp.exp(scores - jnp.concatenate([logs, logs], axis=1))
            if masked:
                probs = jnp.where(causal_mask(b, i), probs, 0.0)
            grads = (probs * (last_dims(do, kv) - delta)).astype(BF16)
            acc[...] += jnp.dot(grads, kv, preferred_element_type=F32)
            update = first_dims(grads, q) + first_dims(probs.astype(BF16), do)
            dkv[i // 4, lax.rem(i, 4)] += update.reshape(2, 2, BLOCK // 2, BLOCK)

        pl.loop(0, b // 2)(lambda i: chunk(i, False))
        chunk(b // 2, True)
        dq_buf[j] = (acc[...] * (HEAD_SIZE**-0.5)).astype(BF16)
        to_owner(dq_buf, dq_all, dq_send, dq_recv, j, "start")
    dkv_buf[...] = dkv[...].astype(BF16)
    stage(
        ("x", lambda p: dkv_buf.at[:, p, :, 0], lambda q: one_a.at[q], *take.two(), True),
        ("pair", lambda p: dkv_buf.at[:, :, p, 1], lambda q: one_b.at[q], *take.two(), True),
    )
    sum_a[...] = summed(one_a).astype(BF16)
    sum_b[...] = summed(one_b).astype(BF16)
    stage(
        ("pair", lambda p: sum_a.at[:, p], lambda q: two_a.at[q], *take.two(), True),
        ("x", lambda p: sum_b.at[:, p], lambda q: two_b.at[q], *take.two(), True),
    )
    sum_all[:, 0] = summed(two_a).astype(BF16)
    sum_all[:, 1] = summed(two_b).astype(BF16)
    stage(("z", lambda p: sum_all.at[p], lambda q: dkv_all.at[q], *take.two(), True))
    for j in range(SLOTS):
        to_owner(dq_buf, dq_all, dq_send, dq_recv, j, "wait")
    from_workers(dq_buf, dq_all, dq_send, dq_recv)
    finish("rows", "own", ffn, ffn_all, *ffn_sems)


def backward(do_src, q_buf, kv_buf, o_buf, log_buf, ffn):
    half = BLOCK // 2
    return pl.pallas_call(
        backward_body,
        out_shape=[
            jax.ShapeDtypeStruct((SLOTS, 2 * BLOCK, BLOCK), BF16),
            jax.ShapeDtypeStruct((PAIRS, 2, half, BLOCK), BF16),
            landing("rows", "own", ffn),
        ],
        in_specs=[ANY] + [VMEM] * 4 + [ANY],
        out_specs=[ANY] * 3,
        scratch_shapes=[
            pltpu.VMEM((SLOTS, 2 * BLOCK, BLOCK), BF16),
            pltpu.VMEM((SLOTS, 2 * BLOCK, BLOCK), BF16),
            pltpu.VMEM((4, 4, 2, 2, half, BLOCK), BF16),
            pltpu.VMEM((2 * BLOCK, BLOCK), F32),
            pltpu.VMEM((4, 4, 2, 2, half, BLOCK), F32),
            pltpu.VMEM((4, 4, 2, half, BLOCK), BF16),
            pltpu.VMEM((2, 4, 4, half, BLOCK), BF16),
            pltpu.VMEM((4, 2, half, BLOCK), BF16),
            pltpu.VMEM((4, 4, half, BLOCK), BF16),
            pltpu.VMEM((2, 4, half, BLOCK), BF16),
            pltpu.VMEM((4, 4, half, BLOCK), BF16),
            pltpu.VMEM((4, 2, half, BLOCK), BF16),
        ]
        + [pltpu.SemaphoreType.DMA((SLOTS,))] * 4
        + sems(["rows", "x", "pair", "pair", "x", "z"]),
        compiler_params=pltpu.CompilerParams(
            collective_id=6, has_side_effects=True, vmem_limit_bytes=24 * 2**20
        ),
        name="attention_backward",
    )(do_src, q_buf, kv_buf, o_buf, log_buf, ffn)


def row_back(grads, normed, scale, gain):
    scaled = grads * gain
    return scale * (scaled - normed * jnp.mean(scaled * normed, axis=1, keepdims=True))


def summed(ref):
    total = ref[0].astype(F32)
    for k in range(1, ref.shape[0]):
        total += ref[k].astype(F32)
    return total


UNITS = 640


def feed_body(
    att, wo, rows_in, gain, w, cot,
    attended, do_src, residual, grad_residual, gain_part, grad_all, grads, ffn_part,
    parts, landed, hidden, hidden_all, grad_units, units, grad_in, back, halved, chip, ringed, grad_bf, *sem,
):
    take = Sems(sem)
    t = lax.axis_index("tp")
    core, h = lax.rem(t, 2), lax.rem(lax.axis_index("ctx"), 2)
    own = residual.shape[0]
    greet(["tp", "ring"])
    for k in range(2):
        for s in range(2):
            first = crossed(att[2 * k + s, :BLOCK].astype(F32))
            second = att[2 * k + s, BLOCK:].astype(F32)
            one = jnp.where(left_lanes(first), first, second).astype(BF16)
            attended[s * BLOCK : (s + 1) * BLOCK, k * 128 : (k + 1) * 128] = one
    out_full = wo[...].reshape(wo.size // wo.shape[5], wo.shape[5])
    parts[...] = last_dims(attended[...], out_full).astype(BF16).reshape(parts.shape)
    share = ("tp", lambda p: parts.at[p], lambda q: landed.at[q], *take.two(), True)
    push(*share)

    @pl.loop(0, 4)
    def _(m):
        at = pl.ds(pl.multiple_of(m * 128, 128), 128)
        grad_units[at] = jnp.dot(cot[at], w[:, 2 * UNITS :], preferred_element_type=F32)

    settle(*share)
    inputs = rows_in[pl.ds(pl.multiple_of(t * own, own), own)].astype(F32)
    rows = inputs + summed(landed)
    residual[...] = rows
    scale = row_scale(rows)
    hidden[...] = (rows * scale * gain[...]).astype(BF16)
    stage(("ring", lambda p: hidden, lambda q: hidden_all.at[q, core], *take.two(), True))
    stage(("core", lambda p: hidden_all.at[:, core], lambda q: hidden_all.at[:, q], *take.two()))

    @pl.loop(0, 2)
    def _(m):
        at = pl.ds(pl.multiple_of(m * 256, 256), 256)
        some = hidden_all[pl.ds(2 * m, 2)].reshape(256, hidden.shape[1])
        gate = jnp.dot(some, w[:, :UNITS], preferred_element_type=F32)
        up = jnp.dot(some, w[:, UNITS : 2 * UNITS], preferred_element_type=F32)
        sigmoid = jax.nn.sigmoid(gate)
        activated = gate * sigmoid
        units[at] = (activated * up).astype(BF16)
        grad = grad_units[at]
        grad_in[at, :UNITS] = (grad * up * sigmoid * (1.0 + gate * (1.0 - sigmoid))).astype(BF16)
        grad_in[at, UNITS:] = (grad * activated).astype(BF16)
        step = last_dims(grad_in[at], w[:, : 2 * UNITS]).astype(BF16)
        back[pl.ds(2 * m, 2)] = step.reshape(2, *back.shape[1:])

    both = ("core", lambda p: back.at[:, p], lambda q: halved.at[q], *take.two(), True)
    push(*both)

    @pl.loop(0, 2)
    def _(m):
        at = pl.ds(pl.multiple_of(m * 256, 256), 256)
        step = last_dims(units[at], w[:, 2 * UNITS :]).astype(BF16)
        ffn_part[pl.ds(4 * m, 4)] = step.reshape(4, *ffn_part.shape[1:])

    settle(*both)
    chip[...] = summed(halved).astype(BF16)
    ring = ("ring", lambda p: chip.at[p], lambda q: ringed.at[q], *take.two(), True)
    push(*ring)

    @pl.loop(0, 4)
    def _(m):
        at = pl.ds(pl.multiple_of(m * 256, 256), 256)
        some = hidden_all[:, :, :, at].reshape(512, 256)
        grads[at, : 2 * UNITS] = first_dims(some, grad_in[...]).astype(BF16)

    settle(*ring)
    total = summed(ringed)
    rows = residual[...]
    scale = row_scale(rows)
    normed = rows * scale
    cot_own = cot[pl.ds(pl.multiple_of((h * 4 + t) * own, own), own)].astype(F32)
    result = cot_own + row_back(total, normed, scale, gain[...])
    grad_bf[...] = result.astype(BF16)
    last = ("tp", lambda p: grad_bf, lambda q: grad_all.at[q], *take.two(), True)
    push(*last)
    grad_residual[...] = result
    gain_part[...] = jnp.sum(total * normed, axis=0, keepdims=True)

    @pl.loop(0, 4)
    def _(m):
        at = pl.ds(pl.multiple_of(m * 256, 256), 256)
        grads[at, 2 * UNITS :] = first_dims(cot[:, at], units[...]).astype(BF16)

    settle(*last)
    grad = jnp.dot(grad_all[...].reshape(4 * own, gain.shape[1]), out_full, preferred_element_type=F32)
    for k in range(2):
        for s in range(2):
            tile = grad[s * BLOCK : (s + 1) * BLOCK, k * 128 : (k + 1) * 128]
            for a, one in enumerate((crossed(tile), tile)):
                one = jnp.where(left_lanes(one), 0.0, one).astype(BF16)
                do_src[2 * k + s, a * BLOCK : (a + 1) * BLOCK] = one


def feed_step(att, wo, rows_in, gain, w, cot):
    rows, width = rows_in.shape
    own = rows // 4
    wide = cot.shape[0]
    return pl.pallas_call(
        feed_body,
        out_shape=[
            jax.ShapeDtypeStruct((rows, wo.shape[5]), BF16),
            jax.ShapeDtypeStruct(att.shape, BF16),
            jax.ShapeDtypeStruct((own, width), F32),
            jax.ShapeDtypeStruct((own, width), F32),
            jax.ShapeDtypeStruct((1, width), F32),
            jax.ShapeDtypeStruct((4, own, width), BF16),
            jax.ShapeDtypeStruct(w.shape, BF16),
            jax.ShapeDtypeStruct((8, own, width), BF16),
        ],
        in_specs=[VMEM] * 6,
        out_specs=[VMEM] * 8,
        scratch_shapes=[
            pltpu.VMEM((4, own, width), BF16),
            pltpu.VMEM((4, own, width), BF16),
            pltpu.VMEM((own, width), BF16),
            pltpu.VMEM((4, 2, own, width), BF16),
            pltpu.VMEM((wide, UNITS), F32),
            pltpu.VMEM((wide, UNITS), BF16),
            pltpu.VMEM((wide, 2 * UNITS), BF16),
            pltpu.VMEM((4, 2, own, width), BF16),
            pltpu.VMEM((2, 4, own, width), BF16),
            pltpu.VMEM((4, own, width), BF16),
            pltpu.VMEM((4, own, width), BF16),
            pltpu.VMEM((own, width), BF16),
        ]
        + sems(["tp", "ring", "core", "core", "ring", "tp"]),
        compiler_params=pltpu.CompilerParams(
            collective_id=3, has_side_effects=True, vmem_limit_bytes=40 * 2**20
        ),
        name="feed_forward",
    )(att, wo, rows_in, gain, w, cot)


def last_body(
    dq, dkv, raw, w_all, cosine, sine, gain_query, gain_key,
    hidden, res_all, attended, ffn, ffn_parts, ffn_gain, residual, grad_residual, rows_in, gain,
    qkv_grad, ffn_all, output_all, input_all, gain_tp,
    parts, grad_in, gains, output, qkv, landed, input_bf, one_a, one_b, one_g, sum_a, sum_b, sum_g, two_a, two_b, two_g,
    part_a, part_b, part_g, three_a, three_b, three_g, gain_sum, *sem,
):
    take = Sems(sem)
    greet(["z", "x", "pair", "tp"])
    t = lax.axis_index("tp")
    own, width = residual.shape
    cos, sin = twice(cosine), -twice(sine)

    def head_back(u, tile, gain_row):
        turn = turned(u, cos, sin)
        scale = head_scale(tile)
        hat = tile * scale
        scaled = turn * gain_row
        back = scale * (scaled - hat * head_mean(scaled * hat))
        return back.astype(BF16), jnp.sum(turn * hat, axis=0, keepdims=True)

    def both(first, second):
        return jnp.concatenate([first.astype(F32), second.astype(F32)], axis=0)

    query_gain = jnp.zeros((1, 128), F32)
    for k in range(2):
        first = both(dq[2 * k, :BLOCK], dq[2 * k + 1, :BLOCK])
        second = crossed(both(dq[2 * k, BLOCK:], dq[2 * k + 1, BLOCK:]))
        lanes = slice(k * 128, (k + 1) * 128)
        back, part = head_back(
            jnp.where(left_lanes(first), first, second), raw[:, lanes], gain_query[...]
        )
        grad_in[:, lanes] = back
        query_gain = query_gain + part
    first, second = [
        both(dkv[2 * k].reshape(BLOCK, 128), dkv[2 * k + 1].reshape(BLOCK, 128)) for k in range(2)
    ]
    left = left_lanes(first)
    back, key_gain = head_back(
        jnp.where(left, first, crossed(second)), raw[:, 256:384], gain_key[...]
    )
    grad_in[:, 256:384] = back
    grad_in[:, 384:] = jnp.where(left, crossed(first), second).astype(BF16)
    attn_gain = jnp.zeros((1, width), F32)
    weights = w_all[...].reshape(width, grad_in.shape[1])
    for q in range(4):
        at = slice(q * own, (q + 1) * own)
        back = last_dims(grad_in[at], weights)
        parts[q] = back.astype(BF16)
        rows = rows_in[at].astype(F32)
        attn_gain = attn_gain + jnp.sum(back * (rows * row_scale(rows)), axis=0, keepdims=True)
    rows_sums, rows_output, rows_input, gains_out = [take.two() for _ in range(4)]
    begin("tp", "own", parts, landed, *rows_sums)

    @pl.loop(0, 4)
    def _(m):
        at = pl.ds(pl.multiple_of(m * 256, 256), 256)
        wide = grad_in.shape[1]
        res_rows = res_all[:, :, at].reshape(4 * own, 256)
        step = first_dims(hidden[:, at], grad_in[...]).astype(BF16)
        qkv[m, :, :, :, :, :wide] = step.reshape(4, 2, 2, 16, wide)
        step = first_dims(res_rows, attended[...]).astype(BF16)
        qkv[m, :, :, :, :, wide:] = step.reshape(4, 2, 2, 16, attended.shape[1])

    pieces = jnp.zeros((NCTX, 8, 128), F32)
    vectors = ((attn_gain, 32), (ffn_gain[...], 32), (query_gain, 2), (key_gain, 2))
    for row, (vector, per) in enumerate(vectors):
        piece = jnp.broadcast_to(owner_pieces(vector, per)[:, None, :], pieces.shape)
        pieces = jnp.where(iota(pieces.shape, 1) == row, piece, pieces)
    gains[...] = pieces.reshape(gains.shape)
    first = [
        ("x", lambda p: qkv.at[:, p, :, 0], lambda q: one_a.at[q], *take.two(), True),
        ("z", lambda p: qkv.at[p, :, :, 1], lambda q: one_b.at[q], *take.two(), True),
        ("x", lambda p: gains.at[:, p], lambda q: one_g.at[q], *take.two(), True),
    ]
    for move in first:
        push(*move)
    output[...] = (residual[...] + summed(ffn_parts)).astype(BF16)
    rows = rows_in[pl.ds(pl.multiple_of(t * own, own), own)].astype(F32)
    scale = row_scale(rows)
    normed = rows * scale
    finish("tp", "own", parts, landed, *rows_sums)
    result = grad_residual[...] + row_back(summed(landed), normed, scale, gain[...])
    input_bf[...] = result.astype(BF16)
    begin("tp", "same", input_bf, input_all, *rows_input)
    begin("tp", "same", output, output_all, *rows_output)
    swap = ("pair", lambda p: ffn.at[p], lambda q: ffn_all.at[q], *take.two(), True)
    push(*swap)
    for move in first:
        settle(*move)
    sum_a[...] = summed(one_a).astype(BF16)
    sum_b[...] = summed(one_b).astype(BF16)
    sum_g[...] = summed(one_g)
    stage(
        ("z", lambda p: sum_a.at[p], lambda q: two_a.at[q], *take.two(), True),
        ("x", lambda p: sum_b.at[p], lambda q: two_b.at[q], *take.two(), True),
        ("z", lambda p: sum_g.at[p], lambda q: two_g.at[q], *take.two(), True),
    )
    part_a[...] = summed(two_a).astype(BF16)
    part_b[...] = summed(two_b).astype(BF16)
    part_g[...] = summed(two_g)
    stage(
        ("pair", lambda p: part_a.at[p], lambda q: three_a.at[q], *take.two(), True),
        ("pair", lambda p: part_b.at[p], lambda q: three_b.at[q], *take.two(), True),
        ("pair", lambda p: part_g.at[p], lambda q: three_g.at[q], *take.two(), True),
    )
    gain_sum[...] = summed(three_g)
    begin("tp", "same", gain_sum, gain_tp, *gains_out)
    qkv_grad[0] = summed(three_a)
    qkv_grad[1] = summed(three_b)
    finish("tp", "same", output, output_all, *rows_output)
    finish("tp", "same", input_bf, input_all, *rows_input)
    finish("tp", "same", gain_sum, gain_tp, *gains_out)
    settle(*swap)


def last_step(
    dq, dkv, raw, w_all, cosine, sine, gain_query, gain_key,
    hidden, res_all, attended, ffn, ffn_parts, ffn_gain, residual, grad_residual, rows_in, gain,
):
    own, width = residual.shape
    cols = w_all.shape[5]
    piece, small = (16, cols + attended.shape[1]), (8, 128)

    def scratch(*shape):
        return [pltpu.VMEM((*shape, *piece), BF16)] * 2 + [pltpu.VMEM((*shape, *small), F32)]

    return pl.pallas_call(
        last_body,
        out_shape=[
            jax.ShapeDtypeStruct((2, *piece), F32),
            jax.ShapeDtypeStruct(ffn.shape, BF16),
            jax.ShapeDtypeStruct((4, own, width), BF16),
            jax.ShapeDtypeStruct((4, own, width), BF16),
            jax.ShapeDtypeStruct((4, *small), F32),
        ],
        in_specs=[VMEM] * 11 + [ANY] + [VMEM] * 6,
        out_specs=[VMEM] + [ANY] * 4,
        scratch_shapes=[
            pltpu.VMEM((4, own, width), BF16),
            pltpu.VMEM((4 * own, cols), BF16),
            pltpu.VMEM((4, 4, 2, *small), F32),
            pltpu.VMEM((own, width), BF16),
            pltpu.VMEM((4, 4, 2, 2, *piece), BF16),
        ]
        + [pltpu.VMEM((4, own, width), BF16), pltpu.VMEM((own, width), BF16)]
        + scratch(4, 4, 2)
        + scratch(4, 2)
        + scratch(4, 2)
        + scratch(2)
        + scratch(2)
        + [pltpu.VMEM(small, F32)]
        + sems(["tp"] * 4 + ["x", "z", "x", "pair", "z", "x", "z"] + ["pair"] * 3),
        compiler_params=pltpu.CompilerParams(
            collective_id=8, has_side_effects=True, vmem_limit_bytes=24 * 2**20
        ),
        name="last_step",
    )(
        dq, dkv, raw, w_all, cosine, sine, gain_query, gain_key,
        hidden, res_all, attended, ffn, ffn_parts, ffn_gain, residual, grad_residual, rows_in, gain,
    )


def rope_tables(tokens, offset):
    half = HEAD_SIZE // 2
    inverse = ROPE_BASE ** (-(jnp.arange(half, dtype=F32) * 2.0 / HEAD_SIZE))
    steps = (offset + jnp.arange(tokens, dtype=jnp.int32)).astype(F32)
    angles = steps[:, None] * jnp.tile(inverse, 4)[None, :]
    signs = jnp.where(jnp.arange(4 * half) % HEAD_SIZE < half, -1.0, 1.0)
    return jnp.cos(angles), jnp.sin(angles) * signs[None, :]


def halves(*weights):
    rows, cols = weights[0].shape
    w = jnp.stack(weights).reshape(len(weights), rows, 2, cols // 2)
    w = jnp.pad(w, ((0, 0), (0, 0), (0, 0), (0, UNITS - cols // 2)))
    return w.transpose(2, 1, 0, 3).reshape(2, rows, len(weights) * UNITS)


def local(
    block_input, cotangent, w_query, key_weight, w_value, w_out, w_gate, w_up, w_down,
    norm_gains, head_gains,
):
    seqs, tokens, width = block_input.shape
    rows = seqs * tokens
    unit_half = w_gate.shape[1] // 2
    rows_in = block_input.reshape(rows, width)
    cot_rows = cotangent.reshape(rows, width)
    cosine, sine = rope_tables(tokens, lax.axis_index("ctx") * tokens)
    weight_rows = jnp.concatenate([w_query, key_weight, w_value], axis=1)
    gains = jnp.pad(norm_gains, ((0, 14), (0, 96))) + jnp.pad(head_gains, ((2, 12), (0, 126)))
    (
        weights_all, ffn_pair, hidden_attn, raw, q_src, kv_src,
        gain_attn, gain_ffn, gain_query, gain_key,
    ) = gather(
        weight_rows.reshape(2, 16, weight_rows.shape[1]),
        gains,
        halves(w_gate, w_up, w_down),
        rows_in,
        cosine,
        sine,
    )
    planes = [[2 * g + h for g in range(NCTX // 2)] for h in range(2)]
    ffn_full = lax.all_gather(
        ffn_pair.reshape(2 * 32, 3 * UNITS), "ctx", axis_index_groups=planes, tiled=True
    )
    att, q_buf, kv_buf, o_buf, log_buf, wo_all, cot_all = forward(
        q_src, kv_src, w_out.reshape(2, 16, 256), cot_rows
    )
    (
        attended, do_src, residual, grad_residual, ffn_gain, residual_all, ffn_grads, ffn_part,
    ) = feed_step(att, wo_all, rows_in, gain_ffn, ffn_full, cot_all.reshape(2 * rows, width))
    grads_own = lax.psum_scatter(ffn_grads, "ctx", axis_index_groups=planes, tiled=True)
    dq_all, dkv_all, ffn_parts = backward(do_src, q_buf, kv_buf, o_buf, log_buf, ffn_part)
    qkv_grad, pair_grads, output_all, input_all, gain_tp = last_step(
        dq_all, dkv_all, raw, weights_all, cosine, sine, gain_query, gain_key,
        hidden_attn, residual_all, attended, grads_own.reshape(2, 32, -1), ffn_parts, ffn_gain,
        residual, grad_residual, rows_in, gain_attn,
    )
    pair_grads = pair_grads.astype(F32)
    gain_sum = jnp.sum(gain_tp, axis=0)
    qkv_grad = qkv_grad.reshape(32, 768)

    def joined(first):
        last = first + unit_half
        return jnp.concatenate([pair_grads[0, :, first:last], pair_grads[1, :, first:last]], axis=1)

    gate_grad, up_grad, down_grad = joined(0), joined(UNITS), joined(2 * UNITS)
    return (
        output_all.reshape(seqs, tokens, width),
        input_all.astype(F32).reshape(seqs, tokens, width),
        qkv_grad[:, :256],
        qkv_grad[:, 256:384],
        qkv_grad[:, 384:512],
        qkv_grad[:, 512:],
        gate_grad,
        up_grad,
        down_grad,
        gain_sum[0:2, :32],
        gain_sum[2:4, :2],
    )


def solution(mesh):
    tokens, weights = P(None, "ctx", None), P("ctx", "tp")
    return jax.shard_map(
        local,
        mesh=mesh,
        in_specs=(tokens,) * 2 + (weights,) * 7 + (P(None, "ctx"),) * 2,
        out_specs=(tokens,) * 2 + (weights,) * 7 + (P(None, "ctx"),) * 2,
        check_vma=False,
    )
```

```python
import functools
import types

import jax
import jax.numpy as jnp
from jax import lax
from jax.experimental import pallas as pl
from jax.experimental.pallas import tpu as pltpu
from jax.sharding import PartitionSpec as P

HEAD_SIZE = 64
EPSILON = 1e-06
ROPE_BASE = 1000000.0
MESH = pl.DeviceIdType.MESH
F32 = jnp.float32
BF16 = jnp.bfloat16
ANY = pl.BlockSpec(memory_space=pl.ANY)
VMEM = pl.BlockSpec(memory_space=pltpu.VMEM)
NCTX = 32
PAIRS = 4
WORKERS = 8
SLOTS = 4
BLOCK = 128


def group(kind):
    c, t = lax.axis_index("ctx"), lax.axis_index("tp")
    h = lax.rem(c, 2)
    if kind == "ctx":
        return NCTX, c, lambda p: (p, t)
    if kind == "tp":
        return 4, t, lambda p: (c, p)
    if kind == "pair":
        return 2, h, lambda p: (c - h + p, t)
    z, x, core = c // 8, lax.rem(c // 2, 4), lax.rem(t, 2)
    if kind == "z":
        return 4, z, lambda p: (c + (p - z) * 8, t)
    if kind == "x":
        return 4, x, lambda p: (c + (p - x) * 2, t)
    if kind == "core":
        return 2, core, lambda p: (c, t - core + p)
    if kind == "ring":
        return 4, h * 2 + t // 2, lambda p: (c - h + p // 2, lax.rem(p, 2) * 2 + core)
    return 8, h * 4 + t, lambda p: (c - h + p // 4, lax.rem(p, 4))


def push(kind, src_of, dst_of, send, recv, local=False):
    n, me, dev = group(kind)

    @pl.loop(1, n)
    def _(i):
        p = lax.rem(me + i, n)
        pltpu.make_async_remote_copy(
            src_ref=src_of(p),
            dst_ref=dst_of(me),
            send_sem=send.at[p],
            recv_sem=recv.at[me],
            device_id=dev(p),
            device_id_type=MESH,
        ).start()

    if local:
        pltpu.make_async_copy(src_of(me), dst_of(me), recv.at[me]).start()


def settle(kind, src_of, dst_of, send, recv, local=False):
    n, me, dev = group(kind)

    @pl.loop(1, n)
    def _(i):
        p = lax.rem(me + i, n)
        copy = pltpu.make_async_remote_copy(
            src_ref=src_of(p),
            dst_ref=dst_of(p),
            send_sem=send.at[p],
            recv_sem=recv.at[p],
            device_id=dev(p),
            device_id_type=MESH,
        )
        copy.wait_send()
        copy.wait_recv()

    if local:
        pltpu.make_async_copy(src_of(me), dst_of(me), recv.at[me]).wait()


def stage(*moves):
    for move in moves:
        push(*move)
    for move in moves:
        settle(*move)


class Sems:
    def __init__(self, ref):
        self.ref, self.used = ref, 0

    def two(self):
        self.used += 1
        return self.ref.at[self.used - 1, 0], self.ref.at[self.used - 1, 1]


def position():
    c = lax.axis_index("ctx")
    return c // 8, lax.rem(c // 2, 4), lax.rem(c, 2)


def iota(shape, axis):
    return lax.broadcasted_iota(jnp.int32, shape, axis)


def two_parts(v):
    high = v.astype(BF16)
    return high, (v - high.astype(F32)).astype(BF16)


def exact_dot(v, pattern):
    high, low = two_parts(v)
    return jnp.dot(high, pattern, preferred_element_type=F32) + jnp.dot(
        low, pattern, preferred_element_type=F32
    )


def head_mean(v):
    n = v.shape[1]
    same = lax.div(iota((n, n), 0), HEAD_SIZE) == lax.div(iota((n, n), 1), HEAD_SIZE)
    return exact_dot(v, jnp.where(same, 1.0 / HEAD_SIZE, 0.0).astype(BF16))


def head_scale(v):
    return lax.rsqrt(head_mean(v * v) + EPSILON)


def turned(u, cosine, sine):
    half, n = HEAD_SIZE // 2, 2 * HEAD_SIZE
    first = lax.rem(iota(u.shape, 1), HEAD_SIZE) < half
    other = jnp.where(first, pltpu.roll(u, n - half, 1), pltpu.roll(u, half, 1))
    return u * cosine + other * sine


def crossed(tile):
    return pltpu.roll(tile, HEAD_SIZE, 1)


def left_lanes(tile):
    return iota(tile.shape, 1) < HEAD_SIZE


def spread_gain(pieces, row, per, lanes):
    pattern = (lax.rem(iota((128, lanes), 1), per) == iota((128, lanes), 0)).astype(F32)
    wide = jnp.dot(pieces, pattern.astype(BF16), preferred_element_type=F32)
    r, lane = iota(wide.shape, 0), iota(wide.shape, 1)
    owner = lax.div(lax.rem(lane, NCTX * per), per)
    keep = jnp.logical_and(lax.rem(r, 16) == row, lax.div(r, 16) == owner)
    return jnp.sum(jnp.where(keep, wide, 0.0), axis=0, keepdims=True)


def owner_pieces(vector, per):
    lanes = vector.shape[1]
    shape = (NCTX, lanes)
    owner = lax.div(lax.rem(iota(shape, 1), NCTX * per), per)
    parts = jnp.where(owner == iota(shape, 0), jnp.broadcast_to(vector, shape), 0.0)
    pattern = (lax.rem(iota((lanes, 128), 0), per) == iota((lanes, 128), 1)).astype(F32)
    return exact_dot(parts, pattern.astype(BF16))


def row_scale(rows):
    return lax.rsqrt(jnp.mean(rows * rows, axis=1, keepdims=True) + EPSILON)


def twice(table):
    return jnp.concatenate([table[...], table[...]], axis=0)


def places():
    c, t = lax.axis_index("ctx"), lax.axis_index("tp")
    slot, low = c // WORKERS, lax.rem(c, WORKERS)
    to = low + lax.rem(slot, 2) * (WORKERS - 1 - 2 * low)
    return c, t, slot, low, to


def block_of(low, j):
    return j * WORKERS + (low if j % 2 == 0 else WORKERS - 1 - low)


def greet_attention(kinds):
    c, t, slot, low, to = places()
    barrier = pltpu.get_barrier_semaphore()
    total = 0
    others = [p * WORKERS + to for p in range(PAIRS)] + [block_of(low, j) for j in range(SLOTS)]
    for other in others:

        @pl.when(other != c)
        def _():
            pl.semaphore_signal(barrier, inc=1, device_id=(other, t), device_id_type=MESH)

        total = total + jnp.where(other != c, 1, 0)
    for kind in kinds:
        n, me, dev = group(kind)

        @pl.loop(1, n)
        def _(i):
            pl.semaphore_signal(
                barrier, inc=1, device_id=dev(lax.rem(me + i, n)), device_id_type=MESH
            )

        total = total + (n - 1)
    pl.semaphore_wait(barrier, total)


def to_workers(src, dst, send, recv, act):
    c, t, slot, low, to = places()
    for p in range(PAIRS):
        target = p * WORKERS + to
        far = pltpu.make_async_remote_copy(
            src_ref=src.at[p],
            dst_ref=dst.at[slot],
            send_sem=send.at[p],
            recv_sem=recv.at[slot],
            device_id=(target, t),
            device_id_type=MESH,
        )
        near = pltpu.make_async_copy(src.at[p], dst.at[slot], send.at[p])

        @pl.when(target != c)
        def _():
            far.start() if act == "start" else far.wait_send()

        @pl.when(target == c)
        def _():
            near.start() if act == "start" else near.wait()


def from_owners(src, dst, send, recv):
    c, t, slot, low, to = places()
    for j in range(SLOTS):
        owner = block_of(low, j)

        @pl.when(owner != c)
        def _():
            pltpu.make_async_remote_copy(
                src_ref=src.at[j],
                dst_ref=dst.at[j],
                send_sem=send.at[j],
                recv_sem=recv.at[j],
                device_id=(owner, t),
                device_id_type=MESH,
            ).wait_recv()


def to_owner(src, dst, send, recv, j, act):
    c, t, slot, low, to = places()
    owner = block_of(low, j)
    far = pltpu.make_async_remote_copy(
        src_ref=src.at[j],
        dst_ref=dst.at[slot],
        send_sem=send.at[j],
        recv_sem=recv.at[slot],
        device_id=(owner, t),
        device_id_type=MESH,
    )
    near = pltpu.make_async_copy(src.at[j], dst.at[slot], send.at[j])

    @pl.when(owner != c)
    def _():
        far.start() if act == "start" else far.wait_send()

    @pl.when(owner == c)
    def _():
        near.start() if act == "start" else near.wait()


def from_workers(src, dst, send, recv):
    c, t, slot, low, to = places()
    for p in range(PAIRS):
        target = p * WORKERS + to

        @pl.when(target != c)
        def _():
            pltpu.make_async_remote_copy(
                src_ref=src.at[p],
                dst_ref=dst.at[p],
                send_sem=send.at[p],
                recv_sem=recv.at[p],
                device_id=(target, t),
                device_id_type=MESH,
            ).wait_recv()


def last_dims(a, b):
    return lax.dot_general(a, b, (((1,), (1,)), ((), ())), preferred_element_type=F32)


def first_dims(a, b):
    return lax.dot_general(a, b, (((0,), (0,)), ((), ())), preferred_element_type=F32)


def causal_mask(b, i):
    shape = (2 * BLOCK, 2 * BLOCK)
    rows = lax.broadcasted_iota(jnp.int32, shape, 0)
    token = b * BLOCK + jnp.where(rows >= BLOCK, rows - BLOCK, rows)
    key = i * 2 * BLOCK + lax.broadcasted_iota(jnp.int32, shape, 1)
    return token >= key


def row_back(grads, normed, scale, gain):
    scaled = grads * gain
    return scale * (scaled - normed * jnp.mean(scaled * normed, axis=1, keepdims=True))


def summed(ref):
    total = ref[0].astype(F32)
    for k in range(1, ref.shape[0]):
        total += ref[k].astype(F32)
    return total


UNITS = 640
INPUTS = ("weights", "gains", "ffn", "wo", "cot", "rows_in", "cosine", "sine")
OUTPUTS = ("qkv_grad", "ffn_all", "output_all", "input_all", "gain_tp")
MOVES = 48


def scratch_arrays(rows, width, qkv_cols, out_cols):
    own, half = rows // 4, BLOCK // 2
    stack = (SLOTS, 2 * BLOCK, BLOCK)
    grid, piece = (4, 4, 2, 2), (16, qkv_cols + out_cols)
    units = (16, 3 * UNITS)
    return dict(
        w_all=((*grid, 16, qkv_cols), BF16),
        gains_all=((4, 4, 2, 16, 128), BF16),
        w_ffn=((*grid, *units), BF16),
        wo_all=((*grid, 16, out_cols), BF16),
        cot_all=((2, rows, width), BF16),
        hidden=((rows, width), BF16),
        raw=((rows, qkv_cols), F32),
        q_src=(stack, BF16),
        kv_src=((PAIRS, 2, half, BLOCK), BF16),
        gain_attn=((1, width), F32),
        gain_ffn=((1, width), F32),
        gain_query=((1, 128), F32),
        gain_key=((1, 128), F32),
        q_buf=(stack, BF16),
        kv_buf=((*grid, half, BLOCK), BF16),
        o_buf=(stack, BF16),
        log_buf=(stack, F32),
        att=(stack, BF16),
        acc=((2 * BLOCK, BLOCK), F32),
        den=((2 * BLOCK, BLOCK), F32),
        attended=((rows, out_cols), BF16),
        parts=((4, own, width), BF16),
        landed=((4, own, width), BF16),
        residual=((own, width), F32),
        hidden_own=((own, width), BF16),
        hidden_all=((4, 2, own, width), BF16),
        grad_units=((2 * rows, UNITS), F32),
        units=((2 * rows, UNITS), BF16),
        units_in=((2 * rows, 2 * UNITS), BF16),
        back=((4, 2, own, width), BF16),
        halved=((2, 4, own, width), BF16),
        chip=((4, own, width), BF16),
        ringed=((4, own, width), BF16),
        grad_bf=((own, width), BF16),
        grad_all=((4, own, width), BF16),
        grad_residual=((own, width), F32),
        ffn_gain=((1, width), F32),
        grads=((*grid, *units), BF16),
        ffn_part=((8, own, width), BF16),
        ffn_parts=((8, own, width), BF16),
        far_a=((4, 4, 2, *units), BF16),
        far_b=((4, 4, 2, *units), BF16),
        mid_a=((4, 2, *units), BF16),
        mid_b=((4, 2, *units), BF16),
        mid_far_a=((4, 2, *units), BF16),
        mid_far_b=((4, 2, *units), BF16),
        end_ab=((2, 2, *units), BF16),
        do_src=(stack, BF16),
        do_buf=(stack, BF16),
        dq_buf=(stack, BF16),
        dq=(stack, BF16),
        dkv_sum=((*grid, half, BLOCK), F32),
        dkv_buf=((*grid, half, BLOCK), BF16),
        kv_one_a=((4, 4, 2, half, BLOCK), BF16),
        kv_one_b=((2, 4, 4, half, BLOCK), BF16),
        kv_sum_a=((4, 2, half, BLOCK), BF16),
        kv_sum_b=((4, 4, half, BLOCK), BF16),
        kv_two_a=((2, 4, half, BLOCK), BF16),
        kv_two_b=((4, 4, half, BLOCK), BF16),
        kv_sum=((4, 2, half, BLOCK), BF16),
        dkv=((PAIRS, 2, half, BLOCK), BF16),
        parts_back=((4, own, width), BF16),
        landed_back=((4, own, width), BF16),
        grad_in=((rows, qkv_cols), BF16),
        gain_pieces=((4, 4, 2, 8, 128), F32),
        output=((own, width), BF16),
        input_bf=((own, width), BF16),
        qkv=((*grid, *piece), BF16),
        one_a=((4, 4, 2, *piece), BF16),
        one_b=((4, 4, 2, *piece), BF16),
        one_g=((4, 4, 2, 8, 128), F32),
        sum_a=((4, 2, *piece), BF16),
        sum_b=((4, 2, *piece), BF16),
        sum_g=((4, 2, 8, 128), F32),
        two_a=((4, 2, *piece), BF16),
        two_b=((4, 2, *piece), BF16),
        two_g=((4, 2, 8, 128), F32),
        part_a=((2, *piece), BF16),
        part_b=((2, *piece), BF16),
        part_g=((2, 8, 128), F32),
        three_a=((2, *piece), BF16),
        three_b=((2, *piece), BF16),
        three_g=((2, 8, 128), F32),
        gain_sum=((8, 128), F32),
    )


def project(r):
    pieces = r.gains_all[...].reshape(NCTX * 16, 128)
    r.gain_attn[...] = spread_gain(pieces, 0, 32, r.gain_attn.shape[1])
    r.gain_ffn[...] = spread_gain(pieces, 1, 32, r.gain_ffn.shape[1])
    r.gain_query[...] = spread_gain(pieces, 2, 2, 128)
    r.gain_key[...] = spread_gain(pieces, 3, 2, 128)
    rows = r.rows_in[...].astype(F32)
    r.hidden[...] = (rows * row_scale(rows) * r.gain_attn[...]).astype(BF16)
    weights = r.w_all[...].reshape(r.hidden.shape[1], r.w_all.shape[5])
    r.raw[...] = jnp.dot(r.hidden[...], weights, preferred_element_type=F32)
    cos, sin = twice(r.cosine), twice(r.sine)
    for k in range(2):
        tile = r.raw[:, k * 128 : k * 128 + 128]
        tile = turned(tile * head_scale(tile) * r.gain_query[...], cos, sin) * (HEAD_SIZE**-0.5)
        for a, one in enumerate((tile, crossed(tile))):
            one = jnp.where(left_lanes(one), one, 0.0).astype(BF16)
            for s in range(2):
                r.q_src[2 * k + s, a * BLOCK : (a + 1) * BLOCK] = one[s * BLOCK : (s + 1) * BLOCK]
    tile = r.raw[:, 256:384]
    keys = turned(tile * head_scale(tile) * r.gain_key[...], cos, sin)
    values = r.raw[:, 384:512]
    for k in range(2):
        key, value = (keys, crossed(values)) if k == 0 else (crossed(keys), values)
        one = jnp.where(left_lanes(key), key, value).astype(BF16)
        for s in range(2):
            part = one[s * BLOCK : (s + 1) * BLOCK]
            r.kv_src[2 * k + s] = part.reshape(2, BLOCK // 2, 128)


def attend(r, low, j):
    b = block_of(low, j)
    r.acc[...] = jnp.zeros_like(r.acc)
    r.den[...] = jnp.zeros_like(r.den)

    def chunk(i, masked):
        kv = r.kv_buf[i // 4, lax.rem(i, 4)].reshape(2 * BLOCK, BLOCK)
        powered = jnp.exp(last_dims(r.q_buf[j], kv))
        if masked:
            powered = jnp.where(causal_mask(b, i), powered, 0.0)
        r.den[...] += powered[:, :BLOCK] + powered[:, BLOCK:]
        r.acc[...] += jnp.dot(powered.astype(BF16), kv, preferred_element_type=F32)

    pl.loop(0, b // 2)(lambda i: chunk(i, False))
    chunk(b // 2, True)
    total = jnp.sum(r.den[...], axis=1, keepdims=True)
    lanes = iota((2 * BLOCK, BLOCK), 1)
    r.o_buf[j] = jnp.where(lanes >= HEAD_SIZE, r.acc[...] / total, 0.0).astype(BF16)
    r.log_buf[j] = jnp.broadcast_to(jnp.log(total), (2 * BLOCK, BLOCK))


def attend_back(r, low, j):
    b = block_of(low, j)
    r.acc[...] = jnp.zeros_like(r.acc)
    delta = jnp.sum(r.do_buf[j].astype(F32) * r.o_buf[j].astype(F32), axis=1, keepdims=True)

    def chunk(i, masked):
        q, do, logs = r.q_buf[j], r.do_buf[j], r.log_buf[j]
        kv = r.kv_buf[i // 4, lax.rem(i, 4)].reshape(2 * BLOCK, BLOCK)
        probs = jnp.exp(last_dims(q, kv) - jnp.concatenate([logs, logs], axis=1))
        if masked:
            probs = jnp.where(causal_mask(b, i), probs, 0.0)
        grads = (probs * (last_dims(do, kv) - delta)).astype(BF16)
        r.acc[...] += jnp.dot(grads, kv, preferred_element_type=F32)
        update = first_dims(grads, q) + first_dims(probs.astype(BF16), do)
        r.dkv_sum[i // 4, lax.rem(i, 4)] += update.reshape(2, 2, BLOCK // 2, BLOCK)

    pl.loop(0, b // 2)(lambda i: chunk(i, False))
    chunk(b // 2, True)
    r.dq_buf[j] = (r.acc[...] * (HEAD_SIZE**-0.5)).astype(BF16)


def tiles(m, n):
    return pl.ds(pl.multiple_of(m * n, n), n)


def project_back(r):
    cos, sin = twice(r.cosine), -twice(r.sine)
    own, width = r.residual.shape

    def head_back(u, tile, gain_row):
        turn = turned(u, cos, sin)
        scale = head_scale(tile)
        hat = tile * scale
        scaled = turn * gain_row
        back = scale * (scaled - hat * head_mean(scaled * hat))
        return back.astype(BF16), jnp.sum(turn * hat, axis=0, keepdims=True)

    def both(first, second):
        return jnp.concatenate([first.astype(F32), second.astype(F32)], axis=0)

    query_gain = jnp.zeros((1, 128), F32)
    for k in range(2):
        first = both(r.dq[2 * k, :BLOCK], r.dq[2 * k + 1, :BLOCK])
        second = crossed(both(r.dq[2 * k, BLOCK:], r.dq[2 * k + 1, BLOCK:]))
        lanes = slice(k * 128, (k + 1) * 128)
        back, part = head_back(
            jnp.where(left_lanes(first), first, second), r.raw[:, lanes], r.gain_query[...]
        )
        r.grad_in[:, lanes] = back
        query_gain = query_gain + part
    first, second = [
        both(r.dkv[2 * k].reshape(BLOCK, 128), r.dkv[2 * k + 1].reshape(BLOCK, 128))
        for k in range(2)
    ]
    left = left_lanes(first)
    back, key_gain = head_back(
        jnp.where(left, first, crossed(second)), r.raw[:, 256:384], r.gain_key[...]
    )
    r.grad_in[:, 256:384] = back
    r.grad_in[:, 384:] = jnp.where(left, crossed(first), second).astype(BF16)
    attn_gain = jnp.zeros((1, width), F32)
    weights = r.w_all[...].reshape(width, r.grad_in.shape[1])
    for q in range(4):
        at = slice(q * own, (q + 1) * own)
        back = last_dims(r.grad_in[at], weights)
        r.parts_back[q] = back.astype(BF16)
        rows = r.rows_in[at].astype(F32)
        attn_gain = attn_gain + jnp.sum(back * (rows * row_scale(rows)), axis=0, keepdims=True)
    return ((attn_gain, 32), (r.ffn_gain[...], 32), (query_gain, 2), (key_gain, 2))


def begin(moves):
    for move in moves:
        push(*move)


def finish(moves):
    for move in moves:
        settle(*move)


def whole_body(names, *refs):
    r = types.SimpleNamespace(**dict(zip(names, refs)))
    take = Sems(refs[-1])
    c, t, slot, low, to = places()
    z, x, h = position()
    core = lax.rem(t, 2)
    own, width = r.residual.shape

    def spread(kind, src_of, dst_of, local=False):
        return (kind, src_of, dst_of, *take.two(), local)

    def gathered(ref):
        second = [
            spread("x", lambda p: ref.at[z, x, :, 0], lambda q: ref.at[z, q, :, 0]),
            spread("z", lambda p: ref.at[z, x, :, 1], lambda q: ref.at[q, x, :, 1]),
        ]
        third = [
            spread("z", lambda p: ref.at[z, :, :, 0], lambda q: ref.at[q, :, :, 0]),
            spread("x", lambda p: ref.at[:, x, :, 1], lambda q: ref.at[:, q, :, 1]),
        ]
        return second, third

    greet_attention(["z", "x", "rows"])
    first = [
        spread("pair", lambda p: r.weights, lambda q: r.w_all.at[z, x, q], True),
        spread("pair", lambda p: r.gains, lambda q: r.gains_all.at[z, x, q], True),
    ]
    late = [
        spread("pair", lambda p: r.wo, lambda q: r.wo_all.at[z, x, q], True),
        spread("pair", lambda p: r.ffn.at[p], lambda q: r.w_ffn.at[z, x, q], True),
    ]
    begin(first)
    begin(late)
    finish(first)
    second, third = gathered(r.w_all)
    second.append(spread("x", lambda p: r.gains_all.at[z, x], lambda q: r.gains_all.at[z, q]))
    third.append(spread("z", lambda p: r.gains_all.at[z], lambda q: r.gains_all.at[q]))
    stage(*second)
    stage(*third)
    finish(late)
    out_second, out_third = gathered(r.wo_all)
    ffn_second, ffn_third = gathered(r.w_ffn)
    begin(out_second + ffn_second)
    project(r)

    q_send, q_recv = take.two()
    near = spread("z", lambda p: r.kv_src.at[p], lambda q: r.kv_buf.at[q, x, h], True)
    push(*near)
    to_workers(r.q_src, r.q_buf, q_send, q_recv, "start")
    settle(*near)
    kv = r.kv_buf
    stage(
        spread("x", lambda p: kv.at[:, x, h, 0], lambda q: kv.at[:, q, h, 0]),
        spread("pair", lambda p: kv.at[:, x, h, 1], lambda q: kv.at[:, x, q, 1]),
    )
    stage(
        spread("pair", lambda p: kv.at[:, :, h, 0], lambda q: kv.at[:, :, q, 0]),
        spread("x", lambda p: kv.at[:, x, :, 1], lambda q: kv.at[:, q, :, 1]),
    )
    finish(out_second + ffn_second)
    begin(out_third)
    begin(ffn_third)
    cot_swap = spread("pair", lambda p: r.cot, lambda q: r.cot_all.at[q], True)
    push(*cot_swap)
    to_workers(r.q_src, r.q_buf, q_send, q_recv, "wait")
    from_owners(r.q_src, r.q_buf, q_send, q_recv)
    o_send, o_recv = take.two()
    for j in range(SLOTS):
        attend(r, low, j)
        to_owner(r.o_buf, r.att, o_send, o_recv, j, "start")
    for j in range(SLOTS):
        to_owner(r.o_buf, r.att, o_send, o_recv, j, "wait")
    from_workers(r.o_buf, r.att, o_send, o_recv)

    for k in range(2):
        for s in range(2):
            left = crossed(r.att[2 * k + s, :BLOCK].astype(F32))
            right = r.att[2 * k + s, BLOCK:].astype(F32)
            one = jnp.where(left_lanes(left), left, right).astype(BF16)
            r.attended[s * BLOCK : (s + 1) * BLOCK, k * 128 : (k + 1) * 128] = one
    finish(out_third)
    out_full = r.wo_all[...].reshape(width, r.attended.shape[1])
    r.parts[...] = last_dims(r.attended[...], out_full).astype(BF16).reshape(r.parts.shape)
    stage(spread("tp", lambda p: r.parts.at[p], lambda q: r.landed.at[q], True))
    rows = r.rows_in[tiles(t, own)].astype(F32) + summed(r.landed)
    r.residual[...] = rows
    r.hidden_own[...] = (rows * row_scale(rows) * r.gain_ffn[...]).astype(BF16)
    ring = spread("ring", lambda p: r.hidden_own, lambda q: r.hidden_all.at[q, core], True)
    push(*ring)
    settle(*cot_swap)
    finish(ffn_third)
    w = r.w_ffn.reshape(width, 3 * UNITS)
    cot = r.cot_all.reshape(8 * own, width)

    @pl.loop(0, 4)
    def _(m):
        at = tiles(m, 2 * own)
        r.grad_units[at] = jnp.dot(cot[at], w[:, 2 * UNITS :], preferred_element_type=F32)

    settle(*ring)
    hidden = r.hidden_all
    stage(spread("core", lambda p: hidden.at[:, core], lambda q: hidden.at[:, q]))

    @pl.loop(0, 2)
    def _(m):
        at = tiles(m, 4 * own)
        some = hidden[pl.ds(2 * m, 2)].reshape(4 * own, width)
        gate = jnp.dot(some, w[:, :UNITS], preferred_element_type=F32)
        up = jnp.dot(some, w[:, UNITS : 2 * UNITS], preferred_element_type=F32)
        sigmoid = jax.nn.sigmoid(gate)
        activated = gate * sigmoid
        r.units[at] = (activated * up).astype(BF16)
        grad = r.grad_units[at]
        r.units_in[at, :UNITS] = (grad * up * sigmoid * (1.0 + gate * (1.0 - sigmoid))).astype(BF16)
        r.units_in[at, UNITS:] = (grad * activated).astype(BF16)
        step = last_dims(r.units_in[at], w[:, : 2 * UNITS]).astype(BF16)
        r.back[pl.ds(2 * m, 2)] = step.reshape(2, *r.back.shape[1:])

    both = spread("core", lambda p: r.back.at[:, p], lambda q: r.halved.at[q], True)
    push(*both)

    @pl.loop(0, 2)
    def _(m):
        step = last_dims(r.units[tiles(m, 4 * own)], w[:, 2 * UNITS :]).astype(BF16)
        r.ffn_part[pl.ds(4 * m, 4)] = step.reshape(4, *r.ffn_part.shape[1:])

    settle(*both)
    r.chip[...] = summed(r.halved).astype(BF16)
    ring = spread("ring", lambda p: r.chip.at[p], lambda q: r.ringed.at[q], True)
    push(*ring)

    @pl.loop(0, 4)
    def _(m):
        some = hidden[:, :, :, tiles(m, 256)].reshape(8 * own, 256)
        step = first_dims(some, r.units_in[...]).astype(BF16)
        r.grads[m, :, :, :, :, : 2 * UNITS] = step.reshape(4, 2, 2, 16, 2 * UNITS)

    settle(*ring)
    total = summed(r.ringed)
    rows = r.residual[...]
    scale = row_scale(rows)
    normed = rows * scale
    cot_own = cot[tiles(h * 4 + t, own)].astype(F32)
    result = cot_own + row_back(total, normed, scale, r.gain_ffn[...])
    r.grad_bf[...] = result.astype(BF16)
    share = spread("tp", lambda p: r.grad_bf, lambda q: r.grad_all.at[q], True)
    push(*share)
    r.grad_residual[...] = result
    r.ffn_gain[...] = jnp.sum(total * normed, axis=0, keepdims=True)

    @pl.loop(0, 4)
    def _(m):
        step = first_dims(cot[:, tiles(m, 256)], r.units[...]).astype(BF16)
        r.grads[m, :, :, :, :, 2 * UNITS :] = step.reshape(4, 2, 2, 16, UNITS)

    settle(*share)
    grad = jnp.dot(
        r.grad_all[...].reshape(4 * own, width), out_full, preferred_element_type=F32
    )
    for k in range(2):
        for s in range(2):
            tile = grad[s * BLOCK : (s + 1) * BLOCK, k * 128 : (k + 1) * 128]
            for a, one in enumerate((crossed(tile), tile)):
                one = jnp.where(left_lanes(one), 0.0, one).astype(BF16)
                r.do_src[2 * k + s, a * BLOCK : (a + 1) * BLOCK] = one

    do_send, do_recv = take.two()
    to_workers(r.do_src, r.do_buf, do_send, do_recv, "start")
    far = [
        spread("x", lambda p: r.grads.at[:, p, :, 0], lambda q: r.far_a.at[q], True),
        spread("z", lambda p: r.grads.at[p, :, :, 1], lambda q: r.far_b.at[q], True),
    ]
    begin(far)
    ffn_rows = spread("rows", lambda p: r.ffn_part.at[p], lambda q: r.ffn_parts.at[q], True)
    push(*ffn_rows)
    r.dkv_sum[...] = jnp.zeros_like(r.dkv_sum)
    to_workers(r.do_src, r.do_buf, do_send, do_recv, "wait")
    from_owners(r.do_src, r.do_buf, do_send, do_recv)
    dq_send, dq_recv = take.two()
    for j in range(SLOTS):
        attend_back(r, low, j)
        to_owner(r.dq_buf, r.dq, dq_send, dq_recv, j, "start")
    r.dkv_buf[...] = r.dkv_sum[...].astype(BF16)
    kv_first = [
        spread("x", lambda p: r.dkv_buf.at[:, p, :, 0], lambda q: r.kv_one_a.at[q], True),
        spread("pair", lambda p: r.dkv_buf.at[:, :, p, 1], lambda q: r.kv_one_b.at[q], True),
    ]
    begin(kv_first)
    finish(far)

    @pl.loop(0, 4)
    def _(m):
        for src, dst in ((r.far_a, r.mid_a), (r.far_b, r.mid_b)):
            total = src[0, m].astype(F32)
            for k in range(1, 4):
                total += src[k, m].astype(F32)
            dst[m] = total.astype(BF16)

    finish(kv_first)
    r.kv_sum_a[...] = summed(r.kv_one_a).astype(BF16)
    r.kv_sum_b[...] = summed(r.kv_one_b).astype(BF16)
    kv_second = [
        spread("pair", lambda p: r.kv_sum_a.at[:, p], lambda q: r.kv_two_a.at[q], True),
        spread("x", lambda p: r.kv_sum_b.at[:, p], lambda q: r.kv_two_b.at[q], True),
    ]
    begin(kv_second)
    mid = [
        spread("z", lambda p: r.mid_a.at[p], lambda q: r.mid_far_a.at[q], True),
        spread("x", lambda p: r.mid_b.at[p], lambda q: r.mid_far_b.at[q], True),
    ]
    finish(kv_second)
    r.kv_sum[:, 0] = summed(r.kv_two_a).astype(BF16)
    r.kv_sum[:, 1] = summed(r.kv_two_b).astype(BF16)
    kv_third = spread("z", lambda p: r.kv_sum.at[p], lambda q: r.dkv.at[q], True)
    push(*kv_third)
    begin(mid)
    settle(*kv_third)
    for j in range(SLOTS):
        to_owner(r.dq_buf, r.dq, dq_send, dq_recv, j, "wait")
    from_workers(r.dq_buf, r.dq, dq_send, dq_recv)

    vectors = project_back(r)
    sums = spread("tp", lambda p: r.parts_back.at[p], lambda q: r.landed_back.at[q], True)
    push(*sums)

    @pl.loop(0, 4)
    def _(m):
        at = tiles(m, 256)
        cols = r.grad_in.shape[1]
        step = first_dims(r.hidden[:, at], r.grad_in[...]).astype(BF16)
        r.qkv[m, :, :, :, :, :cols] = step.reshape(4, 2, 2, 16, cols)
        some = r.grad_all[:, :, at].reshape(4 * own, 256)
        step = first_dims(some, r.attended[...]).astype(BF16)
        r.qkv[m, :, :, :, :, cols:] = step.reshape(4, 2, 2, 16, r.attended.shape[1])

    pieces = jnp.zeros((NCTX, 8, 128), F32)
    for row, (vector, per) in enumerate(vectors):
        piece = jnp.broadcast_to(owner_pieces(vector, per)[:, None, :], pieces.shape)
        pieces = jnp.where(iota(pieces.shape, 1) == row, piece, pieces)
    r.gain_pieces[...] = pieces.reshape(r.gain_pieces.shape)
    one = [
        spread("x", lambda p: r.qkv.at[:, p, :, 0], lambda q: r.one_a.at[q], True),
        spread("z", lambda p: r.qkv.at[p, :, :, 1], lambda q: r.one_b.at[q], True),
        spread("x", lambda p: r.gain_pieces.at[:, p], lambda q: r.one_g.at[q], True),
    ]
    begin(one)
    finish(mid)
    r.end_ab[:, 0] = summed(r.mid_far_a).astype(BF16)
    r.end_ab[:, 1] = summed(r.mid_far_b).astype(BF16)
    swap = spread("pair", lambda p: r.end_ab.at[p], lambda q: r.ffn_all.at[q], True)
    push(*swap)
    settle(*ffn_rows)
    r.output[...] = (r.residual[...] + summed(r.ffn_parts)).astype(BF16)
    share = [spread("tp", lambda p: r.output, lambda q: r.output_all.at[q], True)]
    rows = r.rows_in[tiles(t, own)].astype(F32)
    scale = row_scale(rows)
    normed = rows * scale
    settle(*sums)
    result = r.grad_residual[...] + row_back(
        summed(r.landed_back), normed, scale, r.gain_attn[...]
    )
    r.input_bf[...] = result.astype(BF16)
    share.append(spread("tp", lambda p: r.input_bf, lambda q: r.input_all.at[q], True))
    begin(share)
    finish(one)
    r.sum_a[...] = summed(r.one_a).astype(BF16)
    r.sum_b[...] = summed(r.one_b).astype(BF16)
    r.sum_g[...] = summed(r.one_g)
    stage(
        spread("z", lambda p: r.sum_a.at[p], lambda q: r.two_a.at[q], True),
        spread("x", lambda p: r.sum_b.at[p], lambda q: r.two_b.at[q], True),
        spread("z", lambda p: r.sum_g.at[p], lambda q: r.two_g.at[q], True),
    )
    r.part_a[...] = summed(r.two_a).astype(BF16)
    r.part_b[...] = summed(r.two_b).astype(BF16)
    r.part_g[...] = summed(r.two_g)
    stage(
        spread("pair", lambda p: r.part_a.at[p], lambda q: r.three_a.at[q], True),
        spread("pair", lambda p: r.part_b.at[p], lambda q: r.three_b.at[q], True),
        spread("pair", lambda p: r.part_g.at[p], lambda q: r.three_g.at[q], True),
    )
    r.gain_sum[...] = summed(r.three_g)
    share.append(spread("tp", lambda p: r.gain_sum, lambda q: r.gain_tp.at[q], True))
    push(*share[-1])
    r.qkv_grad[0] = summed(r.three_a)
    r.qkv_grad[1] = summed(r.three_b)
    finish(share)
    settle(*swap)


def whole(weights, gains, ffn, wo, cot, rows_in, cosine, sine):
    rows, width = rows_in.shape
    arrays = scratch_arrays(rows, width, weights.shape[2], wo.shape[2])
    names = INPUTS + OUTPUTS + tuple(arrays)
    return pl.pallas_call(
        functools.partial(whole_body, names),
        out_shape=[
            jax.ShapeDtypeStruct((2, 16, weights.shape[2] + wo.shape[2]), F32),
            jax.ShapeDtypeStruct(ffn.shape, BF16),
            jax.ShapeDtypeStruct((4, rows // 4, width), BF16),
            jax.ShapeDtypeStruct((4, rows // 4, width), BF16),
            jax.ShapeDtypeStruct((4, 8, 128), F32),
        ],
        in_specs=[ANY] * 5 + [VMEM] * 3,
        out_specs=[VMEM] + [ANY] * 4,
        scratch_shapes=[pltpu.VMEM(shape, dtype) for shape, dtype in arrays.values()]
        + [pltpu.SemaphoreType.DMA((MOVES + 32, 2, 8))],
        compiler_params=pltpu.CompilerParams(
            collective_id=1, has_side_effects=True, vmem_limit_bytes=60 * 2**20
        ),
        name="block",
    )(weights, gains, ffn, wo, cot, rows_in, cosine, sine)


def rope_tables(tokens, offset):
    half = HEAD_SIZE // 2
    inverse = ROPE_BASE ** (-(jnp.arange(half, dtype=F32) * 2.0 / HEAD_SIZE))
    steps = (offset + jnp.arange(tokens, dtype=jnp.int32)).astype(F32)
    angles = steps[:, None] * jnp.tile(inverse, 4)[None, :]
    signs = jnp.where(jnp.arange(4 * half) % HEAD_SIZE < half, -1.0, 1.0)
    return jnp.cos(angles), jnp.sin(angles) * signs[None, :]


def halves(*weights):
    rows, cols = weights[0].shape
    w = jnp.stack(weights).reshape(len(weights), rows, 2, cols // 2)
    w = jnp.pad(w, ((0, 0), (0, 0), (0, 0), (0, UNITS - cols // 2)))
    return w.transpose(2, 1, 0, 3).reshape(2, rows, len(weights) * UNITS)


def local(
    block_input, cotangent, w_query, key_weight, w_value, w_out, w_gate, w_up, w_down,
    norm_gains, head_gains,
):
    seqs, tokens, width = block_input.shape
    rows = seqs * tokens
    unit_half = w_gate.shape[1] // 2
    rows_in = block_input.reshape(rows, width)
    cot_rows = cotangent.reshape(rows, width)
    cosine, sine = rope_tables(tokens, lax.axis_index("ctx") * tokens)
    weight_rows = jnp.concatenate([w_query, key_weight, w_value], axis=1)
    gains = jnp.pad(norm_gains, ((0, 14), (0, 96))) + jnp.pad(head_gains, ((2, 12), (0, 126)))
    ffn = halves(w_gate, w_up, w_down)
    qkv_grad, pair_grads, output_all, input_all, gain_tp = whole(
        weight_rows.reshape(2, 16, weight_rows.shape[1]),
        gains,
        ffn.reshape(2, 2, 16, ffn.shape[2]),
        w_out.reshape(2, 16, w_out.shape[1]),
        cot_rows,
        rows_in,
        cosine,
        sine,
    )
    pair_grads = pair_grads.reshape(ffn.shape)
    pair_grads = pair_grads.astype(F32)
    gain_sum = jnp.sum(gain_tp, axis=0)
    qkv_grad = qkv_grad.reshape(32, 768)

    def joined(first):
        last = first + unit_half
        return jnp.concatenate([pair_grads[0, :, first:last], pair_grads[1, :, first:last]], axis=1)

    gate_grad, up_grad, down_grad = joined(0), joined(UNITS), joined(2 * UNITS)
    return (
        output_all.reshape(seqs, tokens, width),
        input_all.astype(F32).reshape(seqs, tokens, width),
        qkv_grad[:, :256],
        qkv_grad[:, 256:384],
        qkv_grad[:, 384:512],
        qkv_grad[:, 512:],
        gate_grad,
        up_grad,
        down_grad,
        gain_sum[0:2, :32],
        gain_sum[2:4, :2],
    )


def solution(mesh):
    tokens, weights = P(None, "ctx", None), P("ctx", "tp")
    return jax.shard_map(
        local,
        mesh=mesh,
        in_specs=(tokens,) * 2 + (weights,) * 7 + (P(None, "ctx"),) * 2,
        out_specs=(tokens,) * 2 + (weights,) * 7 + (P(None, "ctx"),) * 2,
        check_vma=False,
    )
```

```python
import functools
import types

import jax
import jax.numpy as jnp
from jax import lax
from jax.experimental import pallas as pl
from jax.experimental.pallas import tpu as pltpu
from jax.sharding import PartitionSpec as P

HEAD_SIZE = 64
EPSILON = 1e-06
ROPE_BASE = 1000000.0
MESH = pl.DeviceIdType.MESH
F32 = jnp.float32
BF16 = jnp.bfloat16
ANY = pl.BlockSpec(memory_space=pl.ANY)
VMEM = pl.BlockSpec(memory_space=pltpu.VMEM)
NCTX = 32
PAIRS = 4
WORKERS = 8
SLOTS = 4
BLOCK = 128


def group(kind):
    c, t = lax.axis_index("ctx"), lax.axis_index("tp")
    h = lax.rem(c, 2)
    if kind == "ctx":
        return NCTX, c, lambda p: (p, t)
    if kind == "tp":
        return 4, t, lambda p: (c, p)
    if kind == "pair":
        return 2, h, lambda p: (c - h + p, t)
    z, x, core = c // 8, lax.rem(c // 2, 4), lax.rem(t, 2)
    if kind == "z":
        return 4, z, lambda p: (c + (p - z) * 8, t)
    if kind == "x":
        return 4, x, lambda p: (c + (p - x) * 2, t)
    if kind == "core":
        return 2, core, lambda p: (c, t - core + p)
    if kind == "near":
        return 2, t // 2, lambda p: (c, p * 2 + core)
    if kind == "ring":
        return 4, h * 2 + t // 2, lambda p: (c - h + p // 2, lax.rem(p, 2) * 2 + core)
    return 8, h * 4 + t, lambda p: (c - h + p // 4, lax.rem(p, 4))


def push(kind, src_of, dst_of, send, recv, local=False):
    n, me, dev = group(kind)

    @pl.loop(1, n)
    def _(i):
        p = lax.rem(me + i, n)
        pltpu.make_async_remote_copy(
            src_ref=src_of(p),
            dst_ref=dst_of(me),
            send_sem=send.at[p],
            recv_sem=recv.at[me],
            device_id=dev(p),
            device_id_type=MESH,
        ).start()

    if local:
        pltpu.make_async_copy(src_of(me), dst_of(me), recv.at[me]).start()


def settle(kind, src_of, dst_of, send, recv, local=False):
    n, me, dev = group(kind)

    @pl.loop(1, n)
    def _(i):
        p = lax.rem(me + i, n)
        copy = pltpu.make_async_remote_copy(
            src_ref=src_of(p),
            dst_ref=dst_of(p),
            send_sem=send.at[p],
            recv_sem=recv.at[p],
            device_id=dev(p),
            device_id_type=MESH,
        )
        copy.wait_send()
        copy.wait_recv()

    if local:
        pltpu.make_async_copy(src_of(me), dst_of(me), recv.at[me]).wait()


def stage(*moves):
    for move in moves:
        push(*move)
    for move in moves:
        settle(*move)


class Sems:
    def __init__(self, ref):
        self.ref, self.used = ref, 0

    def two(self, n):
        at = self.used
        self.used += 2 * n
        return self.ref.at[pl.ds(at, n)], self.ref.at[pl.ds(at + n, n)]


def position():
    c = lax.axis_index("ctx")
    return c // 8, lax.rem(c // 2, 4), lax.rem(c, 2)


def iota(shape, axis):
    return lax.broadcasted_iota(jnp.int32, shape, axis)


def two_parts(v):
    high = v.astype(BF16)
    return high, (v - high.astype(F32)).astype(BF16)


def exact_dot(v, pattern):
    high, low = two_parts(v)
    return jnp.dot(high, pattern, preferred_element_type=F32) + jnp.dot(
        low, pattern, preferred_element_type=F32
    )


def head_mean(v):
    n = v.shape[1]
    same = lax.div(iota((n, n), 0), HEAD_SIZE) == lax.div(iota((n, n), 1), HEAD_SIZE)
    return exact_dot(v, jnp.where(same, 1.0 / HEAD_SIZE, 0.0).astype(BF16))


def head_scale(v):
    return lax.rsqrt(head_mean(v * v) + EPSILON)


def turned(u, cosine, sine):
    half, n = HEAD_SIZE // 2, 2 * HEAD_SIZE
    first = lax.rem(iota(u.shape, 1), HEAD_SIZE) < half
    other = jnp.where(first, pltpu.roll(u, n - half, 1), pltpu.roll(u, half, 1))
    return u * cosine + other * sine


def crossed(tile):
    return pltpu.roll(tile, HEAD_SIZE, 1)


def left_lanes(tile):
    return iota(tile.shape, 1) < HEAD_SIZE


def spread_gain(pieces, row, per, lanes):
    pattern = (lax.rem(iota((128, lanes), 1), per) == iota((128, lanes), 0)).astype(F32)
    wide = jnp.dot(pieces, pattern.astype(BF16), preferred_element_type=F32)
    r, lane = iota(wide.shape, 0), iota(wide.shape, 1)
    owner = lax.div(lax.rem(lane, NCTX * per), per)
    keep = jnp.logical_and(lax.rem(r, 16) == row, lax.div(r, 16) == owner)
    return jnp.sum(jnp.where(keep, wide, 0.0), axis=0, keepdims=True)


def owner_pieces(vector, per):
    lanes = vector.shape[1]
    shape = (NCTX, lanes)
    owner = lax.div(lax.rem(iota(shape, 1), NCTX * per), per)
    parts = jnp.where(owner == iota(shape, 0), jnp.broadcast_to(vector, shape), 0.0)
    pattern = (lax.rem(iota((lanes, 128), 0), per) == iota((lanes, 128), 1)).astype(F32)
    return exact_dot(parts, pattern.astype(BF16))


def row_scale(rows):
    return lax.rsqrt(jnp.mean(rows * rows, axis=1, keepdims=True) + EPSILON)


def twice(table):
    return jnp.concatenate([table[...], table[...]], axis=0)


def places():
    c, t = lax.axis_index("ctx"), lax.axis_index("tp")
    slot, low = c // WORKERS, lax.rem(c, WORKERS)
    to = low + lax.rem(slot, 2) * (WORKERS - 1 - 2 * low)
    return c, t, slot, low, to


def block_of(low, j):
    return j * WORKERS + (low if j % 2 == 0 else WORKERS - 1 - low)


def greet_attention(kinds):
    c, t, slot, low, to = places()
    barrier = pltpu.get_barrier_semaphore()
    total = 0
    others = [p * WORKERS + to for p in range(PAIRS)] + [block_of(low, j) for j in range(SLOTS)]
    for other in others:

        @pl.when(other != c)
        def _():
            pl.semaphore_signal(barrier, inc=1, device_id=(other, t), device_id_type=MESH)

        total = total + jnp.where(other != c, 1, 0)
    for kind in kinds:
        n, me, dev = group(kind)

        @pl.loop(1, n)
        def _(i):
            pl.semaphore_signal(
                barrier, inc=1, device_id=dev(lax.rem(me + i, n)), device_id_type=MESH
            )

        total = total + (n - 1)
    pl.semaphore_wait(barrier, total)


def to_workers(src, dst, send, recv, act):
    c, t, slot, low, to = places()
    for p in range(PAIRS):
        target = p * WORKERS + to
        far = pltpu.make_async_remote_copy(
            src_ref=src.at[p],
            dst_ref=dst.at[slot],
            send_sem=send.at[p],
            recv_sem=recv.at[slot],
            device_id=(target, t),
            device_id_type=MESH,
        )
        near = pltpu.make_async_copy(src.at[p], dst.at[slot], send.at[p])

        @pl.when(target != c)
        def _():
            far.start() if act == "start" else far.wait_send()

        @pl.when(target == c)
        def _():
            near.start() if act == "start" else near.wait()


def from_owners(src, dst, send, recv):
    c, t, slot, low, to = places()
    for j in range(SLOTS):
        owner = block_of(low, j)

        @pl.when(owner != c)
        def _():
            pltpu.make_async_remote_copy(
                src_ref=src.at[j],
                dst_ref=dst.at[j],
                send_sem=send.at[j],
                recv_sem=recv.at[j],
                device_id=(owner, t),
                device_id_type=MESH,
            ).wait_recv()


def to_owner(src, dst, send, recv, j, act):
    c, t, slot, low, to = places()
    owner = block_of(low, j)
    far = pltpu.make_async_remote_copy(
        src_ref=src.at[j],
        dst_ref=dst.at[slot],
        send_sem=send.at[j],
        recv_sem=recv.at[slot],
        device_id=(owner, t),
        device_id_type=MESH,
    )
    near = pltpu.make_async_copy(src.at[j], dst.at[slot], send.at[j])

    @pl.when(owner != c)
    def _():
        far.start() if act == "start" else far.wait_send()

    @pl.when(owner == c)
    def _():
        near.start() if act == "start" else near.wait()


def from_workers(src, dst, send, recv):
    c, t, slot, low, to = places()
    for p in range(PAIRS):
        target = p * WORKERS + to

        @pl.when(target != c)
        def _():
            pltpu.make_async_remote_copy(
                src_ref=src.at[p],
                dst_ref=dst.at[p],
                send_sem=send.at[p],
                recv_sem=recv.at[p],
                device_id=(target, t),
                device_id_type=MESH,
            ).wait_recv()


def last_dims(a, b):
    return lax.dot_general(a, b, (((1,), (1,)), ((), ())), preferred_element_type=F32)


def first_dims(a, b):
    return lax.dot_general(a, b, (((0,), (0,)), ((), ())), preferred_element_type=F32)


def causal_mask(b, i):
    shape = (2 * BLOCK, 2 * BLOCK)
    rows = lax.broadcasted_iota(jnp.int32, shape, 0)
    token = b * BLOCK + jnp.where(rows >= BLOCK, rows - BLOCK, rows)
    key = i * 2 * BLOCK + lax.broadcasted_iota(jnp.int32, shape, 1)
    return token >= key


def row_back(grads, normed, scale, gain):
    scaled = grads * gain
    return scale * (scaled - normed * jnp.mean(scaled * normed, axis=1, keepdims=True))


def summed(ref):
    total = ref[0].astype(F32)
    for k in range(1, ref.shape[0]):
        total += ref[k].astype(F32)
    return total


UNITS = 640
INPUTS = ("weights", "gains", "ffn", "wo", "cot", "rows_in", "cosine", "sine")
OUTPUTS = ("qkv_grad", "ffn_all", "output_all", "input_all", "gain_tp")
SIZES = {"tp": 4, "pair": 2, "rows": 8, "z": 4, "x": 4, "core": 2, "ring": 4, "near": 2}
SEMAPHORES = 412


def scratch_arrays(rows, width, qkv_cols, out_cols):
    own, half = rows // 4, BLOCK // 2
    stack = (SLOTS, 2 * BLOCK, BLOCK)
    grid, piece = (4, 4, 2, 2), (16, qkv_cols + out_cols)
    units = (16, 3 * UNITS)
    return dict(
        w_all=((*grid, 16, qkv_cols), BF16),
        gains_all=((4, 4, 2, 16, 128), BF16),
        w_ffn=((*grid, *units), BF16),
        wo_all=((*grid, 16, out_cols), BF16),
        cot_all=((2, rows, width), BF16),
        hidden=((rows, width), BF16),
        raw=((rows, qkv_cols), F32),
        q_src=(stack, BF16),
        kv_src=((PAIRS, 2, half, BLOCK), BF16),
        gain_attn=((1, width), F32),
        gain_ffn=((1, width), F32),
        gain_query=((1, 128), F32),
        gain_key=((1, 128), F32),
        q_buf=(stack, BF16),
        kv_buf=((*grid, half, BLOCK), BF16),
        o_buf=(stack, BF16),
        log_buf=(stack, F32),
        att=(stack, BF16),
        acc=((2 * BLOCK, BLOCK), F32),
        den=((2 * BLOCK, BLOCK), F32),
        attended=((rows, out_cols), BF16),
        parts=((2, 2, own, width), BF16),
        parts_half=((2, 2, own, width), BF16),
        parts_chip=((2, own, width), BF16),
        landed=((2, own, width), BF16),
        residual=((own, width), F32),
        hidden_own=((own, width), BF16),
        hidden_all=((4, 2, own, width), BF16),
        grad_units=((2 * rows, UNITS), F32),
        units=((2 * rows, UNITS), BF16),
        units_in=((2 * rows, 2 * UNITS), BF16),
        back=((4, 2, own, width), BF16),
        halved=((2, 4, own, width), BF16),
        chip=((4, own, width), BF16),
        ringed=((4, own, width), BF16),
        grad_bf=((own, width), BF16),
        grad_all=((2, 2, own, width), BF16),
        grad_residual=((own, width), F32),
        ffn_gain=((1, width), F32),
        grads=((*grid, *units), BF16),
        ffn_part=((8, own, width), BF16),
        ffn_parts=((8, own, width), BF16),
        far_a=((4, 4, 2, *units), BF16),
        far_b=((4, 4, 2, *units), BF16),
        mid_a=((4, 2, *units), BF16),
        mid_b=((4, 2, *units), BF16),
        mid_far_a=((4, 2, *units), BF16),
        mid_far_b=((4, 2, *units), BF16),
        end_ab=((2, 2, *units), BF16),
        do_src=(stack, BF16),
        do_buf=(stack, BF16),
        dq_buf=(stack, BF16),
        dq=(stack, BF16),
        dkv_sum=((*grid, half, BLOCK), F32),
        dkv_buf=((*grid, half, BLOCK), BF16),
        kv_one_a=((4, 4, 2, half, BLOCK), BF16),
        kv_one_b=((2, 4, 4, half, BLOCK), BF16),
        kv_sum_a=((4, 2, half, BLOCK), BF16),
        kv_sum_b=((4, 4, half, BLOCK), BF16),
        kv_two_a=((2, 4, half, BLOCK), BF16),
        kv_two_b=((4, 4, half, BLOCK), BF16),
        kv_sum=((4, 2, half, BLOCK), BF16),
        dkv=((PAIRS, 2, half, BLOCK), BF16),
        parts_back=((2, 2, own, width), BF16),
        back_half=((2, 2, own, width), BF16),
        back_chip=((2, own, width), BF16),
        landed_back=((2, own, width), BF16),
        grad_in=((rows, qkv_cols), BF16),
        gain_pieces=((4, 4, 2, 8, 128), F32),
        output=((own, width), BF16),
        input_bf=((own, width), BF16),
        qkv=((*grid, *piece), BF16),
        one_a=((4, 4, 2, *piece), BF16),
        one_b=((4, 4, 2, *piece), BF16),
        one_g=((4, 4, 2, 8, 128), F32),
        sum_a=((4, 2, *piece), BF16),
        sum_b=((4, 2, *piece), BF16),
        sum_g=((4, 2, 8, 128), F32),
        two_a=((4, 2, *piece), BF16),
        two_b=((4, 2, *piece), BF16),
        two_g=((4, 2, 8, 128), F32),
        part_a=((2, *piece), BF16),
        part_b=((2, *piece), BF16),
        part_g=((2, 8, 128), F32),
        three_a=((2, *piece), BF16),
        three_b=((2, *piece), BF16),
        three_g=((2, 8, 128), F32),
        gain_sum=((8, 128), F32),
    )


def project(r):
    pieces = r.gains_all[...].reshape(NCTX * 16, 128)
    r.gain_attn[...] = spread_gain(pieces, 0, 32, r.gain_attn.shape[1])
    r.gain_ffn[...] = spread_gain(pieces, 1, 32, r.gain_ffn.shape[1])
    r.gain_query[...] = spread_gain(pieces, 2, 2, 128)
    r.gain_key[...] = spread_gain(pieces, 3, 2, 128)
    rows = r.rows_in[...].astype(F32)
    r.hidden[...] = (rows * row_scale(rows) * r.gain_attn[...]).astype(BF16)
    weights = r.w_all[...].reshape(r.hidden.shape[1], r.w_all.shape[5])
    r.raw[...] = jnp.dot(r.hidden[...], weights, preferred_element_type=F32)
    cos, sin = twice(r.cosine), twice(r.sine)
    for k in range(2):
        tile = r.raw[:, k * 128 : k * 128 + 128]
        tile = turned(tile * head_scale(tile) * r.gain_query[...], cos, sin) * (HEAD_SIZE**-0.5)
        for a, one in enumerate((tile, crossed(tile))):
            one = jnp.where(left_lanes(one), one, 0.0).astype(BF16)
            for s in range(2):
                r.q_src[2 * k + s, a * BLOCK : (a + 1) * BLOCK] = one[s * BLOCK : (s + 1) * BLOCK]
    tile = r.raw[:, 256:384]
    keys = turned(tile * head_scale(tile) * r.gain_key[...], cos, sin)
    values = r.raw[:, 384:512]
    for k in range(2):
        key, value = (keys, crossed(values)) if k == 0 else (crossed(keys), values)
        one = jnp.where(left_lanes(key), key, value).astype(BF16)
        for s in range(2):
            part = one[s * BLOCK : (s + 1) * BLOCK]
            r.kv_src[2 * k + s] = part.reshape(2, BLOCK // 2, 128)


def attend(r, low, j):
    b = block_of(low, j)
    r.acc[...] = jnp.zeros_like(r.acc)
    r.den[...] = jnp.zeros_like(r.den)

    def chunk(i, masked):
        kv = r.kv_buf[i // 4, lax.rem(i, 4)].reshape(2 * BLOCK, BLOCK)
        powered = jnp.exp(last_dims(r.q_buf[j], kv))
        if masked:
            powered = jnp.where(causal_mask(b, i), powered, 0.0)
        r.den[...] += powered[:, :BLOCK] + powered[:, BLOCK:]
        r.acc[...] += jnp.dot(powered.astype(BF16), kv, preferred_element_type=F32)

    pl.loop(0, b // 2)(lambda i: chunk(i, False))
    chunk(b // 2, True)
    total = jnp.sum(r.den[...], axis=1, keepdims=True)
    lanes = iota((2 * BLOCK, BLOCK), 1)
    r.o_buf[j] = jnp.where(lanes >= HEAD_SIZE, r.acc[...] / total, 0.0).astype(BF16)
    r.log_buf[j] = jnp.broadcast_to(jnp.log(total), (2 * BLOCK, BLOCK))


def attend_back(r, low, j):
    b = block_of(low, j)
    r.acc[...] = jnp.zeros_like(r.acc)
    delta = jnp.sum(r.do_buf[j].astype(F32) * r.o_buf[j].astype(F32), axis=1, keepdims=True)

    def chunk(i, masked):
        q, do, logs = r.q_buf[j], r.do_buf[j], r.log_buf[j]
        kv = r.kv_buf[i // 4, lax.rem(i, 4)].reshape(2 * BLOCK, BLOCK)
        probs = jnp.exp(last_dims(q, kv) - jnp.concatenate([logs, logs], axis=1))
        if masked:
            probs = jnp.where(causal_mask(b, i), probs, 0.0)
        grads = (probs * (last_dims(do, kv) - delta)).astype(BF16)
        r.acc[...] += jnp.dot(grads, kv, preferred_element_type=F32)
        update = first_dims(grads, q) + first_dims(probs.astype(BF16), do)
        r.dkv_sum[i // 4, lax.rem(i, 4)] += update.reshape(2, 2, BLOCK // 2, BLOCK)

    pl.loop(0, b // 2)(lambda i: chunk(i, False))
    chunk(b // 2, True)
    r.dq_buf[j] = (r.acc[...] * (HEAD_SIZE**-0.5)).astype(BF16)


def tiles(m, n):
    return pl.ds(pl.multiple_of(m * n, n), n)


def project_back(r):
    cos, sin = twice(r.cosine), -twice(r.sine)
    own, width = r.residual.shape

    def head_back(u, tile, gain_row):
        turn = turned(u, cos, sin)
        scale = head_scale(tile)
        hat = tile * scale
        scaled = turn * gain_row
        back = scale * (scaled - hat * head_mean(scaled * hat))
        return back.astype(BF16), jnp.sum(turn * hat, axis=0, keepdims=True)

    def both(first, second):
        return jnp.concatenate([first.astype(F32), second.astype(F32)], axis=0)

    query_gain = jnp.zeros((1, 128), F32)
    for k in range(2):
        first = both(r.dq[2 * k, :BLOCK], r.dq[2 * k + 1, :BLOCK])
        second = crossed(both(r.dq[2 * k, BLOCK:], r.dq[2 * k + 1, BLOCK:]))
        lanes = slice(k * 128, (k + 1) * 128)
        back, part = head_back(
            jnp.where(left_lanes(first), first, second), r.raw[:, lanes], r.gain_query[...]
        )
        r.grad_in[:, lanes] = back
        query_gain = query_gain + part
    first, second = [
        both(r.dkv[2 * k].reshape(BLOCK, 128), r.dkv[2 * k + 1].reshape(BLOCK, 128))
        for k in range(2)
    ]
    left = left_lanes(first)
    back, key_gain = head_back(
        jnp.where(left, first, crossed(second)), r.raw[:, 256:384], r.gain_key[...]
    )
    r.grad_in[:, 256:384] = back
    r.grad_in[:, 384:] = jnp.where(left, crossed(first), second).astype(BF16)
    attn_gain = jnp.zeros((1, width), F32)
    weights = r.w_all[...].reshape(width, r.grad_in.shape[1])
    for q in range(4):
        at = slice(q * own, (q + 1) * own)
        back = last_dims(r.grad_in[at], weights)
        r.parts_back[q // 2, q % 2] = back.astype(BF16)
        rows = r.rows_in[at].astype(F32)
        attn_gain = attn_gain + jnp.sum(back * (rows * row_scale(rows)), axis=0, keepdims=True)
    return ((attn_gain, 32), (r.ffn_gain[...], 32), (query_gain, 2), (key_gain, 2))


def begin(moves):
    for move in moves:
        push(*move)


def finish(moves):
    for move in moves:
        settle(*move)


def whole_body(names, *refs):
    r = types.SimpleNamespace(**dict(zip(names, refs)))
    take = Sems(refs[-1])
    c, t, slot, low, to = places()
    z, x, h = position()
    core = lax.rem(t, 2)
    own, width = r.residual.shape

    def spread(kind, src_of, dst_of, local=False):
        return (kind, src_of, dst_of, *take.two(SIZES[kind]), local)

    def gathered(ref):
        second = [
            spread("x", lambda p: ref.at[z, x, :, 0], lambda q: ref.at[z, q, :, 0]),
            spread("z", lambda p: ref.at[z, x, :, 1], lambda q: ref.at[q, x, :, 1]),
        ]
        third = [
            spread("z", lambda p: ref.at[z, :, :, 0], lambda q: ref.at[q, :, :, 0]),
            spread("x", lambda p: ref.at[:, x, :, 1], lambda q: ref.at[:, q, :, 1]),
        ]
        return second, third

    greet_attention(["z", "x", "rows"])
    first = [
        spread("pair", lambda p: r.weights, lambda q: r.w_all.at[z, x, q], True),
        spread("pair", lambda p: r.gains, lambda q: r.gains_all.at[z, x, q], True),
    ]
    late = [
        spread("pair", lambda p: r.wo, lambda q: r.wo_all.at[z, x, q], True),
        spread("pair", lambda p: r.ffn.at[p], lambda q: r.w_ffn.at[z, x, q], True),
    ]
    begin(first)
    begin(late)
    finish(first)
    second, third = gathered(r.w_all)
    second.append(spread("x", lambda p: r.gains_all.at[z, x], lambda q: r.gains_all.at[z, q]))
    third.append(spread("z", lambda p: r.gains_all.at[z], lambda q: r.gains_all.at[q]))
    stage(*second)
    stage(*third)
    finish(late)
    out_second, out_third = gathered(r.wo_all)
    ffn_second, ffn_third = gathered(r.w_ffn)
    begin(out_second + ffn_second)
    project(r)

    q_send, q_recv = take.two(SLOTS)
    near = spread("z", lambda p: r.kv_src.at[p], lambda q: r.kv_buf.at[q, x, h], True)
    push(*near)
    to_workers(r.q_src, r.q_buf, q_send, q_recv, "start")
    settle(*near)
    kv = r.kv_buf
    stage(
        spread("x", lambda p: kv.at[:, x, h, 0], lambda q: kv.at[:, q, h, 0]),
        spread("pair", lambda p: kv.at[:, x, h, 1], lambda q: kv.at[:, x, q, 1]),
    )
    stage(
        spread("pair", lambda p: kv.at[:, :, h, 0], lambda q: kv.at[:, :, q, 0]),
        spread("x", lambda p: kv.at[:, x, :, 1], lambda q: kv.at[:, q, :, 1]),
    )
    finish(out_second + ffn_second)
    begin(out_third)
    begin(ffn_third)
    cot_swap = spread("pair", lambda p: r.cot, lambda q: r.cot_all.at[q], True)
    push(*cot_swap)
    to_workers(r.q_src, r.q_buf, q_send, q_recv, "wait")
    from_owners(r.q_src, r.q_buf, q_send, q_recv)
    o_send, o_recv = take.two(SLOTS)
    for j in range(SLOTS):
        attend(r, low, j)
        to_owner(r.o_buf, r.att, o_send, o_recv, j, "start")
    for j in range(SLOTS):
        to_owner(r.o_buf, r.att, o_send, o_recv, j, "wait")
    from_workers(r.o_buf, r.att, o_send, o_recv)

    for k in range(2):
        for s in range(2):
            left = crossed(r.att[2 * k + s, :BLOCK].astype(F32))
            right = r.att[2 * k + s, BLOCK:].astype(F32)
            one = jnp.where(left_lanes(left), left, right).astype(BF16)
            r.attended[s * BLOCK : (s + 1) * BLOCK, k * 128 : (k + 1) * 128] = one
    finish(out_third)
    out_full = r.wo_all[...].reshape(width, r.attended.shape[1])
    r.parts[...] = last_dims(r.attended[...], out_full).astype(BF16).reshape(r.parts.shape)
    stage(spread("core", lambda p: r.parts.at[:, p], lambda q: r.parts_half.at[q], True))
    r.parts_chip[...] = summed(r.parts_half).astype(BF16)
    stage(spread("near", lambda p: r.parts_chip.at[p], lambda q: r.landed.at[q], True))
    rows = r.rows_in[tiles(t, own)].astype(F32) + summed(r.landed)
    r.residual[...] = rows
    r.hidden_own[...] = (rows * row_scale(rows) * r.gain_ffn[...]).astype(BF16)
    ring = spread("ring", lambda p: r.hidden_own, lambda q: r.hidden_all.at[q, core], True)
    push(*ring)
    settle(*cot_swap)
    finish(ffn_third)
    w = r.w_ffn.reshape(width, 3 * UNITS)
    cot = r.cot_all.reshape(8 * own, width)

    @pl.loop(0, 4)
    def _(m):
        at = tiles(m, 2 * own)
        r.grad_units[at] = jnp.dot(cot[at], w[:, 2 * UNITS :], preferred_element_type=F32)

    settle(*ring)
    hidden = r.hidden_all
    stage(spread("core", lambda p: hidden.at[:, core], lambda q: hidden.at[:, q]))

    @pl.loop(0, 2)
    def _(m):
        at = tiles(m, 4 * own)
        some = hidden[pl.ds(2 * m, 2)].reshape(4 * own, width)
        gate = jnp.dot(some, w[:, :UNITS], preferred_element_type=F32)
        up = jnp.dot(some, w[:, UNITS : 2 * UNITS], preferred_element_type=F32)
        sigmoid = jax.nn.sigmoid(gate)
        activated = gate * sigmoid
        r.units[at] = (activated * up).astype(BF16)
        grad = r.grad_units[at]
        r.units_in[at, :UNITS] = (grad * up * sigmoid * (1.0 + gate * (1.0 - sigmoid))).astype(BF16)
        r.units_in[at, UNITS:] = (grad * activated).astype(BF16)
        step = last_dims(r.units_in[at], w[:, : 2 * UNITS]).astype(BF16)
        r.back[pl.ds(2 * m, 2)] = step.reshape(2, *r.back.shape[1:])

    both = spread("core", lambda p: r.back.at[:, p], lambda q: r.halved.at[q], True)
    push(*both)

    @pl.loop(0, 4)
    def _(m):
        step = first_dims(cot[:, tiles(m, 256)], r.units[...]).astype(BF16)
        r.grads[m, :, :, :, :, 2 * UNITS :] = step.reshape(4, 2, 2, 16, UNITS)

    settle(*both)
    r.chip[...] = summed(r.halved).astype(BF16)
    ring = spread("ring", lambda p: r.chip.at[p], lambda q: r.ringed.at[q], True)
    push(*ring)

    @pl.loop(0, 4)
    def _(m):
        some = hidden[:, :, :, tiles(m, 256)].reshape(8 * own, 256)
        step = first_dims(some, r.units_in[...]).astype(BF16)
        r.grads[m, :, :, :, :, : 2 * UNITS] = step.reshape(4, 2, 2, 16, 2 * UNITS)

    far = [
        spread("x", lambda p: r.grads.at[:, p, :, 0], lambda q: r.far_a.at[q], True),
        spread("z", lambda p: r.grads.at[p, :, :, 1], lambda q: r.far_b.at[q], True),
    ]
    begin(far)
    settle(*ring)
    total = summed(r.ringed)
    rows = r.residual[...]
    scale = row_scale(rows)
    normed = rows * scale
    cot_own = cot[tiles(h * 4 + t, own)].astype(F32)
    result = cot_own + row_back(total, normed, scale, r.gain_ffn[...])
    r.grad_bf[...] = result.astype(BF16)
    share = spread("near", lambda p: r.grad_bf, lambda q: r.grad_all.at[q, core], True)
    push(*share)
    r.grad_residual[...] = result
    r.ffn_gain[...] = jnp.sum(total * normed, axis=0, keepdims=True)

    @pl.loop(0, 2)
    def _(m):
        step = last_dims(r.units[tiles(m, 4 * own)], w[:, 2 * UNITS :]).astype(BF16)
        r.ffn_part[pl.ds(4 * m, 4)] = step.reshape(4, *r.ffn_part.shape[1:])

    settle(*share)
    grad_all = r.grad_all
    stage(spread("core", lambda p: grad_all.at[:, core], lambda q: grad_all.at[:, q]))
    grad = jnp.dot(
        r.grad_all[...].reshape(4 * own, width), out_full, preferred_element_type=F32
    )
    for k in range(2):
        for s in range(2):
            tile = grad[s * BLOCK : (s + 1) * BLOCK, k * 128 : (k + 1) * 128]
            for a, one in enumerate((crossed(tile), tile)):
                one = jnp.where(left_lanes(one), 0.0, one).astype(BF16)
                r.do_src[2 * k + s, a * BLOCK : (a + 1) * BLOCK] = one

    do_send, do_recv = take.two(SLOTS)
    to_workers(r.do_src, r.do_buf, do_send, do_recv, "start")
    ffn_rows = spread("rows", lambda p: r.ffn_part.at[p], lambda q: r.ffn_parts.at[q], True)
    push(*ffn_rows)
    r.dkv_sum[...] = jnp.zeros_like(r.dkv_sum)
    to_workers(r.do_src, r.do_buf, do_send, do_recv, "wait")
    from_owners(r.do_src, r.do_buf, do_send, do_recv)
    dq_send, dq_recv = take.two(SLOTS)
    for j in range(SLOTS):
        attend_back(r, low, j)
        to_owner(r.dq_buf, r.dq, dq_send, dq_recv, j, "start")
    r.dkv_buf[...] = r.dkv_sum[...].astype(BF16)
    kv_first = [
        spread("x", lambda p: r.dkv_buf.at[:, p, :, 0], lambda q: r.kv_one_a.at[q], True),
        spread("pair", lambda p: r.dkv_buf.at[:, :, p, 1], lambda q: r.kv_one_b.at[q], True),
    ]
    begin(kv_first)
    finish(far)

    @pl.loop(0, 4)
    def _(m):
        for src, dst in ((r.far_a, r.mid_a), (r.far_b, r.mid_b)):
            total = src[0, m].astype(F32)
            for k in range(1, 4):
                total += src[k, m].astype(F32)
            dst[m] = total.astype(BF16)

    finish(kv_first)
    r.kv_sum_a[...] = summed(r.kv_one_a).astype(BF16)
    r.kv_sum_b[...] = summed(r.kv_one_b).astype(BF16)
    kv_second = [
        spread("pair", lambda p: r.kv_sum_a.at[:, p], lambda q: r.kv_two_a.at[q], True),
        spread("x", lambda p: r.kv_sum_b.at[:, p], lambda q: r.kv_two_b.at[q], True),
    ]
    begin(kv_second)
    mid = [
        spread("z", lambda p: r.mid_a.at[p], lambda q: r.mid_far_a.at[q], True),
        spread("x", lambda p: r.mid_b.at[p], lambda q: r.mid_far_b.at[q], True),
    ]
    finish(kv_second)
    r.kv_sum[:, 0] = summed(r.kv_two_a).astype(BF16)
    r.kv_sum[:, 1] = summed(r.kv_two_b).astype(BF16)
    kv_third = spread("z", lambda p: r.kv_sum.at[p], lambda q: r.dkv.at[q], True)
    push(*kv_third)
    begin(mid)
    settle(*kv_third)
    for j in range(SLOTS):
        to_owner(r.dq_buf, r.dq, dq_send, dq_recv, j, "wait")
    from_workers(r.dq_buf, r.dq, dq_send, dq_recv)

    vectors = project_back(r)
    stage(spread("core", lambda p: r.parts_back.at[:, p], lambda q: r.back_half.at[q], True))
    r.back_chip[...] = summed(r.back_half).astype(BF16)
    sums = spread("near", lambda p: r.back_chip.at[p], lambda q: r.landed_back.at[q], True)
    push(*sums)

    @pl.loop(0, 4)
    def _(m):
        at = tiles(m, 256)
        cols = r.grad_in.shape[1]
        step = first_dims(r.hidden[:, at], r.grad_in[...]).astype(BF16)
        r.qkv[m, :, :, :, :, :cols] = step.reshape(4, 2, 2, 16, cols)
        some = r.grad_all[:, :, :, at].reshape(4 * own, 256)
        step = first_dims(some, r.attended[...]).astype(BF16)
        r.qkv[m, :, :, :, :, cols:] = step.reshape(4, 2, 2, 16, r.attended.shape[1])

    pieces = jnp.zeros((NCTX, 8, 128), F32)
    for row, (vector, per) in enumerate(vectors):
        piece = jnp.broadcast_to(owner_pieces(vector, per)[:, None, :], pieces.shape)
        pieces = jnp.where(iota(pieces.shape, 1) == row, piece, pieces)
    r.gain_pieces[...] = pieces.reshape(r.gain_pieces.shape)
    one = [
        spread("x", lambda p: r.qkv.at[:, p, :, 0], lambda q: r.one_a.at[q], True),
        spread("z", lambda p: r.qkv.at[p, :, :, 1], lambda q: r.one_b.at[q], True),
        spread("x", lambda p: r.gain_pieces.at[:, p], lambda q: r.one_g.at[q], True),
    ]
    begin(one)
    finish(mid)
    r.end_ab[:, 0] = summed(r.mid_far_a).astype(BF16)
    r.end_ab[:, 1] = summed(r.mid_far_b).astype(BF16)
    swap = spread("pair", lambda p: r.end_ab.at[p], lambda q: r.ffn_all.at[q], True)
    push(*swap)
    settle(*ffn_rows)
    r.output[...] = (r.residual[...] + summed(r.ffn_parts)).astype(BF16)
    share = [spread("tp", lambda p: r.output, lambda q: r.output_all.at[q], True)]
    rows = r.rows_in[tiles(t, own)].astype(F32)
    scale = row_scale(rows)
    normed = rows * scale
    settle(*sums)
    result = r.grad_residual[...] + row_back(
        summed(r.landed_back), normed, scale, r.gain_attn[...]
    )
    r.input_bf[...] = result.astype(BF16)
    share.append(spread("tp", lambda p: r.input_bf, lambda q: r.input_all.at[q], True))
    begin(share)
    finish(one)
    r.sum_a[...] = summed(r.one_a).astype(BF16)
    r.sum_b[...] = summed(r.one_b).astype(BF16)
    r.sum_g[...] = summed(r.one_g)
    stage(
        spread("z", lambda p: r.sum_a.at[p], lambda q: r.two_a.at[q], True),
        spread("x", lambda p: r.sum_b.at[p], lambda q: r.two_b.at[q], True),
        spread("z", lambda p: r.sum_g.at[p], lambda q: r.two_g.at[q], True),
    )
    r.part_a[...] = summed(r.two_a).astype(BF16)
    r.part_b[...] = summed(r.two_b).astype(BF16)
    r.part_g[...] = summed(r.two_g)
    stage(
        spread("pair", lambda p: r.part_a.at[p], lambda q: r.three_a.at[q], True),
        spread("pair", lambda p: r.part_b.at[p], lambda q: r.three_b.at[q], True),
        spread("pair", lambda p: r.part_g.at[p], lambda q: r.three_g.at[q], True),
    )
    r.gain_sum[...] = summed(r.three_g)
    share.append(spread("tp", lambda p: r.gain_sum, lambda q: r.gain_tp.at[q], True))
    push(*share[-1])
    r.qkv_grad[0] = summed(r.three_a)
    r.qkv_grad[1] = summed(r.three_b)
    finish(share)
    settle(*swap)


def whole(weights, gains, ffn, wo, cot, rows_in, cosine, sine):
    rows, width = rows_in.shape
    arrays = scratch_arrays(rows, width, weights.shape[2], wo.shape[2])
    names = INPUTS + OUTPUTS + tuple(arrays)
    return pl.pallas_call(
        functools.partial(whole_body, names),
        out_shape=[
            jax.ShapeDtypeStruct((2, 16, weights.shape[2] + wo.shape[2]), F32),
            jax.ShapeDtypeStruct(ffn.shape, BF16),
            jax.ShapeDtypeStruct((4, rows // 4, width), BF16),
            jax.ShapeDtypeStruct((4, rows // 4, width), BF16),
            jax.ShapeDtypeStruct((4, 8, 128), F32),
        ],
        in_specs=[ANY] * 5 + [VMEM] * 3,
        out_specs=[VMEM] + [ANY] * 4,
        scratch_shapes=[pltpu.VMEM(shape, dtype) for shape, dtype in arrays.values()]
        + [pltpu.SemaphoreType.DMA((SEMAPHORES,))],
        compiler_params=pltpu.CompilerParams(
            collective_id=1, has_side_effects=True, vmem_limit_bytes=60 * 2**20
        ),
        name="block",
    )(weights, gains, ffn, wo, cot, rows_in, cosine, sine)


def rope_tables(tokens, offset):
    half = HEAD_SIZE // 2
    inverse = ROPE_BASE ** (-(jnp.arange(half, dtype=F32) * 2.0 / HEAD_SIZE))
    steps = (offset + jnp.arange(tokens, dtype=jnp.int32)).astype(F32)
    angles = steps[:, None] * jnp.tile(inverse, 4)[None, :]
    signs = jnp.where(jnp.arange(4 * half) % HEAD_SIZE < half, -1.0, 1.0)
    return jnp.cos(angles), jnp.sin(angles) * signs[None, :]


def halves(*weights):
    rows, cols = weights[0].shape
    w = jnp.stack(weights).reshape(len(weights), rows, 2, cols // 2)
    w = jnp.pad(w, ((0, 0), (0, 0), (0, 0), (0, UNITS - cols // 2)))
    return w.transpose(2, 1, 0, 3).reshape(2, rows, len(weights) * UNITS)


def local(
    block_input, cotangent, w_query, key_weight, w_value, w_out, w_gate, w_up, w_down,
    norm_gains, head_gains,
):
    seqs, tokens, width = block_input.shape
    rows = seqs * tokens
    unit_half = w_gate.shape[1] // 2
    rows_in = block_input.reshape(rows, width)
    cot_rows = cotangent.reshape(rows, width)
    cosine, sine = rope_tables(tokens, lax.axis_index("ctx") * tokens)
    weight_rows = jnp.concatenate([w_query, key_weight, w_value], axis=1)
    gains = jnp.pad(norm_gains, ((0, 14), (0, 96))) + jnp.pad(head_gains, ((2, 12), (0, 126)))
    ffn = halves(w_gate, w_up, w_down)
    qkv_grad, pair_grads, output_all, input_all, gain_tp = whole(
        weight_rows.reshape(2, 16, weight_rows.shape[1]),
        gains,
        ffn.reshape(2, 2, 16, ffn.shape[2]),
        w_out.reshape(2, 16, w_out.shape[1]),
        cot_rows,
        rows_in,
        cosine,
        sine,
    )
    pair_grads = pair_grads.reshape(ffn.shape)
    pair_grads = pair_grads.astype(F32)
    gain_sum = jnp.sum(gain_tp, axis=0)
    qkv_grad = qkv_grad.reshape(32, 768)

    def joined(first):
        last = first + unit_half
        return jnp.concatenate([pair_grads[0, :, first:last], pair_grads[1, :, first:last]], axis=1)

    gate_grad, up_grad, down_grad = joined(0), joined(UNITS), joined(2 * UNITS)
    return (
        output_all.reshape(seqs, tokens, width),
        input_all.astype(F32).reshape(seqs, tokens, width),
        qkv_grad[:, :256],
        qkv_grad[:, 256:384],
        qkv_grad[:, 384:512],
        qkv_grad[:, 512:],
        gate_grad,
        up_grad,
        down_grad,
        gain_sum[0:2, :32],
        gain_sum[2:4, :2],
    )


def solution(mesh):
    tokens, weights = P(None, "ctx", None), P("ctx", "tp")
    return jax.shard_map(
        local,
        mesh=mesh,
        in_specs=(tokens,) * 2 + (weights,) * 7 + (P(None, "ctx"),) * 2,
        out_specs=(tokens,) * 2 + (weights,) * 7 + (P(None, "ctx"),) * 2,
        check_vma=False,
    )
```

```python
import functools
import types

import jax
import jax.numpy as jnp
from jax import lax
from jax.experimental import pallas as pl
from jax.experimental.pallas import tpu as pltpu
from jax.sharding import PartitionSpec as P

HEAD_SIZE = 64
EPSILON = 1e-06
ROPE_BASE = 1000000.0
MESH = pl.DeviceIdType.MESH
F32 = jnp.float32
BF16 = jnp.bfloat16
ANY = pl.BlockSpec(memory_space=pl.ANY)
VMEM = pl.BlockSpec(memory_space=pltpu.VMEM)
NCTX = 32
PAIRS = 4
WORKERS = 8
SLOTS = 4
BLOCK = 128
CHUNK = 512


def group(kind):
    c, t = lax.axis_index("ctx"), lax.axis_index("tp")
    h = lax.rem(c, 2)
    if kind == "ctx":
        return NCTX, c, lambda p: (p, t)
    if kind == "tp":
        return 4, t, lambda p: (c, p)
    if kind == "pair":
        return 2, h, lambda p: (c - h + p, t)
    z, x, core = c // 8, lax.rem(c // 2, 4), lax.rem(t, 2)
    if kind == "z":
        return 4, z, lambda p: (c + (p - z) * 8, t)
    if kind == "x":
        return 4, x, lambda p: (c + (p - x) * 2, t)
    if kind == "core":
        return 2, core, lambda p: (c, t - core + p)
    if kind == "near":
        return 2, t // 2, lambda p: (c, p * 2 + core)
    if kind == "ring":
        return 4, h * 2 + t // 2, lambda p: (c - h + p // 2, lax.rem(p, 2) * 2 + core)
    return 8, h * 4 + t, lambda p: (c - h + p // 4, lax.rem(p, 4))


def push(kind, src_of, dst_of, send, recv, local=False):
    n, me, dev = group(kind)

    @pl.loop(1, n)
    def _(i):
        p = lax.rem(me + i, n)
        pltpu.make_async_remote_copy(
            src_ref=src_of(p),
            dst_ref=dst_of(me),
            send_sem=send.at[p],
            recv_sem=recv.at[me],
            device_id=dev(p),
            device_id_type=MESH,
        ).start()

    if local:
        pltpu.make_async_copy(src_of(me), dst_of(me), recv.at[me]).start()


def settle(kind, src_of, dst_of, send, recv, local=False):
    n, me, dev = group(kind)

    @pl.loop(1, n)
    def _(i):
        p = lax.rem(me + i, n)
        copy = pltpu.make_async_remote_copy(
            src_ref=src_of(p),
            dst_ref=dst_of(p),
            send_sem=send.at[p],
            recv_sem=recv.at[p],
            device_id=dev(p),
            device_id_type=MESH,
        )
        copy.wait_send()
        copy.wait_recv()

    if local:
        pltpu.make_async_copy(src_of(me), dst_of(me), recv.at[me]).wait()


def stage(*moves):
    for move in moves:
        push(*move)
    for move in moves:
        settle(*move)


class Sems:
    def __init__(self, ref):
        self.ref, self.used = ref, 0

    def two(self, n):
        at = self.used
        self.used += 2 * n
        return self.ref.at[pl.ds(at, n)], self.ref.at[pl.ds(at + n, n)]


def position():
    c = lax.axis_index("ctx")
    return c // 8, lax.rem(c // 2, 4), lax.rem(c, 2)


def iota(shape, axis):
    return lax.broadcasted_iota(jnp.int32, shape, axis)


def two_parts(v):
    high = v.astype(BF16)
    return high, (v - high.astype(F32)).astype(BF16)


def exact_dot(v, pattern):
    high, low = two_parts(v)
    return jnp.dot(high, pattern, preferred_element_type=F32) + jnp.dot(
        low, pattern, preferred_element_type=F32
    )


def head_mean(v):
    n = v.shape[1]
    same = lax.div(iota((n, n), 0), HEAD_SIZE) == lax.div(iota((n, n), 1), HEAD_SIZE)
    return exact_dot(v, jnp.where(same, 1.0 / HEAD_SIZE, 0.0).astype(BF16))


def head_scale(v):
    return lax.rsqrt(head_mean(v * v) + EPSILON)


def turned(u, cosine, sine):
    half, n = HEAD_SIZE // 2, 2 * HEAD_SIZE
    first = lax.rem(iota(u.shape, 1), HEAD_SIZE) < half
    other = jnp.where(first, pltpu.roll(u, n - half, 1), pltpu.roll(u, half, 1))
    return u * cosine + other * sine


def crossed(tile):
    return pltpu.roll(tile, HEAD_SIZE, 1)


def left_lanes(tile):
    return iota(tile.shape, 1) < HEAD_SIZE


def spread_gain(pieces, row, per, lanes):
    n = pieces.shape[0]
    pick = iota((NCTX, n), 1) == iota((NCTX, n), 0) * (n // NCTX) + row
    mine = jnp.dot(pick.astype(F32).astype(BF16), pieces, preferred_element_type=F32).astype(BF16)
    pattern = (lax.rem(iota((128, lanes), 1), per) == iota((128, lanes), 0)).astype(F32)
    wide = jnp.dot(mine, pattern.astype(BF16), preferred_element_type=F32)
    owner = lax.div(lax.rem(iota(wide.shape, 1), NCTX * per), per)
    return jnp.sum(jnp.where(owner == iota(wide.shape, 0), wide, 0.0), axis=0, keepdims=True)


def owner_pieces(vector, per):
    lanes = vector.shape[1]
    shape = (NCTX, lanes)
    owner = lax.div(lax.rem(iota(shape, 1), NCTX * per), per)
    parts = jnp.where(owner == iota(shape, 0), jnp.broadcast_to(vector, shape), 0.0)
    pattern = (lax.rem(iota((lanes, 128), 0), per) == iota((lanes, 128), 1)).astype(F32)
    return exact_dot(parts, pattern.astype(BF16))


def row_scale(rows):
    return lax.rsqrt(jnp.mean(rows * rows, axis=1, keepdims=True) + EPSILON)


def twice(table):
    return jnp.concatenate([table[...], table[...]], axis=0)


def places():
    c, t = lax.axis_index("ctx"), lax.axis_index("tp")
    slot, low = c // WORKERS, lax.rem(c, WORKERS)
    to = low + lax.rem(slot, 2) * (WORKERS - 1 - 2 * low)
    return c, t, slot, low, to


def block_of(low, j):
    return j * WORKERS + (low if j % 2 == 0 else WORKERS - 1 - low)


def greet_attention(kinds):
    c, t, slot, low, to = places()
    barrier = pltpu.get_barrier_semaphore()
    total = 0
    others = [p * WORKERS + to for p in range(PAIRS)] + [block_of(low, j) for j in range(SLOTS)]
    for other in others:

        @pl.when(other != c)
        def _():
            pl.semaphore_signal(barrier, inc=1, device_id=(other, t), device_id_type=MESH)

        total = total + jnp.where(other != c, 1, 0)
    for kind in kinds:
        n, me, dev = group(kind)

        @pl.loop(1, n)
        def _(i):
            pl.semaphore_signal(
                barrier, inc=1, device_id=dev(lax.rem(me + i, n)), device_id_type=MESH
            )

        total = total + (n - 1)
    pl.semaphore_wait(barrier, total)


def to_workers(src, dst, send, recv, act):
    c, t, slot, low, to = places()
    for p in range(PAIRS):
        target = p * WORKERS + to
        far = pltpu.make_async_remote_copy(
            src_ref=src.at[p],
            dst_ref=dst.at[slot],
            send_sem=send.at[p],
            recv_sem=recv.at[slot],
            device_id=(target, t),
            device_id_type=MESH,
        )
        near = pltpu.make_async_copy(src.at[p], dst.at[slot], send.at[p])

        @pl.when(target != c)
        def _():
            far.start() if act == "start" else far.wait_send()

        @pl.when(target == c)
        def _():
            near.start() if act == "start" else near.wait()


def from_owners(src, dst, send, recv):
    c, t, slot, low, to = places()
    for j in range(SLOTS):
        owner = block_of(low, j)

        @pl.when(owner != c)
        def _():
            pltpu.make_async_remote_copy(
                src_ref=src.at[j],
                dst_ref=dst.at[j],
                send_sem=send.at[j],
                recv_sem=recv.at[j],
                device_id=(owner, t),
                device_id_type=MESH,
            ).wait_recv()


def to_owner(src, dst, send, recv, j, act):
    c, t, slot, low, to = places()
    owner = block_of(low, j)
    far = pltpu.make_async_remote_copy(
        src_ref=src.at[j],
        dst_ref=dst.at[slot],
        send_sem=send.at[j],
        recv_sem=recv.at[slot],
        device_id=(owner, t),
        device_id_type=MESH,
    )
    near = pltpu.make_async_copy(src.at[j], dst.at[slot], send.at[j])

    @pl.when(owner != c)
    def _():
        far.start() if act == "start" else far.wait_send()

    @pl.when(owner == c)
    def _():
        near.start() if act == "start" else near.wait()


def from_workers(src, dst, send, recv):
    c, t, slot, low, to = places()
    for p in range(PAIRS):
        target = p * WORKERS + to

        @pl.when(target != c)
        def _():
            pltpu.make_async_remote_copy(
                src_ref=src.at[p],
                dst_ref=dst.at[p],
                send_sem=send.at[p],
                recv_sem=recv.at[p],
                device_id=(target, t),
                device_id_type=MESH,
            ).wait_recv()


def last_dims(a, b):
    return lax.dot_general(a, b, (((1,), (1,)), ((), ())), preferred_element_type=F32)


def first_dims(a, b):
    return lax.dot_general(a, b, (((0,), (0,)), ((), ())), preferred_element_type=F32)


def causal_mask(b, i):
    shape = (2 * BLOCK, CHUNK)
    rows = lax.broadcasted_iota(jnp.int32, shape, 0)
    token = b * BLOCK + jnp.where(rows >= BLOCK, rows - BLOCK, rows)
    key = i * CHUNK + lax.broadcasted_iota(jnp.int32, shape, 1)
    return token >= key


def row_back(grads, normed, scale, gain):
    scaled = grads * gain
    return scale * (scaled - normed * jnp.mean(scaled * normed, axis=1, keepdims=True))


def summed(ref):
    total = ref[0].astype(F32)
    for k in range(1, ref.shape[0]):
        total += ref[k].astype(F32)
    return total


UNITS = 640
INPUTS = ("weights", "gains", "ffn", "wo", "cot", "rows_in", "cosine", "sine")
OUTPUTS = ("qkv_grad", "ffn_all", "output_all", "input_all", "gain_tp")
SIZES = {"tp": 4, "pair": 2, "rows": 8, "z": 4, "x": 4, "core": 2, "ring": 4, "near": 2}
SEMAPHORES = 484


def scratch_arrays(rows, width, qkv_cols, out_cols):
    own, half = rows // 4, BLOCK // 2
    stack = (SLOTS, 2 * BLOCK, BLOCK)
    grid, piece = (4, 4, 2, 2), (16, qkv_cols + out_cols)
    units = (16, 3 * UNITS)
    return dict(
        w_all=((*grid, 16, qkv_cols), BF16),
        gains_all=((4, 4, 2, 16, 128), BF16),
        w_ffn=((*grid, *units), BF16),
        wo_all=((*grid, 16, out_cols), BF16),
        cot_all=((2, rows, width), BF16),
        hidden=((rows, width), BF16),
        raw=((rows, qkv_cols), F32),
        q_src=(stack, BF16),
        kv_src=((PAIRS, 2, half, BLOCK), BF16),
        gain_attn=((1, width), F32),
        gain_ffn=((1, width), F32),
        gain_query=((1, 128), F32),
        gain_key=((1, 128), F32),
        q_buf=(stack, BF16),
        kv_buf=((*grid, half, BLOCK), BF16),
        o_buf=(stack, BF16),
        log_buf=(stack, F32),
        att=(stack, BF16),
        acc=((2 * BLOCK, BLOCK), F32),
        den=((2 * BLOCK, BLOCK), F32),
        attended=((rows, out_cols), BF16),
        parts=((2, 2, own, width), BF16),
        parts_half=((2, 2, own, width), BF16),
        parts_chip=((2, own, width), BF16),
        landed=((2, own, width), BF16),
        residual=((own, width), F32),
        hidden_own=((own, width), BF16),
        hidden_all=((4, 2, own, width), BF16),
        grad_units=((2 * rows, UNITS), F32),
        units=((2 * rows, UNITS), BF16),
        units_in=((2 * rows, 2 * UNITS), BF16),
        back=((4, 2, own, width), BF16),
        halved=((2, 4, own, width), BF16),
        chip=((4, own, width), BF16),
        ringed=((4, own, width), BF16),
        grad_bf=((own, width), BF16),
        grad_all=((2, 2, own, width), BF16),
        grad_residual=((own, width), F32),
        ffn_gain=((1, width), F32),
        grads=((*grid, *units), BF16),
        ffn_part=((8, own, width), BF16),
        ffn_parts=((8, own, width), BF16),
        far_a=((4, 4, 2, *units), BF16),
        far_b=((4, 4, 2, *units), BF16),
        mid_a=((4, 2, *units), BF16),
        mid_b=((4, 2, *units), BF16),
        mid_far_a=((4, 2, *units), BF16),
        mid_far_b=((4, 2, *units), BF16),
        end_ab=((2, 2, *units), BF16),
        do_src=(stack, BF16),
        do_buf=(stack, BF16),
        dq_buf=(stack, BF16),
        dq=(stack, BF16),
        dkv_sum=((*grid, half, BLOCK), F32),
        dkv_buf=((*grid, half, BLOCK), BF16),
        kv_one_a=((4, 4, 2, half, BLOCK), BF16),
        kv_one_b=((4, 2, 4, half, BLOCK), BF16),
        kv_sum_a=((4, 2, half, BLOCK), BF16),
        kv_sum_b=((4, 4, half, BLOCK), BF16),
        kv_two_a=((4, 2, half, BLOCK), BF16),
        kv_two_b=((4, 4, half, BLOCK), BF16),
        kv_sum=((4, 2, half, BLOCK), BF16),
        dkv=((PAIRS, 2, half, BLOCK), BF16),
        parts_back=((2, 2, own, width), BF16),
        back_half=((2, 2, own, width), BF16),
        back_chip=((2, own, width), BF16),
        landed_back=((2, own, width), BF16),
        grad_in=((rows, qkv_cols), BF16),
        gain_pieces=((4, 4, 2, 8, 128), F32),
        output=((own, width), BF16),
        input_bf=((own, width), BF16),
        qkv=((*grid, *piece), BF16),
        one_a=((4, 4, 2, *piece), BF16),
        one_b=((4, 4, 2, *piece), BF16),
        one_g=((4, 4, 2, 8, 128), F32),
        sum_a=((4, 2, *piece), BF16),
        sum_b=((4, 2, *piece), BF16),
        sum_g=((4, 2, 8, 128), F32),
        two_a=((4, 2, *piece), BF16),
        two_b=((4, 2, *piece), BF16),
        two_g=((4, 2, 8, 128), F32),
        part_a=((2, *piece), BF16),
        part_b=((2, *piece), BF16),
        part_g=((2, 8, 128), F32),
        three_a=((2, *piece), BF16),
        three_b=((2, *piece), BF16),
        three_g=((2, 8, 128), F32),
        gain_sum=((8, 128), F32),
    )


def project_keys(r):
    pieces = r.gains_all[...].reshape(NCTX * 16, 128)
    r.gain_attn[...] = spread_gain(pieces, 0, 32, r.gain_attn.shape[1])
    r.gain_query[...] = spread_gain(pieces, 2, 2, 128)
    r.gain_key[...] = spread_gain(pieces, 3, 2, 128)
    rows = r.rows_in[...].astype(F32)
    r.hidden[...] = (rows * row_scale(rows) * r.gain_attn[...]).astype(BF16)
    weights = r.w_all[:, :, :, :, :, 256:].reshape(r.hidden.shape[1], 256)
    r.raw[:, 256:] = jnp.dot(r.hidden[...], weights, preferred_element_type=F32)
    tile = r.raw[:, 256:384]
    keys = turned(tile * head_scale(tile) * r.gain_key[...], twice(r.cosine), twice(r.sine))
    values = r.raw[:, 384:512]
    for k in range(2):
        key, value = (keys, crossed(values)) if k == 0 else (crossed(keys), values)
        one = jnp.where(left_lanes(key), key, value).astype(BF16)
        for s in range(2):
            part = one[s * BLOCK : (s + 1) * BLOCK]
            r.kv_src[2 * k + s] = part.reshape(2, BLOCK // 2, 128)


def project_queries(r):
    weights = r.w_all[:, :, :, :, :, :256].reshape(r.hidden.shape[1], 256)
    r.raw[:, :256] = jnp.dot(r.hidden[...], weights, preferred_element_type=F32)
    cos, sin = twice(r.cosine), twice(r.sine)
    for k in range(2):
        tile = r.raw[:, k * 128 : k * 128 + 128]
        tile = turned(tile * head_scale(tile) * r.gain_query[...], cos, sin) * (HEAD_SIZE**-0.5)
        for a, one in enumerate((tile, crossed(tile))):
            one = jnp.where(left_lanes(one), one, 0.0).astype(BF16)
            for s in range(2):
                r.q_src[2 * k + s, a * BLOCK : (a + 1) * BLOCK] = one[s * BLOCK : (s + 1) * BLOCK]
    pieces = r.gains_all[...].reshape(NCTX * 16, 128)
    r.gain_ffn[...] = spread_gain(pieces, 1, 32, r.gain_ffn.shape[1])


def attend(r, low, j):
    b = block_of(low, j)
    r.acc[...] = jnp.zeros_like(r.acc)
    r.den[...] = jnp.zeros_like(r.den)

    def chunk(i, masked):
        kv = r.kv_buf[i // 2, pl.ds(2 * lax.rem(i, 2), 2)].reshape(CHUNK, BLOCK)
        powered = jnp.exp(last_dims(r.q_buf[j], kv))
        if masked:
            powered = jnp.where(causal_mask(b, i), powered, 0.0)
        r.den[...] += sum(powered[:, k : k + BLOCK] for k in range(0, CHUNK, BLOCK))
        r.acc[...] += jnp.dot(powered.astype(BF16), kv, preferred_element_type=F32)

    last = b // (CHUNK // BLOCK)
    pl.loop(0, last)(lambda i: chunk(i, False))
    chunk(last, True)
    total = jnp.sum(r.den[...], axis=1, keepdims=True)
    lanes = iota((2 * BLOCK, BLOCK), 1)
    r.o_buf[j] = jnp.where(lanes >= HEAD_SIZE, r.acc[...] / total, 0.0).astype(BF16)
    r.log_buf[j] = jnp.broadcast_to(jnp.log(total), (2 * BLOCK, BLOCK))


def attend_back(r, low, j):
    b = block_of(low, j)
    r.acc[...] = jnp.zeros_like(r.acc)
    delta = jnp.sum(r.do_buf[j].astype(F32) * r.o_buf[j].astype(F32), axis=1, keepdims=True)

    def chunk(i, masked):
        q, do, logs = r.q_buf[j], r.do_buf[j], r.log_buf[j]
        kv = r.kv_buf[i // 2, pl.ds(2 * lax.rem(i, 2), 2)].reshape(CHUNK, BLOCK)
        probs = jnp.exp(last_dims(q, kv) - jnp.concatenate([logs] * (CHUNK // BLOCK), axis=1))
        if masked:
            probs = jnp.where(causal_mask(b, i), probs, 0.0)
        grads = (probs * (last_dims(do, kv) - delta)).astype(BF16)
        r.acc[...] += jnp.dot(grads, kv, preferred_element_type=F32)
        update = first_dims(grads, q) + first_dims(probs.astype(BF16), do)
        at = pl.ds(2 * lax.rem(i, 2), 2)
        r.dkv_sum[i // 2, at] += update.reshape(2, 2, 2, BLOCK // 2, BLOCK)

    last = b // (CHUNK // BLOCK)
    pl.loop(0, last)(lambda i: chunk(i, False))
    chunk(last, True)
    r.dq_buf[j] = (r.acc[...] * (HEAD_SIZE**-0.5)).astype(BF16)


def tiles(m, n):
    return pl.ds(pl.multiple_of(m * n, n), n)


def project_back(r):
    cos, sin = twice(r.cosine), -twice(r.sine)
    own, width = r.residual.shape

    def head_back(u, tile, gain_row):
        turn = turned(u, cos, sin)
        scale = head_scale(tile)
        hat = tile * scale
        scaled = turn * gain_row
        back = scale * (scaled - hat * head_mean(scaled * hat))
        return back.astype(BF16), jnp.sum(turn * hat, axis=0, keepdims=True)

    def both(first, second):
        return jnp.concatenate([first.astype(F32), second.astype(F32)], axis=0)

    query_gain = jnp.zeros((1, 128), F32)
    for k in range(2):
        first = both(r.dq[2 * k, :BLOCK], r.dq[2 * k + 1, :BLOCK])
        second = crossed(both(r.dq[2 * k, BLOCK:], r.dq[2 * k + 1, BLOCK:]))
        lanes = slice(k * 128, (k + 1) * 128)
        back, part = head_back(
            jnp.where(left_lanes(first), first, second), r.raw[:, lanes], r.gain_query[...]
        )
        r.grad_in[:, lanes] = back
        query_gain = query_gain + part
    first, second = [
        both(r.dkv[2 * k].reshape(BLOCK, 128), r.dkv[2 * k + 1].reshape(BLOCK, 128))
        for k in range(2)
    ]
    left = left_lanes(first)
    back, key_gain = head_back(
        jnp.where(left, first, crossed(second)), r.raw[:, 256:384], r.gain_key[...]
    )
    r.grad_in[:, 256:384] = back
    r.grad_in[:, 384:] = jnp.where(left, crossed(first), second).astype(BF16)
    attn_gain = jnp.zeros((1, width), F32)
    weights = r.w_all[...].reshape(width, r.grad_in.shape[1])
    for q in range(4):
        at = slice(q * own, (q + 1) * own)
        back = last_dims(r.grad_in[at], weights)
        r.parts_back[q // 2, q % 2] = back.astype(BF16)
        rows = r.rows_in[at].astype(F32)
        attn_gain = attn_gain + jnp.sum(back * (rows * row_scale(rows)), axis=0, keepdims=True)
    return ((attn_gain, 32), (r.ffn_gain[...], 32), (query_gain, 2), (key_gain, 2))


def begin(moves):
    for move in moves:
        push(*move)


def finish(moves):
    for move in moves:
        settle(*move)


def whole_body(names, *refs):
    r = types.SimpleNamespace(**dict(zip(names, refs)))
    take = Sems(refs[-1])
    c, t, slot, low, to = places()
    z, x, h = position()
    core = lax.rem(t, 2)
    own, width = r.residual.shape

    def spread(kind, src_of, dst_of, local=False):
        return (kind, src_of, dst_of, *take.two(SIZES[kind]), local)

    def gathered(ref):
        second = [
            spread("x", lambda p: ref.at[z, x, :, 0], lambda q: ref.at[z, q, :, 0]),
            spread("z", lambda p: ref.at[z, x, :, 1], lambda q: ref.at[q, x, :, 1]),
        ]
        third = [
            spread("z", lambda p: ref.at[z, :, :, 0], lambda q: ref.at[q, :, :, 0]),
            spread("x", lambda p: ref.at[:, x, :, 1], lambda q: ref.at[:, q, :, 1]),
        ]
        return second, third

    greet_attention(["z", "x", "rows"])
    first = [
        spread("pair", lambda p: r.weights, lambda q: r.w_all.at[z, x, q], True),
        spread("pair", lambda p: r.gains, lambda q: r.gains_all.at[z, x, q], True),
    ]
    late = [
        spread("pair", lambda p: r.wo, lambda q: r.wo_all.at[z, x, q], True),
        spread("pair", lambda p: r.ffn.at[p], lambda q: r.w_ffn.at[z, x, q], True),
    ]
    begin(first)
    begin(late)
    finish(first)
    second, third = gathered(r.w_all)
    second.append(spread("x", lambda p: r.gains_all.at[z, x], lambda q: r.gains_all.at[z, q]))
    third.append(spread("z", lambda p: r.gains_all.at[z], lambda q: r.gains_all.at[q]))
    stage(*second)
    stage(*third)
    finish(late)
    out_second, out_third = gathered(r.wo_all)
    ffn_second, ffn_third = gathered(r.w_ffn)
    begin(out_second + ffn_second)
    project_keys(r)

    q_send, q_recv = take.two(SLOTS)
    near = spread("z", lambda p: r.kv_src.at[p], lambda q: r.kv_buf.at[q, x, h], True)
    push(*near)
    project_queries(r)
    to_workers(r.q_src, r.q_buf, q_send, q_recv, "start")
    settle(*near)
    kv = r.kv_buf
    stage(
        spread("x", lambda p: kv.at[:, x, h, 0], lambda q: kv.at[:, q, h, 0]),
        spread("pair", lambda p: kv.at[:, x, h, 1], lambda q: kv.at[:, x, q, 1]),
    )
    stage(
        spread("pair", lambda p: kv.at[:, :, h, 0], lambda q: kv.at[:, :, q, 0]),
        spread("x", lambda p: kv.at[:, x, :, 1], lambda q: kv.at[:, q, :, 1]),
    )
    finish(out_second + ffn_second)
    begin(out_third)
    begin(ffn_third)
    cot_swap = spread("pair", lambda p: r.cot, lambda q: r.cot_all.at[q], True)
    push(*cot_swap)
    to_workers(r.q_src, r.q_buf, q_send, q_recv, "wait")
    from_owners(r.q_src, r.q_buf, q_send, q_recv)
    o_send, o_recv = take.two(SLOTS)
    for j in range(SLOTS):
        attend(r, low, j)
        to_owner(r.o_buf, r.att, o_send, o_recv, j, "start")
    for j in range(SLOTS):
        to_owner(r.o_buf, r.att, o_send, o_recv, j, "wait")
    from_workers(r.o_buf, r.att, o_send, o_recv)

    for k in range(2):
        for s in range(2):
            left = crossed(r.att[2 * k + s, :BLOCK].astype(F32))
            right = r.att[2 * k + s, BLOCK:].astype(F32)
            one = jnp.where(left_lanes(left), left, right).astype(BF16)
            r.attended[s * BLOCK : (s + 1) * BLOCK, k * 128 : (k + 1) * 128] = one
    finish(out_third)
    out_full = r.wo_all[...].reshape(width, r.attended.shape[1])
    r.parts[...] = last_dims(r.attended[...], out_full).astype(BF16).reshape(r.parts.shape)
    stage(spread("core", lambda p: r.parts.at[:, p], lambda q: r.parts_half.at[q], True))
    r.parts_chip[...] = summed(r.parts_half).astype(BF16)
    stage(spread("near", lambda p: r.parts_chip.at[p], lambda q: r.landed.at[q], True))
    rows = r.rows_in[tiles(t, own)].astype(F32) + summed(r.landed)
    r.residual[...] = rows
    r.hidden_own[...] = (rows * row_scale(rows) * r.gain_ffn[...]).astype(BF16)
    ring = spread("ring", lambda p: r.hidden_own, lambda q: r.hidden_all.at[q, core], True)
    push(*ring)
    settle(*cot_swap)
    finish(ffn_third)
    w = r.w_ffn.reshape(width, 3 * UNITS)
    cot = r.cot_all.reshape(8 * own, width)

    @pl.loop(0, 4)
    def _(m):
        at = tiles(m, 2 * own)
        r.grad_units[at] = jnp.dot(cot[at], w[:, 2 * UNITS :], preferred_element_type=F32)

    settle(*ring)
    hidden = r.hidden_all
    stage(spread("core", lambda p: hidden.at[:, core], lambda q: hidden.at[:, q]))

    @pl.loop(0, 2)
    def _(m):
        at = tiles(m, 4 * own)
        some = hidden[pl.ds(2 * m, 2)].reshape(4 * own, width)
        gate = jnp.dot(some, w[:, :UNITS], preferred_element_type=F32)
        up = jnp.dot(some, w[:, UNITS : 2 * UNITS], preferred_element_type=F32)
        sigmoid = jax.nn.sigmoid(gate)
        activated = gate * sigmoid
        r.units[at] = (activated * up).astype(BF16)
        grad = r.grad_units[at]
        r.units_in[at, :UNITS] = (grad * up * sigmoid * (1.0 + gate * (1.0 - sigmoid))).astype(BF16)
        r.units_in[at, UNITS:] = (grad * activated).astype(BF16)
        step = last_dims(r.units_in[at], w[:, : 2 * UNITS]).astype(BF16)
        r.back[pl.ds(2 * m, 2)] = step.reshape(2, *r.back.shape[1:])

    both = spread("core", lambda p: r.back.at[:, p], lambda q: r.halved.at[q], True)
    push(*both)

    @pl.loop(0, 4)
    def _(m):
        step = first_dims(cot[:, tiles(m, 256)], r.units[...]).astype(BF16)
        r.grads[m, :, :, :, :, 2 * UNITS :] = step.reshape(4, 2, 2, 16, UNITS)

    settle(*both)
    r.chip[...] = summed(r.halved).astype(BF16)
    ring = spread("ring", lambda p: r.chip.at[p], lambda q: r.ringed.at[q], True)
    push(*ring)

    @pl.loop(0, 4)
    def _(m):
        some = hidden[:, :, :, tiles(m, 256)].reshape(8 * own, 256)
        step = first_dims(some, r.units_in[...]).astype(BF16)
        r.grads[m, :, :, :, :, : 2 * UNITS] = step.reshape(4, 2, 2, 16, 2 * UNITS)

    far = [
        spread("x", lambda p: r.grads.at[:, p, :, 0], lambda q: r.far_a.at[q], True),
        spread("z", lambda p: r.grads.at[p, :, :, 1], lambda q: r.far_b.at[q], True),
    ]
    begin(far)
    settle(*ring)
    total = summed(r.ringed)
    rows = r.residual[...]
    scale = row_scale(rows)
    normed = rows * scale
    cot_own = cot[tiles(h * 4 + t, own)].astype(F32)
    result = cot_own + row_back(total, normed, scale, r.gain_ffn[...])
    r.grad_bf[...] = result.astype(BF16)
    share = spread("near", lambda p: r.grad_bf, lambda q: r.grad_all.at[q, core], True)
    push(*share)
    r.grad_residual[...] = result
    r.ffn_gain[...] = jnp.sum(total * normed, axis=0, keepdims=True)

    @pl.loop(0, 2)
    def _(m):
        step = last_dims(r.units[tiles(m, 4 * own)], w[:, 2 * UNITS :]).astype(BF16)
        r.ffn_part[pl.ds(4 * m, 4)] = step.reshape(4, *r.ffn_part.shape[1:])

    settle(*share)
    grad_all = r.grad_all
    stage(spread("core", lambda p: grad_all.at[:, core], lambda q: grad_all.at[:, q]))
    grad = jnp.dot(
        r.grad_all[...].reshape(4 * own, width), out_full, preferred_element_type=F32
    )
    for k in range(2):
        for s in range(2):
            tile = grad[s * BLOCK : (s + 1) * BLOCK, k * 128 : (k + 1) * 128]
            for a, one in enumerate((crossed(tile), tile)):
                one = jnp.where(left_lanes(one), 0.0, one).astype(BF16)
                r.do_src[2 * k + s, a * BLOCK : (a + 1) * BLOCK] = one

    do_send, do_recv = take.two(SLOTS)
    to_workers(r.do_src, r.do_buf, do_send, do_recv, "start")
    ffn_rows = spread("rows", lambda p: r.ffn_part.at[p], lambda q: r.ffn_parts.at[q], True)
    push(*ffn_rows)
    r.dkv_sum[...] = jnp.zeros_like(r.dkv_sum)
    to_workers(r.do_src, r.do_buf, do_send, do_recv, "wait")
    from_owners(r.do_src, r.do_buf, do_send, do_recv)
    dq_send, dq_recv = take.two(SLOTS)

    def kv_first(k):
        r.dkv_buf[k] = r.dkv_sum[k].astype(BF16)
        moves = [
            spread("x", lambda p: r.dkv_buf.at[k, p, :, 0], lambda q: r.kv_one_a.at[k, q], True),
            spread("pair", lambda p: r.dkv_buf.at[k, :, p, 1], lambda q: r.kv_one_b.at[k, q], True),
        ]
        begin(moves)
        return moves

    def kv_second(k, moves):
        finish(moves)
        r.kv_sum_a[k] = summed(r.kv_one_a.at[k]).astype(BF16)
        r.kv_sum_b[k] = summed(r.kv_one_b.at[k]).astype(BF16)
        moves = [
            spread("pair", lambda p: r.kv_sum_a.at[k, p], lambda q: r.kv_two_a.at[k, q], True),
            spread("x", lambda p: r.kv_sum_b.at[k, p], lambda q: r.kv_two_b.at[k, q], True),
        ]
        begin(moves)
        return moves

    firsts, seconds = {}, []
    for j in reversed(range(SLOTS)):
        attend_back(r, low, j)
        to_owner(r.dq_buf, r.dq, dq_send, dq_recv, j, "start")
        firsts[j] = kv_first(j)
        if j + 1 in firsts:
            seconds += kv_second(j + 1, firsts[j + 1])
    finish(far)

    @pl.loop(0, 4)
    def _(m):
        for src, dst in ((r.far_a, r.mid_a), (r.far_b, r.mid_b)):
            total = src[0, m].astype(F32)
            for k in range(1, 4):
                total += src[k, m].astype(F32)
            dst[m] = total.astype(BF16)

    seconds += kv_second(0, firsts[0])
    mid = [
        spread("z", lambda p: r.mid_a.at[p], lambda q: r.mid_far_a.at[q], True),
        spread("x", lambda p: r.mid_b.at[p], lambda q: r.mid_far_b.at[q], True),
    ]
    finish(seconds)
    for k in range(4):
        r.kv_sum[k, 0] = summed(r.kv_two_a.at[k]).astype(BF16)
        r.kv_sum[k, 1] = summed(r.kv_two_b.at[k]).astype(BF16)
    kv_third = spread("z", lambda p: r.kv_sum.at[p], lambda q: r.dkv.at[q], True)
    push(*kv_third)
    begin(mid)
    settle(*kv_third)
    for j in range(SLOTS):
        to_owner(r.dq_buf, r.dq, dq_send, dq_recv, j, "wait")
    from_workers(r.dq_buf, r.dq, dq_send, dq_recv)

    vectors = project_back(r)
    stage(spread("core", lambda p: r.parts_back.at[:, p], lambda q: r.back_half.at[q], True))
    r.back_chip[...] = summed(r.back_half).astype(BF16)
    sums = spread("near", lambda p: r.back_chip.at[p], lambda q: r.landed_back.at[q], True)
    push(*sums)

    @pl.loop(0, 4)
    def _(m):
        at = tiles(m, 256)
        cols = r.grad_in.shape[1]
        step = first_dims(r.hidden[:, at], r.grad_in[...]).astype(BF16)
        r.qkv[m, :, :, :, :, :cols] = step.reshape(4, 2, 2, 16, cols)
        some = r.grad_all[:, :, :, at].reshape(4 * own, 256)
        step = first_dims(some, r.attended[...]).astype(BF16)
        r.qkv[m, :, :, :, :, cols:] = step.reshape(4, 2, 2, 16, r.attended.shape[1])

    pieces = jnp.zeros((NCTX, 8, 128), F32)
    for row, (vector, per) in enumerate(vectors):
        piece = jnp.broadcast_to(owner_pieces(vector, per)[:, None, :], pieces.shape)
        pieces = jnp.where(iota(pieces.shape, 1) == row, piece, pieces)
    r.gain_pieces[...] = pieces.reshape(r.gain_pieces.shape)
    one = [
        spread("x", lambda p: r.qkv.at[:, p, :, 0], lambda q: r.one_a.at[q], True),
        spread("z", lambda p: r.qkv.at[p, :, :, 1], lambda q: r.one_b.at[q], True),
        spread("x", lambda p: r.gain_pieces.at[:, p], lambda q: r.one_g.at[q], True),
    ]
    begin(one)
    finish(mid)
    r.end_ab[:, 0] = summed(r.mid_far_a).astype(BF16)
    r.end_ab[:, 1] = summed(r.mid_far_b).astype(BF16)
    swap = spread("pair", lambda p: r.end_ab.at[p], lambda q: r.ffn_all.at[q], True)
    push(*swap)
    settle(*ffn_rows)
    r.output[...] = (r.residual[...] + summed(r.ffn_parts)).astype(BF16)
    share = [spread("tp", lambda p: r.output, lambda q: r.output_all.at[q], True)]
    rows = r.rows_in[tiles(t, own)].astype(F32)
    scale = row_scale(rows)
    normed = rows * scale
    settle(*sums)
    result = r.grad_residual[...] + row_back(
        summed(r.landed_back), normed, scale, r.gain_attn[...]
    )
    r.input_bf[...] = result.astype(BF16)
    share.append(spread("tp", lambda p: r.input_bf, lambda q: r.input_all.at[q], True))
    begin(share)
    finish(one)
    r.sum_a[...] = summed(r.one_a).astype(BF16)
    r.sum_b[...] = summed(r.one_b).astype(BF16)
    r.sum_g[...] = summed(r.one_g)
    stage(
        spread("z", lambda p: r.sum_a.at[p], lambda q: r.two_a.at[q], True),
        spread("x", lambda p: r.sum_b.at[p], lambda q: r.two_b.at[q], True),
        spread("z", lambda p: r.sum_g.at[p], lambda q: r.two_g.at[q], True),
    )
    r.part_a[...] = summed(r.two_a).astype(BF16)
    r.part_b[...] = summed(r.two_b).astype(BF16)
    r.part_g[...] = summed(r.two_g)
    stage(
        spread("pair", lambda p: r.part_a.at[p], lambda q: r.three_a.at[q], True),
        spread("pair", lambda p: r.part_b.at[p], lambda q: r.three_b.at[q], True),
        spread("pair", lambda p: r.part_g.at[p], lambda q: r.three_g.at[q], True),
    )
    r.gain_sum[...] = summed(r.three_g)
    share.append(spread("tp", lambda p: r.gain_sum, lambda q: r.gain_tp.at[q], True))
    push(*share[-1])
    r.qkv_grad[0] = summed(r.three_a)
    r.qkv_grad[1] = summed(r.three_b)
    finish(share)
    settle(*swap)


def whole(weights, gains, ffn, wo, cot, rows_in, cosine, sine):
    rows, width = rows_in.shape
    arrays = scratch_arrays(rows, width, weights.shape[2], wo.shape[2])
    names = INPUTS + OUTPUTS + tuple(arrays)
    return pl.pallas_call(
        functools.partial(whole_body, names),
        out_shape=[
            jax.ShapeDtypeStruct((2, 16, weights.shape[2] + wo.shape[2]), F32),
            jax.ShapeDtypeStruct(ffn.shape, BF16),
            jax.ShapeDtypeStruct((4, rows // 4, width), BF16),
            jax.ShapeDtypeStruct((4, rows // 4, width), BF16),
            jax.ShapeDtypeStruct((4, 8, 128), F32),
        ],
        in_specs=[ANY] * 5 + [VMEM] * 3,
        out_specs=[VMEM] + [ANY] * 4,
        scratch_shapes=[pltpu.VMEM(shape, dtype) for shape, dtype in arrays.values()]
        + [pltpu.SemaphoreType.DMA((SEMAPHORES,))],
        compiler_params=pltpu.CompilerParams(
            collective_id=1, has_side_effects=True, vmem_limit_bytes=60 * 2**20
        ),
        name="block",
    )(weights, gains, ffn, wo, cot, rows_in, cosine, sine)


def rope_tables(tokens, offset):
    half = HEAD_SIZE // 2
    inverse = ROPE_BASE ** (-(jnp.arange(half, dtype=F32) * 2.0 / HEAD_SIZE))
    steps = (offset + jnp.arange(tokens, dtype=jnp.int32)).astype(F32)
    angles = steps[:, None] * jnp.tile(inverse, 4)[None, :]
    signs = jnp.where(jnp.arange(4 * half) % HEAD_SIZE < half, -1.0, 1.0)
    return jnp.cos(angles), jnp.sin(angles) * signs[None, :]


def halves(*weights):
    rows, cols = weights[0].shape
    w = jnp.stack(weights).reshape(len(weights), rows, 2, cols // 2)
    w = jnp.pad(w, ((0, 0), (0, 0), (0, 0), (0, UNITS - cols // 2)))
    return w.transpose(2, 1, 0, 3).reshape(2, rows, len(weights) * UNITS)


def local(
    block_input, cotangent, w_query, key_weight, w_value, w_out, w_gate, w_up, w_down,
    norm_gains, head_gains,
):
    seqs, tokens, width = block_input.shape
    rows = seqs * tokens
    unit_half = w_gate.shape[1] // 2
    rows_in = block_input.reshape(rows, width)
    cot_rows = cotangent.reshape(rows, width)
    cosine, sine = rope_tables(tokens, lax.axis_index("ctx") * tokens)
    weight_rows = jnp.concatenate([w_query, key_weight, w_value], axis=1)
    gains = jnp.pad(norm_gains, ((0, 14), (0, 96))) + jnp.pad(head_gains, ((2, 12), (0, 126)))
    ffn = halves(w_gate, w_up, w_down)
    qkv_grad, pair_grads, output_all, input_all, gain_tp = whole(
        weight_rows.reshape(2, 16, weight_rows.shape[1]),
        gains,
        ffn.reshape(2, 2, 16, ffn.shape[2]),
        w_out.reshape(2, 16, w_out.shape[1]),
        cot_rows,
        rows_in,
        cosine,
        sine,
    )
    pair_grads = pair_grads.reshape(ffn.shape)
    pair_grads = pair_grads.astype(F32)
    gain_sum = jnp.sum(gain_tp, axis=0)
    qkv_grad = qkv_grad.reshape(32, 768)

    def joined(first):
        last = first + unit_half
        return jnp.concatenate([pair_grads[0, :, first:last], pair_grads[1, :, first:last]], axis=1)

    gate_grad, up_grad, down_grad = joined(0), joined(UNITS), joined(2 * UNITS)
    return (
        output_all.reshape(seqs, tokens, width),
        input_all.astype(F32).reshape(seqs, tokens, width),
        qkv_grad[:, :256],
        qkv_grad[:, 256:384],
        qkv_grad[:, 384:512],
        qkv_grad[:, 512:],
        gate_grad,
        up_grad,
        down_grad,
        gain_sum[0:2, :32],
        gain_sum[2:4, :2],
    )


def solution(mesh):
    tokens, weights = P(None, "ctx", None), P("ctx", "tp")
    return jax.shard_map(
        local,
        mesh=mesh,
        in_specs=(tokens,) * 2 + (weights,) * 7 + (P(None, "ctx"),) * 2,
        out_specs=(tokens,) * 2 + (weights,) * 7 + (P(None, "ctx"),) * 2,
        check_vma=False,
    )
```

```python
import functools
import types

import jax
import jax.numpy as jnp
from jax import lax
from jax.experimental import pallas as pl
from jax.experimental.pallas import tpu as pltpu
from jax.sharding import PartitionSpec as P

HEAD_SIZE = 64
EPSILON = 1e-06
ROPE_BASE = 1000000.0
MESH = pl.DeviceIdType.MESH
F32 = jnp.float32
BF16 = jnp.bfloat16
ANY = pl.BlockSpec(memory_space=pl.ANY)
VMEM = pl.BlockSpec(memory_space=pltpu.VMEM)
NCTX = 32
PAIRS = 4
WORKERS = 8
SLOTS = 4
BLOCK = 128
CHUNK = 512


def group(kind):
    c, t = lax.axis_index("ctx"), lax.axis_index("tp")
    h = lax.rem(c, 2)
    if kind == "ctx":
        return NCTX, c, lambda p: (p, t)
    if kind == "tp":
        return 4, t, lambda p: (c, p)
    if kind == "pair":
        return 2, h, lambda p: (c - h + p, t)
    z, x, core = c // 8, lax.rem(c // 2, 4), lax.rem(t, 2)
    if kind == "z":
        return 4, z, lambda p: (c + (p - z) * 8, t)
    if kind == "x":
        return 4, x, lambda p: (c + (p - x) * 2, t)
    if kind == "core":
        return 2, core, lambda p: (c, t - core + p)
    if kind == "near":
        return 2, t // 2, lambda p: (c, p * 2 + core)
    if kind == "ring":
        return 4, h * 2 + t // 2, lambda p: (c - h + p // 2, lax.rem(p, 2) * 2 + core)
    return 8, h * 4 + t, lambda p: (c - h + p // 4, lax.rem(p, 4))


def push(kind, src_of, dst_of, send, recv, local=False):
    n, me, dev = group(kind)

    @pl.loop(1, n)
    def _(i):
        p = lax.rem(me + i, n)
        pltpu.make_async_remote_copy(
            src_ref=src_of(p),
            dst_ref=dst_of(me),
            send_sem=send.at[p],
            recv_sem=recv.at[me],
            device_id=dev(p),
            device_id_type=MESH,
        ).start()

    if local:
        pltpu.make_async_copy(src_of(me), dst_of(me), recv.at[me]).start()


def settle(kind, src_of, dst_of, send, recv, local=False):
    n, me, dev = group(kind)

    @pl.loop(1, n)
    def _(i):
        p = lax.rem(me + i, n)
        copy = pltpu.make_async_remote_copy(
            src_ref=src_of(p),
            dst_ref=dst_of(p),
            send_sem=send.at[p],
            recv_sem=recv.at[p],
            device_id=dev(p),
            device_id_type=MESH,
        )
        copy.wait_send()
        copy.wait_recv()

    if local:
        pltpu.make_async_copy(src_of(me), dst_of(me), recv.at[me]).wait()


def stage(*moves):
    for move in moves:
        push(*move)
    for move in moves:
        settle(*move)


class Sems:
    def __init__(self, ref):
        self.ref, self.used = ref, 0

    def two(self, n):
        at = self.used
        self.used += 2 * n
        return self.ref.at[pl.ds(at, n)], self.ref.at[pl.ds(at + n, n)]


def position():
    c = lax.axis_index("ctx")
    return c // 8, lax.rem(c // 2, 4), lax.rem(c, 2)


def iota(shape, axis):
    return lax.broadcasted_iota(jnp.int32, shape, axis)


def two_parts(v):
    high = v.astype(BF16)
    return high, (v - high.astype(F32)).astype(BF16)


def exact_dot(v, pattern):
    high, low = two_parts(v)
    return jnp.dot(high, pattern, preferred_element_type=F32) + jnp.dot(
        low, pattern, preferred_element_type=F32
    )


def head_mean(v):
    n = v.shape[1]
    same = lax.div(iota((n, n), 0), HEAD_SIZE) == lax.div(iota((n, n), 1), HEAD_SIZE)
    return exact_dot(v, jnp.where(same, 1.0 / HEAD_SIZE, 0.0).astype(BF16))


def head_scale(v):
    return lax.rsqrt(head_mean(v * v) + EPSILON)


def turned(u, cosine, sine):
    half, n = HEAD_SIZE // 2, 2 * HEAD_SIZE
    first = lax.rem(iota(u.shape, 1), HEAD_SIZE) < half
    other = jnp.where(first, pltpu.roll(u, n - half, 1), pltpu.roll(u, half, 1))
    return u * cosine + other * sine


def crossed(tile):
    return pltpu.roll(tile, HEAD_SIZE, 1)


def left_lanes(tile):
    return iota(tile.shape, 1) < HEAD_SIZE


def spread_gain(pieces, row, per, lanes):
    n = pieces.shape[0]
    pick = iota((NCTX, n), 1) == iota((NCTX, n), 0) * (n // NCTX) + row
    mine = jnp.dot(pick.astype(F32).astype(BF16), pieces, preferred_element_type=F32).astype(BF16)
    pattern = (lax.rem(iota((128, lanes), 1), per) == iota((128, lanes), 0)).astype(F32)
    wide = jnp.dot(mine, pattern.astype(BF16), preferred_element_type=F32)
    owner = lax.div(lax.rem(iota(wide.shape, 1), NCTX * per), per)
    return jnp.sum(jnp.where(owner == iota(wide.shape, 0), wide, 0.0), axis=0, keepdims=True)


def owner_pieces(vector, per):
    lanes = vector.shape[1]
    shape = (NCTX, lanes)
    owner = lax.div(lax.rem(iota(shape, 1), NCTX * per), per)
    parts = jnp.where(owner == iota(shape, 0), jnp.broadcast_to(vector, shape), 0.0)
    pattern = (lax.rem(iota((lanes, 128), 0), per) == iota((lanes, 128), 1)).astype(F32)
    return exact_dot(parts, pattern.astype(BF16))


def row_scale(rows):
    return lax.rsqrt(jnp.mean(rows * rows, axis=1, keepdims=True) + EPSILON)


def twice(table):
    return jnp.concatenate([table[...], table[...]], axis=0)


def places():
    c, t = lax.axis_index("ctx"), lax.axis_index("tp")
    slot, low = c // WORKERS, lax.rem(c, WORKERS)
    to = low + lax.rem(slot, 2) * (WORKERS - 1 - 2 * low)
    return c, t, slot, low, to


def block_of(low, j):
    return j * WORKERS + (low if j % 2 == 0 else WORKERS - 1 - low)


def greet_attention(kinds):
    c, t, slot, low, to = places()
    barrier = pltpu.get_barrier_semaphore()
    total = 0
    others = [p * WORKERS + to for p in range(PAIRS)] + [block_of(low, j) for j in range(SLOTS)]
    for other in others:

        @pl.when(other != c)
        def _():
            pl.semaphore_signal(barrier, inc=1, device_id=(other, t), device_id_type=MESH)

        total = total + jnp.where(other != c, 1, 0)
    for kind in kinds:
        n, me, dev = group(kind)

        @pl.loop(1, n)
        def _(i):
            pl.semaphore_signal(
                barrier, inc=1, device_id=dev(lax.rem(me + i, n)), device_id_type=MESH
            )

        total = total + (n - 1)
    pl.semaphore_wait(barrier, total)


def to_workers(src, dst, send, recv, act):
    c, t, slot, low, to = places()
    for p in range(PAIRS):
        target = p * WORKERS + to
        far = pltpu.make_async_remote_copy(
            src_ref=src.at[p],
            dst_ref=dst.at[slot],
            send_sem=send.at[p],
            recv_sem=recv.at[slot],
            device_id=(target, t),
            device_id_type=MESH,
        )
        near = pltpu.make_async_copy(src.at[p], dst.at[slot], send.at[p])

        @pl.when(target != c)
        def _():
            far.start() if act == "start" else far.wait_send()

        @pl.when(target == c)
        def _():
            near.start() if act == "start" else near.wait()


def from_owners(src, dst, send, recv):
    c, t, slot, low, to = places()
    for j in range(SLOTS):
        owner = block_of(low, j)

        @pl.when(owner != c)
        def _():
            pltpu.make_async_remote_copy(
                src_ref=src.at[j],
                dst_ref=dst.at[j],
                send_sem=send.at[j],
                recv_sem=recv.at[j],
                device_id=(owner, t),
                device_id_type=MESH,
            ).wait_recv()


def to_owner(src, dst, send, recv, j, act):
    c, t, slot, low, to = places()
    owner = block_of(low, j)
    far = pltpu.make_async_remote_copy(
        src_ref=src.at[j],
        dst_ref=dst.at[slot],
        send_sem=send.at[j],
        recv_sem=recv.at[slot],
        device_id=(owner, t),
        device_id_type=MESH,
    )
    near = pltpu.make_async_copy(src.at[j], dst.at[slot], send.at[j])

    @pl.when(owner != c)
    def _():
        far.start() if act == "start" else far.wait_send()

    @pl.when(owner == c)
    def _():
        near.start() if act == "start" else near.wait()


def from_workers(src, dst, send, recv):
    c, t, slot, low, to = places()
    for p in range(PAIRS):
        target = p * WORKERS + to

        @pl.when(target != c)
        def _():
            pltpu.make_async_remote_copy(
                src_ref=src.at[p],
                dst_ref=dst.at[p],
                send_sem=send.at[p],
                recv_sem=recv.at[p],
                device_id=(target, t),
                device_id_type=MESH,
            ).wait_recv()


def last_dims(a, b):
    return lax.dot_general(a, b, (((1,), (1,)), ((), ())), preferred_element_type=F32)


def first_dims(a, b):
    return lax.dot_general(a, b, (((0,), (0,)), ((), ())), preferred_element_type=F32)


def causal_mask(b, i):
    shape = (2 * BLOCK, CHUNK)
    rows = lax.broadcasted_iota(jnp.int32, shape, 0)
    token = b * BLOCK + jnp.where(rows >= BLOCK, rows - BLOCK, rows)
    key = i * CHUNK + lax.broadcasted_iota(jnp.int32, shape, 1)
    return token >= key


def row_back(grads, normed, scale, gain):
    scaled = grads * gain
    return scale * (scaled - normed * jnp.mean(scaled * normed, axis=1, keepdims=True))


def summed(ref):
    total = ref[0].astype(F32)
    for k in range(1, ref.shape[0]):
        total += ref[k].astype(F32)
    return total


UNITS = 640
INPUTS = ("weights", "gains", "ffn", "wo", "cot", "rows_in", "cosine", "sine")
OUTPUTS = ("qkv_grad", "ffn_all", "output_all", "input_all", "gain_tp")
SIZES = {"tp": 4, "pair": 2, "rows": 8, "z": 4, "x": 4, "core": 2, "ring": 4, "near": 2}
SEMAPHORES = 572


def scratch_arrays(rows, width, qkv_cols, out_cols):
    own, half = rows // 4, BLOCK // 2
    stack = (SLOTS, 2 * BLOCK, BLOCK)
    grid, piece = (4, 4, 2, 2), (16, qkv_cols + out_cols)
    units = (16, 3 * UNITS)
    return dict(
        w_all=((*grid, 16, qkv_cols), BF16),
        gains_all=((4, 4, 2, 16, 128), BF16),
        w_ffn=((*grid, *units), BF16),
        wo_all=((*grid, 16, out_cols), BF16),
        cot_all=((2, rows, width), BF16),
        hidden=((rows, width), BF16),
        raw=((rows, qkv_cols), F32),
        q_src=(stack, BF16),
        kv_src=((PAIRS, 2, half, BLOCK), BF16),
        gain_attn=((1, width), F32),
        gain_ffn=((1, width), F32),
        gain_query=((1, 128), F32),
        gain_key=((1, 128), F32),
        q_buf=(stack, BF16),
        kv_buf=((*grid, half, BLOCK), BF16),
        o_buf=(stack, BF16),
        log_buf=(stack, F32),
        att=(stack, BF16),
        acc=((2 * BLOCK, BLOCK), F32),
        den=((2 * BLOCK, BLOCK), F32),
        attended=((rows, out_cols), BF16),
        parts=((2, 2, own, width), BF16),
        parts_half=((2, 2, own, width), BF16),
        parts_chip=((2, own, width), BF16),
        landed=((2, own, width), BF16),
        residual=((own, width), F32),
        hidden_own=((own, width), BF16),
        hidden_all=((4, 2, own, width), BF16),
        grad_units=((2 * rows, UNITS), F32),
        units=((2 * rows, UNITS), BF16),
        units_in=((2 * rows, 2 * UNITS), BF16),
        back=((4, 2, own, width), BF16),
        halved=((2, 4, own, width), BF16),
        chip=((4, own, width), BF16),
        ringed=((4, own, width), BF16),
        grad_bf=((own, width), BF16),
        grad_all=((2, 2, own, width), BF16),
        grad_residual=((own, width), F32),
        ffn_gain=((1, width), F32),
        grads=((*grid, *units), BF16),
        ffn_part=((8, own, width), BF16),
        ffn_parts=((8, own, width), BF16),
        far_a=((4, 4, 2, *units), BF16),
        far_b=((4, 4, 2, *units), BF16),
        mid_a=((4, 2, *units), BF16),
        mid_b=((4, 2, *units), BF16),
        mid_far_a=((4, 2, *units), BF16),
        mid_far_b=((4, 2, *units), BF16),
        end_ab=((2, 2, *units), BF16),
        do_src=(stack, BF16),
        do_buf=(stack, BF16),
        dq_buf=(stack, BF16),
        dq=(stack, BF16),
        dkv_sum=((*grid, half, BLOCK), F32),
        dkv_buf=((*grid, half, BLOCK), BF16),
        kv_one_a=((4, 4, 2, half, BLOCK), BF16),
        kv_one_b=((4, 2, 4, half, BLOCK), BF16),
        kv_sum_a=((4, 2, half, BLOCK), BF16),
        kv_sum_b=((4, 4, half, BLOCK), BF16),
        kv_two_a=((4, 2, half, BLOCK), BF16),
        kv_two_b=((4, 4, half, BLOCK), BF16),
        kv_sum=((4, 2, half, BLOCK), BF16),
        dkv=((PAIRS, 2, half, BLOCK), BF16),
        parts_back=((2, 2, own, width), BF16),
        back_half=((2, 2, own, width), BF16),
        back_chip=((2, own, width), BF16),
        landed_back=((2, own, width), BF16),
        grad_in=((rows, qkv_cols), BF16),
        gain_pieces=((4, 4, 2, 8, 128), F32),
        output=((own, width), BF16),
        input_bf=((own, width), BF16),
        qkv=((*grid, *piece), BF16),
        one_a=((4, 4, 2, *piece), BF16),
        one_b=((4, 4, 2, *piece), BF16),
        one_g=((4, 4, 2, 8, 128), F32),
        sum_a=((4, 2, *piece), BF16),
        sum_b=((4, 2, *piece), BF16),
        sum_g=((4, 2, 8, 128), F32),
        two_a=((4, 2, *piece), BF16),
        two_b=((4, 2, *piece), BF16),
        two_g=((4, 2, 8, 128), F32),
        part_a=((2, *piece), BF16),
        part_b=((2, *piece), BF16),
        part_g=((2, 8, 128), F32),
        three_a=((2, *piece), BF16),
        three_b=((2, *piece), BF16),
        three_g=((2, 8, 128), F32),
        gain_sum=((8, 128), F32),
    )


def project_keys(r):
    pieces = r.gains_all[...].reshape(NCTX * 16, 128)
    r.gain_attn[...] = spread_gain(pieces, 0, 32, r.gain_attn.shape[1])
    r.gain_query[...] = spread_gain(pieces, 2, 2, 128)
    r.gain_key[...] = spread_gain(pieces, 3, 2, 128)
    rows = r.rows_in[...].astype(F32)
    r.hidden[...] = (rows * row_scale(rows) * r.gain_attn[...]).astype(BF16)
    weights = r.w_all[:, :, :, :, :, 256:].reshape(r.hidden.shape[1], 256)
    r.raw[:, 256:] = jnp.dot(r.hidden[...], weights, preferred_element_type=F32)
    tile = r.raw[:, 256:384]
    keys = turned(tile * head_scale(tile) * r.gain_key[...], twice(r.cosine), twice(r.sine))
    values = r.raw[:, 384:512]
    for k in range(2):
        key, value = (keys, crossed(values)) if k == 0 else (crossed(keys), values)
        one = jnp.where(left_lanes(key), key, value).astype(BF16)
        for s in range(2):
            part = one[s * BLOCK : (s + 1) * BLOCK]
            r.kv_src[2 * k + s] = part.reshape(2, BLOCK // 2, 128)


def project_queries(r):
    weights = r.w_all[:, :, :, :, :, :256].reshape(r.hidden.shape[1], 256)
    r.raw[:, :256] = jnp.dot(r.hidden[...], weights, preferred_element_type=F32)
    cos, sin = twice(r.cosine), twice(r.sine)
    for k in range(2):
        tile = r.raw[:, k * 128 : k * 128 + 128]
        tile = turned(tile * head_scale(tile) * r.gain_query[...], cos, sin) * (HEAD_SIZE**-0.5)
        for a, one in enumerate((tile, crossed(tile))):
            one = jnp.where(left_lanes(one), one, 0.0).astype(BF16)
            for s in range(2):
                r.q_src[2 * k + s, a * BLOCK : (a + 1) * BLOCK] = one[s * BLOCK : (s + 1) * BLOCK]
    pieces = r.gains_all[...].reshape(NCTX * 16, 128)
    r.gain_ffn[...] = spread_gain(pieces, 1, 32, r.gain_ffn.shape[1])


def attend(r, low, j):
    b = block_of(low, j)
    r.acc[...] = jnp.zeros_like(r.acc)
    r.den[...] = jnp.zeros_like(r.den)

    def chunk(i, masked):
        kv = r.kv_buf[i // 2, pl.ds(2 * lax.rem(i, 2), 2)].reshape(CHUNK, BLOCK)
        powered = jnp.exp(last_dims(r.q_buf[j], kv))
        if masked:
            powered = jnp.where(causal_mask(b, i), powered, 0.0)
        r.den[...] += sum(powered[:, k : k + BLOCK] for k in range(0, CHUNK, BLOCK))
        r.acc[...] += jnp.dot(powered.astype(BF16), kv, preferred_element_type=F32)

    last = b // (CHUNK // BLOCK)
    pl.loop(0, last)(lambda i: chunk(i, False))
    chunk(last, True)
    total = jnp.sum(r.den[...], axis=1, keepdims=True)
    lanes = iota((2 * BLOCK, BLOCK), 1)
    r.o_buf[j] = jnp.where(lanes >= HEAD_SIZE, r.acc[...] / total, 0.0).astype(BF16)
    r.log_buf[j] = jnp.broadcast_to(jnp.log(total), (2 * BLOCK, BLOCK))


def attend_back(r, low, j):
    b = block_of(low, j)
    r.acc[...] = jnp.zeros_like(r.acc)
    delta = jnp.sum(r.do_buf[j].astype(F32) * r.o_buf[j].astype(F32), axis=1, keepdims=True)

    def chunk(i, masked):
        q, do, logs = r.q_buf[j], r.do_buf[j], r.log_buf[j]
        kv = r.kv_buf[i // 2, pl.ds(2 * lax.rem(i, 2), 2)].reshape(CHUNK, BLOCK)
        probs = jnp.exp(last_dims(q, kv) - jnp.concatenate([logs] * (CHUNK // BLOCK), axis=1))
        if masked:
            probs = jnp.where(causal_mask(b, i), probs, 0.0)
        grads = (probs * (last_dims(do, kv) - delta)).astype(BF16)
        r.acc[...] += jnp.dot(grads, kv, preferred_element_type=F32)
        update = first_dims(grads, q) + first_dims(probs.astype(BF16), do)
        at = pl.ds(2 * lax.rem(i, 2), 2)
        r.dkv_sum[i // 2, at] += update.reshape(2, 2, 2, BLOCK // 2, BLOCK)

    last = b // (CHUNK // BLOCK)
    pl.loop(0, last)(lambda i: chunk(i, False))
    chunk(last, True)
    r.dq_buf[j] = (r.acc[...] * (HEAD_SIZE**-0.5)).astype(BF16)


def tiles(m, n):
    return pl.ds(pl.multiple_of(m * n, n), n)


def both_rows(first, second):
    return jnp.concatenate([first.astype(F32), second.astype(F32)], axis=0)


def head_back(r, u, tile, gain_row):
    turn = turned(u, twice(r.cosine), -twice(r.sine))
    scale = head_scale(tile)
    hat = tile * scale
    scaled = turn * gain_row
    back = scale * (scaled - hat * head_mean(scaled * hat))
    return back.astype(BF16), jnp.sum(turn * hat, axis=0, keepdims=True)


def queries_back(r):
    query_gain = jnp.zeros((1, 128), F32)
    for k in range(2):
        first = both_rows(r.dq[2 * k, :BLOCK], r.dq[2 * k + 1, :BLOCK])
        second = crossed(both_rows(r.dq[2 * k, BLOCK:], r.dq[2 * k + 1, BLOCK:]))
        lanes = slice(k * 128, (k + 1) * 128)
        u = jnp.where(left_lanes(first), first, second)
        r.grad_in[:, lanes], part = head_back(r, u, r.raw[:, lanes], r.gain_query[...])
        query_gain = query_gain + part
    return query_gain


def keys_back(r):
    own, width = r.residual.shape
    first, second = [
        both_rows(r.dkv[2 * k].reshape(BLOCK, 128), r.dkv[2 * k + 1].reshape(BLOCK, 128))
        for k in range(2)
    ]
    left = left_lanes(first)
    u = jnp.where(left, first, crossed(second))
    r.grad_in[:, 256:384], key_gain = head_back(r, u, r.raw[:, 256:384], r.gain_key[...])
    r.grad_in[:, 384:] = jnp.where(left, crossed(first), second).astype(BF16)
    attn_gain = jnp.zeros((1, width), F32)
    weights = r.w_all[...].reshape(width, r.grad_in.shape[1])
    for q in range(4):
        at = slice(q * own, (q + 1) * own)
        back = last_dims(r.grad_in[at], weights)
        r.parts_back[q // 2, q % 2] = back.astype(BF16)
        rows = r.rows_in[at].astype(F32)
        attn_gain = attn_gain + jnp.sum(back * (rows * row_scale(rows)), axis=0, keepdims=True)
    return key_gain, attn_gain


def begin(moves):
    for move in moves:
        push(*move)


def finish(moves):
    for move in moves:
        settle(*move)


def whole_body(names, *refs):
    r = types.SimpleNamespace(**dict(zip(names, refs)))
    take = Sems(refs[-1])
    c, t, slot, low, to = places()
    z, x, h = position()
    core = lax.rem(t, 2)
    own, width = r.residual.shape

    def spread(kind, src_of, dst_of, local=False):
        return (kind, src_of, dst_of, *take.two(SIZES[kind]), local)

    def gathered(ref):
        second = [
            spread("x", lambda p: ref.at[z, x, :, 0], lambda q: ref.at[z, q, :, 0]),
            spread("z", lambda p: ref.at[z, x, :, 1], lambda q: ref.at[q, x, :, 1]),
        ]
        third = [
            spread("z", lambda p: ref.at[z, :, :, 0], lambda q: ref.at[q, :, :, 0]),
            spread("x", lambda p: ref.at[:, x, :, 1], lambda q: ref.at[:, q, :, 1]),
        ]
        return second, third

    greet_attention(["z", "x", "rows"])
    first = [
        spread("pair", lambda p: r.weights, lambda q: r.w_all.at[z, x, q], True),
        spread("pair", lambda p: r.gains, lambda q: r.gains_all.at[z, x, q], True),
    ]
    late = [
        spread("pair", lambda p: r.wo, lambda q: r.wo_all.at[z, x, q], True),
        spread("pair", lambda p: r.ffn.at[p], lambda q: r.w_ffn.at[z, x, q], True),
    ]
    begin(first)
    begin(late)
    finish(first)
    second, third = gathered(r.w_all)
    second.append(spread("x", lambda p: r.gains_all.at[z, x], lambda q: r.gains_all.at[z, q]))
    third.append(spread("z", lambda p: r.gains_all.at[z], lambda q: r.gains_all.at[q]))
    stage(*second)
    stage(*third)
    finish(late)
    out_second, out_third = gathered(r.wo_all)
    ffn_second, ffn_third = gathered(r.w_ffn)
    begin(out_second + ffn_second)
    project_keys(r)

    q_send, q_recv = take.two(SLOTS)
    near = spread("z", lambda p: r.kv_src.at[p], lambda q: r.kv_buf.at[q, x, h], True)
    push(*near)
    project_queries(r)
    to_workers(r.q_src, r.q_buf, q_send, q_recv, "start")
    settle(*near)
    kv = r.kv_buf

    def planes(k):
        return [
            spread("x", lambda p: kv.at[k, x, h, 0], lambda q: kv.at[k, q, h, 0]),
            spread("pair", lambda p: kv.at[k, x, h, 1], lambda q: kv.at[k, x, q, 1]),
        ], [
            spread("pair", lambda p: kv.at[k, :, h, 0], lambda q: kv.at[k, :, q, 0]),
            spread("x", lambda p: kv.at[k, x, :, 1], lambda q: kv.at[k, q, :, 1]),
        ]

    plane_moves = [planes(k) for k in range(4)]
    for early, _ in plane_moves:
        begin(early)
    for early, then in plane_moves:
        finish(early)
        begin(then)
    finish(out_second + ffn_second)
    begin(out_third)
    begin(ffn_third)
    cot_swap = spread("pair", lambda p: r.cot, lambda q: r.cot_all.at[q], True)
    push(*cot_swap)
    to_workers(r.q_src, r.q_buf, q_send, q_recv, "wait")
    from_owners(r.q_src, r.q_buf, q_send, q_recv)
    o_send, o_recv = take.two(SLOTS)
    for j in range(SLOTS):
        finish(plane_moves[j][1])
        attend(r, low, j)
        to_owner(r.o_buf, r.att, o_send, o_recv, j, "start")
    for j in range(SLOTS):
        to_owner(r.o_buf, r.att, o_send, o_recv, j, "wait")
    from_workers(r.o_buf, r.att, o_send, o_recv)

    for k in range(2):
        for s in range(2):
            left = crossed(r.att[2 * k + s, :BLOCK].astype(F32))
            right = r.att[2 * k + s, BLOCK:].astype(F32)
            one = jnp.where(left_lanes(left), left, right).astype(BF16)
            r.attended[s * BLOCK : (s + 1) * BLOCK, k * 128 : (k + 1) * 128] = one
    finish(out_third)
    out_full = r.wo_all[...].reshape(width, r.attended.shape[1])
    r.parts[...] = last_dims(r.attended[...], out_full).astype(BF16).reshape(r.parts.shape)
    stage(spread("core", lambda p: r.parts.at[:, p], lambda q: r.parts_half.at[q], True))
    r.parts_chip[...] = summed(r.parts_half).astype(BF16)
    stage(spread("near", lambda p: r.parts_chip.at[p], lambda q: r.landed.at[q], True))
    rows = r.rows_in[tiles(t, own)].astype(F32) + summed(r.landed)
    r.residual[...] = rows
    r.hidden_own[...] = (rows * row_scale(rows) * r.gain_ffn[...]).astype(BF16)
    ring = spread("ring", lambda p: r.hidden_own, lambda q: r.hidden_all.at[q, core], True)
    push(*ring)
    settle(*cot_swap)
    finish(ffn_third)
    w = r.w_ffn.reshape(width, 3 * UNITS)
    cot = r.cot_all.reshape(8 * own, width)

    @pl.loop(0, 4)
    def _(m):
        at = tiles(m, 2 * own)
        r.grad_units[at] = jnp.dot(cot[at], w[:, 2 * UNITS :], preferred_element_type=F32)

    settle(*ring)
    hidden = r.hidden_all
    stage(spread("core", lambda p: hidden.at[:, core], lambda q: hidden.at[:, q]))

    @pl.loop(0, 2)
    def _(m):
        at = tiles(m, 4 * own)
        some = hidden[pl.ds(2 * m, 2)].reshape(4 * own, width)
        gate = jnp.dot(some, w[:, :UNITS], preferred_element_type=F32)
        up = jnp.dot(some, w[:, UNITS : 2 * UNITS], preferred_element_type=F32)
        sigmoid = jax.nn.sigmoid(gate)
        activated = gate * sigmoid
        r.units[at] = (activated * up).astype(BF16)
        grad = r.grad_units[at]
        r.units_in[at, :UNITS] = (grad * up * sigmoid * (1.0 + gate * (1.0 - sigmoid))).astype(BF16)
        r.units_in[at, UNITS:] = (grad * activated).astype(BF16)
        step = last_dims(r.units_in[at], w[:, : 2 * UNITS]).astype(BF16)
        r.back[pl.ds(2 * m, 2)] = step.reshape(2, *r.back.shape[1:])

    both = spread("core", lambda p: r.back.at[:, p], lambda q: r.halved.at[q], True)
    push(*both)

    @pl.loop(0, 4)
    def _(m):
        step = first_dims(cot[:, tiles(m, 256)], r.units[...]).astype(BF16)
        r.grads[m, :, :, :, :, 2 * UNITS :] = step.reshape(4, 2, 2, 16, UNITS)

    settle(*both)
    r.chip[...] = summed(r.halved).astype(BF16)
    ring = spread("ring", lambda p: r.chip.at[p], lambda q: r.ringed.at[q], True)
    push(*ring)

    @pl.loop(0, 4)
    def _(m):
        some = hidden[:, :, :, tiles(m, 256)].reshape(8 * own, 256)
        step = first_dims(some, r.units_in[...]).astype(BF16)
        r.grads[m, :, :, :, :, : 2 * UNITS] = step.reshape(4, 2, 2, 16, 2 * UNITS)

    far = [
        spread("x", lambda p: r.grads.at[:, p, :, 0], lambda q: r.far_a.at[q], True),
        spread("z", lambda p: r.grads.at[p, :, :, 1], lambda q: r.far_b.at[q], True),
    ]
    begin(far)
    settle(*ring)
    total = summed(r.ringed)
    rows = r.residual[...]
    scale = row_scale(rows)
    normed = rows * scale
    cot_own = cot[tiles(h * 4 + t, own)].astype(F32)
    result = cot_own + row_back(total, normed, scale, r.gain_ffn[...])
    r.grad_bf[...] = result.astype(BF16)
    share = spread("near", lambda p: r.grad_bf, lambda q: r.grad_all.at[q, core], True)
    push(*share)
    r.grad_residual[...] = result
    r.ffn_gain[...] = jnp.sum(total * normed, axis=0, keepdims=True)

    @pl.loop(0, 2)
    def _(m):
        step = last_dims(r.units[tiles(m, 4 * own)], w[:, 2 * UNITS :]).astype(BF16)
        r.ffn_part[pl.ds(4 * m, 4)] = step.reshape(4, *r.ffn_part.shape[1:])

    settle(*share)
    grad_all = r.grad_all
    stage(spread("core", lambda p: grad_all.at[:, core], lambda q: grad_all.at[:, q]))
    grad = jnp.dot(
        r.grad_all[...].reshape(4 * own, width), out_full, preferred_element_type=F32
    )
    for k in range(2):
        for s in range(2):
            tile = grad[s * BLOCK : (s + 1) * BLOCK, k * 128 : (k + 1) * 128]
            for a, one in enumerate((crossed(tile), tile)):
                one = jnp.where(left_lanes(one), 0.0, one).astype(BF16)
                r.do_src[2 * k + s, a * BLOCK : (a + 1) * BLOCK] = one

    do_send, do_recv = take.two(SLOTS)
    to_workers(r.do_src, r.do_buf, do_send, do_recv, "start")
    ffn_rows = spread("rows", lambda p: r.ffn_part.at[p], lambda q: r.ffn_parts.at[q], True)
    push(*ffn_rows)
    r.dkv_sum[...] = jnp.zeros_like(r.dkv_sum)

    @pl.loop(0, 4)
    def _(m):
        some = r.grad_all[:, :, :, tiles(m, 256)].reshape(4 * own, 256)
        step = first_dims(some, r.attended[...]).astype(BF16)
        r.qkv[m, :, :, :, :, 256:512] = step.reshape(4, 2, 2, 16, 256)

    to_workers(r.do_src, r.do_buf, do_send, do_recv, "wait")
    from_owners(r.do_src, r.do_buf, do_send, do_recv)
    dq_send, dq_recv = take.two(SLOTS)

    def kv_first(k):
        r.dkv_buf[k] = r.dkv_sum[k].astype(BF16)
        moves = [
            spread("x", lambda p: r.dkv_buf.at[k, p, :, 0], lambda q: r.kv_one_a.at[k, q], True),
            spread("pair", lambda p: r.dkv_buf.at[k, :, p, 1], lambda q: r.kv_one_b.at[k, q], True),
        ]
        begin(moves)
        return moves

    def kv_second(k, moves):
        finish(moves)
        r.kv_sum_a[k] = summed(r.kv_one_a.at[k]).astype(BF16)
        r.kv_sum_b[k] = summed(r.kv_one_b.at[k]).astype(BF16)
        moves = [
            spread("pair", lambda p: r.kv_sum_a.at[k, p], lambda q: r.kv_two_a.at[k, q], True),
            spread("x", lambda p: r.kv_sum_b.at[k, p], lambda q: r.kv_two_b.at[k, q], True),
        ]
        begin(moves)
        return moves

    firsts, seconds = {}, []
    for j in reversed(range(SLOTS)):
        attend_back(r, low, j)
        to_owner(r.dq_buf, r.dq, dq_send, dq_recv, j, "start")
        firsts[j] = kv_first(j)
        if j + 1 in firsts:
            seconds += kv_second(j + 1, firsts[j + 1])
    finish(far)

    @pl.loop(0, 4)
    def _(m):
        for src, dst in ((r.far_a, r.mid_a), (r.far_b, r.mid_b)):
            total = src[0, m].astype(F32)
            for k in range(1, 4):
                total += src[k, m].astype(F32)
            dst[m] = total.astype(BF16)

    seconds += kv_second(0, firsts[0])
    mid = [
        spread("z", lambda p: r.mid_a.at[p], lambda q: r.mid_far_a.at[q], True),
        spread("x", lambda p: r.mid_b.at[p], lambda q: r.mid_far_b.at[q], True),
    ]
    finish(seconds)
    for k in range(4):
        r.kv_sum[k, 0] = summed(r.kv_two_a.at[k]).astype(BF16)
        r.kv_sum[k, 1] = summed(r.kv_two_b.at[k]).astype(BF16)
    kv_third = spread("z", lambda p: r.kv_sum.at[p], lambda q: r.dkv.at[q], True)
    push(*kv_third)
    begin(mid)
    for j in range(SLOTS):
        to_owner(r.dq_buf, r.dq, dq_send, dq_recv, j, "wait")
    from_workers(r.dq_buf, r.dq, dq_send, dq_recv)

    query_gain = queries_back(r)

    @pl.loop(0, 4)
    def _(m):
        step = first_dims(r.hidden[:, tiles(m, 256)], r.grad_in[:, :256]).astype(BF16)
        r.qkv[m, :, :, :, :, :256] = step.reshape(4, 2, 2, 16, 256)

    def columns(first, last):
        at = pl.ds(first, last - first)
        return [
            spread(
                "x",
                lambda p: r.qkv.at[:, p, :, 0, :, at],
                lambda q: r.one_a.at[q, :, :, :, at],
                True,
            ),
            spread(
                "z",
                lambda p: r.qkv.at[p, :, :, 1, :, at],
                lambda q: r.one_b.at[q, :, :, :, at],
                True,
            ),
        ]

    one = columns(0, 512)
    begin(one)
    settle(*kv_third)
    key_gain, attn_gain = keys_back(r)
    vectors = ((attn_gain, 32), (r.ffn_gain[...], 32), (query_gain, 2), (key_gain, 2))
    stage(spread("core", lambda p: r.parts_back.at[:, p], lambda q: r.back_half.at[q], True))
    r.back_chip[...] = summed(r.back_half).astype(BF16)
    sums = spread("near", lambda p: r.back_chip.at[p], lambda q: r.landed_back.at[q], True)
    push(*sums)

    @pl.loop(0, 4)
    def _(m):
        step = first_dims(r.hidden[:, tiles(m, 256)], r.grad_in[:, 256:]).astype(BF16)
        r.qkv[m, :, :, :, :, 512:] = step.reshape(4, 2, 2, 16, 256)

    pieces = jnp.zeros((NCTX, 8, 128), F32)
    for row, (vector, per) in enumerate(vectors):
        piece = jnp.broadcast_to(owner_pieces(vector, per)[:, None, :], pieces.shape)
        pieces = jnp.where(iota(pieces.shape, 1) == row, piece, pieces)
    r.gain_pieces[...] = pieces.reshape(r.gain_pieces.shape)
    rest = columns(512, 768)
    rest.append(spread("x", lambda p: r.gain_pieces.at[:, p], lambda q: r.one_g.at[q], True))
    begin(rest)
    one += rest
    finish(mid)
    r.end_ab[:, 0] = summed(r.mid_far_a).astype(BF16)
    r.end_ab[:, 1] = summed(r.mid_far_b).astype(BF16)
    swap = spread("pair", lambda p: r.end_ab.at[p], lambda q: r.ffn_all.at[q], True)
    push(*swap)
    settle(*ffn_rows)
    r.output[...] = (r.residual[...] + summed(r.ffn_parts)).astype(BF16)
    share = [spread("tp", lambda p: r.output, lambda q: r.output_all.at[q], True)]
    rows = r.rows_in[tiles(t, own)].astype(F32)
    scale = row_scale(rows)
    normed = rows * scale
    settle(*sums)
    result = r.grad_residual[...] + row_back(
        summed(r.landed_back), normed, scale, r.gain_attn[...]
    )
    r.input_bf[...] = result.astype(BF16)
    share.append(spread("tp", lambda p: r.input_bf, lambda q: r.input_all.at[q], True))
    begin(share)
    finish(one)
    r.sum_a[...] = summed(r.one_a).astype(BF16)
    r.sum_b[...] = summed(r.one_b).astype(BF16)
    r.sum_g[...] = summed(r.one_g)
    stage(
        spread("z", lambda p: r.sum_a.at[p], lambda q: r.two_a.at[q], True),
        spread("x", lambda p: r.sum_b.at[p], lambda q: r.two_b.at[q], True),
        spread("z", lambda p: r.sum_g.at[p], lambda q: r.two_g.at[q], True),
    )
    r.part_a[...] = summed(r.two_a).astype(BF16)
    r.part_b[...] = summed(r.two_b).astype(BF16)
    r.part_g[...] = summed(r.two_g)
    stage(
        spread("pair", lambda p: r.part_a.at[p], lambda q: r.three_a.at[q], True),
        spread("pair", lambda p: r.part_b.at[p], lambda q: r.three_b.at[q], True),
        spread("pair", lambda p: r.part_g.at[p], lambda q: r.three_g.at[q], True),
    )
    r.gain_sum[...] = summed(r.three_g)
    share.append(spread("tp", lambda p: r.gain_sum, lambda q: r.gain_tp.at[q], True))
    push(*share[-1])
    r.qkv_grad[0] = summed(r.three_a)
    r.qkv_grad[1] = summed(r.three_b)
    finish(share)
    settle(*swap)


def whole(weights, gains, ffn, wo, cot, rows_in, cosine, sine):
    rows, width = rows_in.shape
    arrays = scratch_arrays(rows, width, weights.shape[2], wo.shape[2])
    names = INPUTS + OUTPUTS + tuple(arrays)
    return pl.pallas_call(
        functools.partial(whole_body, names),
        out_shape=[
            jax.ShapeDtypeStruct((2, 16, weights.shape[2] + wo.shape[2]), F32),
            jax.ShapeDtypeStruct(ffn.shape, BF16),
            jax.ShapeDtypeStruct((4, rows // 4, width), BF16),
            jax.ShapeDtypeStruct((4, rows // 4, width), BF16),
            jax.ShapeDtypeStruct((4, 8, 128), F32),
        ],
        in_specs=[ANY] * 5 + [VMEM] * 3,
        out_specs=[VMEM] + [ANY] * 4,
        scratch_shapes=[pltpu.VMEM(shape, dtype) for shape, dtype in arrays.values()]
        + [pltpu.SemaphoreType.DMA((SEMAPHORES,))],
        compiler_params=pltpu.CompilerParams(
            collective_id=1, has_side_effects=True, vmem_limit_bytes=60 * 2**20
        ),
        name="block",
    )(weights, gains, ffn, wo, cot, rows_in, cosine, sine)


def rope_tables(tokens, offset):
    half = HEAD_SIZE // 2
    inverse = ROPE_BASE ** (-(jnp.arange(half, dtype=F32) * 2.0 / HEAD_SIZE))
    steps = (offset + jnp.arange(tokens, dtype=jnp.int32)).astype(F32)
    angles = steps[:, None] * jnp.tile(inverse, 4)[None, :]
    signs = jnp.where(jnp.arange(4 * half) % HEAD_SIZE < half, -1.0, 1.0)
    return jnp.cos(angles), jnp.sin(angles) * signs[None, :]


def halves(*weights):
    rows, cols = weights[0].shape
    w = jnp.stack(weights).reshape(len(weights), rows, 2, cols // 2)
    w = jnp.pad(w, ((0, 0), (0, 0), (0, 0), (0, UNITS - cols // 2)))
    return w.transpose(2, 1, 0, 3).reshape(2, rows, len(weights) * UNITS)


def local(
    block_input, cotangent, w_query, key_weight, w_value, w_out, w_gate, w_up, w_down,
    norm_gains, head_gains,
):
    seqs, tokens, width = block_input.shape
    rows = seqs * tokens
    unit_half = w_gate.shape[1] // 2
    rows_in = block_input.reshape(rows, width)
    cot_rows = cotangent.reshape(rows, width)
    cosine, sine = rope_tables(tokens, lax.axis_index("ctx") * tokens)
    weight_rows = jnp.concatenate([w_query, key_weight, w_value], axis=1)
    gains = jnp.pad(norm_gains, ((0, 14), (0, 96))) + jnp.pad(head_gains, ((2, 12), (0, 126)))
    ffn = halves(w_gate, w_up, w_down)
    qkv_grad, pair_grads, output_all, input_all, gain_tp = whole(
        weight_rows.reshape(2, 16, weight_rows.shape[1]),
        gains,
        ffn.reshape(2, 2, 16, ffn.shape[2]),
        w_out.reshape(2, 16, w_out.shape[1]),
        cot_rows,
        rows_in,
        cosine,
        sine,
    )
    pair_grads = pair_grads.reshape(ffn.shape)
    pair_grads = pair_grads.astype(F32)
    gain_sum = jnp.sum(gain_tp, axis=0)
    qkv_grad = qkv_grad.reshape(32, 768)

    def joined(first):
        last = first + unit_half
        return jnp.concatenate([pair_grads[0, :, first:last], pair_grads[1, :, first:last]], axis=1)

    gate_grad, up_grad, down_grad = joined(0), joined(UNITS), joined(2 * UNITS)
    return (
        output_all.reshape(seqs, tokens, width),
        input_all.astype(F32).reshape(seqs, tokens, width),
        qkv_grad[:, :256],
        qkv_grad[:, 512:640],
        qkv_grad[:, 640:],
        qkv_grad[:, 256:512],
        gate_grad,
        up_grad,
        down_grad,
        gain_sum[0:2, :32],
        gain_sum[2:4, :2],
    )


def solution(mesh):
    tokens, weights = P(None, "ctx", None), P("ctx", "tp")
    return jax.shard_map(
        local,
        mesh=mesh,
        in_specs=(tokens,) * 2 + (weights,) * 7 + (P(None, "ctx"),) * 2,
        out_specs=(tokens,) * 2 + (weights,) * 7 + (P(None, "ctx"),) * 2,
        check_vma=False,
    )
```

```python
import functools
import types

import jax
import jax.numpy as jnp
from jax import lax
from jax.experimental import pallas as pl
from jax.experimental.pallas import tpu as pltpu
from jax.sharding import PartitionSpec as P

HEAD_SIZE = 64
EPSILON = 1e-06
ROPE_BASE = 1000000.0
MESH = pl.DeviceIdType.MESH
F32 = jnp.float32
BF16 = jnp.bfloat16
ANY = pl.BlockSpec(memory_space=pl.ANY)
VMEM = pl.BlockSpec(memory_space=pltpu.VMEM)
NCTX = 32
PAIRS = 4
WORKERS = 8
SLOTS = 4
BLOCK = 128
CHUNK = 512


def group(kind):
    c, t = lax.axis_index("ctx"), lax.axis_index("tp")
    h = lax.rem(c, 2)
    if kind == "ctx":
        return NCTX, c, lambda p: (p, t)
    if kind == "tp":
        return 4, t, lambda p: (c, p)
    if kind == "pair":
        return 2, h, lambda p: (c - h + p, t)
    z, x, core = c // 8, lax.rem(c // 2, 4), lax.rem(t, 2)
    if kind == "z":
        return 4, z, lambda p: (c + (p - z) * 8, t)
    if kind == "x":
        return 4, x, lambda p: (c + (p - x) * 2, t)
    if kind == "core":
        return 2, core, lambda p: (c, t - core + p)
    if kind == "near":
        return 2, t // 2, lambda p: (c, p * 2 + core)
    if kind == "ring":
        return 4, h * 2 + t // 2, lambda p: (c - h + p // 2, lax.rem(p, 2) * 2 + core)
    return 8, h * 4 + t, lambda p: (c - h + p // 4, lax.rem(p, 4))


def push(kind, src_of, dst_of, send, recv, local=False):
    n, me, dev = group(kind)

    @pl.loop(1, n)
    def _(i):
        p = lax.rem(me + i, n)
        pltpu.make_async_remote_copy(
            src_ref=src_of(p),
            dst_ref=dst_of(me),
            send_sem=send.at[p],
            recv_sem=recv.at[me],
            device_id=dev(p),
            device_id_type=MESH,
        ).start()

    if local:
        pltpu.make_async_copy(src_of(me), dst_of(me), recv.at[me]).start()


def settle(kind, src_of, dst_of, send, recv, local=False):
    n, me, dev = group(kind)

    @pl.loop(1, n)
    def _(i):
        p = lax.rem(me + i, n)
        copy = pltpu.make_async_remote_copy(
            src_ref=src_of(p),
            dst_ref=dst_of(p),
            send_sem=send.at[p],
            recv_sem=recv.at[p],
            device_id=dev(p),
            device_id_type=MESH,
        )
        copy.wait_send()
        copy.wait_recv()

    if local:
        pltpu.make_async_copy(src_of(me), dst_of(me), recv.at[me]).wait()


def stage(*moves):
    for move in moves:
        push(*move)
    for move in moves:
        settle(*move)


class Sems:
    def __init__(self, ref):
        self.ref, self.used = ref, 0

    def two(self, n):
        at = self.used
        self.used += 2 * n
        return self.ref.at[pl.ds(at, n)], self.ref.at[pl.ds(at + n, n)]


def position():
    c = lax.axis_index("ctx")
    return c // 8, lax.rem(c // 2, 4), lax.rem(c, 2)


def iota(shape, axis):
    return lax.broadcasted_iota(jnp.int32, shape, axis)


def two_parts(v):
    high = v.astype(BF16)
    return high, (v - high.astype(F32)).astype(BF16)


def exact_dot(v, pattern):
    high, low = two_parts(v)
    return jnp.dot(high, pattern, preferred_element_type=F32) + jnp.dot(
        low, pattern, preferred_element_type=F32
    )


def head_mean(v):
    n = v.shape[1]
    same = lax.div(iota((n, n), 0), HEAD_SIZE) == lax.div(iota((n, n), 1), HEAD_SIZE)
    return exact_dot(v, jnp.where(same, 1.0 / HEAD_SIZE, 0.0).astype(BF16))


def head_scale(v):
    return lax.rsqrt(head_mean(v * v) + EPSILON)


def turned(u, cosine, sine):
    half, n = HEAD_SIZE // 2, 2 * HEAD_SIZE
    first = lax.rem(iota(u.shape, 1), HEAD_SIZE) < half
    other = jnp.where(first, pltpu.roll(u, n - half, 1), pltpu.roll(u, half, 1))
    return u * cosine + other * sine


def crossed(tile):
    return pltpu.roll(tile, HEAD_SIZE, 1)


def left_lanes(tile):
    return iota(tile.shape, 1) < HEAD_SIZE


def spread_gain(pieces, row, per, lanes):
    n = pieces.shape[0]
    pick = iota((NCTX, n), 1) == iota((NCTX, n), 0) * (n // NCTX) + row
    mine = jnp.dot(pick.astype(F32).astype(BF16), pieces, preferred_element_type=F32).astype(BF16)
    pattern = (lax.rem(iota((128, lanes), 1), per) == iota((128, lanes), 0)).astype(F32)
    wide = jnp.dot(mine, pattern.astype(BF16), preferred_element_type=F32)
    owner = lax.div(lax.rem(iota(wide.shape, 1), NCTX * per), per)
    return jnp.sum(jnp.where(owner == iota(wide.shape, 0), wide, 0.0), axis=0, keepdims=True)


def owner_pieces(vector, per):
    lanes = vector.shape[1]
    shape = (NCTX, lanes)
    owner = lax.div(lax.rem(iota(shape, 1), NCTX * per), per)
    parts = jnp.where(owner == iota(shape, 0), jnp.broadcast_to(vector, shape), 0.0)
    pattern = (lax.rem(iota((lanes, 128), 0), per) == iota((lanes, 128), 1)).astype(F32)
    return exact_dot(parts, pattern.astype(BF16))


def row_scale(rows):
    return lax.rsqrt(jnp.mean(rows * rows, axis=1, keepdims=True) + EPSILON)


def twice(table):
    return jnp.concatenate([table[...], table[...]], axis=0)


def places():
    c, t = lax.axis_index("ctx"), lax.axis_index("tp")
    slot, low = c // WORKERS, lax.rem(c, WORKERS)
    to = low + lax.rem(slot, 2) * (WORKERS - 1 - 2 * low)
    return c, t, slot, low, to


def block_of(low, j):
    return j * WORKERS + (low if j % 2 == 0 else WORKERS - 1 - low)


def greet_attention(kinds):
    c, t, slot, low, to = places()
    barrier = pltpu.get_barrier_semaphore()
    total = 0
    others = [p * WORKERS + to for p in range(PAIRS)] + [block_of(low, j) for j in range(SLOTS)]
    for other in others:

        @pl.when(other != c)
        def _():
            pl.semaphore_signal(barrier, inc=1, device_id=(other, t), device_id_type=MESH)

        total = total + jnp.where(other != c, 1, 0)
    for kind in kinds:
        n, me, dev = group(kind)

        @pl.loop(1, n)
        def _(i):
            pl.semaphore_signal(
                barrier, inc=1, device_id=dev(lax.rem(me + i, n)), device_id_type=MESH
            )

        total = total + (n - 1)
    pl.semaphore_wait(barrier, total)


def to_workers(src, dst, send, recv, act):
    c, t, slot, low, to = places()
    for p in range(PAIRS):
        target = p * WORKERS + to
        far = pltpu.make_async_remote_copy(
            src_ref=src.at[p],
            dst_ref=dst.at[slot],
            send_sem=send.at[p],
            recv_sem=recv.at[slot],
            device_id=(target, t),
            device_id_type=MESH,
        )
        near = pltpu.make_async_copy(src.at[p], dst.at[slot], send.at[p])

        @pl.when(target != c)
        def _():
            far.start() if act == "start" else far.wait_send()

        @pl.when(target == c)
        def _():
            near.start() if act == "start" else near.wait()


def from_owners(src, dst, send, recv):
    c, t, slot, low, to = places()
    for j in range(SLOTS):
        owner = block_of(low, j)

        @pl.when(owner != c)
        def _():
            pltpu.make_async_remote_copy(
                src_ref=src.at[j],
                dst_ref=dst.at[j],
                send_sem=send.at[j],
                recv_sem=recv.at[j],
                device_id=(owner, t),
                device_id_type=MESH,
            ).wait_recv()


def to_owner(src, dst, send, recv, j, act):
    c, t, slot, low, to = places()
    owner = block_of(low, j)
    far = pltpu.make_async_remote_copy(
        src_ref=src.at[j],
        dst_ref=dst.at[slot],
        send_sem=send.at[j],
        recv_sem=recv.at[slot],
        device_id=(owner, t),
        device_id_type=MESH,
    )
    near = pltpu.make_async_copy(src.at[j], dst.at[slot], send.at[j])

    @pl.when(owner != c)
    def _():
        far.start() if act == "start" else far.wait_send()

    @pl.when(owner == c)
    def _():
        near.start() if act == "start" else near.wait()


def from_workers(src, dst, send, recv):
    c, t, slot, low, to = places()
    for p in range(PAIRS):
        target = p * WORKERS + to

        @pl.when(target != c)
        def _():
            pltpu.make_async_remote_copy(
                src_ref=src.at[p],
                dst_ref=dst.at[p],
                send_sem=send.at[p],
                recv_sem=recv.at[p],
                device_id=(target, t),
                device_id_type=MESH,
            ).wait_recv()


def last_dims(a, b):
    return lax.dot_general(a, b, (((1,), (1,)), ((), ())), preferred_element_type=F32)


def first_dims(a, b):
    return lax.dot_general(a, b, (((0,), (0,)), ((), ())), preferred_element_type=F32)


def causal_mask(b, i):
    shape = (2 * BLOCK, CHUNK)
    rows = lax.broadcasted_iota(jnp.int32, shape, 0)
    token = b * BLOCK + jnp.where(rows >= BLOCK, rows - BLOCK, rows)
    key = i * CHUNK + lax.broadcasted_iota(jnp.int32, shape, 1)
    return token >= key


def row_back(grads, normed, scale, gain):
    scaled = grads * gain
    return scale * (scaled - normed * jnp.mean(scaled * normed, axis=1, keepdims=True))


def summed(ref):
    total = ref[0].astype(F32)
    for k in range(1, ref.shape[0]):
        total += ref[k].astype(F32)
    return total


UNITS = 640
INPUTS = ("w_query", "w_key", "w_value", "gains", "ffn", "wo", "cot", "rows_in", "cosine", "sine")
OUTPUTS = ("qkv_grad", "ffn_all", "output_all", "input_all", "gain_tp")
SIZES = {"tp": 4, "pair": 2, "rows": 8, "z": 4, "x": 4, "core": 2, "ring": 4, "near": 2}
SEMAPHORES = 580


def scratch_arrays(rows, width, qkv_cols, out_cols):
    own, half = rows // 4, BLOCK // 2
    stack = (SLOTS, 2 * BLOCK, BLOCK)
    grid, piece = (4, 4, 2, 2), (16, qkv_cols + out_cols)
    units = (16, 3 * UNITS)
    return dict(
        w_own=((2, 16, qkv_cols), BF16),
        w_all=((*grid, 16, qkv_cols), BF16),
        gains_all=((4, 4, 2, 16, 128), BF16),
        w_ffn=((*grid, *units), BF16),
        wo_all=((*grid, 16, out_cols), BF16),
        cot_all=((2, rows, width), BF16),
        hidden=((rows, width), BF16),
        raw=((rows, qkv_cols), F32),
        q_src=(stack, BF16),
        kv_src=((PAIRS, 2, half, BLOCK), BF16),
        gain_attn=((1, width), F32),
        gain_ffn=((1, width), F32),
        gain_query=((1, 128), F32),
        gain_key=((1, 128), F32),
        q_buf=(stack, BF16),
        kv_buf=((*grid, half, BLOCK), BF16),
        o_buf=(stack, BF16),
        log_buf=(stack, F32),
        att=(stack, BF16),
        acc=((2 * BLOCK, BLOCK), F32),
        den=((2 * BLOCK, BLOCK), F32),
        attended=((rows, out_cols), BF16),
        parts=((2, 2, own, width), BF16),
        parts_half=((2, 2, own, width), BF16),
        parts_chip=((2, own, width), BF16),
        landed=((2, own, width), BF16),
        residual=((own, width), F32),
        hidden_own=((own, width), BF16),
        hidden_all=((4, 2, own, width), BF16),
        grad_units=((2 * rows, UNITS), F32),
        units=((2 * rows, UNITS), BF16),
        units_in=((2 * rows, 2 * UNITS), BF16),
        back=((4, 2, own, width), BF16),
        halved=((2, 4, own, width), BF16),
        chip=((4, own, width), BF16),
        ringed=((4, own, width), BF16),
        grad_bf=((own, width), BF16),
        grad_all=((2, 2, own, width), BF16),
        grad_residual=((own, width), F32),
        ffn_gain=((1, width), F32),
        grads=((*grid, *units), BF16),
        ffn_part=((8, own, width), BF16),
        ffn_parts=((8, own, width), BF16),
        far_a=((4, 4, 2, *units), BF16),
        far_b=((4, 4, 2, *units), BF16),
        mid_a=((4, 2, *units), BF16),
        mid_b=((4, 2, *units), BF16),
        mid_far_a=((4, 2, *units), BF16),
        mid_far_b=((4, 2, *units), BF16),
        end_ab=((2, 2, *units), BF16),
        do_src=(stack, BF16),
        do_buf=(stack, BF16),
        dq_buf=(stack, BF16),
        dq=(stack, BF16),
        dkv_sum=((*grid, half, BLOCK), F32),
        dkv_buf=((*grid, half, BLOCK), BF16),
        kv_one_a=((4, 4, 2, half, BLOCK), BF16),
        kv_one_b=((4, 2, 4, half, BLOCK), BF16),
        kv_sum_a=((4, 2, half, BLOCK), BF16),
        kv_sum_b=((4, 4, half, BLOCK), BF16),
        kv_two_a=((4, 2, half, BLOCK), BF16),
        kv_two_b=((4, 4, half, BLOCK), BF16),
        kv_sum=((4, 2, half, BLOCK), BF16),
        dkv=((PAIRS, 2, half, BLOCK), BF16),
        parts_back=((2, 2, own, width), BF16),
        back_half=((2, 2, own, width), BF16),
        back_chip=((2, own, width), BF16),
        landed_back=((2, own, width), BF16),
        grad_in=((rows, qkv_cols), BF16),
        gain_pieces=((4, 4, 2, 8, 128), F32),
        output=((own, width), BF16),
        input_bf=((own, width), BF16),
        qkv=((*grid, *piece), BF16),
        one_a=((4, 4, 2, *piece), BF16),
        one_b=((4, 4, 2, *piece), BF16),
        one_g=((4, 4, 2, 8, 128), F32),
        sum_a=((4, 2, *piece), BF16),
        sum_b=((4, 2, *piece), BF16),
        sum_g=((4, 2, 8, 128), F32),
        two_a=((4, 2, *piece), BF16),
        two_b=((4, 2, *piece), BF16),
        two_g=((4, 2, 8, 128), F32),
        part_a=((2, *piece), BF16),
        part_b=((2, *piece), BF16),
        part_g=((2, 8, 128), F32),
        three_a=((2, *piece), BF16),
        three_b=((2, *piece), BF16),
        three_g=((2, 8, 128), F32),
        gain_sum=((8, 128), F32),
    )


def project_keys(r):
    pieces = r.gains_all[...].reshape(NCTX * 16, 128)
    r.gain_attn[...] = spread_gain(pieces, 0, 32, r.gain_attn.shape[1])
    r.gain_query[...] = spread_gain(pieces, 2, 2, 128)
    r.gain_key[...] = spread_gain(pieces, 3, 2, 128)
    rows = r.rows_in[...].astype(F32)
    r.hidden[...] = (rows * row_scale(rows) * r.gain_attn[...]).astype(BF16)
    weights = r.w_all[:, :, :, :, :, 256:].reshape(r.hidden.shape[1], 256)
    r.raw[:, 256:] = jnp.dot(r.hidden[...], weights, preferred_element_type=F32)
    tile = r.raw[:, 256:384]
    keys = turned(tile * head_scale(tile) * r.gain_key[...], twice(r.cosine), twice(r.sine))
    values = r.raw[:, 384:512]
    for k in range(2):
        key, value = (keys, crossed(values)) if k == 0 else (crossed(keys), values)
        one = jnp.where(left_lanes(key), key, value).astype(BF16)
        for s in range(2):
            part = one[s * BLOCK : (s + 1) * BLOCK]
            r.kv_src[2 * k + s] = part.reshape(2, BLOCK // 2, 128)


def project_queries(r):
    weights = r.w_all[:, :, :, :, :, :256].reshape(r.hidden.shape[1], 256)
    r.raw[:, :256] = jnp.dot(r.hidden[...], weights, preferred_element_type=F32)
    cos, sin = twice(r.cosine), twice(r.sine)
    for k in range(2):
        tile = r.raw[:, k * 128 : k * 128 + 128]
        tile = turned(tile * head_scale(tile) * r.gain_query[...], cos, sin) * (HEAD_SIZE**-0.5)
        for a, one in enumerate((tile, crossed(tile))):
            one = jnp.where(left_lanes(one), one, 0.0).astype(BF16)
            for s in range(2):
                r.q_src[2 * k + s, a * BLOCK : (a + 1) * BLOCK] = one[s * BLOCK : (s + 1) * BLOCK]
    pieces = r.gains_all[...].reshape(NCTX * 16, 128)
    r.gain_ffn[...] = spread_gain(pieces, 1, 32, r.gain_ffn.shape[1])


def attend(r, low, j):
    b = block_of(low, j)
    r.acc[...] = jnp.zeros_like(r.acc)
    r.den[...] = jnp.zeros_like(r.den)

    def chunk(i, masked):
        kv = r.kv_buf[i // 2, pl.ds(2 * lax.rem(i, 2), 2)].reshape(CHUNK, BLOCK)
        powered = jnp.exp(last_dims(r.q_buf[j], kv))
        if masked:
            powered = jnp.where(causal_mask(b, i), powered, 0.0)
        r.den[...] += sum(powered[:, k : k + BLOCK] for k in range(0, CHUNK, BLOCK))
        r.acc[...] += jnp.dot(powered.astype(BF16), kv, preferred_element_type=F32)

    last = b // (CHUNK // BLOCK)
    pl.loop(0, last)(lambda i: chunk(i, False))
    chunk(last, True)
    total = jnp.sum(r.den[...], axis=1, keepdims=True)
    lanes = iota((2 * BLOCK, BLOCK), 1)
    r.o_buf[j] = jnp.where(lanes >= HEAD_SIZE, r.acc[...] / total, 0.0).astype(BF16)
    r.log_buf[j] = jnp.broadcast_to(jnp.log(total), (2 * BLOCK, BLOCK))


def attend_back(r, low, j):
    b = block_of(low, j)
    r.acc[...] = jnp.zeros_like(r.acc)
    delta = jnp.sum(r.do_buf[j].astype(F32) * r.o_buf[j].astype(F32), axis=1, keepdims=True)

    def chunk(i, masked):
        q, do, logs = r.q_buf[j], r.do_buf[j], r.log_buf[j]
        kv = r.kv_buf[i // 2, pl.ds(2 * lax.rem(i, 2), 2)].reshape(CHUNK, BLOCK)
        probs = jnp.exp(last_dims(q, kv) - jnp.concatenate([logs] * (CHUNK // BLOCK), axis=1))
        if masked:
            probs = jnp.where(causal_mask(b, i), probs, 0.0)
        grads = (probs * (last_dims(do, kv) - delta)).astype(BF16)
        r.acc[...] += jnp.dot(grads, kv, preferred_element_type=F32)
        update = first_dims(grads, q) + first_dims(probs.astype(BF16), do)
        at = pl.ds(2 * lax.rem(i, 2), 2)
        r.dkv_sum[i // 2, at] += update.reshape(2, 2, 2, BLOCK // 2, BLOCK)

    last = b // (CHUNK // BLOCK)
    pl.loop(0, last)(lambda i: chunk(i, False))
    chunk(last, True)
    r.dq_buf[j] = (r.acc[...] * (HEAD_SIZE**-0.5)).astype(BF16)


def tiles(m, n):
    return pl.ds(pl.multiple_of(m * n, n), n)


def both_rows(first, second):
    return jnp.concatenate([first.astype(F32), second.astype(F32)], axis=0)


def head_back(r, u, tile, gain_row):
    turn = turned(u, twice(r.cosine), -twice(r.sine))
    scale = head_scale(tile)
    hat = tile * scale
    scaled = turn * gain_row
    back = scale * (scaled - hat * head_mean(scaled * hat))
    return back.astype(BF16), jnp.sum(turn * hat, axis=0, keepdims=True)


def queries_back(r):
    query_gain = jnp.zeros((1, 128), F32)
    for k in range(2):
        first = both_rows(r.dq[2 * k, :BLOCK], r.dq[2 * k + 1, :BLOCK])
        second = crossed(both_rows(r.dq[2 * k, BLOCK:], r.dq[2 * k + 1, BLOCK:]))
        lanes = slice(k * 128, (k + 1) * 128)
        u = jnp.where(left_lanes(first), first, second)
        r.grad_in[:, lanes], part = head_back(r, u, r.raw[:, lanes], r.gain_query[...])
        query_gain = query_gain + part
    return query_gain


def keys_back(r):
    own, width = r.residual.shape
    first, second = [
        both_rows(r.dkv[2 * k].reshape(BLOCK, 128), r.dkv[2 * k + 1].reshape(BLOCK, 128))
        for k in range(2)
    ]
    left = left_lanes(first)
    u = jnp.where(left, first, crossed(second))
    r.grad_in[:, 256:384], key_gain = head_back(r, u, r.raw[:, 256:384], r.gain_key[...])
    r.grad_in[:, 384:] = jnp.where(left, crossed(first), second).astype(BF16)
    attn_gain = jnp.zeros((1, width), F32)
    weights = r.w_all[...].reshape(width, r.grad_in.shape[1])
    for q in range(4):
        at = slice(q * own, (q + 1) * own)
        back = last_dims(r.grad_in[at], weights)
        r.parts_back[q // 2, q % 2] = back.astype(BF16)
        rows = r.rows_in[at].astype(F32)
        attn_gain = attn_gain + jnp.sum(back * (rows * row_scale(rows)), axis=0, keepdims=True)
    return key_gain, attn_gain


def begin(moves):
    for move in moves:
        push(*move)


def finish(moves):
    for move in moves:
        settle(*move)


def whole_body(names, *refs):
    r = types.SimpleNamespace(**dict(zip(names, refs)))
    take = Sems(refs[-1])
    c, t, slot, low, to = places()
    z, x, h = position()
    core = lax.rem(t, 2)
    own, width = r.residual.shape

    def spread(kind, src_of, dst_of, local=False):
        return (kind, src_of, dst_of, *take.two(SIZES[kind]), local)

    def gathered(ref):
        second = [
            spread("x", lambda p: ref.at[z, x, :, 0], lambda q: ref.at[z, q, :, 0]),
            spread("z", lambda p: ref.at[z, x, :, 1], lambda q: ref.at[q, x, :, 1]),
        ]
        third = [
            spread("z", lambda p: ref.at[z, :, :, 0], lambda q: ref.at[q, :, :, 0]),
            spread("x", lambda p: ref.at[:, x, :, 1], lambda q: ref.at[:, q, :, 1]),
        ]
        return second, third

    loads, first = [], 0
    load_sems = take.two(4)[0]
    for k, ref in enumerate((r.w_query, r.w_key, r.w_value)):
        cols = ref.shape[2]
        at = pl.ds(first, cols)
        loads.append(pltpu.make_async_copy(ref, r.w_own.at[:, :, at], load_sems.at[k]))
        first += cols
    for load in loads:
        load.start()
    greet_attention(["z", "x", "rows"])
    for load in loads:
        load.wait()
    first = [
        spread("pair", lambda p: r.w_own, lambda q: r.w_all.at[z, x, q], True),
        spread("pair", lambda p: r.gains, lambda q: r.gains_all.at[z, x, q], True),
    ]
    late = [
        spread("pair", lambda p: r.wo, lambda q: r.wo_all.at[z, x, q], True),
        spread("pair", lambda p: r.ffn.at[p], lambda q: r.w_ffn.at[z, x, q], True),
    ]
    begin(first)
    begin(late)
    finish(first)
    second, third = gathered(r.w_all)
    second.append(spread("x", lambda p: r.gains_all.at[z, x], lambda q: r.gains_all.at[z, q]))
    third.append(spread("z", lambda p: r.gains_all.at[z], lambda q: r.gains_all.at[q]))
    stage(*second)
    stage(*third)
    finish(late)
    out_second, out_third = gathered(r.wo_all)
    ffn_second, ffn_third = gathered(r.w_ffn)
    begin(out_second + ffn_second)
    project_keys(r)

    q_send, q_recv = take.two(SLOTS)
    near = spread("z", lambda p: r.kv_src.at[p], lambda q: r.kv_buf.at[q, x, h], True)
    push(*near)
    project_queries(r)
    to_workers(r.q_src, r.q_buf, q_send, q_recv, "start")
    settle(*near)
    kv = r.kv_buf

    def planes(k):
        return [
            spread("x", lambda p: kv.at[k, x, h, 0], lambda q: kv.at[k, q, h, 0]),
            spread("pair", lambda p: kv.at[k, x, h, 1], lambda q: kv.at[k, x, q, 1]),
        ], [
            spread("pair", lambda p: kv.at[k, :, h, 0], lambda q: kv.at[k, :, q, 0]),
            spread("x", lambda p: kv.at[k, x, :, 1], lambda q: kv.at[k, q, :, 1]),
        ]

    plane_moves = [planes(k) for k in range(4)]
    for early, _ in plane_moves:
        begin(early)
    for early, then in plane_moves:
        finish(early)
        begin(then)
    finish(out_second + ffn_second)
    begin(out_third)
    begin(ffn_third)
    cot_swap = spread("pair", lambda p: r.cot, lambda q: r.cot_all.at[q], True)
    push(*cot_swap)
    to_workers(r.q_src, r.q_buf, q_send, q_recv, "wait")
    from_owners(r.q_src, r.q_buf, q_send, q_recv)
    o_send, o_recv = take.two(SLOTS)
    for j in range(SLOTS):
        finish(plane_moves[j][1])
        attend(r, low, j)
        to_owner(r.o_buf, r.att, o_send, o_recv, j, "start")
    for j in range(SLOTS):
        to_owner(r.o_buf, r.att, o_send, o_recv, j, "wait")
    from_workers(r.o_buf, r.att, o_send, o_recv)

    for k in range(2):
        for s in range(2):
            left = crossed(r.att[2 * k + s, :BLOCK].astype(F32))
            right = r.att[2 * k + s, BLOCK:].astype(F32)
            one = jnp.where(left_lanes(left), left, right).astype(BF16)
            r.attended[s * BLOCK : (s + 1) * BLOCK, k * 128 : (k + 1) * 128] = one
    finish(out_third)
    out_full = r.wo_all[...].reshape(width, r.attended.shape[1])
    r.parts[...] = last_dims(r.attended[...], out_full).astype(BF16).reshape(r.parts.shape)
    stage(spread("core", lambda p: r.parts.at[:, p], lambda q: r.parts_half.at[q], True))
    r.parts_chip[...] = summed(r.parts_half).astype(BF16)
    stage(spread("near", lambda p: r.parts_chip.at[p], lambda q: r.landed.at[q], True))
    rows = r.rows_in[tiles(t, own)].astype(F32) + summed(r.landed)
    r.residual[...] = rows
    r.hidden_own[...] = (rows * row_scale(rows) * r.gain_ffn[...]).astype(BF16)
    ring = spread("ring", lambda p: r.hidden_own, lambda q: r.hidden_all.at[q, core], True)
    push(*ring)
    settle(*cot_swap)
    finish(ffn_third)
    w = r.w_ffn.reshape(width, 3 * UNITS)
    cot = r.cot_all.reshape(8 * own, width)

    @pl.loop(0, 4)
    def _(m):
        at = tiles(m, 2 * own)
        r.grad_units[at] = jnp.dot(cot[at], w[:, 2 * UNITS :], preferred_element_type=F32)

    settle(*ring)
    hidden = r.hidden_all
    stage(spread("core", lambda p: hidden.at[:, core], lambda q: hidden.at[:, q]))

    @pl.loop(0, 2)
    def _(m):
        at = tiles(m, 4 * own)
        some = hidden[pl.ds(2 * m, 2)].reshape(4 * own, width)
        gate = jnp.dot(some, w[:, :UNITS], preferred_element_type=F32)
        up = jnp.dot(some, w[:, UNITS : 2 * UNITS], preferred_element_type=F32)
        sigmoid = jax.nn.sigmoid(gate)
        activated = gate * sigmoid
        r.units[at] = (activated * up).astype(BF16)
        grad = r.grad_units[at]
        r.units_in[at, :UNITS] = (grad * up * sigmoid * (1.0 + gate * (1.0 - sigmoid))).astype(BF16)
        r.units_in[at, UNITS:] = (grad * activated).astype(BF16)
        step = last_dims(r.units_in[at], w[:, : 2 * UNITS]).astype(BF16)
        r.back[pl.ds(2 * m, 2)] = step.reshape(2, *r.back.shape[1:])

    both = spread("core", lambda p: r.back.at[:, p], lambda q: r.halved.at[q], True)
    push(*both)

    @pl.loop(0, 4)
    def _(m):
        step = first_dims(cot[:, tiles(m, 256)], r.units[...]).astype(BF16)
        r.grads[m, :, :, :, :, 2 * UNITS :] = step.reshape(4, 2, 2, 16, UNITS)

    settle(*both)
    r.chip[...] = summed(r.halved).astype(BF16)
    ring = spread("ring", lambda p: r.chip.at[p], lambda q: r.ringed.at[q], True)
    push(*ring)

    @pl.loop(0, 4)
    def _(m):
        some = hidden[:, :, :, tiles(m, 256)].reshape(8 * own, 256)
        step = first_dims(some, r.units_in[...]).astype(BF16)
        r.grads[m, :, :, :, :, : 2 * UNITS] = step.reshape(4, 2, 2, 16, 2 * UNITS)

    far = [
        spread("x", lambda p: r.grads.at[:, p, :, 0], lambda q: r.far_a.at[q], True),
        spread("z", lambda p: r.grads.at[p, :, :, 1], lambda q: r.far_b.at[q], True),
    ]
    begin(far)
    settle(*ring)
    total = summed(r.ringed)
    rows = r.residual[...]
    scale = row_scale(rows)
    normed = rows * scale
    cot_own = cot[tiles(h * 4 + t, own)].astype(F32)
    result = cot_own + row_back(total, normed, scale, r.gain_ffn[...])
    r.grad_bf[...] = result.astype(BF16)
    share = spread("near", lambda p: r.grad_bf, lambda q: r.grad_all.at[q, core], True)
    push(*share)
    r.grad_residual[...] = result
    r.ffn_gain[...] = jnp.sum(total * normed, axis=0, keepdims=True)

    @pl.loop(0, 2)
    def _(m):
        step = last_dims(r.units[tiles(m, 4 * own)], w[:, 2 * UNITS :]).astype(BF16)
        r.ffn_part[pl.ds(4 * m, 4)] = step.reshape(4, *r.ffn_part.shape[1:])

    settle(*share)
    grad_all = r.grad_all
    stage(spread("core", lambda p: grad_all.at[:, core], lambda q: grad_all.at[:, q]))
    grad = jnp.dot(
        r.grad_all[...].reshape(4 * own, width), out_full, preferred_element_type=F32
    )
    for k in range(2):
        for s in range(2):
            tile = grad[s * BLOCK : (s + 1) * BLOCK, k * 128 : (k + 1) * 128]
            for a, one in enumerate((crossed(tile), tile)):
                one = jnp.where(left_lanes(one), 0.0, one).astype(BF16)
                r.do_src[2 * k + s, a * BLOCK : (a + 1) * BLOCK] = one

    do_send, do_recv = take.two(SLOTS)
    to_workers(r.do_src, r.do_buf, do_send, do_recv, "start")
    ffn_rows = spread("rows", lambda p: r.ffn_part.at[p], lambda q: r.ffn_parts.at[q], True)
    push(*ffn_rows)
    r.dkv_sum[...] = jnp.zeros_like(r.dkv_sum)

    @pl.loop(0, 4)
    def _(m):
        some = r.grad_all[:, :, :, tiles(m, 256)].reshape(4 * own, 256)
        step = first_dims(some, r.attended[...]).astype(BF16)
        r.qkv[m, :, :, :, :, 256:512] = step.reshape(4, 2, 2, 16, 256)

    to_workers(r.do_src, r.do_buf, do_send, do_recv, "wait")
    from_owners(r.do_src, r.do_buf, do_send, do_recv)
    dq_send, dq_recv = take.two(SLOTS)

    def kv_first(k):
        r.dkv_buf[k] = r.dkv_sum[k].astype(BF16)
        moves = [
            spread("x", lambda p: r.dkv_buf.at[k, p, :, 0], lambda q: r.kv_one_a.at[k, q], True),
            spread("pair", lambda p: r.dkv_buf.at[k, :, p, 1], lambda q: r.kv_one_b.at[k, q], True),
        ]
        begin(moves)
        return moves

    def kv_second(k, moves):
        finish(moves)
        r.kv_sum_a[k] = summed(r.kv_one_a.at[k]).astype(BF16)
        r.kv_sum_b[k] = summed(r.kv_one_b.at[k]).astype(BF16)
        moves = [
            spread("pair", lambda p: r.kv_sum_a.at[k, p], lambda q: r.kv_two_a.at[k, q], True),
            spread("x", lambda p: r.kv_sum_b.at[k, p], lambda q: r.kv_two_b.at[k, q], True),
        ]
        begin(moves)
        return moves

    firsts, seconds = {}, []
    for j in reversed(range(SLOTS)):
        attend_back(r, low, j)
        to_owner(r.dq_buf, r.dq, dq_send, dq_recv, j, "start")
        firsts[j] = kv_first(j)
        if j + 1 in firsts:
            seconds += kv_second(j + 1, firsts[j + 1])
    finish(far)

    @pl.loop(0, 4)
    def _(m):
        for src, dst in ((r.far_a, r.mid_a), (r.far_b, r.mid_b)):
            total = src[0, m].astype(F32)
            for k in range(1, 4):
                total += src[k, m].astype(F32)
            dst[m] = total.astype(BF16)

    seconds += kv_second(0, firsts[0])
    mid = [
        spread("z", lambda p: r.mid_a.at[p], lambda q: r.mid_far_a.at[q], True),
        spread("x", lambda p: r.mid_b.at[p], lambda q: r.mid_far_b.at[q], True),
    ]
    finish(seconds)
    for k in range(4):
        r.kv_sum[k, 0] = summed(r.kv_two_a.at[k]).astype(BF16)
        r.kv_sum[k, 1] = summed(r.kv_two_b.at[k]).astype(BF16)
    kv_third = spread("z", lambda p: r.kv_sum.at[p], lambda q: r.dkv.at[q], True)
    push(*kv_third)
    begin(mid)
    for j in range(SLOTS):
        to_owner(r.dq_buf, r.dq, dq_send, dq_recv, j, "wait")
    from_workers(r.dq_buf, r.dq, dq_send, dq_recv)

    query_gain = queries_back(r)

    @pl.loop(0, 4)
    def _(m):
        step = first_dims(r.hidden[:, tiles(m, 256)], r.grad_in[:, :256]).astype(BF16)
        r.qkv[m, :, :, :, :, :256] = step.reshape(4, 2, 2, 16, 256)

    def columns(first, last):
        at = pl.ds(first, last - first)
        return [
            spread(
                "x",
                lambda p: r.qkv.at[:, p, :, 0, :, at],
                lambda q: r.one_a.at[q, :, :, :, at],
                True,
            ),
            spread(
                "z",
                lambda p: r.qkv.at[p, :, :, 1, :, at],
                lambda q: r.one_b.at[q, :, :, :, at],
                True,
            ),
        ]

    one = columns(0, 512)
    begin(one)
    settle(*kv_third)
    key_gain, attn_gain = keys_back(r)
    vectors = ((attn_gain, 32), (r.ffn_gain[...], 32), (query_gain, 2), (key_gain, 2))
    stage(spread("core", lambda p: r.parts_back.at[:, p], lambda q: r.back_half.at[q], True))
    r.back_chip[...] = summed(r.back_half).astype(BF16)
    sums = spread("near", lambda p: r.back_chip.at[p], lambda q: r.landed_back.at[q], True)
    push(*sums)

    @pl.loop(0, 4)
    def _(m):
        step = first_dims(r.hidden[:, tiles(m, 256)], r.grad_in[:, 256:]).astype(BF16)
        r.qkv[m, :, :, :, :, 512:] = step.reshape(4, 2, 2, 16, 256)

    pieces = jnp.zeros((NCTX, 8, 128), F32)
    for row, (vector, per) in enumerate(vectors):
        piece = jnp.broadcast_to(owner_pieces(vector, per)[:, None, :], pieces.shape)
        pieces = jnp.where(iota(pieces.shape, 1) == row, piece, pieces)
    r.gain_pieces[...] = pieces.reshape(r.gain_pieces.shape)
    rest = columns(512, 768)
    rest.append(spread("x", lambda p: r.gain_pieces.at[:, p], lambda q: r.one_g.at[q], True))
    begin(rest)
    one += rest
    finish(mid)
    r.end_ab[:, 0] = summed(r.mid_far_a).astype(BF16)
    r.end_ab[:, 1] = summed(r.mid_far_b).astype(BF16)
    swap = spread("pair", lambda p: r.end_ab.at[p], lambda q: r.ffn_all.at[q], True)
    push(*swap)
    settle(*ffn_rows)
    r.output[...] = (r.residual[...] + summed(r.ffn_parts)).astype(BF16)
    share = [spread("tp", lambda p: r.output, lambda q: r.output_all.at[q], True)]
    rows = r.rows_in[tiles(t, own)].astype(F32)
    scale = row_scale(rows)
    normed = rows * scale
    settle(*sums)
    result = r.grad_residual[...] + row_back(
        summed(r.landed_back), normed, scale, r.gain_attn[...]
    )
    r.input_bf[...] = result.astype(BF16)
    share.append(spread("tp", lambda p: r.input_bf, lambda q: r.input_all.at[q], True))
    begin(share)
    finish(one)
    r.sum_a[...] = summed(r.one_a).astype(BF16)
    r.sum_b[...] = summed(r.one_b).astype(BF16)
    r.sum_g[...] = summed(r.one_g)
    stage(
        spread("z", lambda p: r.sum_a.at[p], lambda q: r.two_a.at[q], True),
        spread("x", lambda p: r.sum_b.at[p], lambda q: r.two_b.at[q], True),
        spread("z", lambda p: r.sum_g.at[p], lambda q: r.two_g.at[q], True),
    )
    r.part_a[...] = summed(r.two_a).astype(BF16)
    r.part_b[...] = summed(r.two_b).astype(BF16)
    r.part_g[...] = summed(r.two_g)
    stage(
        spread("pair", lambda p: r.part_a.at[p], lambda q: r.three_a.at[q], True),
        spread("pair", lambda p: r.part_b.at[p], lambda q: r.three_b.at[q], True),
        spread("pair", lambda p: r.part_g.at[p], lambda q: r.three_g.at[q], True),
    )
    r.gain_sum[...] = summed(r.three_g)
    share.append(spread("tp", lambda p: r.gain_sum, lambda q: r.gain_tp.at[q], True))
    push(*share[-1])
    r.qkv_grad[0] = summed(r.three_a)
    r.qkv_grad[1] = summed(r.three_b)
    finish(share)
    settle(*swap)


def whole(w_query, w_key, w_value, gains, ffn, wo, cot, rows_in, cosine, sine):
    rows, width = rows_in.shape
    cols = w_query.shape[2] + w_key.shape[2] + w_value.shape[2]
    arrays = scratch_arrays(rows, width, cols, wo.shape[2])
    names = INPUTS + OUTPUTS + tuple(arrays)
    return pl.pallas_call(
        functools.partial(whole_body, names),
        out_shape=[
            jax.ShapeDtypeStruct((2, 16, cols + wo.shape[2]), F32),
            jax.ShapeDtypeStruct(ffn.shape, BF16),
            jax.ShapeDtypeStruct((4, rows // 4, width), BF16),
            jax.ShapeDtypeStruct((4, rows // 4, width), BF16),
            jax.ShapeDtypeStruct((4, 8, 128), F32),
        ],
        in_specs=[ANY] * 7 + [VMEM] * 3,
        out_specs=[VMEM] + [ANY] * 4,
        scratch_shapes=[pltpu.VMEM(shape, dtype) for shape, dtype in arrays.values()]
        + [pltpu.SemaphoreType.DMA((SEMAPHORES,))],
        compiler_params=pltpu.CompilerParams(
            collective_id=1, has_side_effects=True, vmem_limit_bytes=60 * 2**20
        ),
        name="block",
    )(w_query, w_key, w_value, gains, ffn, wo, cot, rows_in, cosine, sine)


def rope_tables(tokens, offset):
    half = HEAD_SIZE // 2
    inverse = ROPE_BASE ** (-(jnp.arange(half, dtype=F32) * 2.0 / HEAD_SIZE))
    steps = (offset + jnp.arange(tokens, dtype=jnp.int32)).astype(F32)
    angles = steps[:, None] * jnp.tile(inverse, 4)[None, :]
    signs = jnp.where(jnp.arange(4 * half) % HEAD_SIZE < half, -1.0, 1.0)
    return jnp.cos(angles), jnp.sin(angles) * signs[None, :]


def halves(*weights):
    rows, cols = weights[0].shape
    w = jnp.stack(weights).reshape(len(weights), rows, 2, cols // 2)
    w = jnp.pad(w, ((0, 0), (0, 0), (0, 0), (0, UNITS - cols // 2)))
    return w.transpose(2, 1, 0, 3).reshape(2, rows, len(weights) * UNITS)


def local(
    block_input, cotangent, w_query, key_weight, w_value, w_out, w_gate, w_up, w_down,
    norm_gains, head_gains,
):
    seqs, tokens, width = block_input.shape
    rows = seqs * tokens
    unit_half = w_gate.shape[1] // 2
    rows_in = block_input.reshape(rows, width)
    cot_rows = cotangent.reshape(rows, width)
    cosine, sine = rope_tables(tokens, lax.axis_index("ctx") * tokens)
    gains = jnp.pad(norm_gains, ((0, 14), (0, 96))) + jnp.pad(head_gains, ((2, 12), (0, 126)))
    ffn = halves(w_gate, w_up, w_down)
    qkv_grad, pair_grads, output_all, input_all, gain_tp = whole(
        *(w.reshape(2, 16, w.shape[1]) for w in (w_query, key_weight, w_value)),
        gains,
        ffn.reshape(2, 2, 16, ffn.shape[2]),
        w_out.reshape(2, 16, w_out.shape[1]),
        cot_rows,
        rows_in,
        cosine,
        sine,
    )
    pair_grads = pair_grads.reshape(ffn.shape)
    pair_grads = pair_grads.astype(F32)
    gain_sum = jnp.sum(gain_tp, axis=0)
    qkv_grad = qkv_grad.reshape(32, 768)

    def joined(first):
        last = first + unit_half
        return jnp.concatenate([pair_grads[0, :, first:last], pair_grads[1, :, first:last]], axis=1)

    gate_grad, up_grad, down_grad = joined(0), joined(UNITS), joined(2 * UNITS)
    return (
        output_all.reshape(seqs, tokens, width),
        input_all.astype(F32).reshape(seqs, tokens, width),
        qkv_grad[:, :256],
        qkv_grad[:, 512:640],
        qkv_grad[:, 640:],
        qkv_grad[:, 256:512],
        gate_grad,
        up_grad,
        down_grad,
        gain_sum[0:2, :32],
        gain_sum[2:4, :2],
    )


def solution(mesh):
    tokens, weights = P(None, "ctx", None), P("ctx", "tp")
    return jax.shard_map(
        local,
        mesh=mesh,
        in_specs=(tokens,) * 2 + (weights,) * 7 + (P(None, "ctx"),) * 2,
        out_specs=(tokens,) * 2 + (weights,) * 7 + (P(None, "ctx"),) * 2,
        check_vma=False,
    )
```

```python
import functools
import types

import jax
import jax.numpy as jnp
from jax import lax
from jax.experimental import pallas as pl
from jax.experimental.pallas import tpu as pltpu
from jax.sharding import PartitionSpec as P

HEAD_SIZE = 64
EPSILON = 1e-06
ROPE_BASE = 1000000.0
MESH = pl.DeviceIdType.MESH
F32 = jnp.float32
BF16 = jnp.bfloat16
ANY = pl.BlockSpec(memory_space=pl.ANY)
VMEM = pl.BlockSpec(memory_space=pltpu.VMEM)
NCTX = 32
PAIRS = 4
WORKERS = 8
SLOTS = 4
BLOCK = 128
CHUNK = 512


def group(kind):
    c, t = lax.axis_index("ctx"), lax.axis_index("tp")
    h = lax.rem(c, 2)
    if kind == "ctx":
        return NCTX, c, lambda p: (p, t)
    if kind == "tp":
        return 4, t, lambda p: (c, p)
    if kind == "pair":
        return 2, h, lambda p: (c - h + p, t)
    z, x, core = c // 8, lax.rem(c // 2, 4), lax.rem(t, 2)
    if kind == "z":
        return 4, z, lambda p: (c + (p - z) * 8, t)
    if kind == "x":
        return 4, x, lambda p: (c + (p - x) * 2, t)
    if kind == "core":
        return 2, core, lambda p: (c, t - core + p)
    if kind == "near":
        return 2, t // 2, lambda p: (c, p * 2 + core)
    if kind == "ring":
        return 4, h * 2 + t // 2, lambda p: (c - h + p // 2, lax.rem(p, 2) * 2 + core)
    return 8, h * 4 + t, lambda p: (c - h + p // 4, lax.rem(p, 4))


def push(kind, src_of, dst_of, send, recv, local=False):
    n, me, dev = group(kind)

    @pl.loop(1, n)
    def _(i):
        p = lax.rem(me + i, n)
        pltpu.make_async_remote_copy(
            src_ref=src_of(p),
            dst_ref=dst_of(me),
            send_sem=send.at[p],
            recv_sem=recv.at[me],
            device_id=dev(p),
            device_id_type=MESH,
        ).start()

    if local:
        pltpu.make_async_copy(src_of(me), dst_of(me), recv.at[me]).start()


def settle(kind, src_of, dst_of, send, recv, local=False):
    n, me, dev = group(kind)

    @pl.loop(1, n)
    def _(i):
        p = lax.rem(me + i, n)
        copy = pltpu.make_async_remote_copy(
            src_ref=src_of(p),
            dst_ref=dst_of(p),
            send_sem=send.at[p],
            recv_sem=recv.at[p],
            device_id=dev(p),
            device_id_type=MESH,
        )
        copy.wait_send()
        copy.wait_recv()

    if local:
        pltpu.make_async_copy(src_of(me), dst_of(me), recv.at[me]).wait()


def stage(*moves):
    for move in moves:
        push(*move)
    for move in moves:
        settle(*move)


class Sems:
    def __init__(self, ref):
        self.ref, self.used = ref, 0

    def two(self, n):
        at = self.used
        self.used += 2 * n
        return self.ref.at[pl.ds(at, n)], self.ref.at[pl.ds(at + n, n)]


def position():
    c = lax.axis_index("ctx")
    return c // 8, lax.rem(c // 2, 4), lax.rem(c, 2)


def iota(shape, axis):
    return lax.broadcasted_iota(jnp.int32, shape, axis)


def two_parts(v):
    high = v.astype(BF16)
    return high, (v - high.astype(F32)).astype(BF16)


def exact_dot(v, pattern):
    high, low = two_parts(v)
    return jnp.dot(high, pattern, preferred_element_type=F32) + jnp.dot(
        low, pattern, preferred_element_type=F32
    )


def head_mean(v):
    n = v.shape[1]
    same = lax.div(iota((n, n), 0), HEAD_SIZE) == lax.div(iota((n, n), 1), HEAD_SIZE)
    return exact_dot(v, jnp.where(same, 1.0 / HEAD_SIZE, 0.0).astype(BF16))


def head_scale(v):
    return lax.rsqrt(head_mean(v * v) + EPSILON)


def turned(u, cosine, sine):
    half, n = HEAD_SIZE // 2, 2 * HEAD_SIZE
    first = lax.rem(iota(u.shape, 1), HEAD_SIZE) < half
    other = jnp.where(first, pltpu.roll(u, n - half, 1), pltpu.roll(u, half, 1))
    return u * cosine + other * sine


def crossed(tile):
    return pltpu.roll(tile, HEAD_SIZE, 1)


def left_lanes(tile):
    return iota(tile.shape, 1) < HEAD_SIZE


def spread_gain(pieces, row, per, lanes):
    n = pieces.shape[0]
    pick = iota((NCTX, n), 1) == iota((NCTX, n), 0) * (n // NCTX) + row
    mine = jnp.dot(pick.astype(F32).astype(BF16), pieces, preferred_element_type=F32).astype(BF16)
    pattern = (lax.rem(iota((128, lanes), 1), per) == iota((128, lanes), 0)).astype(F32)
    wide = jnp.dot(mine, pattern.astype(BF16), preferred_element_type=F32)
    owner = lax.div(lax.rem(iota(wide.shape, 1), NCTX * per), per)
    return jnp.sum(jnp.where(owner == iota(wide.shape, 0), wide, 0.0), axis=0, keepdims=True)


def owner_pieces(vector, per):
    lanes = vector.shape[1]
    shape = (NCTX, lanes)
    owner = lax.div(lax.rem(iota(shape, 1), NCTX * per), per)
    parts = jnp.where(owner == iota(shape, 0), jnp.broadcast_to(vector, shape), 0.0)
    pattern = (lax.rem(iota((lanes, 128), 0), per) == iota((lanes, 128), 1)).astype(F32)
    return exact_dot(parts, pattern.astype(BF16))


def row_scale(rows):
    return lax.rsqrt(jnp.mean(rows * rows, axis=1, keepdims=True) + EPSILON)


def twice(table):
    return jnp.concatenate([table[...], table[...]], axis=0)


def places():
    c, t = lax.axis_index("ctx"), lax.axis_index("tp")
    slot, low = c // WORKERS, lax.rem(c, WORKERS)
    to = low + lax.rem(slot, 2) * (WORKERS - 1 - 2 * low)
    return c, t, slot, low, to


def block_of(low, j):
    return j * WORKERS + (low if j % 2 == 0 else WORKERS - 1 - low)


def greet_attention(kinds):
    c, t, slot, low, to = places()
    barrier = pltpu.get_barrier_semaphore()
    total = 0
    others = [p * WORKERS + to for p in range(PAIRS)] + [block_of(low, j) for j in range(SLOTS)]
    for other in others:

        @pl.when(other != c)
        def _():
            pl.semaphore_signal(barrier, inc=1, device_id=(other, t), device_id_type=MESH)

        total = total + jnp.where(other != c, 1, 0)
    for kind in kinds:
        n, me, dev = group(kind)

        @pl.loop(1, n)
        def _(i):
            pl.semaphore_signal(
                barrier, inc=1, device_id=dev(lax.rem(me + i, n)), device_id_type=MESH
            )

        total = total + (n - 1)
    pl.semaphore_wait(barrier, total)


def to_workers(src, dst, send, recv, act):
    c, t, slot, low, to = places()
    for p in range(PAIRS):
        target = p * WORKERS + to
        far = pltpu.make_async_remote_copy(
            src_ref=src.at[p],
            dst_ref=dst.at[slot],
            send_sem=send.at[p],
            recv_sem=recv.at[slot],
            device_id=(target, t),
            device_id_type=MESH,
        )
        near = pltpu.make_async_copy(src.at[p], dst.at[slot], send.at[p])

        @pl.when(target != c)
        def _():
            far.start() if act == "start" else far.wait_send()

        @pl.when(target == c)
        def _():
            near.start() if act == "start" else near.wait()


def from_owners(src, dst, send, recv):
    c, t, slot, low, to = places()
    for j in range(SLOTS):
        owner = block_of(low, j)

        @pl.when(owner != c)
        def _():
            pltpu.make_async_remote_copy(
                src_ref=src.at[j],
                dst_ref=dst.at[j],
                send_sem=send.at[j],
                recv_sem=recv.at[j],
                device_id=(owner, t),
                device_id_type=MESH,
            ).wait_recv()


def to_owner(src, dst, send, recv, j, act):
    c, t, slot, low, to = places()
    owner = block_of(low, j)
    far = pltpu.make_async_remote_copy(
        src_ref=src.at[j],
        dst_ref=dst.at[slot],
        send_sem=send.at[j],
        recv_sem=recv.at[slot],
        device_id=(owner, t),
        device_id_type=MESH,
    )
    near = pltpu.make_async_copy(src.at[j], dst.at[slot], send.at[j])

    @pl.when(owner != c)
    def _():
        far.start() if act == "start" else far.wait_send()

    @pl.when(owner == c)
    def _():
        near.start() if act == "start" else near.wait()


def from_workers(src, dst, send, recv):
    c, t, slot, low, to = places()
    for p in range(PAIRS):
        target = p * WORKERS + to

        @pl.when(target != c)
        def _():
            pltpu.make_async_remote_copy(
                src_ref=src.at[p],
                dst_ref=dst.at[p],
                send_sem=send.at[p],
                recv_sem=recv.at[p],
                device_id=(target, t),
                device_id_type=MESH,
            ).wait_recv()


def last_dims(a, b):
    return lax.dot_general(a, b, (((1,), (1,)), ((), ())), preferred_element_type=F32)


def first_dims(a, b):
    return lax.dot_general(a, b, (((0,), (0,)), ((), ())), preferred_element_type=F32)


def causal_mask(b, i):
    shape = (2 * BLOCK, CHUNK)
    rows = lax.broadcasted_iota(jnp.int32, shape, 0)
    token = b * BLOCK + jnp.where(rows >= BLOCK, rows - BLOCK, rows)
    key = i * CHUNK + lax.broadcasted_iota(jnp.int32, shape, 1)
    return token >= key


def row_back(grads, normed, scale, gain):
    scaled = grads * gain
    return scale * (scaled - normed * jnp.mean(scaled * normed, axis=1, keepdims=True))


def summed(ref):
    total = ref[0].astype(F32)
    for k in range(1, ref.shape[0]):
        total += ref[k].astype(F32)
    return total


UNITS = 640
INPUTS = ("w_query", "w_key", "w_value", "gains", "ffn", "wo", "cot", "rows_in", "cosine", "sine")
OUTPUTS = ("qkv_grad", "ffn_all", "output_all", "input_all", "gain_tp")
SIZES = {"tp": 4, "pair": 2, "rows": 8, "z": 4, "x": 4, "core": 2, "ring": 4, "near": 2}
SEMAPHORES = 580


def scratch_arrays(rows, width, qkv_cols, out_cols):
    own, half = rows // 4, BLOCK // 2
    stack = (SLOTS, 2 * BLOCK, BLOCK)
    grid, piece = (4, 4, 2, 2), (16, qkv_cols + out_cols)
    units = (16, 3 * UNITS)
    return dict(
        w_own=((2, 16, qkv_cols), BF16),
        w_all=((*grid, 16, qkv_cols), BF16),
        gains_all=((4, 4, 2, 16, 128), BF16),
        w_ffn=((*grid, *units), BF16),
        wo_all=((*grid, 16, out_cols), BF16),
        cot_all=((2, rows, width), BF16),
        hidden=((rows, width), BF16),
        normed=((rows, width), F32),
        raw=((rows, qkv_cols), F32),
        q_src=(stack, BF16),
        kv_src=((PAIRS, 2, half, BLOCK), BF16),
        gain_attn=((1, width), F32),
        gain_ffn=((1, width), F32),
        gain_query=((1, 128), F32),
        gain_key=((1, 128), F32),
        q_buf=(stack, BF16),
        kv_buf=((*grid, half, BLOCK), BF16),
        o_buf=(stack, BF16),
        log_buf=(stack, F32),
        att=(stack, BF16),
        acc=((2 * BLOCK, BLOCK), F32),
        den=((2 * BLOCK, BLOCK), F32),
        attended=((rows, out_cols), BF16),
        parts=((2, 2, own, width), BF16),
        parts_half=((2, 2, own, width), BF16),
        parts_chip=((2, own, width), BF16),
        landed=((2, own, width), BF16),
        residual=((own, width), F32),
        hidden_own=((own, width), BF16),
        hidden_all=((4, 2, own, width), BF16),
        grad_units=((2 * rows, UNITS), F32),
        units=((2 * rows, UNITS), BF16),
        units_in=((2 * rows, 2 * UNITS), BF16),
        back=((4, 2, own, width), BF16),
        halved=((2, 4, own, width), BF16),
        chip=((4, own, width), BF16),
        ringed=((4, own, width), BF16),
        grad_bf=((own, width), BF16),
        grad_all=((2, 2, own, width), BF16),
        grad_residual=((own, width), F32),
        ffn_gain=((1, width), F32),
        grads=((*grid, *units), BF16),
        ffn_part=((8, own, width), BF16),
        ffn_parts=((8, own, width), BF16),
        far_a=((4, 4, 2, *units), BF16),
        far_b=((4, 4, 2, *units), BF16),
        mid_a=((4, 2, *units), BF16),
        mid_b=((4, 2, *units), BF16),
        mid_far_a=((4, 2, *units), BF16),
        mid_far_b=((4, 2, *units), BF16),
        end_ab=((2, 2, *units), BF16),
        do_src=(stack, BF16),
        do_buf=(stack, BF16),
        dq_buf=(stack, BF16),
        dq=(stack, BF16),
        dkv_sum=((*grid, half, BLOCK), F32),
        dkv_buf=((*grid, half, BLOCK), BF16),
        kv_one_a=((4, 4, 2, half, BLOCK), BF16),
        kv_one_b=((4, 2, 4, half, BLOCK), BF16),
        kv_sum_a=((4, 2, half, BLOCK), BF16),
        kv_sum_b=((4, 4, half, BLOCK), BF16),
        kv_two_a=((4, 2, half, BLOCK), BF16),
        kv_two_b=((4, 4, half, BLOCK), BF16),
        kv_sum=((4, 2, half, BLOCK), BF16),
        dkv=((PAIRS, 2, half, BLOCK), BF16),
        parts_back=((2, 2, own, width), BF16),
        back_half=((2, 2, own, width), BF16),
        back_chip=((2, own, width), BF16),
        landed_back=((2, own, width), BF16),
        grad_in=((rows, qkv_cols), BF16),
        gain_pieces=((4, 4, 2, 8, 128), F32),
        output=((own, width), BF16),
        input_bf=((own, width), BF16),
        qkv=((*grid, *piece), BF16),
        one_a=((4, 4, 2, *piece), BF16),
        one_b=((4, 4, 2, *piece), BF16),
        one_g=((4, 4, 2, 8, 128), F32),
        sum_a=((4, 2, *piece), BF16),
        sum_b=((4, 2, *piece), BF16),
        sum_g=((4, 2, 8, 128), F32),
        two_a=((4, 2, *piece), BF16),
        two_b=((4, 2, *piece), BF16),
        two_g=((4, 2, 8, 128), F32),
        part_a=((2, *piece), BF16),
        part_b=((2, *piece), BF16),
        part_g=((2, 8, 128), F32),
        three_a=((2, *piece), BF16),
        three_b=((2, *piece), BF16),
        three_g=((2, 8, 128), F32),
        gain_sum=((8, 128), F32),
    )


def project_keys(r):
    pieces = r.gains_all[...].reshape(NCTX * 16, 128)
    r.gain_attn[...] = spread_gain(pieces, 0, 32, r.gain_attn.shape[1])
    r.gain_query[...] = spread_gain(pieces, 2, 2, 128)
    r.gain_key[...] = spread_gain(pieces, 3, 2, 128)
    r.hidden[...] = (r.normed[...] * r.gain_attn[...]).astype(BF16)
    weights = r.w_all[:, :, :, :, :, 256:].reshape(r.hidden.shape[1], 256)
    r.raw[:, 256:] = jnp.dot(r.hidden[...], weights, preferred_element_type=F32)
    tile = r.raw[:, 256:384]
    keys = turned(tile * head_scale(tile) * r.gain_key[...], twice(r.cosine), twice(r.sine))
    values = r.raw[:, 384:512]
    for k in range(2):
        key, value = (keys, crossed(values)) if k == 0 else (crossed(keys), values)
        one = jnp.where(left_lanes(key), key, value).astype(BF16)
        for s in range(2):
            part = one[s * BLOCK : (s + 1) * BLOCK]
            r.kv_src[2 * k + s] = part.reshape(2, BLOCK // 2, 128)


def project_queries(r):
    weights = r.w_all[:, :, :, :, :, :256].reshape(r.hidden.shape[1], 256)
    r.raw[:, :256] = jnp.dot(r.hidden[...], weights, preferred_element_type=F32)
    cos, sin = twice(r.cosine), twice(r.sine)
    for k in range(2):
        tile = r.raw[:, k * 128 : k * 128 + 128]
        tile = turned(tile * head_scale(tile) * r.gain_query[...], cos, sin) * (HEAD_SIZE**-0.5)
        for a, one in enumerate((tile, crossed(tile))):
            one = jnp.where(left_lanes(one), one, 0.0).astype(BF16)
            for s in range(2):
                r.q_src[2 * k + s, a * BLOCK : (a + 1) * BLOCK] = one[s * BLOCK : (s + 1) * BLOCK]
    pieces = r.gains_all[...].reshape(NCTX * 16, 128)
    r.gain_ffn[...] = spread_gain(pieces, 1, 32, r.gain_ffn.shape[1])


def attend(r, low, j):
    b = block_of(low, j)
    r.acc[...] = jnp.zeros_like(r.acc)
    r.den[...] = jnp.zeros_like(r.den)

    def chunk(i, masked):
        kv = r.kv_buf[i // 2, pl.ds(2 * lax.rem(i, 2), 2)].reshape(CHUNK, BLOCK)
        powered = jnp.exp(last_dims(r.q_buf[j], kv))
        if masked:
            powered = jnp.where(causal_mask(b, i), powered, 0.0)
        r.den[...] += sum(powered[:, k : k + BLOCK] for k in range(0, CHUNK, BLOCK))
        r.acc[...] += jnp.dot(powered.astype(BF16), kv, preferred_element_type=F32)

    last = b // (CHUNK // BLOCK)
    pl.loop(0, last)(lambda i: chunk(i, False))
    chunk(last, True)
    total = jnp.sum(r.den[...], axis=1, keepdims=True)
    lanes = iota((2 * BLOCK, BLOCK), 1)
    r.o_buf[j] = jnp.where(lanes >= HEAD_SIZE, r.acc[...] / total, 0.0).astype(BF16)
    r.log_buf[j] = jnp.broadcast_to(jnp.log(total), (2 * BLOCK, BLOCK))


def attend_back(r, low, j):
    b = block_of(low, j)
    r.acc[...] = jnp.zeros_like(r.acc)
    delta = jnp.sum(r.do_buf[j].astype(F32) * r.o_buf[j].astype(F32), axis=1, keepdims=True)

    def chunk(i, masked):
        q, do, logs = r.q_buf[j], r.do_buf[j], r.log_buf[j]
        kv = r.kv_buf[i // 2, pl.ds(2 * lax.rem(i, 2), 2)].reshape(CHUNK, BLOCK)
        probs = jnp.exp(last_dims(q, kv) - jnp.concatenate([logs] * (CHUNK // BLOCK), axis=1))
        if masked:
            probs = jnp.where(causal_mask(b, i), probs, 0.0)
        grads = (probs * (last_dims(do, kv) - delta)).astype(BF16)
        r.acc[...] += jnp.dot(grads, kv, preferred_element_type=F32)
        update = first_dims(grads, q) + first_dims(probs.astype(BF16), do)
        at = pl.ds(2 * lax.rem(i, 2), 2)
        r.dkv_sum[i // 2, at] += update.reshape(2, 2, 2, BLOCK // 2, BLOCK)

    last = b // (CHUNK // BLOCK)
    pl.loop(0, last)(lambda i: chunk(i, False))
    chunk(last, True)
    r.dq_buf[j] = (r.acc[...] * (HEAD_SIZE**-0.5)).astype(BF16)


def tiles(m, n):
    return pl.ds(pl.multiple_of(m * n, n), n)


def both_rows(first, second):
    return jnp.concatenate([first.astype(F32), second.astype(F32)], axis=0)


def head_back(r, u, tile, gain_row):
    turn = turned(u, twice(r.cosine), -twice(r.sine))
    scale = head_scale(tile)
    hat = tile * scale
    scaled = turn * gain_row
    back = scale * (scaled - hat * head_mean(scaled * hat))
    return back.astype(BF16), jnp.sum(turn * hat, axis=0, keepdims=True)


def queries_back(r):
    query_gain = jnp.zeros((1, 128), F32)
    for k in range(2):
        first = both_rows(r.dq[2 * k, :BLOCK], r.dq[2 * k + 1, :BLOCK])
        second = crossed(both_rows(r.dq[2 * k, BLOCK:], r.dq[2 * k + 1, BLOCK:]))
        lanes = slice(k * 128, (k + 1) * 128)
        u = jnp.where(left_lanes(first), first, second)
        r.grad_in[:, lanes], part = head_back(r, u, r.raw[:, lanes], r.gain_query[...])
        query_gain = query_gain + part
    return query_gain


def keys_back(r):
    own, width = r.residual.shape
    first, second = [
        both_rows(r.dkv[2 * k].reshape(BLOCK, 128), r.dkv[2 * k + 1].reshape(BLOCK, 128))
        for k in range(2)
    ]
    left = left_lanes(first)
    u = jnp.where(left, first, crossed(second))
    r.grad_in[:, 256:384], key_gain = head_back(r, u, r.raw[:, 256:384], r.gain_key[...])
    r.grad_in[:, 384:] = jnp.where(left, crossed(first), second).astype(BF16)
    attn_gain = jnp.zeros((1, width), F32)
    weights = r.w_all[...].reshape(width, r.grad_in.shape[1])
    for q in range(4):
        at = slice(q * own, (q + 1) * own)
        back = last_dims(r.grad_in[at], weights)
        r.parts_back[q // 2, q % 2] = back.astype(BF16)
        attn_gain = attn_gain + jnp.sum(back * r.normed[at], axis=0, keepdims=True)
    return key_gain, attn_gain


def begin(moves):
    for move in moves:
        push(*move)


def finish(moves):
    for move in moves:
        settle(*move)


def whole_body(names, *refs):
    r = types.SimpleNamespace(**dict(zip(names, refs)))
    take = Sems(refs[-1])
    c, t, slot, low, to = places()
    z, x, h = position()
    core = lax.rem(t, 2)
    own, width = r.residual.shape

    def spread(kind, src_of, dst_of, local=False):
        return (kind, src_of, dst_of, *take.two(SIZES[kind]), local)

    def gathered(ref):
        second = [
            spread("x", lambda p: ref.at[z, x, :, 0], lambda q: ref.at[z, q, :, 0]),
            spread("z", lambda p: ref.at[z, x, :, 1], lambda q: ref.at[q, x, :, 1]),
        ]
        third = [
            spread("z", lambda p: ref.at[z, :, :, 0], lambda q: ref.at[q, :, :, 0]),
            spread("x", lambda p: ref.at[:, x, :, 1], lambda q: ref.at[:, q, :, 1]),
        ]
        return second, third

    loads, first = [], 0
    load_sems = take.two(4)[0]
    for k, ref in enumerate((r.w_query, r.w_key, r.w_value)):
        cols = ref.shape[2]
        at = pl.ds(first, cols)
        loads.append(pltpu.make_async_copy(ref, r.w_own.at[:, :, at], load_sems.at[k]))
        first += cols
    for load in loads:
        load.start()
    greet_attention(["z", "x", "rows"])
    for load in loads:
        load.wait()
    first = [
        spread("pair", lambda p: r.w_own, lambda q: r.w_all.at[z, x, q], True),
        spread("pair", lambda p: r.gains, lambda q: r.gains_all.at[z, x, q], True),
    ]
    late = [
        spread("pair", lambda p: r.wo, lambda q: r.wo_all.at[z, x, q], True),
        spread("pair", lambda p: r.ffn.at[p], lambda q: r.w_ffn.at[z, x, q], True),
    ]
    begin(first)
    begin(late)
    rows = r.rows_in[...].astype(F32)
    r.normed[...] = rows * row_scale(rows)
    finish(first)
    second, third = gathered(r.w_all)
    second.append(spread("x", lambda p: r.gains_all.at[z, x], lambda q: r.gains_all.at[z, q]))
    third.append(spread("z", lambda p: r.gains_all.at[z], lambda q: r.gains_all.at[q]))
    stage(*second)
    stage(*third)
    finish(late)
    out_second, out_third = gathered(r.wo_all)
    ffn_second, ffn_third = gathered(r.w_ffn)
    begin(out_second + ffn_second)
    project_keys(r)

    q_send, q_recv = take.two(SLOTS)
    near = spread("z", lambda p: r.kv_src.at[p], lambda q: r.kv_buf.at[q, x, h], True)
    push(*near)
    project_queries(r)
    to_workers(r.q_src, r.q_buf, q_send, q_recv, "start")
    settle(*near)
    kv = r.kv_buf

    def planes(k):
        return [
            spread("x", lambda p: kv.at[k, x, h, 0], lambda q: kv.at[k, q, h, 0]),
            spread("pair", lambda p: kv.at[k, x, h, 1], lambda q: kv.at[k, x, q, 1]),
        ], [
            spread("pair", lambda p: kv.at[k, :, h, 0], lambda q: kv.at[k, :, q, 0]),
            spread("x", lambda p: kv.at[k, x, :, 1], lambda q: kv.at[k, q, :, 1]),
        ]

    plane_moves = [planes(k) for k in range(4)]
    for early, _ in plane_moves:
        begin(early)
    for early, then in plane_moves:
        finish(early)
        begin(then)
    finish(out_second + ffn_second)
    begin(out_third)
    begin(ffn_third)
    cot_swap = spread("pair", lambda p: r.cot, lambda q: r.cot_all.at[q], True)
    push(*cot_swap)
    to_workers(r.q_src, r.q_buf, q_send, q_recv, "wait")
    from_owners(r.q_src, r.q_buf, q_send, q_recv)
    o_send, o_recv = take.two(SLOTS)
    for j in range(SLOTS):
        finish(plane_moves[j][1])
        attend(r, low, j)
        to_owner(r.o_buf, r.att, o_send, o_recv, j, "start")
    for j in range(SLOTS):
        to_owner(r.o_buf, r.att, o_send, o_recv, j, "wait")
    from_workers(r.o_buf, r.att, o_send, o_recv)

    for k in range(2):
        for s in range(2):
            left = crossed(r.att[2 * k + s, :BLOCK].astype(F32))
            right = r.att[2 * k + s, BLOCK:].astype(F32)
            one = jnp.where(left_lanes(left), left, right).astype(BF16)
            r.attended[s * BLOCK : (s + 1) * BLOCK, k * 128 : (k + 1) * 128] = one
    finish(out_third)
    out_full = r.wo_all[...].reshape(width, r.attended.shape[1])
    r.parts[...] = last_dims(r.attended[...], out_full).astype(BF16).reshape(r.parts.shape)
    stage(spread("core", lambda p: r.parts.at[:, p], lambda q: r.parts_half.at[q], True))
    r.parts_chip[...] = summed(r.parts_half).astype(BF16)
    stage(spread("near", lambda p: r.parts_chip.at[p], lambda q: r.landed.at[q], True))
    rows = r.rows_in[tiles(t, own)].astype(F32) + summed(r.landed)
    r.residual[...] = rows
    r.hidden_own[...] = (rows * row_scale(rows) * r.gain_ffn[...]).astype(BF16)
    ring = spread("ring", lambda p: r.hidden_own, lambda q: r.hidden_all.at[q, core], True)
    push(*ring)
    settle(*cot_swap)
    finish(ffn_third)
    w = r.w_ffn.reshape(width, 3 * UNITS)
    cot = r.cot_all.reshape(8 * own, width)

    @pl.loop(0, 4)
    def _(m):
        at = tiles(m, 2 * own)
        r.grad_units[at] = jnp.dot(cot[at], w[:, 2 * UNITS :], preferred_element_type=F32)

    settle(*ring)
    hidden = r.hidden_all
    stage(spread("core", lambda p: hidden.at[:, core], lambda q: hidden.at[:, q]))

    @pl.loop(0, 2)
    def _(m):
        at = tiles(m, 4 * own)
        some = hidden[pl.ds(2 * m, 2)].reshape(4 * own, width)
        gate = jnp.dot(some, w[:, :UNITS], preferred_element_type=F32)
        up = jnp.dot(some, w[:, UNITS : 2 * UNITS], preferred_element_type=F32)
        sigmoid = jax.nn.sigmoid(gate)
        activated = gate * sigmoid
        r.units[at] = (activated * up).astype(BF16)
        grad = r.grad_units[at]
        r.units_in[at, :UNITS] = (grad * up * sigmoid * (1.0 + gate * (1.0 - sigmoid))).astype(BF16)
        r.units_in[at, UNITS:] = (grad * activated).astype(BF16)
        step = last_dims(r.units_in[at], w[:, : 2 * UNITS]).astype(BF16)
        r.back[pl.ds(2 * m, 2)] = step.reshape(2, *r.back.shape[1:])

    both = spread("core", lambda p: r.back.at[:, p], lambda q: r.halved.at[q], True)
    push(*both)

    @pl.loop(0, 4)
    def _(m):
        step = first_dims(cot[:, tiles(m, 256)], r.units[...]).astype(BF16)
        r.grads[m, :, :, :, :, 2 * UNITS :] = step.reshape(4, 2, 2, 16, UNITS)

    settle(*both)
    r.chip[...] = summed(r.halved).astype(BF16)
    ring = spread("ring", lambda p: r.chip.at[p], lambda q: r.ringed.at[q], True)
    push(*ring)

    @pl.loop(0, 4)
    def _(m):
        some = hidden[:, :, :, tiles(m, 256)].reshape(8 * own, 256)
        step = first_dims(some, r.units_in[...]).astype(BF16)
        r.grads[m, :, :, :, :, : 2 * UNITS] = step.reshape(4, 2, 2, 16, 2 * UNITS)

    far = [
        spread("x", lambda p: r.grads.at[:, p, :, 0], lambda q: r.far_a.at[q], True),
        spread("z", lambda p: r.grads.at[p, :, :, 1], lambda q: r.far_b.at[q], True),
    ]
    begin(far)
    settle(*ring)
    total = summed(r.ringed)
    rows = r.residual[...]
    scale = row_scale(rows)
    normed = rows * scale
    cot_own = cot[tiles(h * 4 + t, own)].astype(F32)
    result = cot_own + row_back(total, normed, scale, r.gain_ffn[...])
    r.grad_bf[...] = result.astype(BF16)
    share = spread("near", lambda p: r.grad_bf, lambda q: r.grad_all.at[q, core], True)
    push(*share)
    r.grad_residual[...] = result
    r.ffn_gain[...] = jnp.sum(total * normed, axis=0, keepdims=True)

    @pl.loop(0, 2)
    def _(m):
        step = last_dims(r.units[tiles(m, 4 * own)], w[:, 2 * UNITS :]).astype(BF16)
        r.ffn_part[pl.ds(4 * m, 4)] = step.reshape(4, *r.ffn_part.shape[1:])

    settle(*share)
    grad_all = r.grad_all
    stage(spread("core", lambda p: grad_all.at[:, core], lambda q: grad_all.at[:, q]))
    grad = jnp.dot(
        r.grad_all[...].reshape(4 * own, width), out_full, preferred_element_type=F32
    )
    for k in range(2):
        for s in range(2):
            tile = grad[s * BLOCK : (s + 1) * BLOCK, k * 128 : (k + 1) * 128]
            for a, one in enumerate((crossed(tile), tile)):
                one = jnp.where(left_lanes(one), 0.0, one).astype(BF16)
                r.do_src[2 * k + s, a * BLOCK : (a + 1) * BLOCK] = one

    do_send, do_recv = take.two(SLOTS)
    to_workers(r.do_src, r.do_buf, do_send, do_recv, "start")
    ffn_rows = spread("rows", lambda p: r.ffn_part.at[p], lambda q: r.ffn_parts.at[q], True)
    push(*ffn_rows)
    r.dkv_sum[...] = jnp.zeros_like(r.dkv_sum)

    @pl.loop(0, 4)
    def _(m):
        some = r.grad_all[:, :, :, tiles(m, 256)].reshape(4 * own, 256)
        step = first_dims(some, r.attended[...]).astype(BF16)
        r.qkv[m, :, :, :, :, 256:512] = step.reshape(4, 2, 2, 16, 256)

    to_workers(r.do_src, r.do_buf, do_send, do_recv, "wait")
    from_owners(r.do_src, r.do_buf, do_send, do_recv)
    dq_send, dq_recv = take.two(SLOTS)

    def kv_first(k):
        r.dkv_buf[k] = r.dkv_sum[k].astype(BF16)
        moves = [
            spread("x", lambda p: r.dkv_buf.at[k, p, :, 0], lambda q: r.kv_one_a.at[k, q], True),
            spread("pair", lambda p: r.dkv_buf.at[k, :, p, 1], lambda q: r.kv_one_b.at[k, q], True),
        ]
        begin(moves)
        return moves

    def kv_second(k, moves):
        finish(moves)
        r.kv_sum_a[k] = summed(r.kv_one_a.at[k]).astype(BF16)
        r.kv_sum_b[k] = summed(r.kv_one_b.at[k]).astype(BF16)
        moves = [
            spread("pair", lambda p: r.kv_sum_a.at[k, p], lambda q: r.kv_two_a.at[k, q], True),
            spread("x", lambda p: r.kv_sum_b.at[k, p], lambda q: r.kv_two_b.at[k, q], True),
        ]
        begin(moves)
        return moves

    firsts, seconds = {}, []
    for j in reversed(range(SLOTS)):
        attend_back(r, low, j)
        to_owner(r.dq_buf, r.dq, dq_send, dq_recv, j, "start")
        firsts[j] = kv_first(j)
        if j + 1 in firsts:
            seconds += kv_second(j + 1, firsts[j + 1])
    finish(far)

    @pl.loop(0, 4)
    def _(m):
        for src, dst in ((r.far_a, r.mid_a), (r.far_b, r.mid_b)):
            total = src[0, m].astype(F32)
            for k in range(1, 4):
                total += src[k, m].astype(F32)
            dst[m] = total.astype(BF16)

    seconds += kv_second(0, firsts[0])
    mid = [
        spread("z", lambda p: r.mid_a.at[p], lambda q: r.mid_far_a.at[q], True),
        spread("x", lambda p: r.mid_b.at[p], lambda q: r.mid_far_b.at[q], True),
    ]
    finish(seconds)
    for k in range(4):
        r.kv_sum[k, 0] = summed(r.kv_two_a.at[k]).astype(BF16)
        r.kv_sum[k, 1] = summed(r.kv_two_b.at[k]).astype(BF16)
    kv_third = spread("z", lambda p: r.kv_sum.at[p], lambda q: r.dkv.at[q], True)
    push(*kv_third)
    begin(mid)
    for j in range(SLOTS):
        to_owner(r.dq_buf, r.dq, dq_send, dq_recv, j, "wait")
    from_workers(r.dq_buf, r.dq, dq_send, dq_recv)

    query_gain = queries_back(r)

    @pl.loop(0, 4)
    def _(m):
        step = first_dims(r.hidden[:, tiles(m, 256)], r.grad_in[:, :256]).astype(BF16)
        r.qkv[m, :, :, :, :, :256] = step.reshape(4, 2, 2, 16, 256)

    def columns(first, last):
        at = pl.ds(first, last - first)
        return [
            spread(
                "x",
                lambda p: r.qkv.at[:, p, :, 0, :, at],
                lambda q: r.one_a.at[q, :, :, :, at],
                True,
            ),
            spread(
                "z",
                lambda p: r.qkv.at[p, :, :, 1, :, at],
                lambda q: r.one_b.at[q, :, :, :, at],
                True,
            ),
        ]

    one = columns(0, 512)
    begin(one)
    settle(*kv_third)
    key_gain, attn_gain = keys_back(r)
    vectors = ((attn_gain, 32), (r.ffn_gain[...], 32), (query_gain, 2), (key_gain, 2))
    stage(spread("core", lambda p: r.parts_back.at[:, p], lambda q: r.back_half.at[q], True))
    r.back_chip[...] = summed(r.back_half).astype(BF16)
    sums = spread("near", lambda p: r.back_chip.at[p], lambda q: r.landed_back.at[q], True)
    push(*sums)

    @pl.loop(0, 4)
    def _(m):
        step = first_dims(r.hidden[:, tiles(m, 256)], r.grad_in[:, 256:]).astype(BF16)
        r.qkv[m, :, :, :, :, 512:] = step.reshape(4, 2, 2, 16, 256)

    pieces = jnp.zeros((NCTX, 8, 128), F32)
    for row, (vector, per) in enumerate(vectors):
        piece = jnp.broadcast_to(owner_pieces(vector, per)[:, None, :], pieces.shape)
        pieces = jnp.where(iota(pieces.shape, 1) == row, piece, pieces)
    r.gain_pieces[...] = pieces.reshape(r.gain_pieces.shape)
    rest = columns(512, 768)
    rest.append(spread("x", lambda p: r.gain_pieces.at[:, p], lambda q: r.one_g.at[q], True))
    begin(rest)
    one += rest
    finish(mid)
    r.end_ab[:, 0] = summed(r.mid_far_a).astype(BF16)
    r.end_ab[:, 1] = summed(r.mid_far_b).astype(BF16)
    swap = spread("pair", lambda p: r.end_ab.at[p], lambda q: r.ffn_all.at[q], True)
    push(*swap)
    settle(*ffn_rows)
    r.output[...] = (r.residual[...] + summed(r.ffn_parts)).astype(BF16)
    share = [spread("tp", lambda p: r.output, lambda q: r.output_all.at[q], True)]
    rows = r.rows_in[tiles(t, own)].astype(F32)
    scale = row_scale(rows)
    normed = rows * scale
    settle(*sums)
    result = r.grad_residual[...] + row_back(
        summed(r.landed_back), normed, scale, r.gain_attn[...]
    )
    r.input_bf[...] = result.astype(BF16)
    share.append(spread("tp", lambda p: r.input_bf, lambda q: r.input_all.at[q], True))
    begin(share)
    finish(one)
    r.sum_a[...] = summed(r.one_a).astype(BF16)
    r.sum_b[...] = summed(r.one_b).astype(BF16)
    r.sum_g[...] = summed(r.one_g)
    stage(
        spread("z", lambda p: r.sum_a.at[p], lambda q: r.two_a.at[q], True),
        spread("x", lambda p: r.sum_b.at[p], lambda q: r.two_b.at[q], True),
        spread("z", lambda p: r.sum_g.at[p], lambda q: r.two_g.at[q], True),
    )
    r.part_a[...] = summed(r.two_a).astype(BF16)
    r.part_b[...] = summed(r.two_b).astype(BF16)
    r.part_g[...] = summed(r.two_g)
    stage(
        spread("pair", lambda p: r.part_a.at[p], lambda q: r.three_a.at[q], True),
        spread("pair", lambda p: r.part_b.at[p], lambda q: r.three_b.at[q], True),
        spread("pair", lambda p: r.part_g.at[p], lambda q: r.three_g.at[q], True),
    )
    r.gain_sum[...] = summed(r.three_g)
    share.append(spread("tp", lambda p: r.gain_sum, lambda q: r.gain_tp.at[q], True))
    push(*share[-1])
    r.qkv_grad[0] = summed(r.three_a)
    r.qkv_grad[1] = summed(r.three_b)
    finish(share)
    settle(*swap)


def whole(w_query, w_key, w_value, gains, ffn, wo, cot, rows_in, cosine, sine):
    rows, width = rows_in.shape
    cols = w_query.shape[2] + w_key.shape[2] + w_value.shape[2]
    arrays = scratch_arrays(rows, width, cols, wo.shape[2])
    names = INPUTS + OUTPUTS + tuple(arrays)
    return pl.pallas_call(
        functools.partial(whole_body, names),
        out_shape=[
            jax.ShapeDtypeStruct((2, 16, cols + wo.shape[2]), F32),
            jax.ShapeDtypeStruct(ffn.shape, BF16),
            jax.ShapeDtypeStruct((4, rows // 4, width), BF16),
            jax.ShapeDtypeStruct((4, rows // 4, width), BF16),
            jax.ShapeDtypeStruct((4, 8, 128), F32),
        ],
        in_specs=[ANY] * 7 + [VMEM] * 3,
        out_specs=[VMEM] + [ANY] * 4,
        scratch_shapes=[pltpu.VMEM(shape, dtype) for shape, dtype in arrays.values()]
        + [pltpu.SemaphoreType.DMA((SEMAPHORES,))],
        compiler_params=pltpu.CompilerParams(
            collective_id=1, has_side_effects=True, vmem_limit_bytes=60 * 2**20
        ),
        name="block",
    )(w_query, w_key, w_value, gains, ffn, wo, cot, rows_in, cosine, sine)


def rope_tables(tokens, offset):
    half = HEAD_SIZE // 2
    inverse = ROPE_BASE ** (-(jnp.arange(half, dtype=F32) * 2.0 / HEAD_SIZE))
    steps = (offset + jnp.arange(tokens, dtype=jnp.int32)).astype(F32)
    angles = steps[:, None] * jnp.tile(inverse, 4)[None, :]
    signs = jnp.where(jnp.arange(4 * half) % HEAD_SIZE < half, -1.0, 1.0)
    return jnp.cos(angles), jnp.sin(angles) * signs[None, :]


def halves(*weights):
    rows, cols = weights[0].shape
    w = jnp.stack(weights).reshape(len(weights), rows, 2, cols // 2)
    w = jnp.pad(w, ((0, 0), (0, 0), (0, 0), (0, UNITS - cols // 2)))
    return w.transpose(2, 1, 0, 3).reshape(2, rows, len(weights) * UNITS)


def local(
    block_input, cotangent, w_query, key_weight, w_value, w_out, w_gate, w_up, w_down,
    norm_gains, head_gains,
):
    seqs, tokens, width = block_input.shape
    rows = seqs * tokens
    unit_half = w_gate.shape[1] // 2
    rows_in = block_input.reshape(rows, width)
    cot_rows = cotangent.reshape(rows, width)
    cosine, sine = rope_tables(tokens, lax.axis_index("ctx") * tokens)
    gains = jnp.pad(norm_gains, ((0, 14), (0, 96))) + jnp.pad(head_gains, ((2, 12), (0, 126)))
    ffn = halves(w_gate, w_up, w_down)
    qkv_grad, pair_grads, output_all, input_all, gain_tp = whole(
        *(w.reshape(2, 16, w.shape[1]) for w in (w_query, key_weight, w_value)),
        gains,
        ffn.reshape(2, 2, 16, ffn.shape[2]),
        w_out.reshape(2, 16, w_out.shape[1]),
        cot_rows,
        rows_in,
        cosine,
        sine,
    )
    pair_grads = pair_grads.reshape(ffn.shape)
    pair_grads = pair_grads.astype(F32)
    gain_sum = jnp.sum(gain_tp, axis=0)
    qkv_grad = qkv_grad.reshape(32, 768)

    def joined(first):
        last = first + unit_half
        return jnp.concatenate([pair_grads[0, :, first:last], pair_grads[1, :, first:last]], axis=1)

    gate_grad, up_grad, down_grad = joined(0), joined(UNITS), joined(2 * UNITS)
    return (
        output_all.reshape(seqs, tokens, width),
        input_all.astype(F32).reshape(seqs, tokens, width),
        qkv_grad[:, :256],
        qkv_grad[:, 512:640],
        qkv_grad[:, 640:],
        qkv_grad[:, 256:512],
        gate_grad,
        up_grad,
        down_grad,
        gain_sum[0:2, :32],
        gain_sum[2:4, :2],
    )


def solution(mesh):
    tokens, weights = P(None, "ctx", None), P("ctx", "tp")
    return jax.shard_map(
        local,
        mesh=mesh,
        in_specs=(tokens,) * 2 + (weights,) * 7 + (P(None, "ctx"),) * 2,
        out_specs=(tokens,) * 2 + (weights,) * 7 + (P(None, "ctx"),) * 2,
        check_vma=False,
    )
```
